32 devices in a mesh: section: 2 (over core), seq: 8 (over z, x), traj: 2 (over y).
Axes of the slice: x: 2, y: 2, z: 4, core: 2. Of those that a mesh axis runs over, the one named last changes fastest.
Arguments:
- tokens: bfloat16 [2048, 2048], P(('traj', 'seq')), parts along dimension 0, may hold values from -6 to 6
- norm_gain: float32 [2, 2048], P('section'), may hold values from 0.25 to 1.75
- w_qkv: bfloat16 [2, 2048, 3072], P('section'), may hold values from -0.125 to 0.125
- w_rate: bfloat16 [2, 2048, 16], P('section'), may hold values from -0.125 to 0.125
- rate_base: float32 [2, 16], P('section'), may hold values from 0.0125 to 0.015625
- init_state: float32 [2, 16, 64, 64], P('section'), may hold values from -6 to 6
- w_out: bfloat16 [2, 1024, 2048], P('section'), may hold values from -0.1875 to 0.1875
Outputs:
- layer_out: bfloat16 [2, 2048, 2048], P('section', ('traj', 'seq')), parts along dimension 1
The draws below stay inside these ranges and needn't reach their ends.
There are 2 independent parts, one for each index of `traj`. The reference program is written for one: setup_inputs(seed, part) draws one part's arguments, and reference() takes and returns one part's arrays. A program takes and returns all parts, laid end to end along the dimension named above; an argument that names none is the same for every part. Nothing has to cross between parts.
All inputs are finite; a program needn't handle non-finite values.
Results may differ from the reference program's by a relative error of at most 0.017.
Values may be sent and summed in bfloat16 or wider, within the bound.
No kernel may reach another device: no remote copies, remote signals or barrier semaphores. Data moves between devices by JAX's collectives and lax.ppermute only.
A program may use at most 128 MiB of HBM per device.

```python
import math
import jax
import jax.numpy as jnp
from jax import lax

D = 2048
HEADS = 16
HD = 64
MB = 64
LAYERS = 2
TOKENS = 1024


def steps_of(own_key, shape, cuts, least, top_value):
    level, own = 1.0, jax.random.fold_in(own_key, 6)
    for position, parts in cuts:
        heights = jnp.exp(jax.random.uniform(jax.random.fold_in(own, position), (parts,), jnp.float32, least / len(cuts), top_value / len(cuts)))
        level = level * jnp.repeat(heights, shape[position] // parts).reshape([-1 if axis == position else 1 for axis in range(len(shape))])
    return level


def gaussian(rng, extent, deviation, bound, pieces=(), kind=jnp.bfloat16):
    drawn = deviation * jax.random.normal(rng, extent, jnp.float32)
    if pieces:
        drawn = drawn * steps_of(rng, extent, pieces, -0.22, 0.18)
    return jnp.clip(drawn, -bound, bound).astype(kind)


def setup_inputs(seed: int = 0, part: int = 0) -> dict:
    streams_of = jax.random.split(jax.random.key(seed), 8)
    part_splits = jax.random.split(jax.random.fold_in(streams_of[7], part), 8)
    return {
        "tokens": gaussian(part_splits[0], (TOKENS, D), 1.0, 6.0, ((0, 8),)),
        "norm_gain": jnp.clip(1.0 + 0.15 * jax.random.normal(streams_of[1], (LAYERS, D), jnp.float32), 0.25, 1.75),
        "w_qkv": gaussian(streams_of[2], (LAYERS, D, 3 * HEADS * HD), D ** -0.5, 0.125, ((0, 2),)),
        "w_rate": gaussian(streams_of[3], (LAYERS, D, HEADS), D ** -0.5, 0.125, ((0, 2),)),
        "rate_base": jnp.clip(jnp.exp(math.log(0.015625) - 0.22314354 * jax.random.uniform(streams_of[4], (LAYERS, HEADS), jnp.float32) ** steps_of(streams_of[4], (LAYERS, HEADS), ((0, 2),), -0.2, 0.2)), 0.0125, 0.015625),
        "init_state": gaussian(streams_of[5], (LAYERS, HEADS, HD, HD), 1.0, 6.0, ((0, 2),), jnp.float32),
        "w_out": gaussian(streams_of[6], (LAYERS, HEADS * HD, D), (HEADS * HD) ** -0.5, 0.1875, ((0, 2),)),
    }


def inner_block(weight_state, block):
    precise_mode = lax.Precision.HIGHEST
    query_rows, key_input, value_input, rates = block
    predicted_values = jnp.einsum('ylc,yci->yli', key_input, weight_state, precision=precise_mode)
    scaled_gradient = rates[..., None] * (predicted_values - value_input)
    causal_mask = jnp.tril(jnp.ones((query_rows.shape[1], query_rows.shape[1]), query_rows.dtype))
    attention_scores = jnp.einsum('kxw,kqw->kxq', query_rows, key_input, precision=precise_mode) * causal_mask
    inner_output = jnp.einsum('ylc,yci->yli', query_rows, weight_state, precision=precise_mode) - jnp.einsum('ixb,ibt->ixt', attention_scores, scaled_gradient, precision=precise_mode)
    updated_state = weight_state - jnp.einsum('ncz,ncp->nzp', key_input, scaled_gradient, precision=precise_mode)
    return (updated_state, inner_output)

def inner_inputs(hidden, gain, w_qkv, w_rate, rate_base):
    wide = hidden.astype(jnp.float32)
    mean_sq = lax.optimization_barrier(jnp.mean(wide * wide, axis=-1, keepdims=True))
    normed = (wide * lax.rsqrt(mean_sq + 1e-06) * gain).astype(jnp.bfloat16)
    projected = jnp.dot(normed, w_qkv, preferred_element_type=jnp.float32)
    rows = hidden.shape[0]
    heads = rate_base.shape[0]
    width = heads * HD
    query_rows = projected[:, :width].reshape(rows, heads, HD)
    key_input = projected[:, width:2 * width].reshape(rows, heads, HD)
    value_input = projected[:, 2 * width:].reshape(rows, heads, HD)
    query_rows = query_rows * lax.rsqrt(lax.optimization_barrier(jnp.sum(query_rows * query_rows, axis=-1, keepdims=True)) + 1e-06)
    key_input = key_input * lax.rsqrt(lax.optimization_barrier(jnp.sum(key_input * key_input, axis=-1, keepdims=True)) + 1e-06)
    rates = rate_base[None, :] * jax.nn.sigmoid(jnp.dot(normed, w_rate, preferred_element_type=jnp.float32))
    blocks = rows // MB

    def to_blocks(array):
        return array.reshape(blocks, MB, heads, HD).transpose(0, 2, 1, 3)
    rate_blocks = rates.reshape(blocks, MB, heads).transpose(0, 2, 1)
    return (to_blocks(query_rows), to_blocks(key_input), to_blocks(value_input), rate_blocks)

def reference(tokens, norm_gain, w_qkv, w_rate, rate_base, init_state, w_out):
    hidden = tokens
    outputs = []
    for layer_index in range(LAYERS):
        blocks = inner_inputs(hidden, norm_gain[layer_index], w_qkv[layer_index], w_rate[layer_index], rate_base[layer_index])
        final_state, inner_output = lax.scan(inner_block, init_state[layer_index], blocks)
        rows = hidden.shape[0]
        inner_bf = inner_output.transpose(0, 2, 1, 3).reshape(rows, -1).astype(jnp.bfloat16)
        mixed = jnp.dot(inner_bf, w_out[layer_index], preferred_element_type=jnp.float32)
        hidden = (hidden.astype(jnp.float32) + mixed).astype(jnp.bfloat16)
        outputs.append(hidden)
    return jnp.stack(outputs)
```

```python
import functools

import jax
import jax.numpy as jnp
from jax import lax
from jax.experimental import pallas as pl
from jax.experimental.pallas import tpu as pltpu
from jax.sharding import PartitionSpec as P

HD = 64
PAIR = 2 * HD
QUAD = 4 * HD
F32 = jnp.float32
BF16 = jnp.bfloat16
EPS = 1e-6
VMEM_LIMIT = 28 * 1024 * 1024


def mm(a, b):
    return jnp.dot(a, b, preferred_element_type=F32)


def mm_nt(a, b):
    return lax.dot_general(a, b, (((1,), (1,)), ((), ())), preferred_element_type=F32)


def mm_tn(a, b):
    return lax.dot_general(a, b, (((0,), (0,)), ((), ())), preferred_element_type=F32)


def head_masks(rows, lanes):
    lane = lax.broadcasted_iota(jnp.int32, (rows, lanes), 1)
    return [lane // HD == index for index in range(lanes // HD)]


def spread(value):
    zero = jnp.zeros_like(value)
    masks = head_masks(*value.shape)
    return jnp.concatenate([jnp.where(mask, value, zero) for mask in masks], axis=0)


def spread_two(left, right):
    return jnp.concatenate([spread(left), spread(right)], axis=1)


def diagonal(product):
    first = lax.broadcasted_iota(jnp.int32, (HD, PAIR), 1) < HD
    return jnp.where(first, product[:HD], product[HD:])


def head_ones():
    row = lax.broadcasted_iota(jnp.int32, (QUAD, QUAD), 0) // HD
    lane = lax.broadcasted_iota(jnp.int32, (QUAD, QUAD), 1) // HD
    return jnp.where(row == lane, 1.0, 0.0).astype(BF16)


def unit_heads(value, ones):
    squares = mm((value * value).astype(BF16), ones)
    return value * lax.rsqrt(squares + EPS)


def norm_rows(hidden, gain):
    wide = hidden.astype(F32)
    mean_sq = jnp.mean(wide * wide, axis=-1, keepdims=True)
    return (wide * lax.rsqrt(mean_sq + EPS) * gain).astype(BF16)


def spread_rates(normed, w_rate, rate_base):
    rates = rate_base * jax.nn.sigmoid(mm(normed, w_rate))
    high = rates.astype(BF16)
    low = (rates - high.astype(F32)).astype(BF16)
    heads = rates.shape[1]
    row = lax.broadcasted_iota(jnp.int32, (heads, heads * HD), 0)
    lane = lax.broadcasted_iota(jnp.int32, (heads, heads * HD), 1) // HD
    pick = jnp.where(row == lane, 1.0, 0.0).astype(BF16)
    return mm(high, pick) + mm(low, pick)


def slab_maps(normed, rates, wkv, wait_group, keys_out, x_out, y_out, maps, lw):
    width = keys_out.shape[1]
    ones = head_ones()
    per_pair = PAIR // lw
    for quad in range(width // QUAD):
        wait_group(quad)
        lanes = slice(quad * QUAD, (quad + 1) * QUAD)
        keys = mm(normed, wkv[:, lanes])
        values = mm(normed, wkv[:, width + quad * QUAD : width + (quad + 1) * QUAD])
        keys = unit_heads(keys, ones)
        keys_bf = keys.astype(BF16)
        rate = rates[:, lanes]
        rated_keys = rate * keys
        rated_values = rate * values
        keys_out[:, lanes] = keys_bf
        for half in range(2):
            pair = quad * 2 + half
            own = slice(half * PAIR, (half + 1) * PAIR)
            first, second = keys_bf[:HD, own], keys_bf[HD:, own]
            x_first = rated_keys[:HD, own]
            y_first = rated_values[:HD, own]
            cross = mm_nt(second, spread(first)).astype(BF16)
            fix = mm(cross, spread_two(x_first.astype(BF16), y_first.astype(BF16)))
            x_second = rated_keys[HD:, own] - rate[HD:, own] * fix[:, :PAIR]
            y_second = rated_values[HD:, own] - rate[HD:, own] * fix[:, PAIR:]
            x_all = jnp.concatenate([x_first, x_second], axis=0).astype(BF16)
            y_all = jnp.concatenate([y_first, y_second], axis=0).astype(BF16)
            place = slice(pair * PAIR, (pair + 1) * PAIR)
            x_out[:, place] = x_all
            y_out[:, place] = y_all
            both = mm_tn(keys_bf[:, own], jnp.concatenate([x_all, y_all], axis=1))
            s_map = diagonal(both[:, :PAIR])
            b_map = diagonal(both[:, PAIR:])
            for part in range(per_pair):
                cut = slice(part * lw, (part + 1) * lw)
                maps[pair * per_pair + part] = jnp.concatenate([s_map[:, cut], b_map[:, cut]], axis=1).astype(BF16)


def place_out(refs, table, count):
    me = lax.axis_index("seq")
    for step, ref in enumerate(refs):
        ref[...] = table[lax.rem(me + step, count)]


def place_in(refs, table, count):
    me = lax.axis_index("seq")
    for step, ref in enumerate(refs):
        table[lax.rem(me + count - step, count)] = ref[...]


def first_front(count, lw, h_ref, gain_ref, w_hbm, w_rate_ref, base_ref, *rest):
    outs = rest[:count]
    wkv, normed_out, keys_out, x_out, y_out, maps, sems = rest[count:]
    width = keys_out.shape[1]
    quads = width // QUAD

    def copies(quad):
        made = []
        for side in range(2):
            made.append(
                pltpu.make_async_copy(
                    w_hbm.at[0, :, pl.ds((side + 1) * width + quad * QUAD, QUAD)],
                    wkv.at[:, pl.ds(side * width + quad * QUAD, QUAD)],
                    sems.at[quad, side],
                )
            )
        return made

    for quad in range(quads):
        for copy in copies(quad):
            copy.start()

    def wait_group(quad):
        for copy in copies(quad):
            copy.wait()

    @pl.when(lax.axis_index("section") == 0)
    def _():
        normed = norm_rows(h_ref[...], gain_ref[...])
        normed_out[...] = normed
        rates = spread_rates(normed, w_rate_ref[0], base_ref[...])
        slab_maps(normed, rates, wkv, wait_group, keys_out, x_out, y_out, maps, lw)
        place_out(outs, maps, count)

    @pl.when(lax.axis_index("section") != 0)
    def _():
        for quad in range(quads):
            wait_group(quad)


def read_out(normed, wq, wait_group, keys_ref, x_ref, y_ref, qo_out):
    rows, width = keys_ref.shape
    ones = head_ones()
    row = lax.broadcasted_iota(jnp.int32, (rows, 2 * rows), 0)
    lane = lax.rem(lax.broadcasted_iota(jnp.int32, (rows, 2 * rows), 1), rows)
    causal = row >= lane
    for quad in range(width // QUAD):
        wait_group(quad)
        queries = unit_heads(mm(normed, wq[:, quad * QUAD : (quad + 1) * QUAD]), ones)
        queries_bf = queries.astype(BF16)
        for half in range(2):
            own = slice(half * PAIR, (half + 1) * PAIR)
            place = slice(quad * QUAD + half * PAIR, quad * QUAD + (half + 1) * PAIR)
            scores = mm_nt(queries_bf[:, own], spread(keys_ref[:, place]))
            scores = jnp.where(causal, scores, 0.0).astype(BF16)
            both = mm(scores, spread_two(x_ref[:, place], y_ref[:, place]))
            qo_out[:, place] = (queries[:, own] - both[:, :PAIR]).astype(BF16)
            qo_out[:, width + place.start : width + place.stop] = both[:, PAIR:].astype(BF16)


def first_reads(normed_ref, keys_ref, x_ref, y_ref, w_hbm, qo_out, wq, sems):
    width = keys_ref.shape[1]
    quads = width // QUAD

    def copy(quad):
        return pltpu.make_async_copy(
            w_hbm.at[0, :, pl.ds(quad * QUAD, QUAD)], wq.at[:, pl.ds(quad * QUAD, QUAD)], sems.at[quad]
        )

    for quad in range(quads):
        copy(quad).start()

    @pl.when(lax.axis_index("section") == 0)
    def _():
        read_out(normed_ref[...], wq, lambda quad: copy(quad).wait(), keys_ref, x_ref, y_ref, qo_out)

    @pl.when(lax.axis_index("section") != 0)
    def _():
        for quad in range(quads):
            copy(quad).wait()


def later_reads(normed_ref, keys_ref, x_ref, y_ref, wq, qo_out):
    @pl.when(lax.axis_index("section") == 1)
    def _():
        read_out(normed_ref[...], wq, lambda quad: None, keys_ref, x_ref, y_ref, qo_out)


def relay(count, lw, active, *refs):
    pieces = refs[:count]
    init_ref = refs[count]
    outs = refs[count + 1 : 2 * count + 1]
    table, states = refs[2 * count + 1 :]

    @pl.when(lax.axis_index("section") == active)
    def _():
        place_in(pieces, table, count)
        heads = lw // HD
        me = lax.axis_index("seq")
        state = jnp.concatenate([init_ref[0, me * heads + index] for index in range(heads)], axis=1)
        states[0] = state.astype(BF16)
        for slab in range(count - 1):
            step = table[slab]
            state = state - mm(step[:, :lw], spread(state.astype(BF16))) + step[:, lw:].astype(F32)
            states[slab + 1] = state.astype(BF16)
        place_out(outs, states, count)


def finish(pieces, table, qo_ref, w_out, h_ref, count, lw):
    place_in(pieces, table, count)
    width = qo_ref.shape[1] // 2
    per_quad = QUAD // lw
    parts = []
    for quad in range(width // QUAD):
        lanes = slice(quad * QUAD, (quad + 1) * QUAD)
        state = jnp.concatenate([table[quad * per_quad + index] for index in range(per_quad)], axis=1)
        inner = mm(qo_ref[:, lanes], spread(state)) + qo_ref[:, width + quad * QUAD : width + (quad + 1) * QUAD].astype(F32)
        parts.append(inner.astype(BF16))
    inner_bf = jnp.concatenate(parts, axis=1)
    return (h_ref[...].astype(F32) + mm(inner_bf, w_out)).astype(BF16)


def later_front(count, lw, *refs):
    pieces = refs[:count]
    qo_ref, w_out_ref, h_ref, gain_ref, wkv, w_rate_ref, base_ref = refs[count : count + 7]
    outs = refs[count + 7 : 2 * count + 7]
    h_out, normed_out, keys_out, x_out, y_out, table, maps = refs[2 * count + 7 :]

    @pl.when(lax.axis_index("section") == 1)
    def _():
        result = finish(pieces, table, qo_ref, w_out_ref[...], h_ref, count, lw)
        h_out[...] = result
        normed = norm_rows(result, gain_ref[...])
        normed_out[...] = normed
        rates = spread_rates(normed, w_rate_ref[0], base_ref[...])
        slab_maps(normed, rates, wkv, lambda quad: None, keys_out, x_out, y_out, maps, lw)
        place_out(outs, maps, count)


def last_finish(count, lw, *refs):
    pieces = refs[:count]
    qo_ref, w_out_ref, h_ref, back_ref, out_ref, table = refs[count:]

    @pl.when(lax.axis_index("section") == 1)
    def _():
        out_ref[0] = finish(pieces, table, qo_ref, w_out_ref[0], h_ref, count, lw)

    @pl.when(lax.axis_index("section") == 0)
    def _():
        out_ref[0] = back_ref[...]


def call(body, outs, scratch, args, kinds=None, name=None):
    specs = [pl.BlockSpec(memory_space=kind) for kind in (kinds or [pltpu.VMEM] * len(args))]
    return pl.pallas_call(
        body,
        out_shape=outs,
        in_specs=specs,
        out_specs=[pl.BlockSpec(memory_space=pltpu.VMEM)] * len(outs),
        scratch_shapes=scratch,
        compiler_params=pltpu.CompilerParams(vmem_limit_bytes=VMEM_LIMIT),
        name=name,
    )(*args)


def exchange(pieces, source, target, count):
    received = []
    for step, piece in enumerate(pieces):
        if step == 0 and source == target:
            received.append(piece)
            continue
        pairs = [(source * count + place, target * count + (place + step) % count) for place in range(count)]
        received.append(lax.ppermute(piece, ("section", "seq"), pairs))
    return received


def shards(tokens, norm_gain, w_qkv, w_rate, rate_base, init_state, w_out):
    count = lax.axis_size("seq")
    heads = rate_base.shape[1]
    lw = heads // count * HD
    rows, model = tokens.shape
    width = heads * HD
    depth = w_qkv.shape[1]
    quads = width // QUAD
    shape = jax.ShapeDtypeStruct
    in_vmem = functools.partial(pltpu.with_memory_space_constraint, memory_space=pltpu.VMEM)
    pieces_out = [shape((HD, 2 * lw), BF16)] * count
    states_out = [shape((HD, lw), BF16)] * count
    rows_out = [shape((rows, model), BF16)] + [shape((rows, width), BF16)] * 3
    maps = pltpu.VMEM((count, HD, 2 * lw), BF16)
    states = pltpu.VMEM((count, HD, lw), BF16)

    w_out_first = lax.ppermute(w_out[0], "section", [(0, 1)])

    done = call(
        functools.partial(first_front, count, lw),
        pieces_out + [pltpu.VMEM((depth, 2 * width), BF16)] + rows_out,
        [maps, pltpu.SemaphoreType.DMA((quads, 2))],
        [tokens, norm_gain, w_qkv, w_rate, rate_base],
        [pltpu.VMEM, pltpu.VMEM, pl.ANY, pltpu.VMEM, pltpu.VMEM],
        name="first_front",
    )
    pieces, (wkv, normed, keys, x_all, y_all) = done[:count], done[count:]
    received = exchange(pieces, 0, 0, count)
    reads, wq = call(
        first_reads,
        [shape((rows, 2 * width), BF16), pltpu.VMEM((depth, width), BF16)],
        [pltpu.SemaphoreType.DMA((quads,))],
        [normed, keys, x_all, y_all, w_qkv],
        [pltpu.VMEM] * 4 + [pl.ANY],
        name="first_reads",
    )
    reads = lax.ppermute(reads, "section", [(0, 1)])
    begun = call(functools.partial(relay, count, lw, 0), states_out, [maps, states], received + [init_state], name="relay0")
    received = exchange(begun, 0, 1, count)

    done = call(
        functools.partial(later_front, count, lw),
        pieces_out + [shape((rows, model), BF16)] + rows_out,
        [states, maps],
        received + [reads, w_out_first, tokens, norm_gain, in_vmem(wkv), w_rate, rate_base],
        name="later_front",
    )
    pieces, (hidden, normed, keys, x_all, y_all) = done[:count], done[count:]
    received = exchange(pieces, 1, 1, count)
    back = lax.ppermute(hidden, "section", [(1, 0)])
    (reads,) = call(
        later_reads,
        [shape((rows, 2 * width), BF16)],
        [],
        [normed, keys, x_all, y_all, in_vmem(wq)],
        name="later_reads",
    )
    begun = call(functools.partial(relay, count, lw, 1), states_out, [maps, states], received + [init_state], name="relay1")
    received = exchange(begun, 1, 1, count)
    (result,) = call(
        functools.partial(last_finish, count, lw),
        [shape((1, rows, model), BF16)],
        [states],
        received + [reads, w_out, hidden, back],
        name="last_finish",
    )
    return result


def solution(mesh):
    return jax.shard_map(
        shards,
        mesh=mesh,
        in_specs=(
            P(("traj", "seq"), None),
            P("section", None),
            P("section", None, None),
            P("section", None, None),
            P("section", None),
            P("section", None, None, None),
            P("section", None, None),
        ),
        out_specs=P("section", ("traj", "seq"), None),
        check_vma=False,
    )
```

```python
import functools

import jax
import jax.numpy as jnp
from jax import lax
from jax.experimental import pallas as pl
from jax.experimental.pallas import tpu as pltpu
from jax.sharding import PartitionSpec as P

HD = 64
PAIR = 2 * HD
QUAD = 4 * HD
F32 = jnp.float32
BF16 = jnp.bfloat16
EPS = 1e-6
VMEM_LIMIT = 28 * 1024 * 1024


def mm(a, b):
    return jnp.dot(a, b, preferred_element_type=F32)


def mm_nt(a, b):
    return lax.dot_general(a, b, (((1,), (1,)), ((), ())), preferred_element_type=F32)


def mm_tn(a, b):
    return lax.dot_general(a, b, (((0,), (0,)), ((), ())), preferred_element_type=F32)


def head_masks(rows, lanes):
    lane = lax.broadcasted_iota(jnp.int32, (rows, lanes), 1)
    return [lane // HD == index for index in range(lanes // HD)]


def spread(value):
    zero = jnp.zeros_like(value)
    masks = head_masks(*value.shape)
    return jnp.concatenate([jnp.where(mask, value, zero) for mask in masks], axis=0)


def spread_two(left, right):
    return jnp.concatenate([spread(left), spread(right)], axis=1)


def diagonal(product):
    first = lax.broadcasted_iota(jnp.int32, (HD, PAIR), 1) < HD
    return jnp.where(first, product[:HD], product[HD:])


def head_ones():
    row = lax.broadcasted_iota(jnp.int32, (QUAD, QUAD), 0) // HD
    lane = lax.broadcasted_iota(jnp.int32, (QUAD, QUAD), 1) // HD
    return jnp.where(row == lane, 1.0, 0.0).astype(BF16)


def unit_heads(value, ones):
    squares = mm((value * value).astype(BF16), ones)
    return value * lax.rsqrt(squares + EPS)


def norm_rows(hidden, gain):
    wide = hidden.astype(F32)
    mean_sq = jnp.mean(wide * wide, axis=-1, keepdims=True)
    return (wide * lax.rsqrt(mean_sq + EPS) * gain).astype(BF16)


def spread_rates(normed, w_rate, rate_base):
    rates = rate_base * jax.nn.sigmoid(mm_nt(normed, w_rate))
    high = rates.astype(BF16)
    low = (rates - high.astype(F32)).astype(BF16)
    heads = rates.shape[1]
    row = lax.broadcasted_iota(jnp.int32, (heads, heads * HD), 0)
    lane = lax.broadcasted_iota(jnp.int32, (heads, heads * HD), 1) // HD
    pick = jnp.where(row == lane, 1.0, 0.0).astype(BF16)
    return mm(high, pick) + mm(low, pick)


def slab_maps(normed, rates, wkv, wait_group, keys_out, x_out, y_out, maps, lw):
    width = keys_out.shape[1]
    ones = head_ones()
    per_pair = PAIR // lw
    for quad in range(width // QUAD):
        wait_group(quad)
        lanes = slice(quad * QUAD, (quad + 1) * QUAD)
        keys = mm(normed, wkv[:, lanes])
        values = mm(normed, wkv[:, width + quad * QUAD : width + (quad + 1) * QUAD])
        keys = unit_heads(keys, ones)
        keys_bf = keys.astype(BF16)
        rate = rates[:, lanes]
        rated_keys = rate * keys
        rated_values = rate * values
        keys_out[:, lanes] = keys_bf
        for half in range(2):
            pair = quad * 2 + half
            own = slice(half * PAIR, (half + 1) * PAIR)
            first, second = keys_bf[:HD, own], keys_bf[HD:, own]
            x_first = rated_keys[:HD, own]
            y_first = rated_values[:HD, own]
            cross = mm_nt(second, spread(first)).astype(BF16)
            fix = mm(cross, spread_two(x_first.astype(BF16), y_first.astype(BF16)))
            x_second = rated_keys[HD:, own] - rate[HD:, own] * fix[:, :PAIR]
            y_second = rated_values[HD:, own] - rate[HD:, own] * fix[:, PAIR:]
            x_all = jnp.concatenate([x_first, x_second], axis=0).astype(BF16)
            y_all = jnp.concatenate([y_first, y_second], axis=0).astype(BF16)
            place = slice(pair * PAIR, (pair + 1) * PAIR)
            x_out[:, place] = x_all
            y_out[:, place] = y_all
            both = mm_tn(keys_bf[:, own], jnp.concatenate([x_all, y_all], axis=1))
            s_map = diagonal(both[:, :PAIR])
            b_map = diagonal(both[:, PAIR:])
            for part in range(per_pair):
                cut = slice(part * lw, (part + 1) * lw)
                maps[pair * per_pair + part] = jnp.concatenate([s_map[:, cut], b_map[:, cut]], axis=1).astype(BF16)


def first_front(lw, h_hbm, gain_hbm, w_hbm, w_rate_hbm, base_hbm, maps, wkv, normed_out, keys_out, x_out, y_out, h_ref, gain_ref, w_rate_ref, base_ref, small_sems, sems):
    width = keys_out.shape[1]
    quads = width // QUAD
    small = [
        pltpu.make_async_copy(source, target, small_sems.at[index])
        for index, (source, target) in enumerate(
            [(h_hbm, h_ref), (gain_hbm, gain_ref), (w_rate_hbm, w_rate_ref), (base_hbm, base_ref)]
        )
    ]

    def copies(quad):
        return [
            pltpu.make_async_copy(
                w_hbm.at[0, :, pl.ds((side + 1) * width + quad * QUAD, QUAD)],
                wkv.at[:, pl.ds(side * width + quad * QUAD, QUAD)],
                sems.at[quad, side],
            )
            for side in range(2)
        ]

    for copy in small:
        copy.start()
    for quad in range(quads):
        for copy in copies(quad):
            copy.start()

    def wait_group(quad):
        for copy in copies(quad):
            copy.wait()

    for copy in small:
        copy.wait()

    @pl.when(lax.axis_index("section") == 0)
    def _():
        normed = norm_rows(h_ref[...], gain_ref[...])
        normed_out[...] = normed
        rates = spread_rates(normed, w_rate_ref[0], base_ref[...])
        slab_maps(normed, rates, wkv, wait_group, keys_out, x_out, y_out, maps, lw)

    @pl.when(lax.axis_index("section") != 0)
    def _():
        for quad in range(quads):
            wait_group(quad)


def read_out(normed, wq, wait_group, keys_ref, x_ref, y_ref, qo_out):
    rows, width = keys_ref.shape
    ones = head_ones()
    row = lax.broadcasted_iota(jnp.int32, (rows, 2 * rows), 0)
    lane = lax.rem(lax.broadcasted_iota(jnp.int32, (rows, 2 * rows), 1), rows)
    causal = row >= lane
    for quad in range(width // QUAD):
        wait_group(quad)
        queries = unit_heads(mm(normed, wq[:, quad * QUAD : (quad + 1) * QUAD]), ones)
        queries_bf = queries.astype(BF16)
        for half in range(2):
            own = slice(half * PAIR, (half + 1) * PAIR)
            place = slice(quad * QUAD + half * PAIR, quad * QUAD + (half + 1) * PAIR)
            scores = mm_nt(queries_bf[:, own], spread(keys_ref[:, place]))
            scores = jnp.where(causal, scores, 0.0).astype(BF16)
            both = mm(scores, spread_two(x_ref[:, place], y_ref[:, place]))
            qo_out[:, place] = (queries[:, own] - both[:, :PAIR]).astype(BF16)
            qo_out[:, width + place.start : width + place.stop] = both[:, PAIR:].astype(BF16)


def first_reads(normed_ref, keys_ref, x_ref, y_ref, w_hbm, qo_out, wq, sems):
    width = keys_ref.shape[1]
    quads = width // QUAD

    def copy(quad):
        return pltpu.make_async_copy(
            w_hbm.at[0, :, pl.ds(quad * QUAD, QUAD)], wq.at[:, pl.ds(quad * QUAD, QUAD)], sems.at[quad]
        )

    for quad in range(quads):
        copy(quad).start()

    @pl.when(lax.axis_index("section") == 0)
    def _():
        read_out(normed_ref[...], wq, lambda quad: copy(quad).wait(), keys_ref, x_ref, y_ref, qo_out)

    @pl.when(lax.axis_index("section") != 0)
    def _():
        for quad in range(quads):
            copy(quad).wait()


def later_reads(normed_ref, keys_ref, x_ref, y_ref, wq, qo_out):
    @pl.when(lax.axis_index("section") == 1)
    def _():
        read_out(normed_ref[...], wq, lambda quad: None, keys_ref, x_ref, y_ref, qo_out)


def relay(count, lw, active, table, init_ref, states):
    @pl.when(lax.axis_index("section") == active)
    def _():
        heads = lw // HD
        me = lax.axis_index("seq")
        state = jnp.concatenate([init_ref[0, me * heads + index] for index in range(heads)], axis=1)
        states[0] = state.astype(BF16)
        for slab in range(count - 1):
            step = table[slab]
            state = state - mm(step[:, :lw], spread(state.astype(BF16))) + step[:, lw:].astype(F32)
            states[slab + 1] = state.astype(BF16)


def finish(lw, active, table, qo_ref, w_out_ref, h_ref, out_ref):
    @pl.when(lax.axis_index("section") == active)
    def _():
        width = qo_ref.shape[1] // 2
        per_quad = QUAD // lw
        parts = []
        for quad in range(width // QUAD):
            lanes = slice(quad * QUAD, (quad + 1) * QUAD)
            state = jnp.concatenate([table[quad * per_quad + index] for index in range(per_quad)], axis=1)
            offset = qo_ref[:, width + quad * QUAD : width + (quad + 1) * QUAD]
            inner = mm(qo_ref[:, lanes], spread(state)) + offset.astype(F32)
            parts.append(inner.astype(BF16))
        inner_bf = jnp.concatenate(parts, axis=1)
        out_ref[...] = (h_ref[...].astype(F32) + mm(inner_bf, w_out_ref[0])).astype(BF16)


def later_front(lw, h_ref, gain_ref, wkv, w_rate_ref, base_ref, maps, normed_out, keys_out, x_out, y_out):
    @pl.when(lax.axis_index("section") == 1)
    def _():
        normed = norm_rows(h_ref[...], gain_ref[...])
        normed_out[...] = normed
        rates = spread_rates(normed, w_rate_ref[0], base_ref[...])
        slab_maps(normed, rates, wkv, lambda quad: None, keys_out, x_out, y_out, maps, lw)


def last_finish(lw, table, qo_ref, w_out_ref, h_ref, first_ref, out_ref):
    finish(lw, 1, table, qo_ref, w_out_ref, h_ref, out_ref.at[0])

    @pl.when(lax.axis_index("section") == 0)
    def _():
        out_ref[0] = first_ref[...]


def call(body, outs, scratch, args, kinds=None, name=None):
    specs = [pl.BlockSpec(memory_space=kind) for kind in (kinds or [pltpu.VMEM] * len(args))]
    return pl.pallas_call(
        body,
        out_shape=outs,
        in_specs=specs,
        out_specs=[pl.BlockSpec(memory_space=pltpu.VMEM)] * len(outs),
        scratch_shapes=scratch,
        compiler_params=pltpu.CompilerParams(vmem_limit_bytes=VMEM_LIMIT),
        name=name,
    )(*args)


def exchange(pieces):
    return lax.all_to_all(pieces, "seq", 0, 0)


def shards(tokens, norm_gain, w_qkv, w_rate, rate_base, init_state, w_out):
    count = lax.axis_size("seq")
    heads = rate_base.shape[1]
    lw = heads // count * HD
    rows, model = tokens.shape
    width = heads * HD
    depth = w_qkv.shape[1]
    quads = width // QUAD
    shape = jax.ShapeDtypeStruct
    in_vmem = functools.partial(pltpu.with_memory_space_constraint, memory_space=pltpu.VMEM)
    in_hbm = functools.partial(pltpu.with_memory_space_constraint, memory_space=pltpu.HBM)
    maps = shape((count, HD, 2 * lw), BF16)
    states = shape((count, HD, lw), BF16)
    rows_out = [shape((rows, model), BF16)] + [shape((rows, width), BF16)] * 3
    w_rate = jnp.swapaxes(w_rate, 1, 2)

    sent, wkv, normed, keys, x_all, y_all = call(
        functools.partial(first_front, lw),
        [maps, pltpu.VMEM((depth, 2 * width), BF16)] + rows_out,
        [
            pltpu.VMEM(tokens.shape, tokens.dtype),
            pltpu.VMEM(norm_gain.shape, norm_gain.dtype),
            pltpu.VMEM(w_rate.shape, w_rate.dtype),
            pltpu.VMEM(rate_base.shape, rate_base.dtype),
            pltpu.SemaphoreType.DMA((4,)),
            pltpu.SemaphoreType.DMA((quads, 2)),
        ],
        [in_hbm(value) for value in (tokens, norm_gain, w_qkv, w_rate, rate_base)],
        [pltpu.HBM] * 5,
        name="first_front",
    )
    received = exchange(sent)
    reads, wq = call(
        first_reads,
        [shape((rows, 2 * width), BF16), pltpu.VMEM((depth, width), BF16)],
        [pltpu.SemaphoreType.DMA((quads,))],
        [normed, keys, x_all, y_all, in_hbm(w_qkv)],
        [pltpu.VMEM] * 4 + [pltpu.HBM],
        name="first_reads",
    )
    (sent,) = call(functools.partial(relay, count, lw, 0), [states], [], [received, init_state], name="relay0")
    received = exchange(sent)
    (first,) = call(
        functools.partial(finish, lw, 0),
        [shape((rows, model), BF16)],
        [],
        [received, reads, w_out, tokens],
        name="first_finish",
    )
    hidden = lax.ppermute(first, "section", [(0, 1)])

    sent, normed, keys, x_all, y_all = call(
        functools.partial(later_front, lw),
        [maps] + rows_out,
        [],
        [hidden, norm_gain, in_vmem(wkv), w_rate, rate_base],
        name="later_front",
    )
    received = exchange(sent)
    (reads,) = call(
        later_reads,
        [shape((rows, 2 * width), BF16)],
        [],
        [normed, keys, x_all, y_all, in_vmem(wq)],
        name="later_reads",
    )
    (sent,) = call(functools.partial(relay, count, lw, 1), [states], [], [received, init_state], name="relay1")
    received = exchange(sent)
    (result,) = call(
        functools.partial(last_finish, lw),
        [shape((1, rows, model), BF16)],
        [],
        [received, reads, w_out, hidden, first],
        name="last_finish",
    )
    return result


def solution(mesh):
    return jax.shard_map(
        shards,
        mesh=mesh,
        in_specs=(
            P(("traj", "seq"), None),
            P("section", None),
            P("section", None, None),
            P("section", None, None),
            P("section", None),
            P("section", None, None, None),
            P("section", None, None),
        ),
        out_specs=P("section", ("traj", "seq"), None),
        check_vma=False,
    )
```

```python
import functools

import jax
import jax.numpy as jnp
from jax import lax
from jax.experimental import pallas as pl
from jax.experimental.pallas import tpu as pltpu
from jax.sharding import PartitionSpec as P

HD = 64
PAIR = 2 * HD
QUAD = 4 * HD
F32 = jnp.float32
BF16 = jnp.bfloat16
EPS = 1e-6
VMEM_LIMIT = 20 * 1024 * 1024


def mm(a, b):
    return jnp.dot(a, b, preferred_element_type=F32)


def mm_nt(a, b):
    return lax.dot_general(a, b, (((1,), (1,)), ((), ())), preferred_element_type=F32)


def mm_tn(a, b):
    return lax.dot_general(a, b, (((0,), (0,)), ((), ())), preferred_element_type=F32)


def head_masks(rows, lanes):
    lane = lax.broadcasted_iota(jnp.int32, (rows, lanes), 1)
    return [lane // HD == index for index in range(lanes // HD)]


def spread(value):
    zero = jnp.zeros_like(value)
    masks = head_masks(*value.shape)
    return jnp.concatenate([jnp.where(mask, value, zero) for mask in masks], axis=0)


def spread_two(left, right):
    return jnp.concatenate([spread(left), spread(right)], axis=1)


def diagonal(product):
    first = lax.broadcasted_iota(jnp.int32, (HD, PAIR), 1) < HD
    return jnp.where(first, product[:HD], product[HD:])


def head_ones():
    row = lax.broadcasted_iota(jnp.int32, (QUAD, QUAD), 0) // HD
    lane = lax.broadcasted_iota(jnp.int32, (QUAD, QUAD), 1) // HD
    return jnp.where(row == lane, 1.0, 0.0).astype(BF16)


def unit_heads(value, ones):
    squares = mm((value * value).astype(BF16), ones)
    return value * lax.rsqrt(squares + EPS)


def norm_rows(hidden, gain):
    wide = hidden.astype(F32)
    mean_sq = jnp.mean(wide * wide, axis=-1, keepdims=True)
    return (wide * lax.rsqrt(mean_sq + EPS) * gain).astype(BF16)


def spread_rates(normed, w_rate, rate_base):
    rates = rate_base * jax.nn.sigmoid(mm_nt(normed, w_rate))
    high = rates.astype(BF16)
    low = (rates - high.astype(F32)).astype(BF16)
    heads = rates.shape[1]
    row = lax.broadcasted_iota(jnp.int32, (heads, heads * HD), 0)
    lane = lax.broadcasted_iota(jnp.int32, (heads, heads * HD), 1) // HD
    pick = jnp.where(row == lane, 1.0, 0.0).astype(BF16)
    return mm(high, pick) + mm(low, pick)


def staged(groups):
    for group in groups[:2]:
        for copy in group:
            copy.start()

    def wait(index):
        for copy in groups[index]:
            copy.wait()
        if index + 2 < len(groups):
            for copy in groups[index + 2]:
                copy.start()

    return wait


def on_section(active, body):
    pl.when(lax.axis_index("section") == active)(body)


def front(active, h_ref, gain_hbm, w_hbm, w_rate_hbm, base_hbm, maps, normed_out, keys_out, x_out, y_out, wkv, h_in, gain, w_rate, base, small_sems, sems):
    width = keys_out.shape[1]
    quads = width // QUAD

    def body():
        sources = [(gain_hbm, gain), (w_rate_hbm, w_rate), (base_hbm, base)]
        if h_in is not None:
            sources.append((h_ref, h_in))
        small = [pltpu.make_async_copy(source, target, small_sems.at[index]) for index, (source, target) in enumerate(sources)]
        for copy in small:
            copy.start()
        wait_group = staged(
            [
                [
                    pltpu.make_async_copy(
                        w_hbm.at[0, :, pl.ds((side + 1) * width + quad * QUAD, QUAD)],
                        wkv.at[:, pl.ds(side * width + quad * QUAD, QUAD)],
                        sems.at[quad, side],
                    )
                    for side in range(2)
                ]
                for quad in range(quads)
            ]
        )
        for copy in small:
            copy.wait()
        normed = norm_rows((h_ref if h_in is None else h_in)[...], gain[...])
        normed_out[...] = normed
        rates = spread_rates(normed, w_rate[0], base[...])
        ones = head_ones()
        for quad in range(quads):
            wait_group(quad)
            lanes = slice(quad * QUAD, (quad + 1) * QUAD)
            keys = mm(normed, wkv[:, lanes])
            values = mm(normed, wkv[:, width + quad * QUAD : width + (quad + 1) * QUAD])
            keys = unit_heads(keys, ones)
            keys_bf = keys.astype(BF16)
            keys_out[:, lanes] = keys_bf
            rate = rates[:, lanes]
            x_all = rate * keys
            y_all = rate * values
            x_first, y_first = x_all[:HD].astype(BF16), y_all[:HD].astype(BF16)
            cross = mm_nt(keys_bf[HD:], spread(keys_bf[:HD])).astype(BF16)
            fix = mm(cross, spread_two(x_first, y_first))
            x_second = (x_all[HD:] - rate[HD:] * fix[:, :QUAD]).astype(BF16)
            y_second = (y_all[HD:] - rate[HD:] * fix[:, QUAD:]).astype(BF16)
            x_bf = jnp.concatenate([x_first, x_second], axis=0)
            y_bf = jnp.concatenate([y_first, y_second], axis=0)
            x_out[:, lanes] = x_bf
            y_out[:, lanes] = y_bf
            for half in range(2):
                own = slice(half * PAIR, (half + 1) * PAIR)
                start = quad * QUAD + half * PAIR
                both = mm_tn(keys_bf[:, own], jnp.concatenate([x_bf[:, own], y_bf[:, own]], axis=1))
                maps[:, start : start + PAIR] = diagonal(both[:, :PAIR]).astype(BF16)
                maps[:, width + start : width + start + PAIR] = diagonal(both[:, PAIR:]).astype(BF16)

    on_section(active, body)


def first_front(h_hbm, *rest):
    front(0, h_hbm, *rest)


def later_front(h_ref, *rest):
    *rest, small_sems, sems = rest
    front(1, h_ref, *rest[:10], None, *rest[10:], small_sems, sems)


def read_out(active, quads, normed_ref, keys_ref, x_ref, y_ref, w_hbm, reads_out, wq, sems):
    rows = keys_ref.shape[0]
    part = len(quads) * QUAD

    def body():
        wait_group = staged(
            [
                [
                    pltpu.make_async_copy(
                        w_hbm.at[0, :, pl.ds(quad * QUAD, QUAD)], wq.at[:, pl.ds(index * QUAD, QUAD)], sems.at[index]
                    )
                ]
                for index, quad in enumerate(quads)
            ]
        )
        normed = normed_ref[...]
        ones = head_ones()
        row = lax.broadcasted_iota(jnp.int32, (rows, 2 * rows), 0)
        lane = lax.rem(lax.broadcasted_iota(jnp.int32, (rows, 2 * rows), 1), rows)
        causal = row >= lane
        for index, quad in enumerate(quads):
            wait_group(index)
            queries = unit_heads(mm(normed, wq[:, index * QUAD : (index + 1) * QUAD]), ones)
            queries_bf = queries.astype(BF16)
            for half in range(2):
                own = slice(half * PAIR, (half + 1) * PAIR)
                place = slice(quad * QUAD + half * PAIR, quad * QUAD + (half + 1) * PAIR)
                start = index * QUAD + half * PAIR
                scores = mm_nt(queries_bf[:, own], spread(keys_ref[:, place]))
                scores = jnp.where(causal, scores, 0.0).astype(BF16)
                both = mm(scores, spread_two(x_ref[:, place], y_ref[:, place]))
                reads_out[:, start : start + PAIR] = (queries[:, own] - both[:, :PAIR]).astype(BF16)
                reads_out[:, part + start : part + start + PAIR] = both[:, PAIR:].astype(BF16)

    on_section(active, body)


def compose(active, own_ref, got_ref, after_ref, out_ref):
    width = own_ref.shape[1] // 2

    def body():
        for start in range(0, width, PAIR):
            s_lanes, b_lanes = slice(start, start + PAIR), slice(width + start, width + start + PAIR)
            s_own, s_got, b_got = own_ref[:, s_lanes], got_ref[:, s_lanes], got_ref[:, b_lanes]
            step = mm(s_own, spread_two(s_got, b_got))
            out_ref[:, s_lanes] = (s_own.astype(F32) + s_got.astype(F32) - step[:, :PAIR]).astype(BF16)
            out_ref[:, b_lanes] = (own_ref[:, b_lanes].astype(F32) + b_got.astype(F32) - step[:, PAIR:]).astype(BF16)

    on_section(active, body)


def pair_state(init_ref, pair):
    return jnp.concatenate([init_ref[0, 2 * pair], init_ref[0, 2 * pair + 1]], axis=1)


def end_state(active, own_ref, got_ref, init_ref, after_ref, out_ref):
    width = own_ref.shape[1] // 2

    def body():
        states = [pair_state(init_ref, pair) for pair in range(width // PAIR)]
        for ref in (got_ref, own_ref):
            for pair, state in enumerate(states):
                start = pair * PAIR
                step = mm(ref[:, start : start + PAIR], spread(state.astype(BF16)))
                states[pair] = state - step + ref[:, width + start : width + start + PAIR].astype(F32)
        for pair, state in enumerate(states):
            out_ref[:, pair * PAIR : (pair + 1) * PAIR] = state.astype(BF16)

    on_section(active, body)


def fold(active, count, *refs):
    got_refs = refs[:count]
    reads_refs = refs[count : count + 2]
    w_hbm, out_ref, w_out, sem = refs[count + 2 :]
    width = out_ref.shape[1] // 2
    part = width // 2

    def body():
        load = pltpu.make_async_copy(w_hbm.at[0], w_out, sem)
        load.start()
        for start in range(0, width, PAIR):
            reads_ref = reads_refs[start // part]
            inner = start % part
            left = reads_ref[:, inner : inner + PAIR].astype(F32)
            offset = reads_ref[:, part + inner : part + inner + PAIR].astype(F32)
            for ref in got_refs:
                step = mm(left.astype(BF16), spread_two(ref[:, start : start + PAIR], ref[:, width + start : width + start + PAIR]))
                left = left - step[:, :PAIR]
                offset = offset + step[:, PAIR:]
            out_ref[:, start : start + PAIR] = left.astype(BF16)
            out_ref[:, width + start : width + start + PAIR] = offset.astype(BF16)
        load.wait()

    on_section(active, body)


def finish(active, count, state_ref, init_ref, reads_ref, w_out_ref, h_ref, out_ref):
    width = reads_ref.shape[1] // 2

    def body():
        begins = lax.axis_index("seq") < count // 2
        parts = []
        for start in range(0, width, QUAD):
            lanes = slice(start, start + QUAD)
            init = jnp.concatenate([pair_state(init_ref, start // PAIR), pair_state(init_ref, start // PAIR + 1)], axis=1)
            state = jnp.where(begins, init.astype(BF16), state_ref[:, lanes])
            offset = reads_ref[:, width + start : width + start + QUAD]
            parts.append((mm(reads_ref[:, lanes], spread(state)) + offset.astype(F32)).astype(BF16))
        inner_bf = jnp.concatenate(parts, axis=1)
        out_ref[...] = (h_ref[...].astype(F32) + mm(inner_bf, w_out_ref[...])).astype(BF16)

    on_section(active, body)


def last_finish(count, state_ref, init_ref, reads_ref, w_out_ref, h_ref, first_ref, out_ref):
    finish(1, count, state_ref, init_ref, reads_ref, w_out_ref, h_ref, out_ref.at[0])

    @pl.when(lax.axis_index("section") == 0)
    def _():
        out_ref[0] = first_ref[...]


def call(body, outs, scratch, args, kinds=None, name=None):
    specs = [pl.BlockSpec(memory_space=kind) for kind in (kinds or [pltpu.VMEM] * len(args))]
    return pl.pallas_call(
        body,
        out_shape=outs,
        in_specs=specs,
        out_specs=[pl.BlockSpec(memory_space=pltpu.VMEM)] * len(outs),
        scratch_shapes=scratch,
        compiler_params=pltpu.CompilerParams(vmem_limit_bytes=VMEM_LIMIT),
        name=name,
    )(*args)


def shards(tokens, norm_gain, w_qkv, w_rate, rate_base, init_state, w_out):
    count = lax.axis_size("seq")
    heads = rate_base.shape[1]
    rows, model = tokens.shape
    width = heads * HD
    depth = w_qkv.shape[1]
    quads = width // QUAD
    shape = jax.ShapeDtypeStruct
    in_vmem = functools.partial(pltpu.with_memory_space_constraint, memory_space=pltpu.VMEM)
    in_hbm = functools.partial(pltpu.with_memory_space_constraint, memory_space=pltpu.HBM)
    maps = shape((HD, 2 * width), BF16)
    rows_out = [shape((rows, model), BF16)] + [shape((rows, width), BF16)] * 3
    w_rate = jnp.swapaxes(w_rate, 1, 2)
    norm_gain, w_qkv, w_rate, rate_base, w_out = [in_hbm(value) for value in (norm_gain, w_qkv, w_rate, rate_base, w_out)]

    def ahead(value, active, steps):
        pairs = [(active * count + place, active * count + place + steps) for place in range(count - steps)]
        return lax.ppermute(value, ("section", "seq"), pairs)

    def run(active, body, outs, scratch, args, kinds=None):
        return call(functools.partial(body, active), outs, scratch, args, kinds, name=body.__name__ + str(active))

    def layer(active, hidden):
        h_scratch = [] if active else [pltpu.VMEM(hidden.shape, hidden.dtype)]
        own, normed, keys, x_all, y_all = call(
            later_front if active else first_front,
            [maps] + rows_out,
            [pltpu.VMEM((depth, 2 * width), BF16)]
            + h_scratch
            + [pltpu.VMEM(value.shape, value.dtype) for value in (norm_gain, w_rate, rate_base)]
            + [pltpu.SemaphoreType.DMA((4,)), pltpu.SemaphoreType.DMA((quads, 2))],
            [hidden if active else in_hbm(hidden), norm_gain, w_qkv, w_rate, rate_base],
            [pltpu.VMEM if active else pltpu.HBM] + [pltpu.HBM] * 4,
            name="later_front" if active else "first_front",
        )

        def reads_of(picked):
            part = len(picked) * QUAD
            return call(
                functools.partial(read_out, active, picked),
                [shape((rows, 2 * part), BF16)],
                [pltpu.VMEM((depth, part), BF16), pltpu.SemaphoreType.DMA((len(picked),))],
                [normed, keys, x_all, y_all, w_qkv],
                [pltpu.VMEM] * 4 + [pltpu.HBM],
                name=f"reads{active}_{picked[0]}",
            )[0]

        reads = [reads_of(tuple(range(quads // 2))), reads_of(tuple(range(quads // 2, quads)))]
        got = [ahead(own, active, 1)]
        steps = 2
        while steps < count // 2:
            (own,) = run(active, compose, [maps], [], [own, got[-1], reads[0]], [pltpu.VMEM] * 2 + [pl.ANY])
            got.append(ahead(own, active, steps))
            steps *= 2
        (state,) = run(
            active, end_state, [shape((HD, width), BF16)], [], [own, got[-1], init_state, reads[1]], [pltpu.VMEM] * 3 + [pl.ANY]
        )
        state = ahead(state, active, steps)
        folded, w_out_near = call(
            functools.partial(fold, active, len(got)),
            [shape((rows, 2 * width), BF16), pltpu.VMEM(w_out.shape[1:], BF16)],
            [pltpu.SemaphoreType.DMA],
            got + reads + [w_out],
            [pltpu.VMEM] * (len(got) + 2) + [pltpu.HBM],
            name=f"fold{active}",
        )
        return [state, init_state, folded, in_vmem(w_out_near), hidden]

    (first,) = call(functools.partial(finish, 0, count), [shape((rows, model), BF16)], [], layer(0, tokens), name="first_finish")
    hidden = lax.ppermute(first, "section", [(0, 1)])
    (result,) = call(
        functools.partial(last_finish, count), [shape((1, rows, model), BF16)], [], layer(1, hidden) + [first], name="last_finish"
    )
    return result


def solution(mesh):
    return jax.shard_map(
        shards,
        mesh=mesh,
        in_specs=(
            P(("traj", "seq"), None),
            P("section", None),
            P("section", None, None),
            P("section", None, None),
            P("section", None),
            P("section", None, None, None),
            P("section", None, None),
        ),
        out_specs=P("section", ("traj", "seq"), None),
        check_vma=False,
    )
```

```python
import functools

import jax
import jax.numpy as jnp
from jax import lax
from jax.experimental import pallas as pl
from jax.experimental.pallas import tpu as pltpu
from jax.sharding import PartitionSpec as P

HD = 64
PAIR = 2 * HD
QUAD = 4 * HD
F32 = jnp.float32
BF16 = jnp.bfloat16
EPS = 1e-6
VMEM_LIMIT = 20 * 1024 * 1024


def mm(a, b):
    return jnp.dot(a, b, preferred_element_type=F32)


def mm_nt(a, b):
    return lax.dot_general(a, b, (((1,), (1,)), ((), ())), preferred_element_type=F32)


def mm_tn(a, b):
    return lax.dot_general(a, b, (((0,), (0,)), ((), ())), preferred_element_type=F32)


def head_masks(rows, lanes):
    lane = lax.broadcasted_iota(jnp.int32, (rows, lanes), 1)
    return [lane // HD == index for index in range(lanes // HD)]


def spread(value):
    zero = jnp.zeros_like(value)
    masks = head_masks(*value.shape)
    return jnp.concatenate([jnp.where(mask, value, zero) for mask in masks], axis=0)


def spread_two(left, right):
    return jnp.concatenate([spread(left), spread(right)], axis=1)


def diagonal(product):
    first = lax.broadcasted_iota(jnp.int32, (HD, PAIR), 1) < HD
    return jnp.where(first, product[:HD], product[HD:])


def head_ones():
    row = lax.broadcasted_iota(jnp.int32, (QUAD, QUAD), 0) // HD
    lane = lax.broadcasted_iota(jnp.int32, (QUAD, QUAD), 1) // HD
    return jnp.where(row == lane, 1.0, 0.0).astype(BF16)


def unit_heads(value, ones):
    squares = mm((value * value).astype(BF16), ones)
    return value * lax.rsqrt(squares + EPS)


def norm_rows(hidden, gain):
    wide = hidden.astype(F32)
    mean_sq = jnp.mean(wide * wide, axis=-1, keepdims=True)
    return (wide * lax.rsqrt(mean_sq + EPS) * gain).astype(BF16)


def spread_rates(normed, w_rate, rate_base):
    rates = rate_base * jax.nn.sigmoid(mm_nt(normed, w_rate))
    high = rates.astype(BF16)
    low = (rates - high.astype(F32)).astype(BF16)
    heads = rates.shape[1]
    row = lax.broadcasted_iota(jnp.int32, (heads, heads * HD), 0)
    lane = lax.broadcasted_iota(jnp.int32, (heads, heads * HD), 1) // HD
    pick = jnp.where(row == lane, 1.0, 0.0).astype(BF16)
    return mm(high, pick) + mm(low, pick)


def staged(groups):
    for group in groups[:2]:
        for copy in group:
            copy.start()

    def wait(index):
        for copy in groups[index]:
            copy.wait()
        if index + 2 < len(groups):
            for copy in groups[index + 2]:
                copy.start()

    return wait


def on_section(active, body):
    pl.when(lax.axis_index("section") == active)(body)


def front(active, h_ref, gain_hbm, w_hbm, w_rate_hbm, base_hbm, maps, normed_out, keys_out, x_out, y_out, wkv, h_in, gain, w_rate, base, small_sems, sems):
    width = keys_out.shape[1]
    quads = width // QUAD

    def body():
        sources = [(gain_hbm, gain), (w_rate_hbm, w_rate), (base_hbm, base)]
        if h_in is not None:
            sources.append((h_ref, h_in))
        small = [pltpu.make_async_copy(source, target, small_sems.at[index]) for index, (source, target) in enumerate(sources)]
        for copy in small:
            copy.start()
        wait_group = staged(
            [
                [
                    pltpu.make_async_copy(
                        w_hbm.at[0, :, pl.ds((side + 1) * width + quad * QUAD, QUAD)],
                        wkv.at[:, pl.ds(side * width + quad * QUAD, QUAD)],
                        sems.at[quad, side],
                    )
                    for side in range(2)
                ]
                for quad in range(quads)
            ]
        )
        for copy in small:
            copy.wait()
        normed = norm_rows((h_ref if h_in is None else h_in)[...], gain[...])
        normed_out[...] = normed
        rates = spread_rates(normed, w_rate[0], base[...])
        ones = head_ones()
        for quad in range(quads):
            wait_group(quad)
            lanes = slice(quad * QUAD, (quad + 1) * QUAD)
            keys = mm(normed, wkv[:, lanes])
            values = mm(normed, wkv[:, width + quad * QUAD : width + (quad + 1) * QUAD])
            keys = unit_heads(keys, ones)
            keys_bf = keys.astype(BF16)
            keys_out[:, lanes] = keys_bf
            rate = rates[:, lanes]
            x_all = rate * keys
            y_all = rate * values
            x_first, y_first = x_all[:HD].astype(BF16), y_all[:HD].astype(BF16)
            cross = mm_nt(keys_bf[HD:], spread(keys_bf[:HD])).astype(BF16)
            fix = mm(cross, spread_two(x_first, y_first))
            x_second = (x_all[HD:] - rate[HD:] * fix[:, :QUAD]).astype(BF16)
            y_second = (y_all[HD:] - rate[HD:] * fix[:, QUAD:]).astype(BF16)
            x_bf = jnp.concatenate([x_first, x_second], axis=0)
            y_bf = jnp.concatenate([y_first, y_second], axis=0)
            x_out[:, lanes] = x_bf
            y_out[:, lanes] = y_bf
            for half in range(2):
                own = slice(half * PAIR, (half + 1) * PAIR)
                start = quad * QUAD + half * PAIR
                both = mm_tn(keys_bf[:, own], jnp.concatenate([x_bf[:, own], y_bf[:, own]], axis=1))
                maps[:, start : start + PAIR] = diagonal(both[:, :PAIR]).astype(BF16)
                maps[:, width + start : width + start + PAIR] = diagonal(both[:, PAIR:]).astype(BF16)

    on_section(active, body)


def first_front(h_hbm, *rest):
    front(0, h_hbm, *rest)


def later_front(h_ref, *rest):
    *rest, small_sems, sems = rest
    front(1, h_ref, *rest[:10], None, *rest[10:], small_sems, sems)


def read_out(active, quads, normed_ref, keys_ref, x_ref, y_ref, w_hbm, reads_out, wq, sems):
    rows = keys_ref.shape[0]
    part = len(quads) * QUAD

    def body():
        wait_group = staged(
            [
                [
                    pltpu.make_async_copy(
                        w_hbm.at[0, :, pl.ds(quad * QUAD, QUAD)], wq.at[:, pl.ds(index * QUAD, QUAD)], sems.at[index]
                    )
                ]
                for index, quad in enumerate(quads)
            ]
        )
        normed = normed_ref[...]
        ones = head_ones()
        row = lax.broadcasted_iota(jnp.int32, (rows, 2 * rows), 0)
        lane = lax.rem(lax.broadcasted_iota(jnp.int32, (rows, 2 * rows), 1), rows)
        causal = row >= lane
        for index, quad in enumerate(quads):
            wait_group(index)
            queries = unit_heads(mm(normed, wq[:, index * QUAD : (index + 1) * QUAD]), ones)
            queries_bf = queries.astype(BF16)
            for half in range(2):
                own = slice(half * PAIR, (half + 1) * PAIR)
                place = slice(quad * QUAD + half * PAIR, quad * QUAD + (half + 1) * PAIR)
                start = index * QUAD + half * PAIR
                scores = mm_nt(queries_bf[:, own], spread(keys_ref[:, place]))
                scores = jnp.where(causal, scores, 0.0).astype(BF16)
                both = mm(scores, spread_two(x_ref[:, place], y_ref[:, place]))
                reads_out[:, start : start + PAIR] = (queries[:, own] - both[:, :PAIR]).astype(BF16)
                reads_out[:, part + start : part + start + PAIR] = both[:, PAIR:].astype(BF16)

    on_section(active, body)


def pair_state(init_ref, pair):
    return jnp.concatenate([init_ref[0, 2 * pair], init_ref[0, 2 * pair + 1]], axis=1)


def finish(active, table, init_ref, reads_refs, w_hbm, h_ref, out_ref, state, w_out, sems):
    width = state.shape[1]
    part = width // 2
    model = w_out.shape[1]
    chunk = model // 4

    def body():
        loads = [
            pltpu.make_async_copy(
                w_hbm.at[0, :, pl.ds(index * chunk, chunk)], w_out.at[:, pl.ds(index * chunk, chunk)], sems.at[index]
            )
            for index in range(4)
        ]
        for load in loads:
            load.start()
        for pair in range(width // PAIR):
            state[:, pair * PAIR : (pair + 1) * PAIR] = pair_state(init_ref, pair)

        @pl.loop(0, lax.axis_index("seq"))
        def _(slab):
            for start in range(0, width, PAIR):
                lanes = slice(start, start + PAIR)
                before = state[:, lanes]
                step = mm(table[slab, :, lanes], spread(before.astype(BF16)))
                state[:, lanes] = before - step + table[slab, :, width + start : width + start + PAIR].astype(F32)

        parts = []
        for start in range(0, width, QUAD):
            lanes = slice(start, start + QUAD)
            reads_ref, inner = reads_refs[start // part], start % part
            offset = reads_ref[:, part + inner : part + inner + QUAD]
            read = mm(reads_ref[:, inner : inner + QUAD], spread(state[:, lanes].astype(BF16)))
            parts.append((read + offset.astype(F32)).astype(BF16))
        inner_bf = jnp.concatenate(parts, axis=1)
        for index, load in enumerate(loads):
            load.wait()
            lanes = slice(index * chunk, (index + 1) * chunk)
            out_ref[:, lanes] = (h_ref[:, lanes].astype(F32) + mm(inner_bf, w_out[:, lanes])).astype(BF16)

    on_section(active, body)


def first_finish(table, init_ref, reads_a, reads_b, w_hbm, h_ref, out_ref, state, w_out, sems):
    finish(0, table, init_ref, (reads_a, reads_b), w_hbm, h_ref, out_ref, state, w_out, sems)


def last_finish(table, init_ref, reads_a, reads_b, w_hbm, h_ref, first_ref, out_ref, state, w_out, sems):
    finish(1, table, init_ref, (reads_a, reads_b), w_hbm, h_ref, out_ref.at[0], state, w_out, sems)

    @pl.when(lax.axis_index("section") == 0)
    def _():
        out_ref[0] = first_ref[...]


def call(body, outs, scratch, args, kinds=None, name=None):
    specs = [pl.BlockSpec(memory_space=kind) for kind in (kinds or [pltpu.VMEM] * len(args))]
    return pl.pallas_call(
        body,
        out_shape=outs,
        in_specs=specs,
        out_specs=[pl.BlockSpec(memory_space=pltpu.VMEM)] * len(outs),
        scratch_shapes=scratch,
        compiler_params=pltpu.CompilerParams(vmem_limit_bytes=VMEM_LIMIT),
        name=name,
    )(*args)


def shards(tokens, norm_gain, w_qkv, w_rate, rate_base, init_state, w_out):
    heads = rate_base.shape[1]
    rows, model = tokens.shape
    width = heads * HD
    depth = w_qkv.shape[1]
    quads = width // QUAD
    shape = jax.ShapeDtypeStruct
    in_hbm = functools.partial(pltpu.with_memory_space_constraint, memory_space=pltpu.HBM)
    maps = shape((HD, 2 * width), BF16)
    rows_out = [shape((rows, model), BF16)] + [shape((rows, width), BF16)] * 3
    w_rate = jnp.swapaxes(w_rate, 1, 2)
    norm_gain, w_qkv, w_rate, rate_base, w_out = [in_hbm(value) for value in (norm_gain, w_qkv, w_rate, rate_base, w_out)]

    def layer(active, hidden):
        h_scratch = [] if active else [pltpu.VMEM(hidden.shape, hidden.dtype)]
        own, normed, keys, x_all, y_all = call(
            later_front if active else first_front,
            [maps] + rows_out,
            [pltpu.VMEM((depth, 2 * width), BF16)]
            + h_scratch
            + [pltpu.VMEM(value.shape, value.dtype) for value in (norm_gain, w_rate, rate_base)]
            + [pltpu.SemaphoreType.DMA((4,)), pltpu.SemaphoreType.DMA((quads, 2))],
            [hidden if active else in_hbm(hidden), norm_gain, w_qkv, w_rate, rate_base],
            [pltpu.VMEM if active else pltpu.HBM] + [pltpu.HBM] * 4,
            name="later_front" if active else "first_front",
        )

        def reads_of(picked):
            part = len(picked) * QUAD
            return call(
                functools.partial(read_out, active, picked),
                [shape((rows, 2 * part), BF16)],
                [pltpu.VMEM((depth, part), BF16), pltpu.SemaphoreType.DMA((len(picked),))],
                [normed, keys, x_all, y_all, w_qkv],
                [pltpu.VMEM] * 4 + [pltpu.HBM],
                name=f"reads{active}_{picked[0]}",
            )[0]

        reads = [reads_of(tuple(range(quads // 2))), reads_of(tuple(range(quads // 2, quads)))]
        return [lax.all_gather(own, "seq"), init_state, *reads, w_out, hidden]

    scratch = [pltpu.VMEM((HD, width), F32), pltpu.VMEM(w_out.shape[1:], BF16), pltpu.SemaphoreType.DMA((4,))]
    kinds = [pltpu.VMEM] * 4 + [pltpu.HBM] + [pltpu.VMEM]
    (first,) = call(first_finish, [shape((rows, model), BF16)], scratch, layer(0, tokens), kinds, name="first_finish")
    hidden = lax.ppermute(first, "section", [(0, 1)])
    (result,) = call(
        last_finish, [shape((1, rows, model), BF16)], scratch, layer(1, hidden) + [first], kinds + [pltpu.VMEM], name="last_finish"
    )
    return result


def solution(mesh):
    return jax.shard_map(
        shards,
        mesh=mesh,
        in_specs=(
            P(("traj", "seq"), None),
            P("section", None),
            P("section", None, None),
            P("section", None, None),
            P("section", None),
            P("section", None, None, None),
            P("section", None, None),
        ),
        out_specs=P("section", ("traj", "seq"), None),
        check_vma=False,
    )
```

```python
import functools

import jax
import jax.numpy as jnp
from jax import lax
from jax.experimental import pallas as pl
from jax.experimental.pallas import tpu as pltpu
from jax.sharding import PartitionSpec as P

HD = 64
PAIR = 2 * HD
QUAD = 4 * HD
F32 = jnp.float32
BF16 = jnp.bfloat16
EPS = 1e-6
VMEM_LIMIT = 20 * 1024 * 1024


def mm(a, b):
    return jnp.dot(a, b, preferred_element_type=F32)


def mm_nt(a, b):
    return lax.dot_general(a, b, (((1,), (1,)), ((), ())), preferred_element_type=F32)


def mm_tn(a, b):
    return lax.dot_general(a, b, (((0,), (0,)), ((), ())), preferred_element_type=F32)


def head_masks(rows, lanes):
    lane = lax.broadcasted_iota(jnp.int32, (rows, lanes), 1)
    return [lane // HD == index for index in range(lanes // HD)]


def spread(value):
    zero = jnp.zeros_like(value)
    masks = head_masks(*value.shape)
    return jnp.concatenate([jnp.where(mask, value, zero) for mask in masks], axis=0)


def spread_two(left, right):
    return jnp.concatenate([spread(left), spread(right)], axis=1)


def diagonal(product):
    first = lax.broadcasted_iota(jnp.int32, (HD, PAIR), 1) < HD
    return jnp.where(first, product[:HD], product[HD:])


def head_ones():
    row = lax.broadcasted_iota(jnp.int32, (QUAD, QUAD), 0) // HD
    lane = lax.broadcasted_iota(jnp.int32, (QUAD, QUAD), 1) // HD
    return jnp.where(row == lane, 1.0, 0.0).astype(BF16)


def unit_heads(value, ones):
    squares = mm((value * value).astype(BF16), ones)
    return value * lax.rsqrt(squares + EPS)


def norm_rows(hidden, gain):
    wide = hidden.astype(F32)
    mean_sq = jnp.mean(wide * wide, axis=-1, keepdims=True)
    return (wide * lax.rsqrt(mean_sq + EPS) * gain).astype(BF16)


def spread_rates(normed, w_rate, rate_base):
    rates = rate_base * jax.nn.sigmoid(mm_nt(normed, w_rate))
    high = rates.astype(BF16)
    low = (rates - high.astype(F32)).astype(BF16)
    heads = rates.shape[1]
    row = lax.broadcasted_iota(jnp.int32, (heads, heads * HD), 0)
    lane = lax.broadcasted_iota(jnp.int32, (heads, heads * HD), 1) // HD
    pick = jnp.where(row == lane, 1.0, 0.0).astype(BF16)
    return mm(high, pick) + mm(low, pick)


def staged(groups, depth=3):
    for group in groups[:depth]:
        for copy in group:
            copy.start()

    def wait(index):
        for copy in groups[index]:
            copy.wait()
        if index + depth < len(groups):
            for copy in groups[index + depth]:
                copy.start()

    return wait


def on_section(active, body):
    pl.when(lax.axis_index("section") == active)(body)


def front(active, h_ref, gain_hbm, w_hbm, w_rate_hbm, base_hbm, maps, normed_out, keys_out, x_out, y_out, wkv, h_in, gain, w_rate, base, small_sems, sems):
    width = keys_out.shape[1]
    quads = width // QUAD

    def body():
        sources = [(gain_hbm, gain), (w_rate_hbm, w_rate), (base_hbm, base)]
        if h_in is not None:
            sources.append((h_ref, h_in))
        small = [pltpu.make_async_copy(source, target, small_sems.at[index]) for index, (source, target) in enumerate(sources)]
        for copy in small:
            copy.start()
        wait_group = staged(
            [
                [
                    pltpu.make_async_copy(
                        w_hbm.at[0, :, pl.ds((side + 1) * width + quad * QUAD, QUAD)],
                        wkv.at[:, pl.ds(side * width + quad * QUAD, QUAD)],
                        sems.at[quad, side],
                    )
                    for side in range(2)
                ]
                for quad in range(quads)
            ]
        )
        for copy in small:
            copy.wait()
        normed = norm_rows((h_ref if h_in is None else h_in)[...], gain[...])
        normed_out[...] = normed
        rates = spread_rates(normed, w_rate[0], base[...])
        ones = head_ones()

        def project(quad):
            wait_group(quad)
            lanes = slice(quad * QUAD, (quad + 1) * QUAD)
            return mm(normed, wkv[:, lanes]), mm(normed, wkv[:, width + quad * QUAD : width + (quad + 1) * QUAD])

        def chain(quad, keys, values):
            lanes = slice(quad * QUAD, (quad + 1) * QUAD)
            keys = unit_heads(keys, ones)
            keys_bf = keys.astype(BF16)
            keys_out[:, lanes] = keys_bf
            rate = rates[:, lanes]
            x_all = rate * keys
            y_all = rate * values
            x_first, y_first = x_all[:HD].astype(BF16), y_all[:HD].astype(BF16)
            cross = mm_nt(keys_bf[HD:], spread(keys_bf[:HD])).astype(BF16)
            fix = mm(cross, spread_two(x_first, y_first))
            x_second = (x_all[HD:] - rate[HD:] * fix[:, :QUAD]).astype(BF16)
            y_second = (y_all[HD:] - rate[HD:] * fix[:, QUAD:]).astype(BF16)
            x_bf = jnp.concatenate([x_first, x_second], axis=0)
            y_bf = jnp.concatenate([y_first, y_second], axis=0)
            x_out[:, lanes] = x_bf
            y_out[:, lanes] = y_bf
            for half in range(2):
                own = slice(half * PAIR, (half + 1) * PAIR)
                start = quad * QUAD + half * PAIR
                both = mm_tn(keys_bf[:, own], jnp.concatenate([x_bf[:, own], y_bf[:, own]], axis=1))
                maps[:, start : start + PAIR] = diagonal(both[:, :PAIR]).astype(BF16)
                maps[:, width + start : width + start + PAIR] = diagonal(both[:, PAIR:]).astype(BF16)

        before = project(0)
        for quad in range(1, quads):
            after = project(quad)
            chain(quad - 1, *before)
            before = after
        chain(quads - 1, *before)

    on_section(active, body)


def first_front(h_hbm, *rest):
    front(0, h_hbm, *rest)


def later_front(h_ref, *rest):
    *rest, small_sems, sems = rest
    front(1, h_ref, *rest[:10], None, *rest[10:], small_sems, sems)


def read_out(active, quads, normed_ref, keys_ref, x_ref, y_ref, w_hbm, reads_out, wq, sems):
    rows = keys_ref.shape[0]
    part = len(quads) * QUAD

    def body():
        wait_group = staged(
            [
                [
                    pltpu.make_async_copy(
                        w_hbm.at[0, :, pl.ds(quad * QUAD, QUAD)], wq.at[:, pl.ds(index * QUAD, QUAD)], sems.at[index]
                    )
                ]
                for index, quad in enumerate(quads)
            ]
        )
        normed = normed_ref[...]
        ones = head_ones()
        row = lax.broadcasted_iota(jnp.int32, (rows, 2 * rows), 0)
        lane = lax.rem(lax.broadcasted_iota(jnp.int32, (rows, 2 * rows), 1), rows)
        causal = row >= lane
        for index, quad in enumerate(quads):
            wait_group(index)
            queries = unit_heads(mm(normed, wq[:, index * QUAD : (index + 1) * QUAD]), ones)
            queries_bf = queries.astype(BF16)
            for half in range(2):
                own = slice(half * PAIR, (half + 1) * PAIR)
                place = slice(quad * QUAD + half * PAIR, quad * QUAD + (half + 1) * PAIR)
                start = index * QUAD + half * PAIR
                scores = mm_nt(queries_bf[:, own], spread(keys_ref[:, place]))
                scores = jnp.where(causal, scores, 0.0).astype(BF16)
                both = mm(scores, spread_two(x_ref[:, place], y_ref[:, place]))
                reads_out[:, start : start + PAIR] = (queries[:, own] - both[:, :PAIR]).astype(BF16)
                reads_out[:, part + start : part + start + PAIR] = both[:, PAIR:].astype(BF16)

    on_section(active, body)


def compose(active, own_ref, got_ref, after_ref, out_ref):
    width = own_ref.shape[1] // 2

    def body():
        for start in range(0, width, PAIR):
            s_lanes, b_lanes = slice(start, start + PAIR), slice(width + start, width + start + PAIR)
            s_own, s_got, b_got = own_ref[:, s_lanes], got_ref[:, s_lanes], got_ref[:, b_lanes]
            step = mm(s_own, spread_two(s_got, b_got))
            out_ref[:, s_lanes] = (s_own.astype(F32) + s_got.astype(F32) - step[:, :PAIR]).astype(BF16)
            out_ref[:, b_lanes] = (own_ref[:, b_lanes].astype(F32) + b_got.astype(F32) - step[:, PAIR:]).astype(BF16)

    on_section(active, body)


def pair_state(init_ref, pair):
    return jnp.concatenate([init_ref[0, 2 * pair], init_ref[0, 2 * pair + 1]], axis=1)


def end_state(active, own_ref, got_ref, init_ref, after_ref, out_ref):
    width = own_ref.shape[1] // 2

    def body():
        states = [pair_state(init_ref, pair) for pair in range(width // PAIR)]
        for ref in (got_ref, own_ref):
            for pair, state in enumerate(states):
                start = pair * PAIR
                step = mm(ref[:, start : start + PAIR], spread(state.astype(BF16)))
                states[pair] = state - step + ref[:, width + start : width + start + PAIR].astype(F32)
        for pair, state in enumerate(states):
            out_ref[:, pair * PAIR : (pair + 1) * PAIR] = state.astype(BF16)

    on_section(active, body)


def fold(active, count, *refs):
    got_refs = refs[:count]
    reads_refs = refs[count : count + 2]
    w_hbm, out_ref, w_out, sem = refs[count + 2 :]
    width = out_ref.shape[1] // 2
    part = width // 2

    def body():
        load = pltpu.make_async_copy(w_hbm.at[0], w_out, sem)
        load.start()
        for start in range(0, width, PAIR):
            reads_ref = reads_refs[start // part]
            inner = start % part
            left = reads_ref[:, inner : inner + PAIR].astype(F32)
            offset = reads_ref[:, part + inner : part + inner + PAIR].astype(F32)
            for ref in got_refs:
                step = mm(left.astype(BF16), spread_two(ref[:, start : start + PAIR], ref[:, width + start : width + start + PAIR]))
                left = left - step[:, :PAIR]
                offset = offset + step[:, PAIR:]
            out_ref[:, start : start + PAIR] = left.astype(BF16)
            out_ref[:, width + start : width + start + PAIR] = offset.astype(BF16)
        load.wait()

    on_section(active, body)


def finish(active, count, state_ref, init_ref, reads_ref, w_out_ref, h_ref, store):
    width = reads_ref.shape[1] // 2
    model = h_ref.shape[1]
    chunk = model // 4

    def body():
        begins = lax.axis_index("seq") < count // 2
        parts = []
        for start in range(0, width, QUAD):
            lanes = slice(start, start + QUAD)
            init = jnp.concatenate([pair_state(init_ref, start // PAIR), pair_state(init_ref, start // PAIR + 1)], axis=1)
            state = jnp.where(begins, init.astype(BF16), state_ref[:, lanes])
            offset = reads_ref[:, width + start : width + start + QUAD]
            parts.append((mm(reads_ref[:, lanes], spread(state)) + offset.astype(F32)).astype(BF16))
        inner_bf = jnp.concatenate(parts, axis=1)
        for start in range(0, model, chunk):
            lanes = slice(start, start + chunk)
            store(start, (h_ref[:, lanes].astype(F32) + mm(inner_bf, w_out_ref[:, lanes])).astype(BF16))

    on_section(active, body)


def first_finish(count, state_ref, init_ref, reads_ref, w_out_ref, h_ref, out_ref):
    def store(start, value):
        out_ref[:, start : start + value.shape[1]] = value

    finish(0, count, state_ref, init_ref, reads_ref, w_out_ref, h_ref, store)


def last_finish(count, state_ref, init_ref, reads_ref, w_out_ref, h_ref, first_ref, out_hbm, near, sems):
    chunk = near.shape[1] // 4

    def write(start):
        lanes = pl.ds(start, chunk)
        return pltpu.make_async_copy(near.at[:, lanes], out_hbm.at[0, :, lanes], sems.at[start // chunk])

    def store(start, value):
        near[:, start : start + chunk] = value
        write(start).start()

    finish(1, count, state_ref, init_ref, reads_ref, w_out_ref, h_ref, store)

    @pl.when(lax.axis_index("section") == 0)
    def _():
        for start in range(0, near.shape[1], chunk):
            store(start, first_ref[:, start : start + chunk])

    for start in range(0, near.shape[1], chunk):
        write(start).wait()


def call(body, outs, scratch, args, kinds=None, name=None, out_kind=pltpu.VMEM):
    specs = [pl.BlockSpec(memory_space=kind) for kind in (kinds or [pltpu.VMEM] * len(args))]
    return pl.pallas_call(
        body,
        out_shape=outs,
        in_specs=specs,
        out_specs=[pl.BlockSpec(memory_space=out_kind)] * len(outs),
        scratch_shapes=scratch,
        compiler_params=pltpu.CompilerParams(vmem_limit_bytes=VMEM_LIMIT),
        name=name,
    )(*args)


def shards(tokens, norm_gain, w_qkv, w_rate, rate_base, init_state, w_out):
    count = lax.axis_size("seq")
    heads = rate_base.shape[1]
    rows, model = tokens.shape
    width = heads * HD
    depth = w_qkv.shape[1]
    quads = width // QUAD
    shape = jax.ShapeDtypeStruct
    in_vmem = functools.partial(pltpu.with_memory_space_constraint, memory_space=pltpu.VMEM)
    in_hbm = functools.partial(pltpu.with_memory_space_constraint, memory_space=pltpu.HBM)
    maps = shape((HD, 2 * width), BF16)
    rows_out = [shape((rows, model), BF16)] + [shape((rows, width), BF16)] * 3
    w_rate = jnp.swapaxes(w_rate, 1, 2)
    norm_gain, w_qkv, w_rate, rate_base, w_out = [in_hbm(value) for value in (norm_gain, w_qkv, w_rate, rate_base, w_out)]

    def ahead(value, active, steps):
        pairs = [(active * count + place, active * count + place + steps) for place in range(count - steps)]
        return lax.ppermute(value, ("section", "seq"), pairs)

    def run(active, body, outs, scratch, args, kinds=None):
        return call(functools.partial(body, active), outs, scratch, args, kinds, name=body.__name__ + str(active))

    def layer(active, hidden):
        h_scratch = [] if active else [pltpu.VMEM(hidden.shape, hidden.dtype)]
        own, normed, keys, x_all, y_all = call(
            later_front if active else first_front,
            [maps] + rows_out,
            [pltpu.VMEM((depth, 2 * width), BF16)]
            + h_scratch
            + [pltpu.VMEM(value.shape, value.dtype) for value in (norm_gain, w_rate, rate_base)]
            + [pltpu.SemaphoreType.DMA((4,)), pltpu.SemaphoreType.DMA((quads, 2))],
            [hidden if active else in_hbm(hidden), norm_gain, w_qkv, w_rate, rate_base],
            [pltpu.VMEM if active else pltpu.HBM] + [pltpu.HBM] * 4,
            name="later_front" if active else "first_front",
        )

        def reads_of(picked):
            part = len(picked) * QUAD
            return call(
                functools.partial(read_out, active, picked),
                [shape((rows, 2 * part), BF16)],
                [pltpu.VMEM((depth, part), BF16), pltpu.SemaphoreType.DMA((len(picked),))],
                [normed, keys, x_all, y_all, w_qkv],
                [pltpu.VMEM] * 4 + [pltpu.HBM],
                name=f"reads{active}_{picked[0]}",
            )[0]

        reads = [reads_of(tuple(range(quads // 2))), reads_of(tuple(range(quads // 2, quads)))]
        got = [ahead(own, active, 1)]
        steps = 2
        while steps < count // 2:
            (own,) = run(active, compose, [maps], [], [own, got[-1], reads[0]], [pltpu.VMEM] * 2 + [pl.ANY])
            got.append(ahead(own, active, steps))
            steps *= 2
        (state,) = run(
            active, end_state, [shape((HD, width), BF16)], [], [own, got[-1], init_state, reads[1]], [pltpu.VMEM] * 3 + [pl.ANY]
        )
        state = ahead(state, active, steps)
        folded, w_out_near = call(
            functools.partial(fold, active, len(got)),
            [shape((rows, 2 * width), BF16), pltpu.VMEM(w_out.shape[1:], BF16)],
            [pltpu.SemaphoreType.DMA],
            got + reads + [w_out],
            [pltpu.VMEM] * (len(got) + 2) + [pltpu.HBM],
            name=f"fold{active}",
        )
        return [state, init_state, folded, in_vmem(w_out_near), hidden]

    (first,) = call(functools.partial(first_finish, count), [shape((rows, model), BF16)], [], layer(0, tokens), name="first_finish")
    hidden = lax.ppermute(first, "section", [(0, 1)])
    (result,) = call(
        functools.partial(last_finish, count),
        [shape((1, rows, model), BF16)],
        [pltpu.VMEM((rows, model), BF16), pltpu.SemaphoreType.DMA((4,))],
        layer(1, hidden) + [first],
        name="last_finish",
        out_kind=pltpu.HBM,
    )
    return result


def solution(mesh):
    return jax.shard_map(
        shards,
        mesh=mesh,
        in_specs=(
            P(("traj", "seq"), None),
            P("section", None),
            P("section", None, None),
            P("section", None, None),
            P("section", None),
            P("section", None, None, None),
            P("section", None, None),
        ),
        out_specs=P("section", ("traj", "seq"), None),
        check_vma=False,
    )
```

```python
import functools

import jax
import jax.numpy as jnp
from jax import lax
from jax.experimental import pallas as pl
from jax.experimental.pallas import tpu as pltpu
from jax.sharding import PartitionSpec as P

HD = 64
PAIR = 2 * HD
QUAD = 4 * HD
F32 = jnp.float32
BF16 = jnp.bfloat16
EPS = 1e-6
VMEM_LIMIT = 20 * 1024 * 1024


def mm(a, b):
    return jnp.dot(a, b, preferred_element_type=F32)


def mm_nt(a, b):
    return lax.dot_general(a, b, (((1,), (1,)), ((), ())), preferred_element_type=F32)


def mm_tn(a, b):
    return lax.dot_general(a, b, (((0,), (0,)), ((), ())), preferred_element_type=F32)


def head_masks(rows, lanes):
    lane = lax.broadcasted_iota(jnp.int32, (rows, lanes), 1)
    return [lane // HD == index for index in range(lanes // HD)]


def spread(value):
    zero = jnp.zeros_like(value)
    masks = head_masks(*value.shape)
    return jnp.concatenate([jnp.where(mask, value, zero) for mask in masks], axis=0)


def spread_two(left, right):
    return jnp.concatenate([spread(left), spread(right)], axis=1)


def diagonal(product):
    first = lax.broadcasted_iota(jnp.int32, (HD, PAIR), 1) < HD
    return jnp.where(first, product[:HD], product[HD:])


def head_ones():
    row = lax.broadcasted_iota(jnp.int32, (QUAD, QUAD), 0) // HD
    lane = lax.broadcasted_iota(jnp.int32, (QUAD, QUAD), 1) // HD
    return jnp.where(row == lane, 1.0, 0.0).astype(BF16)


def unit_heads(value, ones):
    squares = mm((value * value).astype(BF16), ones)
    return value * lax.rsqrt(squares + EPS)


def norm_rows(hidden, gain):
    wide = hidden.astype(F32)
    mean_sq = jnp.mean(wide * wide, axis=-1, keepdims=True)
    return (wide * lax.rsqrt(mean_sq + EPS) * gain).astype(BF16)


def spread_rates(normed, w_rate, rate_base):
    rates = rate_base * jax.nn.sigmoid(mm_nt(normed, w_rate))
    high = rates.astype(BF16)
    low = (rates - high.astype(F32)).astype(BF16)
    heads = rates.shape[1]
    row = lax.broadcasted_iota(jnp.int32, (heads, heads * HD), 0)
    lane = lax.broadcasted_iota(jnp.int32, (heads, heads * HD), 1) // HD
    pick = jnp.where(row == lane, 1.0, 0.0).astype(BF16)
    return mm(high, pick) + mm(low, pick)


def staged(groups, depth=3):
    for group in groups[:depth]:
        for copy in group:
            copy.start()

    def wait(index):
        for copy in groups[index]:
            copy.wait()
        if index + depth < len(groups):
            for copy in groups[index + depth]:
                copy.start()

    return wait


def on_section(active, body):
    pl.when(lax.axis_index("section") == active)(body)


def front(active, h_ref, gain_hbm, w_hbm, w_rate_hbm, base_hbm, maps, normed_out, keys_out, x_out, y_out, wkv, h_in, gain, w_rate, base, small_sems, sems):
    width = keys_out.shape[1]
    quads = width // QUAD

    def body():
        sources = [(gain_hbm, gain), (w_rate_hbm, w_rate), (base_hbm, base)]
        if h_in is not None:
            sources.append((h_ref, h_in))
        small = [pltpu.make_async_copy(source, target, small_sems.at[index]) for index, (source, target) in enumerate(sources)]
        for copy in small:
            copy.start()
        wait_group = staged(
            [
                [
                    pltpu.make_async_copy(
                        w_hbm.at[0, :, pl.ds((side + 1) * width + quad * QUAD, QUAD)],
                        wkv.at[:, pl.ds(side * width + quad * QUAD, QUAD)],
                        sems.at[quad, side],
                    )
                    for side in range(2)
                ]
                for quad in range(quads)
            ]
        )
        for copy in small:
            copy.wait()
        normed = norm_rows((h_ref if h_in is None else h_in)[...], gain[...])
        normed_out[...] = normed
        rates = spread_rates(normed, w_rate[0], base[...])
        ones = head_ones()

        def project(quad):
            wait_group(quad)
            lanes = slice(quad * QUAD, (quad + 1) * QUAD)
            return mm(normed, wkv[:, lanes]), mm(normed, wkv[:, width + quad * QUAD : width + (quad + 1) * QUAD])

        def chain(quad, keys, values):
            lanes = slice(quad * QUAD, (quad + 1) * QUAD)
            keys = unit_heads(keys, ones)
            keys_bf = keys.astype(BF16)
            keys_out[:, lanes] = keys_bf
            rate = rates[:, lanes]
            x_all = rate * keys
            y_all = rate * values
            x_first, y_first = x_all[:HD].astype(BF16), y_all[:HD].astype(BF16)
            cross = mm_nt(keys_bf[HD:], spread(keys_bf[:HD])).astype(BF16)
            fix = mm(cross, spread_two(x_first, y_first))
            x_second = (x_all[HD:] - rate[HD:] * fix[:, :QUAD]).astype(BF16)
            y_second = (y_all[HD:] - rate[HD:] * fix[:, QUAD:]).astype(BF16)
            x_bf = jnp.concatenate([x_first, x_second], axis=0)
            y_bf = jnp.concatenate([y_first, y_second], axis=0)
            x_out[:, lanes] = x_bf
            y_out[:, lanes] = y_bf
            for half in range(2):
                own = slice(half * PAIR, (half + 1) * PAIR)
                start = quad * QUAD + half * PAIR
                both = mm_tn(keys_bf[:, own], jnp.concatenate([x_bf[:, own], y_bf[:, own]], axis=1))
                maps[:, start : start + PAIR] = diagonal(both[:, :PAIR]).astype(BF16)
                maps[:, width + start : width + start + PAIR] = diagonal(both[:, PAIR:]).astype(BF16)

        before = project(0)
        for quad in range(1, quads):
            after = project(quad)
            chain(quad - 1, *before)
            before = after
        chain(quads - 1, *before)

    on_section(active, body)


def first_front(h_hbm, *rest):
    front(0, h_hbm, *rest)


def later_front(h_ref, *rest):
    *rest, small_sems, sems = rest
    front(1, h_ref, *rest[:10], None, *rest[10:], small_sems, sems)


def read_out(active, quads, normed_ref, keys_ref, x_ref, y_ref, w_hbm, w_out_hbm, after_ref, reads_out, *rest):
    w_out, (wq, sems, load_sem) = rest[:-3], rest[-3:]
    rows = keys_ref.shape[0]
    part = len(quads) * QUAD

    def body():
        wait_group = staged(
            [
                [
                    pltpu.make_async_copy(
                        w_hbm.at[0, :, pl.ds(quad * QUAD, QUAD)], wq.at[:, pl.ds(index * QUAD, QUAD)], sems.at[index]
                    )
                ]
                for index, quad in enumerate(quads)
            ],
            len(quads),
        )
        loads = [pltpu.make_async_copy(w_out_hbm.at[0], target, load_sem) for target in w_out]
        for load in loads:
            load.start()
        normed = normed_ref[...]
        ones = head_ones()
        row = lax.broadcasted_iota(jnp.int32, (rows, 2 * rows), 0)
        lane = lax.rem(lax.broadcasted_iota(jnp.int32, (rows, 2 * rows), 1), rows)
        causal = row >= lane
        for index, quad in enumerate(quads):
            wait_group(index)
            queries = unit_heads(mm(normed, wq[:, index * QUAD : (index + 1) * QUAD]), ones)
            queries_bf = queries.astype(BF16)
            for half in range(2):
                own = slice(half * PAIR, (half + 1) * PAIR)
                place = slice(quad * QUAD + half * PAIR, quad * QUAD + (half + 1) * PAIR)
                start = index * QUAD + half * PAIR
                scores = mm_nt(queries_bf[:, own], spread(keys_ref[:, place]))
                scores = jnp.where(causal, scores, 0.0).astype(BF16)
                both = mm(scores, spread_two(x_ref[:, place], y_ref[:, place]))
                reads_out[:, start : start + PAIR] = (queries[:, own] - both[:, :PAIR]).astype(BF16)
                reads_out[:, part + start : part + start + PAIR] = both[:, PAIR:].astype(BF16)
        for load in loads:
            load.wait()

    on_section(active, body)


def compose(active, own_ref, got_ref, after_ref, out_ref):
    width = own_ref.shape[1] // 2

    def body(first_ref, second_ref):
        for start in range(0, width, PAIR):
            s_lanes, b_lanes = slice(start, start + PAIR), slice(width + start, width + start + PAIR)
            s_second, s_first, b_first = second_ref[:, s_lanes], first_ref[:, s_lanes], first_ref[:, b_lanes]
            step = mm(s_second, spread_two(s_first, b_first))
            out_ref[:, s_lanes] = (s_second.astype(F32) + s_first.astype(F32) - step[:, :PAIR]).astype(BF16)
            out_ref[:, b_lanes] = (second_ref[:, b_lanes].astype(F32) + b_first.astype(F32) - step[:, PAIR:]).astype(BF16)

    here = lax.axis_index("section") == active
    side = lax.rem(lax.axis_index("seq"), 2)
    pl.when(here & (side == 0))(lambda: body(own_ref, got_ref))
    pl.when(here & (side == 1))(lambda: body(got_ref, own_ref))


def pair_state(init_ref, pair):
    return jnp.concatenate([init_ref[0, 2 * pair], init_ref[0, 2 * pair + 1]], axis=1)


def apply_map(state, ref, start, width):
    step = mm(ref[:, start : start + PAIR], spread(state.astype(BF16)))
    return state - step + ref[:, width + start : width + start + PAIR].astype(F32)


def advance(active, place, own_ref, got_ref, state_ref, after_ref, out_ref):
    width = out_ref.shape[1]

    def body(refs):
        for start in range(0, width, PAIR):
            lanes = slice(start, start + PAIR)
            state = state_ref[:, lanes].astype(F32) if place else pair_state(state_ref, start // PAIR)
            for ref in refs:
                state = apply_map(state, ref, start, width)
            out_ref[:, lanes] = state.astype(BF16)

    index = lax.axis_index("seq")
    here = (lax.axis_index("section") == active) & (index // 2 == place)
    if got_ref is None:
        pl.when(here)(lambda: body((own_ref,)))
    else:
        side = lax.rem(index, 2)
        pl.when(here & (side == 0))(lambda: body((own_ref, got_ref)))
        pl.when(here & (side == 1))(lambda: body((got_ref, own_ref)))


def finish(active, state_refs, got_refs, init_ref, reads_refs, w_out_ref, h_ref, store):
    width = w_out_ref.shape[0]
    part = width // len(reads_refs)
    model = h_ref.shape[1]
    chunk = model // 4

    def total(refs, lanes):
        value = refs[0][:, lanes].astype(F32)
        for ref in refs[1:]:
            value = value + ref[:, lanes].astype(F32)
        return value

    def body():
        index = lax.axis_index("seq")
        begins = index // 2 == 0
        follows = lax.rem(index, 2) == 1
        parts = []
        for start in range(0, width, QUAD):
            pieces = []
            for lane in range(start, start + QUAD, PAIR):
                lanes = slice(lane, lane + PAIR)
                state = jnp.where(begins, pair_state(init_ref, lane // PAIR), total(state_refs, lanes))
                step = mm(total(got_refs, lanes).astype(BF16), spread(state.astype(BF16)))
                moved = state - step + total(got_refs, slice(width + lane, width + lane + PAIR))
                pieces.append(jnp.where(follows, moved, state).astype(BF16))
            reads_ref, inner = reads_refs[start // part], start % part
            offset = reads_ref[:, part + inner : part + inner + QUAD]
            read = mm(reads_ref[:, inner : inner + QUAD], spread(jnp.concatenate(pieces, axis=1)))
            parts.append((read + offset.astype(F32)).astype(BF16))
        inner_bf = jnp.concatenate(parts, axis=1)
        for start in range(0, model, chunk):
            lanes = slice(start, start + chunk)
            store(start, (h_ref[:, lanes].astype(F32) + mm(inner_bf, w_out_ref[:, lanes])).astype(BF16))

    on_section(active, body)


def split_finish(counts, refs):
    states, gots, reads = counts
    return refs[:states], refs[states : states + gots], refs[states + gots], refs[states + gots + 1 :][:reads], refs[states + gots + 1 + reads :]


def first_finish(counts, *refs):
    states, gots, init_ref, reads, (w_out_ref, h_ref, out_ref) = split_finish(counts, refs)

    def store(start, value):
        out_ref[:, start : start + value.shape[1]] = value

    finish(0, states, gots, init_ref, reads, w_out_ref, h_ref, store)


def last_finish(counts, *refs):
    states, gots, init_ref, reads, (w_out_ref, h_ref, first_ref, out_hbm, near, sems) = split_finish(counts, refs)
    chunk = near.shape[1] // 4

    def write(start):
        lanes = pl.ds(start, chunk)
        return pltpu.make_async_copy(near.at[:, lanes], out_hbm.at[0, :, lanes], sems.at[start // chunk])

    def store(start, value):
        near[:, start : start + chunk] = value
        write(start).start()

    finish(1, states, gots, init_ref, reads, w_out_ref, h_ref, store)

    @pl.when(lax.axis_index("section") == 0)
    def _():
        for start in range(0, near.shape[1], chunk):
            store(start, first_ref[:, start : start + chunk])

    for start in range(0, near.shape[1], chunk):
        write(start).wait()


def call(body, outs, scratch, args, kinds=None, name=None, out_kind=pltpu.VMEM):
    specs = [pl.BlockSpec(memory_space=kind) for kind in (kinds or [pltpu.VMEM] * len(args))]
    return pl.pallas_call(
        body,
        out_shape=outs,
        in_specs=specs,
        out_specs=[pl.BlockSpec(memory_space=out_kind)] * len(outs),
        scratch_shapes=scratch,
        compiler_params=pltpu.CompilerParams(vmem_limit_bytes=VMEM_LIMIT),
        name=name,
    )(*args)


def shards(tokens, norm_gain, w_qkv, w_rate, rate_base, init_state, w_out):
    count = lax.axis_size("seq")
    heads = rate_base.shape[1]
    rows, model = tokens.shape
    width = heads * HD
    depth = w_qkv.shape[1]
    quads = width // QUAD
    shape = jax.ShapeDtypeStruct
    in_vmem = functools.partial(pltpu.with_memory_space_constraint, memory_space=pltpu.VMEM)
    in_hbm = functools.partial(pltpu.with_memory_space_constraint, memory_space=pltpu.HBM)
    maps = shape((HD, 2 * width), BF16)
    rows_out = [shape((rows, model), BF16)] + [shape((rows, width), BF16)] * 3
    w_rate = jnp.swapaxes(w_rate, 1, 2)
    norm_gain, w_qkv, w_rate, rate_base, w_out = [in_hbm(value) for value in (norm_gain, w_qkv, w_rate, rate_base, w_out)]

    def permute(value, active, pairs):
        base = active * count
        return lax.ppermute(value, ("section", "seq"), [(base + source, base + target) for source, target in pairs])

    def swap(own, active, groups):
        return permute(own, active, [(2 * group + side, 2 * group + 1 - side) for group in groups for side in range(2)])

    def layer(active, hidden):
        h_scratch = [] if active else [pltpu.VMEM(hidden.shape, hidden.dtype)]
        own, normed, keys, x_all, y_all = call(
            later_front if active else first_front,
            [maps] + rows_out,
            [pltpu.VMEM((depth, 2 * width), BF16)]
            + h_scratch
            + [pltpu.VMEM(value.shape, value.dtype) for value in (norm_gain, w_rate, rate_base)]
            + [pltpu.SemaphoreType.DMA((4,)), pltpu.SemaphoreType.DMA((quads, 2))],
            [hidden if active else in_hbm(hidden), norm_gain, w_qkv, w_rate, rate_base],
            [pltpu.VMEM if active else pltpu.HBM] + [pltpu.HBM] * 4,
            name="later_front" if active else "first_front",
        )

        def reads_of(picked, load, after):
            part = len(picked) * QUAD
            return call(
                functools.partial(read_out, active, picked),
                [shape((rows, 2 * part), BF16)] + [pltpu.VMEM(w_out.shape[1:], BF16)] * load,
                [pltpu.VMEM((depth, part), BF16), pltpu.SemaphoreType.DMA((len(picked),)), pltpu.SemaphoreType.DMA],
                [normed, keys, x_all, y_all, w_qkv, w_out, after],
                [pltpu.VMEM] * 4 + [pltpu.HBM] * 2 + [pl.ANY],
                name=f"reads{active}_{picked[0]}",
            )

        def hop(place, maps_here, state, after):
            kinds = [pltpu.VMEM] * (len(maps_here) + 1) + [pl.ANY]

            def body(*refs):
                advance(active, place, refs[0], None if len(maps_here) == 1 else refs[1], *refs[len(maps_here) :])

            (ahead,) = call(body, [shape((HD, width), BF16)], [], maps_here + [state, after], kinds, name=f"advance{active}_{place}")
            pairs = [(2 * place + side, 2 * place + 2 + side) for side in range(2)]
            return ahead, permute(ahead, active, pairs)

        groups = count // 2
        states, state = [], init_state
        if active == 0:
            got = [swap(own, active, range(groups))]
            reads, near = reads_of(tuple(range(quads)), 1, init_state)
            reads = [reads]
            (both,) = call(functools.partial(compose, active), [maps], [], [own, got[0], reads[0]], [pltpu.VMEM] * 2 + [pl.ANY], name="compose")
            for place in range(groups - 1):
                ahead, state = hop(place, [both], state, both)
                states.append(state)
        else:
            got = [swap(own, active, [group]) for group in range(groups)]
            (reads,) = reads_of(tuple(range(quads // 2)), 0, init_state)
            for place in range(groups - 1):
                ahead, state = hop(place, [own, got[place]], state, reads)
                states.append(state)
            more, near = reads_of(tuple(range(quads // 2, quads)), 1, ahead)
            reads = [reads, more]
        return (len(states), len(got), len(reads)), [*states, *got, init_state, *reads, in_vmem(near), hidden]

    counts, args = layer(0, tokens)
    (first,) = call(functools.partial(first_finish, counts), [shape((rows, model), BF16)], [], args, name="first_finish")
    hidden = lax.ppermute(first, "section", [(0, 1)])
    counts, args = layer(1, hidden)
    (result,) = call(
        functools.partial(last_finish, counts),
        [shape((1, rows, model), BF16)],
        [pltpu.VMEM((rows, model), BF16), pltpu.SemaphoreType.DMA((4,))],
        args + [first],
        name="last_finish",
        out_kind=pltpu.HBM,
    )
    return result


def solution(mesh):
    return jax.shard_map(
        shards,
        mesh=mesh,
        in_specs=(
            P(("traj", "seq"), None),
            P("section", None),
            P("section", None, None),
            P("section", None, None),
            P("section", None),
            P("section", None, None, None),
            P("section", None, None),
        ),
        out_specs=P("section", ("traj", "seq"), None),
        check_vma=False,
    )
```

```python
import functools

import jax
import jax.numpy as jnp
from jax import lax
from jax.experimental import pallas as pl
from jax.experimental.pallas import tpu as pltpu
from jax.sharding import PartitionSpec as P

HD = 64
PAIR = 2 * HD
QUAD = 4 * HD
F32 = jnp.float32
BF16 = jnp.bfloat16
EPS = 1e-6
VMEM_LIMIT = 16 * 1024 * 1024


def mm(a, b):
    return jnp.dot(a, b, preferred_element_type=F32)


def mm_nt(a, b):
    return lax.dot_general(a, b, (((1,), (1,)), ((), ())), preferred_element_type=F32)


def mm_tn(a, b):
    return lax.dot_general(a, b, (((0,), (0,)), ((), ())), preferred_element_type=F32)


def head_masks(rows, lanes):
    lane = lax.broadcasted_iota(jnp.int32, (rows, lanes), 1)
    return [lane // HD == index for index in range(lanes // HD)]


def spread(value):
    zero = jnp.zeros_like(value)
    masks = head_masks(*value.shape)
    return jnp.concatenate([jnp.where(mask, value, zero) for mask in masks], axis=0)


def spread_two(left, right):
    return jnp.concatenate([spread(left), spread(right)], axis=1)


def diagonal(product):
    first = lax.broadcasted_iota(jnp.int32, (HD, PAIR), 1) < HD
    return jnp.where(first, product[:HD], product[HD:])


def head_ones():
    row = lax.broadcasted_iota(jnp.int32, (QUAD, QUAD), 0) // HD
    lane = lax.broadcasted_iota(jnp.int32, (QUAD, QUAD), 1) // HD
    return jnp.where(row == lane, 1.0, 0.0).astype(BF16)


def unit_heads(value, ones):
    squares = mm((value * value).astype(BF16), ones)
    return value * lax.rsqrt(squares + EPS)


def norm_rows(hidden, gain):
    wide = hidden.astype(F32)
    mean_sq = jnp.mean(wide * wide, axis=-1, keepdims=True)
    return (wide * lax.rsqrt(mean_sq + EPS) * gain).astype(BF16)


def spread_rates(normed, w_rate, rate_base):
    rates = rate_base * jax.nn.sigmoid(mm_nt(normed, w_rate))
    high = rates.astype(BF16)
    low = (rates - high.astype(F32)).astype(BF16)
    heads = rates.shape[1]
    row = lax.broadcasted_iota(jnp.int32, (heads, heads * HD), 0)
    lane = lax.broadcasted_iota(jnp.int32, (heads, heads * HD), 1) // HD
    pick = jnp.where(row == lane, 1.0, 0.0).astype(BF16)
    return mm(high, pick) + mm(low, pick)


def staged(groups, depth=3):
    for group in groups[:depth]:
        for copy in group:
            copy.start()

    def wait(index):
        for copy in groups[index]:
            copy.wait()
        if index + depth < len(groups):
            for copy in groups[index + depth]:
                copy.start()

    return wait


def on_section(active, body):
    pl.when(lax.axis_index("section") == active)(body)


def front(active, h_ref, gain_hbm, w_ref, w_rate_hbm, base_hbm, maps, normed_out, keys_out, x_out, y_out, wkv, h_in, gain, w_rate, base, small_sems, sems):
    width = keys_out.shape[1]
    quads = width // QUAD

    def body():
        sources = [(gain_hbm, gain), (w_rate_hbm, w_rate), (base_hbm, base)]
        if h_in is not None:
            sources.append((h_ref, h_in))
        small = [pltpu.make_async_copy(source, target, small_sems.at[index]) for index, (source, target) in enumerate(sources)]
        for copy in small:
            copy.start()
        if wkv is not None:
            wait_group = staged(
                [
                    [
                        pltpu.make_async_copy(
                            w_ref.at[0, :, pl.ds((side + 1) * width + quad * QUAD, QUAD)],
                            wkv.at[:, pl.ds(side * width + quad * QUAD, QUAD)],
                            sems.at[quad, side],
                        )
                        for side in range(2)
                    ]
                    for quad in range(quads)
                ]
            )
        for copy in small:
            copy.wait()
        normed = norm_rows((h_ref if h_in is None else h_in)[...], gain[...])
        normed_out[...] = normed
        rates = spread_rates(normed, w_rate[0], base[...])
        ones = head_ones()

        def project(quad):
            if wkv is None:
                weights, base_lane = w_ref, width
            else:
                weights, base_lane = wkv, 0
                wait_group(quad)
            key_lane = base_lane + quad * QUAD
            return [mm(normed, weights[:, lane : lane + QUAD]) for lane in (key_lane, key_lane + width)]

        def chain(quad, keys, values):
            lanes = slice(quad * QUAD, (quad + 1) * QUAD)
            keys = unit_heads(keys, ones)
            keys_bf = keys.astype(BF16)
            keys_out[:, lanes] = keys_bf
            rate = rates[:, lanes]
            x_all = rate * keys
            y_all = rate * values
            x_first, y_first = x_all[:HD].astype(BF16), y_all[:HD].astype(BF16)
            cross = mm_nt(keys_bf[HD:], spread(keys_bf[:HD])).astype(BF16)
            fix = mm(cross, spread_two(x_first, y_first))
            x_second = (x_all[HD:] - rate[HD:] * fix[:, :QUAD]).astype(BF16)
            y_second = (y_all[HD:] - rate[HD:] * fix[:, QUAD:]).astype(BF16)
            x_bf = jnp.concatenate([x_first, x_second], axis=0)
            y_bf = jnp.concatenate([y_first, y_second], axis=0)
            x_out[:, lanes] = x_bf
            y_out[:, lanes] = y_bf
            for half in range(2):
                own = slice(half * PAIR, (half + 1) * PAIR)
                start = quad * QUAD + half * PAIR
                both = mm_tn(keys_bf[:, own], jnp.concatenate([x_bf[:, own], y_bf[:, own]], axis=1))
                maps[:, start : start + PAIR] = diagonal(both[:, :PAIR]).astype(BF16)
                maps[:, width + start : width + start + PAIR] = diagonal(both[:, PAIR:]).astype(BF16)

        before = project(0)
        for quad in range(1, quads):
            after = project(quad)
            chain(quad - 1, *before)
            before = after
        chain(quads - 1, *before)

    on_section(active, body)


def first_front(h_hbm, *rest):
    front(0, h_hbm, *rest)


def later_front(h_ref, *rest):
    *rest, gain, w_rate, base, small_sems = rest
    front(1, h_ref, *rest, None, None, gain, w_rate, base, small_sems, None)


def load(w_hbm, after_ref, near, sem):
    def body():
        copy = pltpu.make_async_copy(w_hbm.at[0], near, sem)
        copy.start()
        copy.wait()

    on_section(1, body)


def read_out(active, normed_ref, keys_ref, x_ref, y_ref, w_ref, w_out_hbm, after_ref, reads_out, w_out, load_sem, wq=None, sems=None):
    rows, width = keys_ref.shape
    quads = width // QUAD

    def body():
        if wq is not None:
            wait_group = staged(
                [
                    [pltpu.make_async_copy(w_ref.at[0, :, pl.ds(quad * QUAD, QUAD)], wq.at[:, pl.ds(quad * QUAD, QUAD)], sems.at[quad])]
                    for quad in range(quads)
                ],
                quads,
            )
        fetch = pltpu.make_async_copy(w_out_hbm.at[0], w_out, load_sem)
        fetch.start()
        weights = w_ref if wq is None else wq
        normed = normed_ref[...]
        ones = head_ones()
        row = lax.broadcasted_iota(jnp.int32, (rows, 2 * rows), 0)
        lane = lax.rem(lax.broadcasted_iota(jnp.int32, (rows, 2 * rows), 1), rows)
        causal = row >= lane
        for quad in range(quads):
            if wq is not None:
                wait_group(quad)
            queries = unit_heads(mm(normed, weights[:, quad * QUAD : (quad + 1) * QUAD]), ones)
            queries_bf = queries.astype(BF16)
            for half in range(2):
                own = slice(half * PAIR, (half + 1) * PAIR)
                start = quad * QUAD + half * PAIR
                place = slice(start, start + PAIR)
                scores = mm_nt(queries_bf[:, own], spread(keys_ref[:, place]))
                scores = jnp.where(causal, scores, 0.0).astype(BF16)
                both = mm(scores, spread_two(x_ref[:, place], y_ref[:, place]))
                reads_out[:, place] = (queries[:, own] - both[:, :PAIR]).astype(BF16)
                reads_out[:, width + start : width + start + PAIR] = both[:, PAIR:].astype(BF16)
        fetch.wait()

    on_section(active, body)


def compose(active, own_ref, got_ref, after_ref, out_ref):
    width = own_ref.shape[1] // 2

    def body(first_ref, second_ref):
        for start in range(0, width, PAIR):
            s_lanes, b_lanes = slice(start, start + PAIR), slice(width + start, width + start + PAIR)
            s_second, s_first, b_first = second_ref[:, s_lanes], first_ref[:, s_lanes], first_ref[:, b_lanes]
            step = mm(s_second, spread_two(s_first, b_first))
            out_ref[:, s_lanes] = (s_second.astype(F32) + s_first.astype(F32) - step[:, :PAIR]).astype(BF16)
            out_ref[:, b_lanes] = (second_ref[:, b_lanes].astype(F32) + b_first.astype(F32) - step[:, PAIR:]).astype(BF16)

    here = lax.axis_index("section") == active
    side = lax.rem(lax.axis_index("seq"), 2)
    pl.when(here & (side == 0))(lambda: body(own_ref, got_ref))
    pl.when(here & (side == 1))(lambda: body(got_ref, own_ref))


def pair_state(init_ref, pair):
    return jnp.concatenate([init_ref[0, 2 * pair], init_ref[0, 2 * pair + 1]], axis=1)


def apply_map(state, ref, start, width):
    step = mm(ref[:, start : start + PAIR], spread(state.astype(BF16)))
    return state - step + ref[:, width + start : width + start + PAIR].astype(F32)


def advance(active, place, own_ref, got_ref, state_ref, after_ref, out_ref):
    width = out_ref.shape[1]

    def body(refs):
        for start in range(0, width, PAIR):
            lanes = slice(start, start + PAIR)
            state = state_ref[:, lanes].astype(F32) if place else pair_state(state_ref, start // PAIR)
            for ref in refs:
                state = apply_map(state, ref, start, width)
            out_ref[:, lanes] = state.astype(BF16)

    index = lax.axis_index("seq")
    here = (lax.axis_index("section") == active) & (index // 2 == place)
    if got_ref is None:
        pl.when(here)(lambda: body((own_ref,)))
    else:
        side = lax.rem(index, 2)
        pl.when(here & (side == 0))(lambda: body((own_ref, got_ref)))
        pl.when(here & (side == 1))(lambda: body((got_ref, own_ref)))


def finish(here, begins, state_refs, got_refs, init_ref, reads_ref, w_out_ref, h_ref, store):
    width = w_out_ref.shape[0]
    model = h_ref.shape[1]
    chunk = model // 4

    def total(refs, lanes):
        value = refs[0][:, lanes].astype(F32)
        for ref in refs[1:]:
            value = value + ref[:, lanes].astype(F32)
        return value

    def body():
        follows = lax.rem(lax.axis_index("seq"), 2) == 1
        parts = []
        for start in range(0, width, QUAD):
            pieces = []
            for lane in range(start, start + QUAD, PAIR):
                lanes = slice(lane, lane + PAIR)
                if begins is True:
                    state = pair_state(init_ref, lane // PAIR)
                else:
                    state = total(state_refs, lanes)
                    if begins is not False:
                        state = jnp.where(begins, pair_state(init_ref, lane // PAIR), state)
                step = mm(total(got_refs, lanes).astype(BF16), spread(state.astype(BF16)))
                moved = state - step + total(got_refs, slice(width + lane, width + lane + PAIR))
                pieces.append(jnp.where(follows, moved, state).astype(BF16))
            offset = reads_ref[:, width + start : width + start + QUAD]
            read = mm(reads_ref[:, start : start + QUAD], spread(jnp.concatenate(pieces, axis=1)))
            parts.append((read + offset.astype(F32)).astype(BF16))
        inner_bf = jnp.concatenate(parts, axis=1)
        for start in range(0, model, chunk):
            lanes = slice(start, start + chunk)
            store(start, (h_ref[:, lanes].astype(F32) + mm(inner_bf, w_out_ref[:, lanes])).astype(BF16))

    pl.when(here)(body)


def first_finish(place, state_ref, got_ref, reads_ref, w_out_ref, h_ref, *rest):
    out_ref = rest[-1]

    def store(start, value):
        out_ref[:, start : start + value.shape[1]] = value

    here = (lax.axis_index("section") == 0) & (lax.axis_index("seq") // 2 == place)
    finish(here, place == 0, [state_ref], [got_ref], state_ref, reads_ref, w_out_ref, h_ref, store)


def last_finish(count, *refs):
    states, gots, refs = refs[: count - 1], refs[count - 1 : 2 * count - 1], refs[2 * count - 1 :]
    init_ref, reads_ref, w_out_ref, h_ref, first_ref, out_hbm, near, sems = refs
    chunk = near.shape[1] // 4

    def write(start):
        lanes = pl.ds(start, chunk)
        return pltpu.make_async_copy(near.at[:, lanes], out_hbm.at[0, :, lanes], sems.at[start // chunk])

    def store(start, value):
        near[:, start : start + chunk] = value
        write(start).start()

    begins = lax.axis_index("seq") // 2 == 0
    finish(lax.axis_index("section") == 1, begins, states, gots, init_ref, reads_ref, w_out_ref, h_ref, store)

    @pl.when(lax.axis_index("section") == 0)
    def _():
        for start in range(0, near.shape[1], chunk):
            store(start, first_ref[:, start : start + chunk])

    for start in range(0, near.shape[1], chunk):
        write(start).wait()


def call(body, outs, scratch, args, kinds=None, name=None, out_kind=pltpu.VMEM, aliases=None):
    specs = [pl.BlockSpec(memory_space=kind) for kind in (kinds or [pltpu.VMEM] * len(args))]
    return pl.pallas_call(
        body,
        out_shape=outs,
        in_specs=specs,
        out_specs=[pl.BlockSpec(memory_space=out_kind)] * len(outs),
        scratch_shapes=scratch,
        input_output_aliases=aliases or {},
        compiler_params=pltpu.CompilerParams(vmem_limit_bytes=VMEM_LIMIT),
        name=name,
    )(*args)


def shards(tokens, norm_gain, w_qkv, w_rate, rate_base, init_state, w_out):
    count = lax.axis_size("seq")
    heads = rate_base.shape[1]
    rows, model = tokens.shape
    width = heads * HD
    depth = w_qkv.shape[1]
    quads = width // QUAD
    shape = jax.ShapeDtypeStruct
    in_vmem = functools.partial(pltpu.with_memory_space_constraint, memory_space=pltpu.VMEM)
    in_hbm = functools.partial(pltpu.with_memory_space_constraint, memory_space=pltpu.HBM)
    maps = shape((HD, 2 * width), BF16)
    rows_out = [shape((rows, model), BF16)] + [shape((rows, width), BF16)] * 3
    w_rate = jnp.swapaxes(w_rate, 1, 2)
    norm_gain, w_qkv, w_rate, rate_base, w_out = [in_hbm(value) for value in (norm_gain, w_qkv, w_rate, rate_base, w_out)]

    def permute(value, active, pairs):
        base = active * count
        return lax.ppermute(value, ("section", "seq"), [(base + source, base + target) for source, target in pairs])

    def swap(own, active, groups):
        return permute(own, active, [(2 * group + side, 2 * group + 1 - side) for group in groups for side in range(2)])

    def layer_front(active, hidden, weights):
        small = [pltpu.VMEM(value.shape, value.dtype) for value in (norm_gain, w_rate, rate_base)]
        near = [pltpu.VMEM((depth, 2 * width), BF16), pltpu.VMEM(hidden.shape, hidden.dtype)]
        sems = [pltpu.SemaphoreType.DMA((quads, 2))]
        return call(
            later_front if active else first_front,
            [maps] + rows_out,
            (near if active == 0 else []) + small + [pltpu.SemaphoreType.DMA((4,))] + (sems if active == 0 else []),
            [hidden, norm_gain, weights, w_rate, rate_base],
            [pltpu.VMEM, pltpu.HBM, pltpu.VMEM, pltpu.HBM, pltpu.HBM] if active else [pltpu.HBM] * 5,
            name="later_front" if active else "first_front",
        )

    def layer_reads(active, rows_of, weights, after):
        near = [pltpu.VMEM((depth, width), BF16), pltpu.SemaphoreType.DMA((quads,))]
        reads, w_out_near = call(
            functools.partial(read_out, active),
            [shape((rows, 2 * width), BF16), pltpu.VMEM(w_out.shape[1:], BF16)],
            [pltpu.SemaphoreType.DMA] + (near if active == 0 else []),
            [*rows_of, weights, w_out, after],
            [pltpu.VMEM] * 4 + [pltpu.VMEM if active else pltpu.HBM, pltpu.HBM, pl.ANY],
            name=f"reads{active}",
        )
        return reads, in_vmem(w_out_near)

    def hop(active, place, maps_here, state, after):
        def body(*refs):
            advance(active, place, refs[0], None if len(maps_here) == 1 else refs[1], *refs[len(maps_here) :])

        kinds = [pltpu.VMEM] * (len(maps_here) + 1) + [pl.ANY]
        (ahead,) = call(body, [shape((HD, width), BF16)], [], maps_here + [state, after], kinds, name=f"advance{active}_{place}")
        return ahead, permute(ahead, active, [(2 * place + side, 2 * place + 2 + side) for side in range(2)])

    groups = count // 2

    own, *rows_of = layer_front(0, in_hbm(tokens), w_qkv)
    got = swap(own, 0, range(groups))
    reads, w_out_near = layer_reads(0, rows_of, w_qkv, init_state)
    (both,) = call(functools.partial(compose, 0), [maps], [], [own, got, reads], [pltpu.VMEM] * 2 + [pl.ANY], name="compose")
    (w_near,) = call(
        load, [pltpu.VMEM(w_qkv.shape[1:], BF16)], [pltpu.SemaphoreType.DMA], [w_qkv, both], [pltpu.HBM, pl.ANY], name="load"
    )
    w_near = in_vmem(w_near)
    state, first = init_state, []
    for place in range(groups):
        here = state
        if place + 1 < groups:
            ahead, state = hop(0, place, [both], here, first[0] if first else both)
        first = call(
            functools.partial(first_finish, place),
            [shape((rows, model), BF16)],
            [],
            [here, got, reads, w_out_near, tokens, ahead, *first],
            [pltpu.VMEM] * 5 + [pl.ANY] + [pltpu.VMEM] * len(first),
            name=f"first_finish_{place}",
            aliases={6: 0} if first else None,
        )
    (first,) = first
    hidden = lax.ppermute(first, "section", [(0, 1)])

    own, *rows_of = layer_front(1, hidden, w_near)
    gots = [swap(own, 1, [group]) for group in range(groups)]
    states, state, ahead = [], init_state, own
    for place in range(groups - 1):
        ahead, state = hop(1, place, [own, gots[place]], state, ahead)
        states.append(state)
    reads, w_out_near = layer_reads(1, rows_of, w_near, ahead)
    (result,) = call(
        functools.partial(last_finish, groups),
        [shape((1, rows, model), BF16)],
        [pltpu.VMEM((rows, model), BF16), pltpu.SemaphoreType.DMA((4,))],
        [*states, *gots, init_state, reads, w_out_near, hidden, first],
        name="last_finish",
        out_kind=pltpu.HBM,
    )
    return result


def solution(mesh):
    return jax.shard_map(
        shards,
        mesh=mesh,
        in_specs=(
            P(("traj", "seq"), None),
            P("section", None),
            P("section", None, None),
            P("section", None, None),
            P("section", None),
            P("section", None, None, None),
            P("section", None, None),
        ),
        out_specs=P("section", ("traj", "seq"), None),
        check_vma=False,
    )
```

```python
import functools

import jax
import jax.numpy as jnp
from jax import lax
from jax.experimental import pallas as pl
from jax.experimental.pallas import tpu as pltpu
from jax.sharding import PartitionSpec as P

HD = 64
PAIR = 2 * HD
QUAD = 4 * HD
F32 = jnp.float32
BF16 = jnp.bfloat16
EPS = 1e-6
VMEM_LIMIT = 16 * 1024 * 1024


def mm(a, b):
    return jnp.dot(a, b, preferred_element_type=F32)


def mm_nt(a, b):
    return lax.dot_general(a, b, (((1,), (1,)), ((), ())), preferred_element_type=F32)


def mm_tn(a, b):
    return lax.dot_general(a, b, (((0,), (0,)), ((), ())), preferred_element_type=F32)


def head_masks(rows, lanes):
    lane = lax.broadcasted_iota(jnp.int32, (rows, lanes), 1)
    return [lane // HD == index for index in range(lanes // HD)]


def spread(value):
    zero = jnp.zeros_like(value)
    masks = head_masks(*value.shape)
    return jnp.concatenate([jnp.where(mask, value, zero) for mask in masks], axis=0)


def spread_two(left, right):
    return jnp.concatenate([spread(left), spread(right)], axis=1)


def diagonal(product):
    first = lax.broadcasted_iota(jnp.int32, (HD, PAIR), 1) < HD
    return jnp.where(first, product[:HD], product[HD:])


def head_ones():
    row = lax.broadcasted_iota(jnp.int32, (QUAD, QUAD), 0) // HD
    lane = lax.broadcasted_iota(jnp.int32, (QUAD, QUAD), 1) // HD
    return jnp.where(row == lane, 1.0, 0.0).astype(BF16)


def unit_heads(value, ones):
    squares = mm((value * value).astype(BF16), ones)
    return value * lax.rsqrt(squares + EPS)


def norm_rows(hidden, gain):
    wide = hidden.astype(F32)
    mean_sq = jnp.mean(wide * wide, axis=-1, keepdims=True)
    return (wide * lax.rsqrt(mean_sq + EPS) * gain).astype(BF16)


def spread_rates(normed, w_rate, rate_base):
    rates = rate_base * jax.nn.sigmoid(mm_nt(normed, w_rate))
    high = rates.astype(BF16)
    low = (rates - high.astype(F32)).astype(BF16)
    heads = rates.shape[1]
    row = lax.broadcasted_iota(jnp.int32, (heads, heads * HD), 0)
    lane = lax.broadcasted_iota(jnp.int32, (heads, heads * HD), 1) // HD
    pick = jnp.where(row == lane, 1.0, 0.0).astype(BF16)
    return mm(high, pick) + mm(low, pick)


def start_all(copies):
    for copy in copies:
        copy.start()


def wait_all(copies):
    for copy in copies:
        copy.wait()


def on_section(active, body):
    pl.when(lax.axis_index("section") == active)(body)


def at_pair(places, active):
    pair = lax.axis_index("seq") // 2
    first, last = places[0], places[-1]
    return (lax.axis_index("section") == active) & (pair >= first) & (pair <= last)


def front(here, h_refs, gain_ref, w_ref, w_rate_ref, base_ref, maps, normed_out, keys_out, x_out, y_out, h_in, near=None):
    width = keys_out.shape[1]
    quads = width // QUAD

    def body():
        if near is None:
            groups = []
            gain, w_rate, base, weights, base_lane = gain_ref, w_rate_ref, base_ref, w_ref, width
            for place, ref in enumerate(h_refs):

                @pl.when(lax.axis_index("seq") // 2 == place)
                def _():
                    h_in[...] = ref[...]
        else:
            gain, w_rate, base, weights, small_sems, sems = near
            base_lane = 0
            pairs = [(gain_ref, gain), (w_rate_ref, w_rate), (base_ref, base), (h_refs[0], h_in)]
            small = [pltpu.make_async_copy(source, target, small_sems.at[index]) for index, (source, target) in enumerate(pairs)]
            groups = [
                [
                    pltpu.make_async_copy(
                        w_ref.at[0, :, pl.ds((side + 1) * width + quad * QUAD, QUAD)],
                        weights.at[:, pl.ds(side * width + quad * QUAD, QUAD)],
                        sems.at[quad, side],
                    )
                    for side in range(2)
                ]
                for quad in range(quads)
            ]
            start_all(small)
            start_all(groups[0])
            wait_all(small)
            start_all(groups[1])
        normed = norm_rows(h_in[...], gain[...])
        normed_out[...] = normed
        rates = spread_rates(normed, w_rate[0], base[...])
        ones = head_ones()

        def project(quad):
            if groups:
                wait_all(groups[quad])
                if quad + 2 < quads:
                    start_all(groups[quad + 2])
            key_lane = base_lane + quad * QUAD
            return [mm(normed, weights[:, lane : lane + QUAD]) for lane in (key_lane, key_lane + width)]

        def chain(quad, keys, values):
            lanes = slice(quad * QUAD, (quad + 1) * QUAD)
            keys = unit_heads(keys, ones)
            keys_bf = keys.astype(BF16)
            keys_out[:, lanes] = keys_bf
            rate = rates[:, lanes]
            x_all = rate * keys
            y_all = rate * values
            x_first, y_first = x_all[:HD].astype(BF16), y_all[:HD].astype(BF16)
            cross = mm_nt(keys_bf[HD:], spread(keys_bf[:HD])).astype(BF16)
            fix = mm(cross, spread_two(x_first, y_first))
            x_second = (x_all[HD:] - rate[HD:] * fix[:, :QUAD]).astype(BF16)
            y_second = (y_all[HD:] - rate[HD:] * fix[:, QUAD:]).astype(BF16)
            x_bf = jnp.concatenate([x_first, x_second], axis=0)
            y_bf = jnp.concatenate([y_first, y_second], axis=0)
            x_out[:, lanes] = x_bf
            y_out[:, lanes] = y_bf
            for half in range(2):
                own = slice(half * PAIR, (half + 1) * PAIR)
                start = quad * QUAD + half * PAIR
                both = mm_tn(keys_bf[:, own], jnp.concatenate([x_bf[:, own], y_bf[:, own]], axis=1))
                maps[:, start : start + PAIR] = diagonal(both[:, :PAIR]).astype(BF16)
                maps[:, width + start : width + start + PAIR] = diagonal(both[:, PAIR:]).astype(BF16)

        before = project(0)
        for quad in range(1, quads):
            after = project(quad)
            chain(quad - 1, *before)
            before = after
        chain(quads - 1, *before)

    pl.when(here)(body)


def first_front(h_hbm, gain, weights, w_rate, base, maps, normed_out, keys_out, x_out, y_out, h_in, *near):
    here = lax.axis_index("section") == 0
    front(here, [h_hbm], gain, weights, w_rate, base, maps, normed_out, keys_out, x_out, y_out, h_in, near)


def later_front(*refs):
    refs, rest = refs[:-10], refs[-10:]
    front(lax.axis_index("section") == 1, refs, *rest)


def load(*refs):
    count = (len(refs) - 2) // 2
    sources, targets, sems = refs[:count], refs[count + 1 : -1], refs[-1]

    def body():
        copies = [pltpu.make_async_copy(source, target, sems.at[index]) for index, (source, target) in enumerate(zip(sources, targets))]
        start_all(copies)
        wait_all(copies)

    on_section(1, body)


def read_out(active, places, normed_ref, keys_ref, x_ref, y_ref, w_ref, w_out_hbm, after_ref, *rest):
    if active:
        reads_out, w_out, load_sem = rest
    else:
        reads_out, w_out, load_sem, wq, sems = rest[-5:]
    rows, width = keys_ref.shape
    quads = width // QUAD

    def body():
        fetch = [pltpu.make_async_copy(w_out_hbm.at[0], w_out, load_sem)]
        if active:
            weights, groups = w_ref, []
            start_all(fetch)
        else:
            weights = wq
            groups = [
                [pltpu.make_async_copy(w_ref.at[0, :, pl.ds(quad * QUAD, QUAD)], wq.at[:, pl.ds(quad * QUAD, QUAD)], sems.at[quad])]
                for quad in range(quads)
            ]
            start_all(groups[0])
            start_all(groups[1])
        normed = normed_ref[...]
        ones = head_ones()
        row = lax.broadcasted_iota(jnp.int32, (rows, 2 * rows), 0)
        lane = lax.rem(lax.broadcasted_iota(jnp.int32, (rows, 2 * rows), 1), rows)
        causal = row >= lane
        for quad in range(quads):
            if groups:
                wait_all(groups[quad])
                if quad + 2 < quads:
                    start_all(groups[quad + 2])
                if quad + 3 == quads:
                    start_all(fetch)
            queries = unit_heads(mm(normed, weights[:, quad * QUAD : (quad + 1) * QUAD]), ones)
            queries_bf = queries.astype(BF16)
            for half in range(2):
                own = slice(half * PAIR, (half + 1) * PAIR)
                start = quad * QUAD + half * PAIR
                place = slice(start, start + PAIR)
                scores = mm_nt(queries_bf[:, own], spread(keys_ref[:, place]))
                scores = jnp.where(causal, scores, 0.0).astype(BF16)
                both = mm(scores, spread_two(x_ref[:, place], y_ref[:, place]))
                reads_out[:, place] = (queries[:, own] - both[:, :PAIR]).astype(BF16)
                reads_out[:, width + start : width + start + PAIR] = both[:, PAIR:].astype(BF16)
        wait_all(fetch)

    pl.when(at_pair(places, active))(body)


def compose(active, own_ref, got_ref, after_ref, out_ref):
    width = own_ref.shape[1] // 2

    def body(first_ref, second_ref):
        for start in range(0, width, PAIR):
            s_lanes, b_lanes = slice(start, start + PAIR), slice(width + start, width + start + PAIR)
            s_second, s_first, b_first = second_ref[:, s_lanes], first_ref[:, s_lanes], first_ref[:, b_lanes]
            step = mm(s_second, spread_two(s_first, b_first))
            out_ref[:, s_lanes] = (s_second.astype(F32) + s_first.astype(F32) - step[:, :PAIR]).astype(BF16)
            out_ref[:, b_lanes] = (second_ref[:, b_lanes].astype(F32) + b_first.astype(F32) - step[:, PAIR:]).astype(BF16)

    here = lax.axis_index("section") == active
    side = lax.rem(lax.axis_index("seq"), 2)
    pl.when(here & (side == 0))(lambda: body(own_ref, got_ref))
    pl.when(here & (side == 1))(lambda: body(got_ref, own_ref))


def pair_state(init_ref, pair):
    return jnp.concatenate([init_ref[0, 2 * pair], init_ref[0, 2 * pair + 1]], axis=1)


def apply_map(state, ref, start, width):
    step = mm(ref[:, start : start + PAIR], spread(state.astype(BF16)))
    return state - step + ref[:, width + start : width + start + PAIR].astype(F32)


def advance(active, place, own_ref, got_ref, state_ref, after_ref, out_ref):
    width = out_ref.shape[1]

    def body(refs):
        for start in range(0, width, PAIR):
            lanes = slice(start, start + PAIR)
            state = state_ref[:, lanes].astype(F32) if place else pair_state(state_ref, start // PAIR)
            for ref in refs:
                state = apply_map(state, ref, start, width)
            out_ref[:, lanes] = state.astype(BF16)

    index = lax.axis_index("seq")
    here = (lax.axis_index("section") == active) & (index // 2 == place)
    if got_ref is None:
        pl.when(here)(lambda: body((own_ref,)))
    else:
        side = lax.rem(index, 2)
        pl.when(here & (side == 0))(lambda: body((own_ref, got_ref)))
        pl.when(here & (side == 1))(lambda: body((got_ref, own_ref)))


def finish(here, begins, state_refs, got_refs, init_ref, reads_ref, w_out_ref, h_ref, store):
    width = w_out_ref.shape[0]
    model = h_ref.shape[1]
    chunk = model // 4

    def total(refs, lanes):
        value = refs[0][:, lanes].astype(F32)
        for ref in refs[1:]:
            value = value + ref[:, lanes].astype(F32)
        return value

    def body():
        follows = lax.rem(lax.axis_index("seq"), 2) == 1
        parts = []
        for start in range(0, width, QUAD):
            pieces = []
            for lane in range(start, start + QUAD, PAIR):
                lanes = slice(lane, lane + PAIR)
                if begins is True:
                    state = pair_state(init_ref, lane // PAIR)
                else:
                    state = total(state_refs, lanes)
                    if begins is not False:
                        state = jnp.where(begins, pair_state(init_ref, lane // PAIR), state)
                step = mm(total(got_refs, lanes).astype(BF16), spread(state.astype(BF16)))
                moved = state - step + total(got_refs, slice(width + lane, width + lane + PAIR))
                pieces.append(jnp.where(follows, moved, state).astype(BF16))
            offset = reads_ref[:, width + start : width + start + QUAD]
            read = mm(reads_ref[:, start : start + QUAD], spread(jnp.concatenate(pieces, axis=1)))
            parts.append((read + offset.astype(F32)).astype(BF16))
        inner_bf = jnp.concatenate(parts, axis=1)
        for start in range(0, model, chunk):
            lanes = slice(start, start + chunk)
            store(start, (h_ref[:, lanes].astype(F32) + mm(inner_bf, w_out_ref[:, lanes])).astype(BF16))

    pl.when(here)(body)


def first_finish(place, state_ref, got_ref, reads_ref, w_out_ref, h_ref, after_ref, out_ref):
    def store(start, value):
        out_ref[:, start : start + value.shape[1]] = value

    finish(at_pair([place], 0), place == 0, [state_ref], [got_ref], state_ref, reads_ref, w_out_ref, h_ref, store)


def last_finish(count, *refs):
    states, gots, refs = refs[: count - 1], refs[count - 1 : 2 * count - 1], refs[2 * count - 1 :]
    init_ref, reads_ref, w_out_ref, h_ref, *first_refs, out_hbm, near, sems = refs
    chunk = near.shape[1] // 4

    def write(start):
        lanes = pl.ds(start, chunk)
        return pltpu.make_async_copy(near.at[:, lanes], out_hbm.at[0, :, lanes], sems.at[start // chunk])

    def store(start, value):
        near[:, start : start + chunk] = value
        write(start).start()

    begins = lax.axis_index("seq") // 2 == 0
    finish(lax.axis_index("section") == 1, begins, states, gots, init_ref, reads_ref, w_out_ref, h_ref, store)

    for place, first_ref in enumerate(first_refs):

        @pl.when(at_pair([place], 0))
        def _():
            for start in range(0, near.shape[1], chunk):
                store(start, first_ref[:, start : start + chunk])

    for start in range(0, near.shape[1], chunk):
        write(start).wait()


def call(body, outs, scratch, args, kinds=None, name=None, out_kind=pltpu.VMEM):
    specs = [pl.BlockSpec(memory_space=kind) for kind in (kinds or [pltpu.VMEM] * len(args))]
    return pl.pallas_call(
        body,
        out_shape=outs,
        in_specs=specs,
        out_specs=[pl.BlockSpec(memory_space=out_kind)] * len(outs),
        scratch_shapes=scratch,
        compiler_params=pltpu.CompilerParams(vmem_limit_bytes=VMEM_LIMIT),
        name=name,
    )(*args)


def shards(tokens, norm_gain, w_qkv, w_rate, rate_base, init_state, w_out):
    count = lax.axis_size("seq")
    heads = rate_base.shape[1]
    rows, model = tokens.shape
    width = heads * HD
    depth = w_qkv.shape[1]
    quads = width // QUAD
    shape = jax.ShapeDtypeStruct
    in_vmem = functools.partial(pltpu.with_memory_space_constraint, memory_space=pltpu.VMEM)
    in_hbm = functools.partial(pltpu.with_memory_space_constraint, memory_space=pltpu.HBM)
    maps = shape((HD, 2 * width), BF16)
    rows_out = [shape((rows, model), BF16)] + [shape((rows, width), BF16)] * 3
    w_rate = jnp.swapaxes(w_rate, 1, 2)
    norm_gain, w_qkv, w_rate, rate_base, w_out = [in_hbm(value) for value in (norm_gain, w_qkv, w_rate, rate_base, w_out)]

    def permute(value, active, pairs):
        base = active * count
        return lax.ppermute(value, ("section", "seq"), [(base + source, base + target) for source, target in pairs])

    def swap(own, active, groups):
        return permute(own, active, [(2 * group + side, 2 * group + 1 - side) for group in groups for side in range(2)])

    def layer_reads(active, places, rows_of, weights, after):
        near = [pltpu.VMEM((depth, width), BF16), pltpu.SemaphoreType.DMA((quads,))]
        reads, w_out_near = call(
            functools.partial(read_out, active, places),
            [shape((rows, 2 * width), BF16), pltpu.VMEM(w_out.shape[1:], BF16)],
            [pltpu.SemaphoreType.DMA] + (near if active == 0 else []),
            [*rows_of, weights, w_out, after],
            [pltpu.VMEM] * 4 + [pltpu.VMEM if active else pltpu.HBM, pltpu.HBM, pl.ANY],
            name=f"reads{active}_{places[0]}",
        )
        return reads, in_vmem(w_out_near)

    def hop(active, place, maps_here, state, after):
        def body(*refs):
            advance(active, place, refs[0], None if len(maps_here) == 1 else refs[1], *refs[len(maps_here) :])

        kinds = [pltpu.VMEM] * (len(maps_here) + 1) + [pl.ANY]
        (ahead,) = call(body, [shape((HD, width), BF16)], [], maps_here + [state, after], kinds, name=f"advance{active}_{place}")
        return ahead, permute(ahead, active, [(2 * place + side, 2 * place + 2 + side) for side in range(2)])

    groups = count // 2

    own, *rows_of = call(
        first_front,
        [maps] + rows_out,
        [pltpu.VMEM(value.shape, value.dtype) for value in (tokens, norm_gain, w_rate, rate_base)]
        + [pltpu.VMEM((depth, 2 * width), BF16), pltpu.SemaphoreType.DMA((4,)), pltpu.SemaphoreType.DMA((quads, 2))],
        [in_hbm(tokens), norm_gain, w_qkv, w_rate, rate_base],
        [pltpu.HBM] * 5,
        name="first_front",
    )
    got_first = swap(own, 0, [0])
    got_rest = swap(own, 0, range(1, groups))
    read_first = layer_reads(0, [0], rows_of, w_qkv, init_state)
    ahead, state = hop(0, 0, [own, got_first], init_state, read_first[0])
    read_rest = layer_reads(0, range(1, groups), rows_of, w_qkv, ahead)
    (both,) = call(
        functools.partial(compose, 0), [maps], [], [own, got_rest, read_rest[0]], [pltpu.VMEM] * 2 + [pl.ANY], name="compose"
    )
    firsts, hiddens, here = [], [], init_state
    for place in range(groups):
        got, (reads, w_out_near) = (got_rest, read_rest) if place else (got_first, read_first)
        if 0 < place < groups - 1:
            ahead, state = hop(0, place, [both], here, firsts[-1])
        (first,) = call(
            functools.partial(first_finish, place),
            [shape((rows, model), BF16)],
            [],
            [here, got, reads, w_out_near, tokens, ahead],
            [pltpu.VMEM] * 5 + [pl.ANY],
            name=f"first_finish_{place}",
        )
        firsts.append(first)
        hiddens.append(lax.ppermute(first, ("section", "seq"), [(2 * place + side, count + 2 * place + side) for side in range(2)]))
        here = state

    params = [norm_gain, w_qkv, w_rate, rate_base]
    gain_near, w_near, rate_near, base_near = call(
        load,
        [pltpu.VMEM(value.shape, value.dtype) for value in params],
        [pltpu.SemaphoreType.DMA((4,))],
        params + [both],
        [pltpu.HBM] * 4 + [pl.ANY],
        name="load",
    )
    params = [in_vmem(value) for value in (gain_near, w_near.reshape(w_qkv.shape[1:]), rate_near, base_near)]
    own, *rows_of, hidden = call(
        later_front, [maps] + rows_out + [shape((rows, model), BF16)], [], [*hiddens, *params], name="later_front"
    )
    gots = [swap(own, 1, [group]) for group in range(groups)]
    states, state, ahead = [], init_state, own
    for place in range(groups - 1):
        ahead, state = hop(1, place, [own, gots[place]], state, ahead)
        states.append(state)
    reads, w_out_near = layer_reads(1, range(groups), rows_of, params[1], ahead)
    (result,) = call(
        functools.partial(last_finish, groups),
        [shape((1, rows, model), BF16)],
        [pltpu.VMEM((rows, model), BF16), pltpu.SemaphoreType.DMA((4,))],
        [*states, *gots, init_state, reads, w_out_near, hidden, *firsts],
        name="last_finish",
        out_kind=pltpu.HBM,
    )
    return result


def solution(mesh):
    return jax.shard_map(
        shards,
        mesh=mesh,
        in_specs=(
            P(("traj", "seq"), None),
            P("section", None),
            P("section", None, None),
            P("section", None, None),
            P("section", None),
            P("section", None, None, None),
            P("section", None, None),
        ),
        out_specs=P("section", ("traj", "seq"), None),
        check_vma=False,
    )
```

```python
import functools

import jax
import jax.numpy as jnp
from jax import lax
from jax.experimental import pallas as pl
from jax.experimental.pallas import tpu as pltpu
from jax.sharding import PartitionSpec as P

HD = 64
PAIR = 2 * HD
QUAD = 4 * HD
F32 = jnp.float32
BF16 = jnp.bfloat16
EPS = 1e-6
VMEM_LIMIT = 16 * 1024 * 1024


def mm(a, b):
    return jnp.dot(a, b, preferred_element_type=F32)


def mm_nt(a, b):
    return lax.dot_general(a, b, (((1,), (1,)), ((), ())), preferred_element_type=F32)


def mm_tn(a, b):
    return lax.dot_general(a, b, (((0,), (0,)), ((), ())), preferred_element_type=F32)


def head_masks(rows, lanes):
    lane = lax.broadcasted_iota(jnp.int32, (rows, lanes), 1)
    return [lane // HD == index for index in range(lanes // HD)]


def spread(value):
    zero = jnp.zeros_like(value)
    masks = head_masks(*value.shape)
    return jnp.concatenate([jnp.where(mask, value, zero) for mask in masks], axis=0)


def spread_two(left, right):
    return jnp.concatenate([spread(left), spread(right)], axis=1)


def diagonal(product):
    first = lax.broadcasted_iota(jnp.int32, (HD, PAIR), 1) < HD
    return jnp.where(first, product[:HD], product[HD:])


def head_ones():
    row = lax.broadcasted_iota(jnp.int32, (QUAD, QUAD), 0) // HD
    lane = lax.broadcasted_iota(jnp.int32, (QUAD, QUAD), 1) // HD
    return jnp.where(row == lane, 1.0, 0.0).astype(BF16)


def unit_heads(value, ones):
    squares = mm((value * value).astype(BF16), ones)
    return value * lax.rsqrt(squares + EPS)


def norm_rows(hidden, gain):
    wide = hidden.astype(F32)
    mean_sq = jnp.mean(wide * wide, axis=-1, keepdims=True)
    return (wide * lax.rsqrt(mean_sq + EPS) * gain).astype(BF16)


def spread_rates(normed, w_rate, rate_base):
    rates = rate_base * jax.nn.sigmoid(mm_nt(normed, w_rate))
    high = rates.astype(BF16)
    low = (rates - high.astype(F32)).astype(BF16)
    heads = rates.shape[1]
    row = lax.broadcasted_iota(jnp.int32, (heads, heads * HD), 0)
    lane = lax.broadcasted_iota(jnp.int32, (heads, heads * HD), 1) // HD
    pick = jnp.where(row == lane, 1.0, 0.0).astype(BF16)
    return mm(high, pick) + mm(low, pick)


def start_all(copies):
    for copy in copies:
        copy.start()


def wait_all(copies):
    for copy in copies:
        copy.wait()


def on_section(active, body):
    pl.when(lax.axis_index("section") == active)(body)


def at_pair(places, active):
    pair = lax.axis_index("seq") // 2
    first, last = places[0], places[-1]
    return (lax.axis_index("section") == active) & (pair >= first) & (pair <= last)


def front(here, h_refs, gain_ref, w_ref, w_rate_ref, base_ref, maps, normed_out, keys_out, x_out, y_out, h_in, near=None):
    width = keys_out.shape[1]
    quads = width // QUAD

    def body():
        if near is None:
            groups = []
            gain, w_rate, base, weights, base_lane = gain_ref, w_rate_ref, base_ref, w_ref, width
            last = lax.axis_index("seq") // 2 == lax.axis_size("seq") // 2 - 1
            for picked, ref in zip((jnp.logical_not(last), last), h_refs):

                @pl.when(picked)
                def _():
                    h_in[...] = ref[...]
        else:
            gain, w_rate, base, weights, small_sems, sems = near
            base_lane = 0
            pairs = [(gain_ref, gain), (w_rate_ref, w_rate), (base_ref, base), (h_refs[0], h_in)]
            small = [pltpu.make_async_copy(source, target, small_sems.at[index]) for index, (source, target) in enumerate(pairs)]
            groups = [
                [
                    pltpu.make_async_copy(
                        w_ref.at[0, :, pl.ds((side + 1) * width + quad * QUAD, QUAD)],
                        weights.at[:, pl.ds(side * width + quad * QUAD, QUAD)],
                        sems.at[quad, side],
                    )
                    for side in range(2)
                ]
                for quad in range(quads)
            ]
            start_all(small)
            start_all(groups[0])
            wait_all(small)
            start_all(groups[1])
        normed = norm_rows(h_in[...], gain[...])
        normed_out[...] = normed
        if groups:
            start_all(groups[2])
        rates = spread_rates(normed, w_rate[0], base[...])
        ones = head_ones()

        def project(quad):
            if groups:
                wait_all(groups[quad])
                if quad + 3 < quads:
                    start_all(groups[quad + 3])
            key_lane = base_lane + quad * QUAD
            return [mm(normed, weights[:, lane : lane + QUAD]) for lane in (key_lane, key_lane + width)]

        def chain(quad, keys, values):
            lanes = slice(quad * QUAD, (quad + 1) * QUAD)
            keys = unit_heads(keys, ones)
            keys_bf = keys.astype(BF16)
            keys_out[:, lanes] = keys_bf
            rate = rates[:, lanes]
            x_all = rate * keys
            y_all = rate * values
            x_first, y_first = x_all[:HD].astype(BF16), y_all[:HD].astype(BF16)
            cross = mm_nt(keys_bf[HD:], spread(keys_bf[:HD])).astype(BF16)
            fix = mm(cross, spread_two(x_first, y_first))
            x_second = (x_all[HD:] - rate[HD:] * fix[:, :QUAD]).astype(BF16)
            y_second = (y_all[HD:] - rate[HD:] * fix[:, QUAD:]).astype(BF16)
            x_bf = jnp.concatenate([x_first, x_second], axis=0)
            y_bf = jnp.concatenate([y_first, y_second], axis=0)
            x_out[:, lanes] = x_bf
            y_out[:, lanes] = y_bf
            for half in range(2):
                own = slice(half * PAIR, (half + 1) * PAIR)
                start = quad * QUAD + half * PAIR
                both = mm_tn(keys_bf[:, own], jnp.concatenate([x_bf[:, own], y_bf[:, own]], axis=1))
                maps[:, start : start + PAIR] = diagonal(both[:, :PAIR]).astype(BF16)
                maps[:, width + start : width + start + PAIR] = diagonal(both[:, PAIR:]).astype(BF16)

        before = project(0)
        for quad in range(1, quads):
            after = project(quad)
            chain(quad - 1, *before)
            before = after
        chain(quads - 1, *before)

    pl.when(here)(body)


def first_front(h_hbm, gain, weights, w_rate, base, maps, normed_out, keys_out, x_out, y_out, h_in, *near):
    here = lax.axis_index("section") == 0
    front(here, [h_hbm], gain, weights, w_rate, base, maps, normed_out, keys_out, x_out, y_out, h_in, near)


def later_front(*refs):
    refs, rest = refs[:-10], refs[-10:]
    front(lax.axis_index("section") == 1, refs, *rest)


def load(*refs):
    count = (len(refs) - 2) // 2
    sources, targets, sems = refs[:count], refs[count + 1 : -1], refs[-1]

    def body():
        copies = [pltpu.make_async_copy(source, target, sems.at[index]) for index, (source, target) in enumerate(zip(sources, targets))]
        start_all(copies)
        wait_all(copies)

    on_section(1, body)


def read_out(active, places, fetches, normed_ref, keys_ref, x_ref, y_ref, w_ref, w_out_hbm, after_ref, reads_out, *rest):
    rows, width = keys_ref.shape
    quads = width // QUAD
    w_out, rest = rest[:fetches], rest[fetches:]
    load_sem, *near = rest

    def body():
        fetch = [pltpu.make_async_copy(w_out_hbm.at[0], target, load_sem) for target in w_out]
        if active:
            weights, groups = w_ref, []
            start_all(fetch)
        else:
            weights, sems = near
            groups = [
                [pltpu.make_async_copy(w_ref.at[0, :, pl.ds(quad * QUAD, QUAD)], weights.at[:, pl.ds(quad * QUAD, QUAD)], sems.at[quad])]
                for quad in range(quads)
            ]
            start_all(groups[0])
            start_all(groups[1])
        normed = normed_ref[...]
        ones = head_ones()
        row = lax.broadcasted_iota(jnp.int32, (rows, 2 * rows), 0)
        lane = lax.rem(lax.broadcasted_iota(jnp.int32, (rows, 2 * rows), 1), rows)
        causal = row >= lane
        for quad in range(quads):
            if groups:
                wait_all(groups[quad])
                if quad + 2 < quads:
                    start_all(groups[quad + 2])
                if quad + 3 == quads:
                    start_all(fetch)
            queries = unit_heads(mm(normed, weights[:, quad * QUAD : (quad + 1) * QUAD]), ones)
            queries_bf = queries.astype(BF16)
            for half in range(2):
                own = slice(half * PAIR, (half + 1) * PAIR)
                start = quad * QUAD + half * PAIR
                place = slice(start, start + PAIR)
                scores = mm_nt(queries_bf[:, own], spread(keys_ref[:, place]))
                scores = jnp.where(causal, scores, 0.0).astype(BF16)
                both = mm(scores, spread_two(x_ref[:, place], y_ref[:, place]))
                reads_out[:, place] = (queries[:, own] - both[:, :PAIR]).astype(BF16)
                reads_out[:, width + start : width + start + PAIR] = both[:, PAIR:].astype(BF16)
        wait_all(fetch)

    pl.when(at_pair(places, active))(body)


def compose(active, own_ref, got_ref, after_ref, out_ref):
    width = own_ref.shape[1] // 2

    def body(first_ref, second_ref):
        for start in range(0, width, PAIR):
            s_lanes, b_lanes = slice(start, start + PAIR), slice(width + start, width + start + PAIR)
            s_second, s_first, b_first = second_ref[:, s_lanes], first_ref[:, s_lanes], first_ref[:, b_lanes]
            step = mm(s_second, spread_two(s_first, b_first))
            out_ref[:, s_lanes] = (s_second.astype(F32) + s_first.astype(F32) - step[:, :PAIR]).astype(BF16)
            out_ref[:, b_lanes] = (second_ref[:, b_lanes].astype(F32) + b_first.astype(F32) - step[:, PAIR:]).astype(BF16)

    here = lax.axis_index("section") == active
    side = lax.rem(lax.axis_index("seq"), 2)
    pl.when(here & (side == 0))(lambda: body(own_ref, got_ref))
    pl.when(here & (side == 1))(lambda: body(got_ref, own_ref))


def pair_state(init_ref, pair):
    return jnp.concatenate([init_ref[0, 2 * pair], init_ref[0, 2 * pair + 1]], axis=1)


def apply_map(state, ref, start, width):
    step = mm(ref[:, start : start + PAIR], spread(state.astype(BF16)))
    return state - step + ref[:, width + start : width + start + PAIR].astype(F32)


def advance(active, place, own_ref, got_ref, state_ref, after_ref, out_ref):
    width = out_ref.shape[1]

    def body(refs):
        for start in range(0, width, PAIR):
            lanes = slice(start, start + PAIR)
            state = state_ref[:, lanes].astype(F32) if place else pair_state(state_ref, start // PAIR)
            for ref in refs:
                state = apply_map(state, ref, start, width)
            out_ref[:, lanes] = state.astype(BF16)

    index = lax.axis_index("seq")
    here = (lax.axis_index("section") == active) & (index // 2 == place)
    if got_ref is None:
        pl.when(here)(lambda: body((own_ref,)))
    else:
        side = lax.rem(index, 2)
        pl.when(here & (side == 0))(lambda: body((own_ref, got_ref)))
        pl.when(here & (side == 1))(lambda: body((got_ref, own_ref)))


def finish(here, begins, state_ref, got_ref, reads_ref, w_out_ref, h_ref, store, fetch=()):
    width = w_out_ref.shape[0]
    model = h_ref.shape[1]
    chunk = model // 4

    def body():
        start_all(fetch)
        follows = lax.rem(lax.axis_index("seq"), 2) == 1
        parts = []
        for start in range(0, width, QUAD):
            pieces = []
            for lane in range(start, start + QUAD, PAIR):
                lanes = slice(lane, lane + PAIR)
                state = pair_state(state_ref, lane // PAIR) if begins else state_ref[:, lanes].astype(F32)
                moved = apply_map(state, got_ref, lane, width)
                pieces.append(jnp.where(follows, moved, state).astype(BF16))
            offset = reads_ref[:, width + start : width + start + QUAD]
            read = mm(reads_ref[:, start : start + QUAD], spread(jnp.concatenate(pieces, axis=1)))
            parts.append((read + offset.astype(F32)).astype(BF16))
        inner_bf = jnp.concatenate(parts, axis=1)
        wait_all(fetch)
        for start in range(0, model, chunk):
            lanes = slice(start, start + chunk)
            store(start, (h_ref[:, lanes].astype(F32) + mm(inner_bf, w_out_ref[:, lanes])).astype(BF16))

    pl.when(here)(body)


def first_finish(place, passed, state_ref, got_ref, reads_ref, w_out_ref, h_ref, after_ref, *rest):
    out_ref, *near = rest[passed:]

    def store(start, value):
        out_ref[:, start : start + value.shape[1]] = value

    fetch = []
    if near:
        fetch = [pltpu.make_async_copy(w_out_ref.at[0], *near)]
        w_out_ref = near[0]
    finish(at_pair([place], 0), place == 0, state_ref, got_ref, reads_ref, w_out_ref, h_ref, store, fetch)


def last_finish(count, *refs):
    states, gots, refs = refs[:count], refs[count : 2 * count], refs[2 * count :]
    reads_early, reads_late, w_out_early, w_out_late, h_ref, first_early, first_late, out_hbm, near, sems = refs
    chunk = near.shape[1] // 4

    def write(start):
        lanes = pl.ds(start, chunk)
        return pltpu.make_async_copy(near.at[:, lanes], out_hbm.at[0, :, lanes], sems.at[start // chunk])

    def store(start, value):
        near[:, start : start + chunk] = value
        write(start).start()

    for place in range(count):
        reads_ref, w_out_ref = (reads_early, w_out_early) if place + 1 < count else (reads_late, w_out_late)
        finish(at_pair([place], 1), place == 0, states[place], gots[place], reads_ref, w_out_ref, h_ref, store)

    for places, first_ref in ((range(count - 1), first_early), ([count - 1], first_late)):

        @pl.when(at_pair(places, 0))
        def _():
            for start in range(0, near.shape[1], chunk):
                store(start, first_ref[:, start : start + chunk])

    for start in range(0, near.shape[1], chunk):
        write(start).wait()


def call(body, outs, scratch, args, kinds=None, name=None, out_kind=pltpu.VMEM, aliases=None):
    specs = [pl.BlockSpec(memory_space=kind) for kind in (kinds or [pltpu.VMEM] * len(args))]
    return pl.pallas_call(
        body,
        out_shape=outs,
        in_specs=specs,
        out_specs=[pl.BlockSpec(memory_space=out_kind)] * len(outs),
        scratch_shapes=scratch,
        input_output_aliases=aliases or {},
        compiler_params=pltpu.CompilerParams(vmem_limit_bytes=VMEM_LIMIT),
        name=name,
    )(*args)


def shards(tokens, norm_gain, w_qkv, w_rate, rate_base, init_state, w_out):
    count = lax.axis_size("seq")
    heads = rate_base.shape[1]
    rows, model = tokens.shape
    width = heads * HD
    depth = w_qkv.shape[1]
    quads = width // QUAD
    shape = jax.ShapeDtypeStruct
    in_vmem = functools.partial(pltpu.with_memory_space_constraint, memory_space=pltpu.VMEM)
    in_hbm = functools.partial(pltpu.with_memory_space_constraint, memory_space=pltpu.HBM)
    maps = shape((HD, 2 * width), BF16)
    rows_out = [shape((rows, model), BF16)] + [shape((rows, width), BF16)] * 3
    w_rate = jnp.swapaxes(w_rate, 1, 2)
    norm_gain, w_qkv, w_rate, rate_base, w_out = [in_hbm(value) for value in (norm_gain, w_qkv, w_rate, rate_base, w_out)]

    def permute(value, active, pairs):
        base = active * count
        return lax.ppermute(value, ("section", "seq"), [(base + source, base + target) for source, target in pairs])

    def swap(own, active, groups):
        return permute(own, active, [(2 * group + side, 2 * group + 1 - side) for group in groups for side in range(2)])

    def layer_reads(active, places, fetches, rows_of, weights, after):
        near = [pltpu.VMEM((depth, width), BF16), pltpu.SemaphoreType.DMA((quads,))]
        reads, *w_out_near = call(
            functools.partial(read_out, active, places, fetches),
            [shape((rows, 2 * width), BF16)] + [pltpu.VMEM(w_out.shape[1:], BF16)] * fetches,
            [pltpu.SemaphoreType.DMA] + (near if active == 0 else []),
            [*rows_of, weights, w_out, after],
            [pltpu.VMEM] * 4 + [pltpu.VMEM if active else pltpu.HBM, pltpu.HBM, pl.ANY],
            name=f"reads{active}_{places[0]}",
        )
        return [reads] + [in_vmem(value) for value in w_out_near]

    def hop(active, place, maps_here, state, after):
        def body(*refs):
            advance(active, place, refs[0], None if len(maps_here) == 1 else refs[1], *refs[len(maps_here) :])

        kinds = [pltpu.VMEM] * (len(maps_here) + 1) + [pl.ANY]
        (ahead,) = call(body, [shape((HD, width), BF16)], [], maps_here + [state, after], kinds, name=f"advance{active}_{place}")
        return ahead, permute(ahead, active, [(2 * place + side, 2 * place + 2 + side) for side in range(2)])

    groups = count // 2

    own, *rows_of = call(
        first_front,
        [maps] + rows_out,
        [pltpu.VMEM(value.shape, value.dtype) for value in (tokens, norm_gain, w_rate, rate_base)]
        + [pltpu.VMEM((depth, 2 * width), BF16), pltpu.SemaphoreType.DMA((4,)), pltpu.SemaphoreType.DMA((quads, 2))],
        [in_hbm(tokens), norm_gain, w_qkv, w_rate, rate_base],
        [pltpu.HBM] * 5,
        name="first_front",
    )
    got_first = swap(own, 0, [0])
    got_rest = swap(own, 0, range(1, groups))
    read_first = layer_reads(0, [0], 0, rows_of, w_qkv, init_state)
    ahead, state = hop(0, 0, [own, got_first], init_state, read_first[0])
    read_rest = layer_reads(0, range(1, groups), 1, rows_of, w_qkv, ahead)
    (both,) = call(
        functools.partial(compose, 0), [maps], [], [own, got_rest, read_rest[0]], [pltpu.VMEM] * 2 + [pl.ANY], name="compose"
    )
    early, here = [], init_state
    for place in range(groups):
        got, (reads, w_out_near) = (got_rest, read_rest) if place else (got_first, read_first + [w_out])
        if 0 < place < groups - 1:
            ahead, state = hop(0, place, [both], here, early[0])
        passed = early if place + 1 < groups else []
        (first,) = call(
            functools.partial(first_finish, place, len(passed)),
            [shape((rows, model), BF16)],
            [] if place else [pltpu.VMEM(w_out.shape[1:], BF16), pltpu.SemaphoreType.DMA],
            [here, got, reads, w_out_near, tokens, ahead, *passed],
            [pltpu.VMEM] * 3 + [pltpu.VMEM if place else pltpu.HBM, pltpu.VMEM, pl.ANY] + [pltpu.VMEM] * len(passed),
            name=f"first_finish_{place}",
            aliases={6: 0} if passed else None,
        )
        if place + 1 < groups:
            early = [first]
        here = state
    firsts = [early[0], first]
    spans = [range(2 * (groups - 1)), range(2 * (groups - 1), count)]
    hiddens = [
        lax.ppermute(value, ("section", "seq"), [(place, count + place) for place in span]) for value, span in zip(firsts, spans)
    ]

    params = [norm_gain, w_qkv, w_rate, rate_base]
    gain_near, w_near, rate_near, base_near = call(
        load,
        [pltpu.VMEM(value.shape, value.dtype) for value in params],
        [pltpu.SemaphoreType.DMA((4,))],
        params + [both],
        [pltpu.HBM] * 4 + [pl.ANY],
        name="load",
    )
    params = [in_vmem(value) for value in (gain_near, w_near.reshape(w_qkv.shape[1:]), rate_near, base_near)]
    own, *rows_of, hidden = call(
        later_front, [maps] + rows_out + [shape((rows, model), BF16)], [], [*hiddens, *params], name="later_front"
    )
    gots = [swap(own, 1, [group]) for group in range(groups)]
    states, after = [init_state], own
    for place in range(groups - 1):
        if place + 2 == groups:
            reads_early = layer_reads(1, range(groups - 1), 1, rows_of, params[1], after)
            after = reads_early[0]
        after, state = hop(1, place, [own, gots[place]], states[-1], after)
        states.append(state)
    reads_late = layer_reads(1, [groups - 1], 1, rows_of, params[1], after)
    (result,) = call(
        functools.partial(last_finish, groups),
        [shape((1, rows, model), BF16)],
        [pltpu.VMEM((rows, model), BF16), pltpu.SemaphoreType.DMA((4,))],
        [*states, *gots, reads_early[0], reads_late[0], reads_early[1], reads_late[1], hidden, *firsts],
        name="last_finish",
        out_kind=pltpu.HBM,
    )
    return result


def solution(mesh):
    return jax.shard_map(
        shards,
        mesh=mesh,
        in_specs=(
            P(("traj", "seq"), None),
            P("section", None),
            P("section", None, None),
            P("section", None, None),
            P("section", None),
            P("section", None, None, None),
            P("section", None, None),
        ),
        out_specs=P("section", ("traj", "seq"), None),
        check_vma=False,
    )
```

```python
import functools

import jax
import jax.numpy as jnp
from jax import lax
from jax.experimental import pallas as pl
from jax.experimental.pallas import tpu as pltpu
from jax.sharding import PartitionSpec as P

HD = 64
PAIR = 2 * HD
QUAD = 4 * HD
F32 = jnp.float32
BF16 = jnp.bfloat16
EPS = 1e-6
VMEM_LIMIT = 16 * 1024 * 1024


def mm(a, b):
    return jnp.dot(a, b, preferred_element_type=F32)


def mm_nt(a, b):
    return lax.dot_general(a, b, (((1,), (1,)), ((), ())), preferred_element_type=F32)


def mm_tn(a, b):
    return lax.dot_general(a, b, (((0,), (0,)), ((), ())), preferred_element_type=F32)


def head_masks(rows, lanes):
    lane = lax.broadcasted_iota(jnp.int32, (rows, lanes), 1)
    return [lane // HD == index for index in range(lanes // HD)]


def spread(value):
    zero = jnp.zeros_like(value)
    masks = head_masks(*value.shape)
    return jnp.concatenate([jnp.where(mask, value, zero) for mask in masks], axis=0)


def spread_two(left, right):
    return jnp.concatenate([spread(left), spread(right)], axis=1)


def diagonal(product):
    first = lax.broadcasted_iota(jnp.int32, (HD, PAIR), 1) < HD
    return jnp.where(first, product[:HD], product[HD:])


def head_ones():
    row = lax.broadcasted_iota(jnp.int32, (QUAD, QUAD), 0) // HD
    lane = lax.broadcasted_iota(jnp.int32, (QUAD, QUAD), 1) // HD
    return jnp.where(row == lane, 1.0, 0.0).astype(BF16)


def unit_heads(value, ones):
    squares = mm((value * value).astype(BF16), ones)
    return value * lax.rsqrt(squares + EPS)


def norm_rows(hidden, gain):
    wide = hidden.astype(F32)
    mean_sq = jnp.mean(wide * wide, axis=-1, keepdims=True)
    return (wide * lax.rsqrt(mean_sq + EPS) * gain).astype(BF16)


def spread_rates(normed, w_rate, rate_base):
    rates = rate_base * jax.nn.sigmoid(mm_nt(normed, w_rate))
    high = rates.astype(BF16)
    low = (rates - high.astype(F32)).astype(BF16)
    heads = rates.shape[1]
    row = lax.broadcasted_iota(jnp.int32, (heads, heads * HD), 0)
    lane = lax.broadcasted_iota(jnp.int32, (heads, heads * HD), 1) // HD
    pick = jnp.where(row == lane, 1.0, 0.0).astype(BF16)
    return mm(high, pick) + mm(low, pick)


def start_all(copies):
    for copy in copies:
        copy.start()


def wait_all(copies):
    for copy in copies:
        copy.wait()


def on_section(active, body):
    pl.when(lax.axis_index("section") == active)(body)


def at_pair(places, active):
    pair = lax.axis_index("seq") // 2
    first, last = places[0], places[-1]
    return (lax.axis_index("section") == active) & (pair >= first) & (pair <= last)


def front(here, h_ref, gain_ref, w_ref, w_rate_ref, base_ref, maps, normed_out, keys_out, x_out, y_out, near=None):
    width = keys_out.shape[1]
    quads = width // QUAD

    def body():
        if near is None:
            groups, last = [], []
            h_in, gain, w_rate, base, weights, base_lane = h_ref, gain_ref, w_rate_ref, base_ref, w_ref, width
        else:
            wq, h_in, gain, w_rate, base, weights, small_sems, sems = near
            base_lane = 0
            pairs = [(gain_ref, gain), (w_rate_ref, w_rate), (base_ref, base), (h_ref, h_in)]
            small = [pltpu.make_async_copy(source, target, small_sems.at[index]) for index, (source, target) in enumerate(pairs)]
            last = [pltpu.make_async_copy(w_ref.at[0, :, pl.ds(0, width)], wq, small_sems.at[len(pairs)])]
            groups = [
                [
                    pltpu.make_async_copy(
                        w_ref.at[0, :, pl.ds((side + 1) * width + quad * QUAD, QUAD)],
                        weights.at[:, pl.ds(side * width + quad * QUAD, QUAD)],
                        sems.at[quad, side],
                    )
                    for side in range(2)
                ]
                for quad in range(quads)
            ]
            start_all(small)
            start_all(groups[0])
            wait_all(small)
            start_all(groups[1])
        normed = norm_rows(h_in[...], gain[...])
        normed_out[...] = normed
        if groups:
            start_all(groups[2])
        rates = spread_rates(normed, w_rate[0], base[...])
        ones = head_ones()

        def project(quad):
            if groups:
                wait_all(groups[quad])
                if quad + 3 < quads:
                    start_all(groups[quad + 3])
                if quad + 1 == quads:
                    start_all(last)
            key_lane = base_lane + quad * QUAD
            return [mm(normed, weights[:, lane : lane + QUAD]) for lane in (key_lane, key_lane + width)]

        def chain(quad, keys, values):
            lanes = slice(quad * QUAD, (quad + 1) * QUAD)
            keys = unit_heads(keys, ones)
            keys_bf = keys.astype(BF16)
            keys_out[:, lanes] = keys_bf
            rate = rates[:, lanes]
            x_all = rate * keys
            y_all = rate * values
            x_first, y_first = x_all[:HD].astype(BF16), y_all[:HD].astype(BF16)
            cross = mm_nt(keys_bf[HD:], spread(keys_bf[:HD])).astype(BF16)
            fix = mm(cross, spread_two(x_first, y_first))
            x_second = (x_all[HD:] - rate[HD:] * fix[:, :QUAD]).astype(BF16)
            y_second = (y_all[HD:] - rate[HD:] * fix[:, QUAD:]).astype(BF16)
            x_bf = jnp.concatenate([x_first, x_second], axis=0)
            y_bf = jnp.concatenate([y_first, y_second], axis=0)
            x_out[:, lanes] = x_bf
            y_out[:, lanes] = y_bf
            for half in range(2):
                own = slice(half * PAIR, (half + 1) * PAIR)
                start = quad * QUAD + half * PAIR
                both = mm_tn(keys_bf[:, own], jnp.concatenate([x_bf[:, own], y_bf[:, own]], axis=1))
                maps[:, start : start + PAIR] = diagonal(both[:, :PAIR]).astype(BF16)
                maps[:, width + start : width + start + PAIR] = diagonal(both[:, PAIR:]).astype(BF16)

        before = project(0)
        for quad in range(1, quads):
            after = project(quad)
            chain(quad - 1, *before)
            before = after
        chain(quads - 1, *before)

        wait_all(last)

    pl.when(here)(body)


def first_front(h_hbm, gain, weights, w_rate, base, maps, normed_out, keys_out, x_out, y_out, *near):
    here = lax.axis_index("section") == 0
    front(here, h_hbm, gain, weights, w_rate, base, maps, normed_out, keys_out, x_out, y_out, near)


def later_front(places, h_ref, gain, weights, w_rate, base, after_ref, *outs):
    front(at_pair(places, 1), h_ref, gain, weights, w_rate, base, *outs)


def load(*refs):
    count = (len(refs) - 2) // 2
    sources, targets, sems = refs[:count], refs[count + 1 : -1], refs[-1]

    def body():
        copies = [pltpu.make_async_copy(source, target, sems.at[index]) for index, (source, target) in enumerate(zip(sources, targets))]
        start_all(copies)
        wait_all(copies)

    on_section(1, body)


def read_out(active, places, fetches, normed_ref, keys_ref, x_ref, y_ref, weights, w_out_hbm, after_ref, reads_out, *rest):
    rows, width = keys_ref.shape
    *w_out, load_sem = rest

    def body():
        fetch = [pltpu.make_async_copy(w_out_hbm.at[0], target, load_sem) for target in w_out]
        start_all(fetch)
        normed = normed_ref[...]
        ones = head_ones()
        row = lax.broadcasted_iota(jnp.int32, (rows, 2 * rows), 0)
        lane = lax.rem(lax.broadcasted_iota(jnp.int32, (rows, 2 * rows), 1), rows)
        causal = row >= lane
        for quad in range(width // QUAD):
            queries = unit_heads(mm(normed, weights[:, quad * QUAD : (quad + 1) * QUAD]), ones)
            queries_bf = queries.astype(BF16)
            for half in range(2):
                own = slice(half * PAIR, (half + 1) * PAIR)
                start = quad * QUAD + half * PAIR
                place = slice(start, start + PAIR)
                scores = mm_nt(queries_bf[:, own], spread(keys_ref[:, place]))
                scores = jnp.where(causal, scores, 0.0).astype(BF16)
                both = mm(scores, spread_two(x_ref[:, place], y_ref[:, place]))
                reads_out[:, place] = (queries[:, own] - both[:, :PAIR]).astype(BF16)
                reads_out[:, width + start : width + start + PAIR] = both[:, PAIR:].astype(BF16)
        wait_all(fetch)

    pl.when(at_pair(places, active))(body)


def compose(active, own_ref, got_ref, after_ref, out_ref):
    width = own_ref.shape[1] // 2

    def body(first_ref, second_ref):
        for start in range(0, width, PAIR):
            s_lanes, b_lanes = slice(start, start + PAIR), slice(width + start, width + start + PAIR)
            s_second, s_first, b_first = second_ref[:, s_lanes], first_ref[:, s_lanes], first_ref[:, b_lanes]
            step = mm(s_second, spread_two(s_first, b_first))
            out_ref[:, s_lanes] = (s_second.astype(F32) + s_first.astype(F32) - step[:, :PAIR]).astype(BF16)
            out_ref[:, b_lanes] = (second_ref[:, b_lanes].astype(F32) + b_first.astype(F32) - step[:, PAIR:]).astype(BF16)

    here = lax.axis_index("section") == active
    side = lax.rem(lax.axis_index("seq"), 2)
    pl.when(here & (side == 0))(lambda: body(own_ref, got_ref))
    pl.when(here & (side == 1))(lambda: body(got_ref, own_ref))


def pair_state(init_ref, pair):
    return jnp.concatenate([init_ref[0, 2 * pair], init_ref[0, 2 * pair + 1]], axis=1)


def apply_map(state, ref, start, width):
    step = mm(ref[:, start : start + PAIR], spread(state.astype(BF16)))
    return state - step + ref[:, width + start : width + start + PAIR].astype(F32)


def advance(active, place, own_ref, got_ref, state_ref, after_ref, out_ref):
    width = out_ref.shape[1]

    def body(refs):
        for start in range(0, width, PAIR):
            lanes = slice(start, start + PAIR)
            state = state_ref[:, lanes].astype(F32) if place else pair_state(state_ref, start // PAIR)
            for ref in refs:
                state = apply_map(state, ref, start, width)
            out_ref[:, lanes] = state.astype(BF16)

    index = lax.axis_index("seq")
    here = (lax.axis_index("section") == active) & (index // 2 == place)
    if got_ref is None:
        pl.when(here)(lambda: body((own_ref,)))
    else:
        side = lax.rem(index, 2)
        pl.when(here & (side == 0))(lambda: body((own_ref, got_ref)))
        pl.when(here & (side == 1))(lambda: body((got_ref, own_ref)))


def finish(here, begins, state_ref, got_ref, reads_ref, w_out_ref, h_ref, store):
    width = w_out_ref.shape[0]
    model = h_ref.shape[1]
    chunk = model // 4

    def body():
        follows = lax.rem(lax.axis_index("seq"), 2) == 1
        parts = []
        for start in range(0, width, QUAD):
            pieces = []
            for lane in range(start, start + QUAD, PAIR):
                lanes = slice(lane, lane + PAIR)
                state = pair_state(state_ref, lane // PAIR) if begins else state_ref[:, lanes].astype(F32)
                moved = apply_map(state, got_ref, lane, width)
                pieces.append(jnp.where(follows, moved, state).astype(BF16))
            offset = reads_ref[:, width + start : width + start + QUAD]
            read = mm(reads_ref[:, start : start + QUAD], spread(jnp.concatenate(pieces, axis=1)))
            parts.append((read + offset.astype(F32)).astype(BF16))
        inner_bf = jnp.concatenate(parts, axis=1)
        for start in range(0, model, chunk):
            lanes = slice(start, start + chunk)
            store(start, (h_ref[:, lanes].astype(F32) + mm(inner_bf, w_out_ref[:, lanes])).astype(BF16))

    pl.when(here)(body)


def first_finish(place, state_ref, got_ref, reads_ref, w_out_ref, h_ref, after_ref, *rest):
    out_ref = rest[-1]

    def store(start, value):
        out_ref[:, start : start + value.shape[1]] = value

    finish(at_pair([place], 0), place == 0, state_ref, got_ref, reads_ref, w_out_ref, h_ref, store)


def last_finish(count, w_out_ref, *refs):
    states, gots, refs = refs[:count], refs[count : 2 * count], refs[2 * count :]
    reads, hiddens, firsts = [[refs[index]] * (count - 1) + [refs[index + 1]] for index in (0, 2, 4)]
    out_hbm, near, sems = refs[6:]
    chunk = near.shape[1] // 4

    def write(start):
        lanes = pl.ds(start, chunk)
        return pltpu.make_async_copy(near.at[:, lanes], out_hbm.at[0, :, lanes], sems.at[start // chunk])

    def store(start, value):
        near[:, start : start + chunk] = value
        write(start).start()

    for place in range(count):
        finish(at_pair([place], 1), place == 0, states[place], gots[place], reads[place], w_out_ref, hiddens[place], store)

        @pl.when(at_pair([place], 0))
        def _():
            for start in range(0, near.shape[1], chunk):
                store(start, firsts[place][:, start : start + chunk])

    for start in range(0, near.shape[1], chunk):
        write(start).wait()


def call(body, outs, scratch, args, kinds=None, name=None, out_kind=pltpu.VMEM, aliases=None):
    specs = [pl.BlockSpec(memory_space=kind) for kind in (kinds or [pltpu.VMEM] * len(args))]
    return pl.pallas_call(
        body,
        out_shape=outs,
        in_specs=specs,
        out_specs=[pl.BlockSpec(memory_space=out_kind)] * len(outs),
        scratch_shapes=scratch,
        input_output_aliases=aliases or {},
        compiler_params=pltpu.CompilerParams(vmem_limit_bytes=VMEM_LIMIT),
        name=name,
    )(*args)


def shards(tokens, norm_gain, w_qkv, w_rate, rate_base, init_state, w_out):
    count = lax.axis_size("seq")
    heads = rate_base.shape[1]
    rows, model = tokens.shape
    width = heads * HD
    depth = w_qkv.shape[1]
    quads = width // QUAD
    shape = jax.ShapeDtypeStruct
    in_vmem = functools.partial(pltpu.with_memory_space_constraint, memory_space=pltpu.VMEM)
    in_hbm = functools.partial(pltpu.with_memory_space_constraint, memory_space=pltpu.HBM)
    maps = shape((HD, 2 * width), BF16)
    rows_out = [shape((rows, model), BF16)] + [shape((rows, width), BF16)] * 3
    w_rate = jnp.swapaxes(w_rate, 1, 2)
    norm_gain, w_qkv, w_rate, rate_base, w_out = [in_hbm(value) for value in (norm_gain, w_qkv, w_rate, rate_base, w_out)]

    def permute(value, active, pairs):
        base = active * count
        return lax.ppermute(value, ("section", "seq"), [(base + source, base + target) for source, target in pairs])

    def swap(own, active, groups):
        return permute(own, active, [(2 * group + side, 2 * group + 1 - side) for group in groups for side in range(2)])

    def layer_reads(active, places, fetches, rows_of, weights, after):
        reads, *w_out_near = call(
            functools.partial(read_out, active, places, fetches),
            [shape((rows, 2 * width), BF16)] + [pltpu.VMEM(w_out.shape[1:], BF16)] * fetches,
            [pltpu.SemaphoreType.DMA],
            [*rows_of, weights, w_out, after],
            [pltpu.VMEM] * 5 + [pltpu.HBM, pl.ANY],
            name=f"reads{active}_{places[0]}",
        )
        return [reads] + [in_vmem(value) for value in w_out_near]

    def hop(active, place, maps_here, state, after):
        def body(*refs):
            advance(active, place, refs[0], None if len(maps_here) == 1 else refs[1], *refs[len(maps_here) :])

        kinds = [pltpu.VMEM] * (len(maps_here) + 1) + [pl.ANY]
        (ahead,) = call(body, [shape((HD, width), BF16)], [], maps_here + [state, after], kinds, name=f"advance{active}_{place}")
        return ahead, permute(ahead, active, [(2 * place + side, 2 * place + 2 + side) for side in range(2)])

    groups = count // 2

    own, *rows_of, wq_near = call(
        first_front,
        [maps] + rows_out + [pltpu.VMEM((depth, width), BF16)],
        [pltpu.VMEM(value.shape, value.dtype) for value in (tokens, norm_gain, w_rate, rate_base)]
        + [pltpu.VMEM((depth, 2 * width), BF16), pltpu.SemaphoreType.DMA((5,)), pltpu.SemaphoreType.DMA((quads, 2))],
        [in_hbm(tokens), norm_gain, w_qkv, w_rate, rate_base],
        [pltpu.HBM] * 5,
        name="first_front",
    )
    wq_near = in_vmem(wq_near)
    got_first = swap(own, 0, [0])
    got_rest = swap(own, 0, range(1, groups))
    read_first = layer_reads(0, [0], 1, rows_of, wq_near, init_state)
    ahead, state = hop(0, 0, [own, got_first], init_state, read_first[0])
    read_rest = layer_reads(0, range(1, groups), 1, rows_of, wq_near, ahead)
    (both,) = call(
        functools.partial(compose, 0), [maps], [], [own, got_rest, read_rest[0]], [pltpu.VMEM] * 2 + [pl.ANY], name="compose"
    )

    params = [norm_gain, w_qkv, w_rate, rate_base, w_out]
    gain_near, w_near, rate_near, base_near, w_out_near = call(
        load,
        [pltpu.VMEM(value.shape, value.dtype) for value in params],
        [pltpu.SemaphoreType.DMA((5,))],
        params + [both],
        [pltpu.HBM] * 5 + [pl.ANY],
        name="load",
    )
    params = [in_vmem(value) for value in (gain_near, w_near.reshape(w_qkv.shape[1:]), rate_near, base_near)]
    w_out_near = in_vmem(w_out_near.reshape(w_out.shape[1:]))

    def begin(places, first, after):
        span = range(2 * places[0], 2 * places[-1] + 2)
        hidden = lax.ppermute(first, ("section", "seq"), [(place, count + place) for place in span])
        own, *rows_of = call(
            functools.partial(later_front, places),
            [maps] + rows_out,
            [],
            [hidden, *params, after],
            [pltpu.VMEM] * 5 + [pl.ANY],
            name=f"later_front_{places[0]}",
        )
        return hidden, own, rows_of, [swap(own, 1, [place]) for place in places]

    here, passed = init_state, []
    for place in range(groups):
        got, (reads, near) = (got_rest, read_rest) if place else (got_first, read_first)
        if 0 < place < groups - 1:
            ahead, state = hop(0, place, [both], here, passed[0])
        if place + 1 == groups:
            firsts, passed = passed, []
        (first,) = call(
            functools.partial(first_finish, place),
            [shape((rows, model), BF16)],
            [],
            [here, got, reads, near, tokens, ahead, *passed],
            [pltpu.VMEM] * 5 + [pl.ANY] + [pltpu.VMEM] * len(passed),
            name=f"first_finish_{place}",
            aliases={6: 0} if passed else None,
        )
        passed, here = [first], state
    firsts += passed

    hidden, own_later, rows_later, gots = begin(range(groups - 1), firsts[0], own)
    hiddens, states, after = [hidden], [init_state], own_later
    for place in range(groups - 1):
        if place + 2 == groups:
            hidden, own_last, rows_last, got = begin([groups - 1], firsts[1], after)
            hiddens.append(hidden)
            gots += got
            reads = layer_reads(1, range(groups - 1), 0, rows_later, params[1], after)
            after = reads[0]
        after, state = hop(1, place, [own_later, gots[place]], states[-1], after)
        states.append(state)
    reads += layer_reads(1, [groups - 1], 0, rows_last, params[1], after)
    (result,) = call(
        functools.partial(last_finish, groups),
        [shape((1, rows, model), BF16)],
        [pltpu.VMEM((rows, model), BF16), pltpu.SemaphoreType.DMA((4,))],
        [w_out_near, *states, *gots, *reads, *hiddens, *firsts],
        name="last_finish",
        out_kind=pltpu.HBM,
    )
    return result


def solution(mesh):
    return jax.shard_map(
        shards,
        mesh=mesh,
        in_specs=(
            P(("traj", "seq"), None),
            P("section", None),
            P("section", None, None),
            P("section", None, None),
            P("section", None),
            P("section", None, None, None),
            P("section", None, None),
        ),
        out_specs=P("section", ("traj", "seq"), None),
        check_vma=False,
    )
```

```python
import functools

import jax
import jax.numpy as jnp
from jax import lax
from jax.experimental import pallas as pl
from jax.experimental.pallas import tpu as pltpu
from jax.sharding import PartitionSpec as P

HD = 64
PAIR = 2 * HD
QUAD = 4 * HD
F32 = jnp.float32
BF16 = jnp.bfloat16
EPS = 1e-6
VMEM_LIMIT = 16 * 1024 * 1024


def mm(a, b):
    return jnp.dot(a, b, preferred_element_type=F32)


def mm_nt(a, b):
    return lax.dot_general(a, b, (((1,), (1,)), ((), ())), preferred_element_type=F32)


def mm_tn(a, b):
    return lax.dot_general(a, b, (((0,), (0,)), ((), ())), preferred_element_type=F32)


def head_masks(rows, lanes):
    lane = lax.broadcasted_iota(jnp.int32, (rows, lanes), 1)
    return [lane // HD == index for index in range(lanes // HD)]


def spread(value):
    zero = jnp.zeros_like(value)
    masks = head_masks(*value.shape)
    return jnp.concatenate([jnp.where(mask, value, zero) for mask in masks], axis=0)


def spread_two(left, right):
    return jnp.concatenate([spread(left), spread(right)], axis=1)


def diagonal(product):
    first = lax.broadcasted_iota(jnp.int32, (HD, PAIR), 1) < HD
    return jnp.where(first, product[:HD], product[HD:])


def head_ones():
    row = lax.broadcasted_iota(jnp.int32, (QUAD, QUAD), 0) // HD
    lane = lax.broadcasted_iota(jnp.int32, (QUAD, QUAD), 1) // HD
    return jnp.where(row == lane, 1.0, 0.0).astype(BF16)


def unit_heads(value, ones):
    squares = mm((value * value).astype(BF16), ones)
    return value * lax.rsqrt(squares + EPS)


def norm_rows(hidden, gain):
    wide = hidden.astype(F32)
    mean_sq = jnp.mean(wide * wide, axis=-1, keepdims=True)
    return (wide * lax.rsqrt(mean_sq + EPS) * gain).astype(BF16)


def spread_rates(normed, w_rate, rate_base):
    rates = rate_base * jax.nn.sigmoid(mm_nt(normed, w_rate))
    high = rates.astype(BF16)
    low = (rates - high.astype(F32)).astype(BF16)
    heads = rates.shape[1]
    row = lax.broadcasted_iota(jnp.int32, (heads, heads * HD), 0)
    lane = lax.broadcasted_iota(jnp.int32, (heads, heads * HD), 1) // HD
    pick = jnp.where(row == lane, 1.0, 0.0).astype(BF16)
    return mm(high, pick) + mm(low, pick)


def start_all(copies):
    for copy in copies:
        copy.start()


def wait_all(copies):
    for copy in copies:
        copy.wait()


def on_section(active, body):
    pl.when(lax.axis_index("section") == active)(body)


def at_pair(places, active):
    pair = lax.axis_index("seq") // 2
    first, last = places[0], places[-1]
    return (lax.axis_index("section") == active) & (pair >= first) & (pair <= last)


def front(here, h_ref, gain_ref, w_ref, w_rate_ref, base_ref, maps, normed_out, keys_out, x_out, y_out, near=None):
    width = keys_out.shape[1]
    quads = width // QUAD

    def body():
        if near is None:
            groups, last = [], []
            h_in, gain, w_rate, base, weights, base_lane = h_ref, gain_ref, w_rate_ref, base_ref, w_ref, width
        else:
            wq, h_in, gain, w_rate, base, weights, small_sems, sems = near
            base_lane = 0
            pairs = [(gain_ref, gain), (w_rate_ref, w_rate), (base_ref, base), (h_ref, h_in)]
            small = [pltpu.make_async_copy(source, target, small_sems.at[index]) for index, (source, target) in enumerate(pairs)]
            half = wq.shape[1]
            last = [pltpu.make_async_copy(w_ref.at[0, :, pl.ds(0, half)], wq, small_sems.at[len(pairs)])]
            groups = [
                [
                    pltpu.make_async_copy(
                        w_ref.at[0, :, pl.ds((side + 1) * width + quad * QUAD, QUAD)],
                        weights.at[:, pl.ds(side * width + quad * QUAD, QUAD)],
                        sems.at[quad, side],
                    )
                    for side in range(2)
                ]
                for quad in range(quads)
            ]
            start_all(small)
            start_all(groups[0])
            wait_all(small)
            start_all(groups[1])
        normed = norm_rows(h_in[...], gain[...])
        normed_out[...] = normed
        if groups:
            start_all(groups[2])
        rates = spread_rates(normed, w_rate[0], base[...])
        ones = head_ones()

        def project(quad):
            if groups:
                wait_all(groups[quad])
                if quad + 3 < quads:
                    start_all(groups[quad + 3])
                if quad + 1 == quads:
                    start_all(last)
            key_lane = base_lane + quad * QUAD
            return [mm(normed, weights[:, lane : lane + QUAD]) for lane in (key_lane, key_lane + width)]

        def unit(quad, keys, values):
            lanes = slice(quad * QUAD, (quad + 1) * QUAD)
            keys = unit_heads(keys, ones)
            keys_bf = keys.astype(BF16)
            keys_out[:, lanes] = keys_bf
            rate = rates[:, lanes]
            return keys_bf, rate * keys, rate * values

        def crossed(quad, keys_bf, x_all, y_all):
            return mm_nt(keys_bf[HD:], spread(keys_bf[:HD])).astype(BF16)

        def fixed(quad, cross, keys_bf, x_all, y_all):
            lanes = slice(quad * QUAD, (quad + 1) * QUAD)
            rate = rates[HD:, lanes]
            x_first, y_first = x_all[:HD].astype(BF16), y_all[:HD].astype(BF16)
            fix = mm(cross, spread_two(x_first, y_first))
            x_second = (x_all[HD:] - rate * fix[:, :QUAD]).astype(BF16)
            y_second = (y_all[HD:] - rate * fix[:, QUAD:]).astype(BF16)
            x_bf = jnp.concatenate([x_first, x_second], axis=0)
            y_bf = jnp.concatenate([y_first, y_second], axis=0)
            x_out[:, lanes] = x_bf
            y_out[:, lanes] = y_bf
            return x_bf, y_bf

        def mapped(quad, keys_bf, x_bf, y_bf):
            for half in range(2):
                own = slice(half * PAIR, (half + 1) * PAIR)
                start = quad * QUAD + half * PAIR
                both = mm_tn(keys_bf[:, own], jnp.concatenate([x_bf[:, own], y_bf[:, own]], axis=1))
                maps[:, start : start + PAIR] = diagonal(both[:, :PAIR]).astype(BF16)
                maps[:, width + start : width + start + PAIR] = diagonal(both[:, PAIR:]).astype(BF16)

        def stages(picked, projected):
            units = [unit(quad, *projected[quad]) for quad in picked]
            crosses = [crossed(quad, *value) for quad, value in zip(picked, units)]
            fixes = [fixed(quad, cross, *value) for quad, cross, value in zip(picked, crosses, units)]
            for quad, value, fix in zip(picked, units, fixes):
                mapped(quad, value[0], *fix)

        if groups:
            projected = {0: project(0)}
            for quad in range(1, quads):
                projected[quad] = project(quad)
                if quad + 1 < quads:
                    stages([quad - 1], projected)
            stages([quads - 2, quads - 1], projected)
        else:
            stages(range(quads), [project(quad) for quad in range(quads)])
        wait_all(last)

    pl.when(here)(body)


def first_front(h_hbm, gain, weights, w_rate, base, maps, normed_out, keys_out, x_out, y_out, *near):
    here = lax.axis_index("section") == 0
    front(here, h_hbm, gain, weights, w_rate, base, maps, normed_out, keys_out, x_out, y_out, near)


def later_front(places, h_ref, gain, weights, w_rate, base, after_ref, *outs):
    front(at_pair(places, 1), h_ref, gain, weights, w_rate, base, *outs)


def load(*refs):
    count = (len(refs) - 2) // 2
    sources, targets, sems = refs[:count], refs[count + 1 : -1], refs[-1]

    def body():
        copies = [pltpu.make_async_copy(source, target, sems.at[index]) for index, (source, target) in enumerate(zip(sources, targets))]
        start_all(copies)
        wait_all(copies)

    on_section(1, body)


def read_out(active, places, fetches, normed_ref, keys_ref, x_ref, y_ref, weights, w_hbm, w_out_hbm, after_ref, reads_out, *rest):
    rows, width = keys_ref.shape
    *w_out, wq, sems = rest
    half = width // 2

    def body():
        late = [pltpu.make_async_copy(w_hbm.at[0, :, pl.ds(half, half)], wq, sems.at[0])] * fetches
        fetch = [pltpu.make_async_copy(w_out_hbm.at[0], target, sems.at[1]) for target in w_out]
        start_all(late)
        normed = normed_ref[...]
        ones = head_ones()
        row = lax.broadcasted_iota(jnp.int32, (rows, 2 * rows), 0)
        lane = lax.rem(lax.broadcasted_iota(jnp.int32, (rows, 2 * rows), 1), rows)
        causal = row >= lane

        def stages(start, stop, source, base):
            quads = range(start, stop, QUAD)
            queries = [unit_heads(mm(normed, source[:, lane - base : lane - base + QUAD]), ones) for lane in quads]
            parts = [value[:, own : own + PAIR] for value in queries for own in range(0, QUAD, PAIR)]
            places = [slice(lane, lane + PAIR) for lane in range(start, stop, PAIR)]
            scores = [mm_nt(part.astype(BF16), spread(keys_ref[:, place])) for part, place in zip(parts, places)]
            scores = [jnp.where(causal, score, 0.0).astype(BF16) for score in scores]
            both = [mm(score, spread_two(x_ref[:, place], y_ref[:, place])) for score, place in zip(scores, places)]
            for part, place, value in zip(parts, places, both):
                reads_out[:, place] = (part - value[:, :PAIR]).astype(BF16)
                reads_out[:, width + place.start : width + place.stop] = value[:, PAIR:].astype(BF16)

        if fetches:
            stages(0, half, weights, 0)
            wait_all(late)
            start_all(fetch)
            stages(half, width, wq, half)
            wait_all(fetch)
        else:
            stages(0, width, weights, 0)

    pl.when(at_pair(places, active))(body)


def compose(active, own_ref, got_ref, after_ref, out_ref):
    width = own_ref.shape[1] // 2

    def body(first_ref, second_ref):
        for start in range(0, width, PAIR):
            s_lanes, b_lanes = slice(start, start + PAIR), slice(width + start, width + start + PAIR)
            s_second, s_first, b_first = second_ref[:, s_lanes], first_ref[:, s_lanes], first_ref[:, b_lanes]
            step = mm(s_second, spread_two(s_first, b_first))
            out_ref[:, s_lanes] = (s_second.astype(F32) + s_first.astype(F32) - step[:, :PAIR]).astype(BF16)
            out_ref[:, b_lanes] = (second_ref[:, b_lanes].astype(F32) + b_first.astype(F32) - step[:, PAIR:]).astype(BF16)

    here = lax.axis_index("section") == active
    side = lax.rem(lax.axis_index("seq"), 2)
    pl.when(here & (side == 0))(lambda: body(own_ref, got_ref))
    pl.when(here & (side == 1))(lambda: body(got_ref, own_ref))


def pair_state(init_ref, pair):
    return jnp.concatenate([init_ref[0, 2 * pair], init_ref[0, 2 * pair + 1]], axis=1)


def apply_map(state, ref, start, width):
    step = mm(ref[:, start : start + PAIR], spread(state.astype(BF16)))
    return state - step + ref[:, width + start : width + start + PAIR].astype(F32)


def advance(active, place, own_ref, got_ref, state_ref, after_ref, out_ref):
    width = out_ref.shape[1]

    def body(refs):
        starts = range(0, width, PAIR)
        states = [state_ref[:, start : start + PAIR].astype(F32) if place else pair_state(state_ref, start // PAIR) for start in starts]
        for ref in refs:
            states = [apply_map(state, ref, start, width) for state, start in zip(states, starts)]
        for state, start in zip(states, starts):
            out_ref[:, start : start + PAIR] = state.astype(BF16)

    index = lax.axis_index("seq")
    here = (lax.axis_index("section") == active) & (index // 2 == place)
    if got_ref is None:
        pl.when(here)(lambda: body((own_ref,)))
    else:
        side = lax.rem(index, 2)
        pl.when(here & (side == 0))(lambda: body((own_ref, got_ref)))
        pl.when(here & (side == 1))(lambda: body((got_ref, own_ref)))


def finish(here, begins, state_ref, got_ref, reads_ref, w_out_ref, h_ref, store):
    width = w_out_ref.shape[0]
    model = h_ref.shape[1]
    chunk = model // 4

    def body():
        follows = lax.rem(lax.axis_index("seq"), 2) == 1
        starts = range(0, width, PAIR)
        states = [pair_state(state_ref, start // PAIR) if begins else state_ref[:, start : start + PAIR].astype(F32) for start in starts]
        moved = [apply_map(state, got_ref, start, width) for state, start in zip(states, starts)]
        states = [jnp.where(follows, after, state).astype(BF16) for after, state in zip(moved, states)]
        quads = range(0, width, QUAD)
        spreads = [spread(jnp.concatenate(states[start // PAIR : (start + QUAD) // PAIR], axis=1)) for start in quads]
        reads = [mm(reads_ref[:, start : start + QUAD], value) for start, value in zip(quads, spreads)]
        inner_bf = jnp.concatenate(
            [
                (read + reads_ref[:, width + start : width + start + QUAD].astype(F32)).astype(BF16)
                for start, read in zip(quads, reads)
            ],
            axis=1,
        )
        for start in range(0, model, chunk):
            lanes = slice(start, start + chunk)
            store(start, (h_ref[:, lanes].astype(F32) + mm(inner_bf, w_out_ref[:, lanes])).astype(BF16))

    pl.when(here)(body)


def first_finish(place, state_ref, got_ref, reads_ref, w_out_ref, h_ref, after_ref, *rest):
    out_ref = rest[-1]

    def store(start, value):
        out_ref[:, start : start + value.shape[1]] = value

    finish(at_pair([place], 0), place == 0, state_ref, got_ref, reads_ref, w_out_ref, h_ref, store)


def last_finish(count, w_out_ref, *refs):
    states, gots, refs = refs[:count], refs[count : 2 * count], refs[2 * count :]
    reads, hiddens, firsts = [[refs[index]] * (count - 1) + [refs[index + 1]] for index in (0, 2, 4)]
    out_hbm, near, sems = refs[6:]
    chunk = near.shape[1] // 4

    def write(start):
        lanes = pl.ds(start, chunk)
        return pltpu.make_async_copy(near.at[:, lanes], out_hbm.at[0, :, lanes], sems.at[start // chunk])

    def store(start, value):
        near[:, start : start + chunk] = value
        write(start).start()

    for place in range(count):
        finish(at_pair([place], 1), place == 0, states[place], gots[place], reads[place], w_out_ref, hiddens[place], store)

        @pl.when(at_pair([place], 0))
        def _():
            for start in range(0, near.shape[1], chunk):
                store(start, firsts[place][:, start : start + chunk])

    for start in range(0, near.shape[1], chunk):
        write(start).wait()


def call(body, outs, scratch, args, kinds=None, name=None, out_kind=pltpu.VMEM, aliases=None):
    specs = [pl.BlockSpec(memory_space=kind) for kind in (kinds or [pltpu.VMEM] * len(args))]
    return pl.pallas_call(
        body,
        out_shape=outs,
        in_specs=specs,
        out_specs=[pl.BlockSpec(memory_space=out_kind)] * len(outs),
        scratch_shapes=scratch,
        input_output_aliases=aliases or {},
        compiler_params=pltpu.CompilerParams(vmem_limit_bytes=VMEM_LIMIT),
        name=name,
    )(*args)


def shards(tokens, norm_gain, w_qkv, w_rate, rate_base, init_state, w_out):
    count = lax.axis_size("seq")
    heads = rate_base.shape[1]
    rows, model = tokens.shape
    width = heads * HD
    depth = w_qkv.shape[1]
    quads = width // QUAD
    shape = jax.ShapeDtypeStruct
    in_vmem = functools.partial(pltpu.with_memory_space_constraint, memory_space=pltpu.VMEM)
    in_hbm = functools.partial(pltpu.with_memory_space_constraint, memory_space=pltpu.HBM)
    maps = shape((HD, 2 * width), BF16)
    rows_out = [shape((rows, model), BF16)] + [shape((rows, width), BF16)] * 3
    w_rate = jnp.swapaxes(w_rate, 1, 2)
    norm_gain, w_qkv, w_rate, rate_base, w_out = [in_hbm(value) for value in (norm_gain, w_qkv, w_rate, rate_base, w_out)]

    def permute(value, active, pairs):
        base = active * count
        return lax.ppermute(value, ("section", "seq"), [(base + source, base + target) for source, target in pairs])

    def swap(own, active, groups):
        return permute(own, active, [(2 * group + side, 2 * group + 1 - side) for group in groups for side in range(2)])

    def layer_reads(active, places, fetches, rows_of, weights, after):
        reads, *w_out_near = call(
            functools.partial(read_out, active, places, fetches),
            [shape((rows, 2 * width), BF16)] + [pltpu.VMEM(w_out.shape[1:], BF16)] * fetches,
            [pltpu.VMEM((depth, width // 2), BF16) if fetches else pltpu.VMEM((16, 128), BF16), pltpu.SemaphoreType.DMA((2,))],
            [*rows_of, weights, w_qkv, w_out, after],
            [pltpu.VMEM] * 5 + [pltpu.HBM, pltpu.HBM, pl.ANY],
            name=f"reads{active}_{places[0]}",
        )
        return [reads] + [in_vmem(value) for value in w_out_near]

    def hop(active, place, maps_here, state, after):
        def body(*refs):
            advance(active, place, refs[0], None if len(maps_here) == 1 else refs[1], *refs[len(maps_here) :])

        kinds = [pltpu.VMEM] * (len(maps_here) + 1) + [pl.ANY]
        (ahead,) = call(body, [shape((HD, width), BF16)], [], maps_here + [state, after], kinds, name=f"advance{active}_{place}")
        return ahead, permute(ahead, active, [(2 * place + side, 2 * place + 2 + side) for side in range(2)])

    groups = count // 2

    own, *rows_of, wq_near = call(
        first_front,
        [maps] + rows_out + [pltpu.VMEM((depth, width // 2), BF16)],
        [pltpu.VMEM(value.shape, value.dtype) for value in (tokens, norm_gain, w_rate, rate_base)]
        + [pltpu.VMEM((depth, 2 * width), BF16), pltpu.SemaphoreType.DMA((5,)), pltpu.SemaphoreType.DMA((quads, 2))],
        [in_hbm(tokens), norm_gain, w_qkv, w_rate, rate_base],
        [pltpu.HBM] * 5,
        name="first_front",
    )
    wq_near = in_vmem(wq_near)
    got_first = swap(own, 0, [0])
    got_rest = swap(own, 0, range(1, groups))
    read_first = layer_reads(0, [0], 1, rows_of, wq_near, init_state)
    ahead, state = hop(0, 0, [own, got_first], init_state, read_first[0])
    read_rest = layer_reads(0, range(1, groups), 1, rows_of, wq_near, ahead)
    (both,) = call(
        functools.partial(compose, 0), [maps], [], [own, got_rest, read_rest[0]], [pltpu.VMEM] * 2 + [pl.ANY], name="compose"
    )

    params = [norm_gain, w_qkv, w_rate, rate_base, w_out]
    gain_near, w_near, rate_near, base_near, w_out_near = call(
        load,
        [pltpu.VMEM(value.shape, value.dtype) for value in params],
        [pltpu.SemaphoreType.DMA((5,))],
        params + [both],
        [pltpu.HBM] * 5 + [pl.ANY],
        name="load",
    )
    params = [in_vmem(value) for value in (gain_near, w_near.reshape(w_qkv.shape[1:]), rate_near, base_near)]
    w_out_near = in_vmem(w_out_near.reshape(w_out.shape[1:]))

    def begin(places, first, after):
        span = range(2 * places[0], 2 * places[-1] + 2)
        hidden = lax.ppermute(first, ("section", "seq"), [(place, count + place) for place in span])
        own, *rows_of = call(
            functools.partial(later_front, places),
            [maps] + rows_out,
            [],
            [hidden, *params, after],
            [pltpu.VMEM] * 5 + [pl.ANY],
            name=f"later_front_{places[0]}",
        )
        return hidden, own, rows_of, [swap(own, 1, [place]) for place in places]

    here, passed = init_state, []
    for place in range(groups):
        got, (reads, near) = (got_rest, read_rest) if place else (got_first, read_first)
        if 0 < place < groups - 1:
            ahead, state = hop(0, place, [both], here, passed[0])
        if place + 1 == groups:
            firsts, passed = passed, []
        (first,) = call(
            functools.partial(first_finish, place),
            [shape((rows, model), BF16)],
            [],
            [here, got, reads, near, tokens, ahead, *passed],
            [pltpu.VMEM] * 5 + [pl.ANY] + [pltpu.VMEM] * len(passed),
            name=f"first_finish_{place}",
            aliases={6: 0} if passed else None,
        )
        passed, here = [first], state
    firsts += passed

    hidden, own_later, rows_later, gots = begin(range(groups - 1), firsts[0], own)
    hiddens, states, after = [hidden], [init_state], own_later
    for place in range(groups - 1):
        if place + 2 == groups:
            hidden, own_last, rows_last, got = begin([groups - 1], firsts[1], after)
            hiddens.append(hidden)
            gots += got
            reads = layer_reads(1, range(groups - 1), 0, rows_later, params[1], after)
            after = reads[0]
        after, state = hop(1, place, [own_later, gots[place]], states[-1], after)
        states.append(state)
    reads += layer_reads(1, [groups - 1], 0, rows_last, params[1], after)
    (result,) = call(
        functools.partial(last_finish, groups),
        [shape((1, rows, model), BF16)],
        [pltpu.VMEM((rows, model), BF16), pltpu.SemaphoreType.DMA((4,))],
        [w_out_near, *states, *gots, *reads, *hiddens, *firsts],
        name="last_finish",
        out_kind=pltpu.HBM,
    )
    return result


def solution(mesh):
    return jax.shard_map(
        shards,
        mesh=mesh,
        in_specs=(
            P(("traj", "seq"), None),
            P("section", None),
            P("section", None, None),
            P("section", None, None),
            P("section", None),
            P("section", None, None, None),
            P("section", None, None),
        ),
        out_specs=P("section", ("traj", "seq"), None),
        check_vma=False,
    )
```

```python
import functools

import jax
import jax.numpy as jnp
from jax import lax
from jax.experimental import pallas as pl
from jax.experimental.pallas import tpu as pltpu
from jax.sharding import PartitionSpec as P

HD = 64
PAIR = 2 * HD
QUAD = 4 * HD
F32 = jnp.float32
BF16 = jnp.bfloat16
EPS = 1e-6
VMEM_LIMIT = 16 * 1024 * 1024


def mm(a, b):
    return jnp.dot(a, b, preferred_element_type=F32)


def mm_nt(a, b):
    return lax.dot_general(a, b, (((1,), (1,)), ((), ())), preferred_element_type=F32)


def mm_tn(a, b):
    return lax.dot_general(a, b, (((0,), (0,)), ((), ())), preferred_element_type=F32)


def head_masks(rows, lanes):
    lane = lax.broadcasted_iota(jnp.int32, (rows, lanes), 1)
    return [lane // HD == index for index in range(lanes // HD)]


def spread(value):
    zero = jnp.zeros_like(value)
    masks = head_masks(*value.shape)
    return jnp.concatenate([jnp.where(mask, value, zero) for mask in masks], axis=0)


def spread_two(left, right):
    return jnp.concatenate([spread(left), spread(right)], axis=1)


def diagonal(product):
    first = lax.broadcasted_iota(jnp.int32, (HD, PAIR), 1) < HD
    return jnp.where(first, product[:HD], product[HD:])


def head_ones():
    row = lax.broadcasted_iota(jnp.int32, (QUAD, QUAD), 0) // HD
    lane = lax.broadcasted_iota(jnp.int32, (QUAD, QUAD), 1) // HD
    return jnp.where(row == lane, 1.0, 0.0).astype(BF16)


def unit_heads(value, ones):
    squares = mm((value * value).astype(BF16), ones)
    return value * lax.rsqrt(squares + EPS)


def norm_rows(hidden, gain):
    wide = hidden.astype(F32)
    mean_sq = jnp.mean(wide * wide, axis=-1, keepdims=True)
    return (wide * lax.rsqrt(mean_sq + EPS) * gain).astype(BF16)


def spread_rates(normed, w_rate, rate_base):
    rates = rate_base * jax.nn.sigmoid(mm_nt(normed, w_rate))
    high = rates.astype(BF16)
    low = (rates - high.astype(F32)).astype(BF16)
    heads = rates.shape[1]
    row = lax.broadcasted_iota(jnp.int32, (heads, heads * HD), 0)
    lane = lax.broadcasted_iota(jnp.int32, (heads, heads * HD), 1) // HD
    pick = jnp.where(row == lane, 1.0, 0.0).astype(BF16)
    return mm(high, pick) + mm(low, pick)


def start_all(copies):
    for copy in copies:
        copy.start()


def wait_all(copies):
    for copy in copies:
        copy.wait()


def on_section(active, body):
    pl.when(lax.axis_index("section") == active)(body)


def at_pair(places, active):
    pair = lax.axis_index("seq") // 2
    first, last = places[0], places[-1]
    return (lax.axis_index("section") == active) & (pair >= first) & (pair <= last)


def front(here, h_ref, gain_ref, w_ref, w_rate_ref, base_ref, maps, normed_out, keys_out, x_out, y_out, near=None):
    width = keys_out.shape[1]
    quads = width // QUAD

    def body():
        if near is None:
            groups, last = [], []
            h_in, gain, w_rate, base, weights, base_lane = h_ref, gain_ref, w_rate_ref, base_ref, w_ref, width
        else:
            wq, h_in, gain, w_rate, base, weights, small_sems, sems = near
            base_lane = 0
            pairs = [(gain_ref, gain), (w_rate_ref, w_rate), (base_ref, base), (h_ref, h_in)]
            small = [pltpu.make_async_copy(source, target, small_sems.at[index]) for index, (source, target) in enumerate(pairs)]
            half = wq.shape[1]
            last = [pltpu.make_async_copy(w_ref.at[0, :, pl.ds(0, half)], wq, small_sems.at[len(pairs)])]
            groups = [
                [
                    pltpu.make_async_copy(
                        w_ref.at[0, :, pl.ds((side + 1) * width + quad * QUAD, QUAD)],
                        weights.at[:, pl.ds(side * width + quad * QUAD, QUAD)],
                        sems.at[quad, side],
                    )
                    for side in range(2)
                ]
                for quad in range(quads)
            ]
            start_all(small)
            start_all(groups[0])
            wait_all(small)
            for group in groups[1:]:
                start_all(group)
        normed = norm_rows(h_in[...], gain[...])
        normed_out[...] = normed
        rates = spread_rates(normed, w_rate[0], base[...])
        ones = head_ones()

        def project(quad):
            if groups:
                wait_all(groups[quad])
                if quad + 1 == quads:
                    start_all(last)
            key_lane = base_lane + quad * QUAD
            return [mm(normed, weights[:, lane : lane + QUAD]) for lane in (key_lane, key_lane + width)]

        def unit(quad, keys, values):
            lanes = slice(quad * QUAD, (quad + 1) * QUAD)
            keys = unit_heads(keys, ones)
            keys_bf = keys.astype(BF16)
            keys_out[:, lanes] = keys_bf
            rate = rates[:, lanes]
            return keys_bf, rate * keys, rate * values

        def crossed(quad, keys_bf, x_all, y_all):
            return mm_nt(keys_bf[HD:], spread(keys_bf[:HD])).astype(BF16)

        def fixed(quad, cross, keys_bf, x_all, y_all):
            lanes = slice(quad * QUAD, (quad + 1) * QUAD)
            rate = rates[HD:, lanes]
            x_first, y_first = x_all[:HD].astype(BF16), y_all[:HD].astype(BF16)
            fix = mm(cross, spread_two(x_first, y_first))
            x_second = (x_all[HD:] - rate * fix[:, :QUAD]).astype(BF16)
            y_second = (y_all[HD:] - rate * fix[:, QUAD:]).astype(BF16)
            x_bf = jnp.concatenate([x_first, x_second], axis=0)
            y_bf = jnp.concatenate([y_first, y_second], axis=0)
            x_out[:, lanes] = x_bf
            y_out[:, lanes] = y_bf
            return x_bf, y_bf

        def mapped(quad, keys_bf, x_bf, y_bf):
            for half in range(2):
                own = slice(half * PAIR, (half + 1) * PAIR)
                start = quad * QUAD + half * PAIR
                both = mm_tn(keys_bf[:, own], jnp.concatenate([x_bf[:, own], y_bf[:, own]], axis=1))
                maps[:, start : start + PAIR] = diagonal(both[:, :PAIR]).astype(BF16)
                maps[:, width + start : width + start + PAIR] = diagonal(both[:, PAIR:]).astype(BF16)

        picked = range(quads)
        units = [unit(quad, *value) for quad, value in zip(picked, [project(quad) for quad in picked])]
        crosses = [crossed(quad, *value) for quad, value in zip(picked, units)]
        fixes = [fixed(quad, cross, *value) for quad, cross, value in zip(picked, crosses, units)]
        for quad, value, fix in zip(picked, units, fixes):
            mapped(quad, value[0], *fix)
        wait_all(last)

    pl.when(here)(body)


def first_front(h_hbm, gain, weights, w_rate, base, maps, normed_out, keys_out, x_out, y_out, *near):
    here = lax.axis_index("section") == 0
    front(here, h_hbm, gain, weights, w_rate, base, maps, normed_out, keys_out, x_out, y_out, near)


def later_front(places, h_ref, gain, weights, w_rate, base, after_ref, *outs):
    front(at_pair(places, 1), h_ref, gain, weights, w_rate, base, *outs)


def load(*refs):
    count = (len(refs) - 2) // 2
    sources, targets, sems = refs[:count], refs[count + 1 : -1], refs[-1]

    def body():
        copies = [pltpu.make_async_copy(source, target, sems.at[index]) for index, (source, target) in enumerate(zip(sources, targets))]
        start_all(copies)
        wait_all(copies)

    on_section(1, body)


def read_out(active, places, fetches, normed_ref, keys_ref, x_ref, y_ref, weights, w_hbm, w_out_hbm, after_ref, reads_out, *rest):
    rows, width = keys_ref.shape
    *w_out, wq, sems = rest
    half = width // 2

    def body():
        late = [pltpu.make_async_copy(w_hbm.at[0, :, pl.ds(half, half)], wq, sems.at[0])] * fetches
        fetch = [pltpu.make_async_copy(w_out_hbm.at[0], target, sems.at[1]) for target in w_out]
        start_all(late + fetch)
        normed = normed_ref[...]
        ones = head_ones()
        row = lax.broadcasted_iota(jnp.int32, (rows, 2 * rows), 0)
        lane = lax.rem(lax.broadcasted_iota(jnp.int32, (rows, 2 * rows), 1), rows)
        causal = row >= lane

        def stages(start, stop, source, base):
            quads = range(start, stop, QUAD)
            queries = [unit_heads(mm(normed, source[:, lane - base : lane - base + QUAD]), ones) for lane in quads]
            parts = [value[:, own : own + PAIR] for value in queries for own in range(0, QUAD, PAIR)]
            places = [slice(lane, lane + PAIR) for lane in range(start, stop, PAIR)]
            scores = [mm_nt(part.astype(BF16), spread(keys_ref[:, place])) for part, place in zip(parts, places)]
            scores = [jnp.where(causal, score, 0.0).astype(BF16) for score in scores]
            both = [mm(score, spread_two(x_ref[:, place], y_ref[:, place])) for score, place in zip(scores, places)]
            for part, place, value in zip(parts, places, both):
                reads_out[:, place] = (part - value[:, :PAIR]).astype(BF16)
                reads_out[:, width + place.start : width + place.stop] = value[:, PAIR:].astype(BF16)

        if fetches:
            stages(0, half, weights, 0)
            wait_all(late)
            stages(half, width, wq, half)
            wait_all(fetch)
        else:
            stages(0, width, weights, 0)

    pl.when(at_pair(places, active))(body)


def compose(active, own_ref, got_ref, after_ref, out_ref):
    width = own_ref.shape[1] // 2

    def body(first_ref, second_ref):
        for start in range(0, width, PAIR):
            s_lanes, b_lanes = slice(start, start + PAIR), slice(width + start, width + start + PAIR)
            s_second, s_first, b_first = second_ref[:, s_lanes], first_ref[:, s_lanes], first_ref[:, b_lanes]
            step = mm(s_second, spread_two(s_first, b_first))
            out_ref[:, s_lanes] = (s_second.astype(F32) + s_first.astype(F32) - step[:, :PAIR]).astype(BF16)
            out_ref[:, b_lanes] = (second_ref[:, b_lanes].astype(F32) + b_first.astype(F32) - step[:, PAIR:]).astype(BF16)

    here = lax.axis_index("section") == active
    side = lax.rem(lax.axis_index("seq"), 2)
    pl.when(here & (side == 0))(lambda: body(own_ref, got_ref))
    pl.when(here & (side == 1))(lambda: body(got_ref, own_ref))


def pair_state(init_ref, pair):
    return jnp.concatenate([init_ref[0, 2 * pair], init_ref[0, 2 * pair + 1]], axis=1)


def apply_map(state, ref, start, width):
    step = mm(ref[:, start : start + PAIR], spread(state.astype(BF16)))
    return state - step + ref[:, width + start : width + start + PAIR].astype(F32)


def moved_states(state_of, refs, width):
    starts = range(0, width, PAIR)
    states = [state_of(start) for start in starts]
    for ref in refs:
        states = [apply_map(state, ref, start, width) for state, start in zip(states, starts)]
    return states


def put_states(out_ref, states):
    for index, state in enumerate(states):
        out_ref[:, index * PAIR : (index + 1) * PAIR] = state.astype(BF16)


def advance(active, place, own_ref, got_ref, state_ref, after_ref, out_ref):
    width = out_ref.shape[1]

    def body(refs):
        def state_of(start):
            return state_ref[:, start : start + PAIR].astype(F32) if place else pair_state(state_ref, start // PAIR)

        put_states(out_ref, moved_states(state_of, refs, width))

    here = at_pair([place], active)
    if got_ref is None:
        pl.when(here)(lambda: body((own_ref,)))
    else:
        side = lax.rem(lax.axis_index("seq"), 2)
        pl.when(here & (side == 0))(lambda: body((own_ref, got_ref)))
        pl.when(here & (side == 1))(lambda: body((got_ref, own_ref)))


def first_step(own_ref, init_ref, out_ref):
    width = out_ref.shape[1]

    @pl.when((lax.axis_index("section") == 0) & (lax.axis_index("seq") == 0))
    def _():
        put_states(out_ref, moved_states(lambda start: pair_state(init_ref, start // PAIR), (own_ref,), width))


def first_advance(own_ref, got_ref, init_ref, state_ref, after_ref, out_ref):
    width = out_ref.shape[1]
    here = at_pair([0], 0)
    side = lax.rem(lax.axis_index("seq"), 2)

    @pl.when(here & (side == 0))
    def _():
        put_states(out_ref, moved_states(lambda start: pair_state(init_ref, start // PAIR), (own_ref, got_ref), width))

    @pl.when(here & (side == 1))
    def _():
        put_states(out_ref, moved_states(lambda start: state_ref[:, start : start + PAIR].astype(F32), (own_ref,), width))


def finish(here, begins, state_ref, got_ref, reads_ref, w_out_ref, h_ref, store, followed=None):
    width = w_out_ref.shape[0]
    model = h_ref.shape[1]
    chunk = model // 4

    def body():
        follows = lax.rem(lax.axis_index("seq"), 2) == 1
        starts = range(0, width, PAIR)
        states = [pair_state(state_ref, start // PAIR) if begins else state_ref[:, start : start + PAIR].astype(F32) for start in starts]
        if followed is None:
            moved = [apply_map(state, got_ref, start, width) for state, start in zip(states, starts)]
        else:
            moved = [followed[:, start : start + PAIR].astype(F32) for start in starts]
        states = [jnp.where(follows, after, state).astype(BF16) for after, state in zip(moved, states)]
        quads = range(0, width, QUAD)
        spreads = [spread(jnp.concatenate(states[start // PAIR : (start + QUAD) // PAIR], axis=1)) for start in quads]
        reads = [mm(reads_ref[:, start : start + QUAD], value) for start, value in zip(quads, spreads)]
        inner_bf = jnp.concatenate(
            [
                (read + reads_ref[:, width + start : width + start + QUAD].astype(F32)).astype(BF16)
                for start, read in zip(quads, reads)
            ],
            axis=1,
        )
        for start in range(0, model, chunk):
            lanes = slice(start, start + chunk)
            store(start, (h_ref[:, lanes].astype(F32) + mm(inner_bf, w_out_ref[:, lanes])).astype(BF16))

    pl.when(here)(body)


def first_finish(place, state_ref, got_ref, reads_ref, w_out_ref, h_ref, after_ref, *rest):
    out_ref = rest[-1]

    def store(start, value):
        out_ref[:, start : start + value.shape[1]] = value

    followed = None if place else got_ref
    finish(at_pair([place], 0), place == 0, state_ref, got_ref, reads_ref, w_out_ref, h_ref, store, followed)


def last_finish(count, w_out_ref, *refs):
    states, gots, refs = refs[:count], refs[count : 2 * count], refs[2 * count :]
    reads, hiddens, firsts = [[refs[index]] * (count - 1) + [refs[index + 1]] for index in (0, 2, 4)]
    out_hbm, near, sems = refs[6:]
    chunk = near.shape[1] // 4

    def write(start):
        lanes = pl.ds(start, chunk)
        return pltpu.make_async_copy(near.at[:, lanes], out_hbm.at[0, :, lanes], sems.at[start // chunk])

    def store(start, value):
        near[:, start : start + chunk] = value
        write(start).start()

    for place in range(count):
        finish(at_pair([place], 1), place == 0, states[place], gots[place], reads[place], w_out_ref, hiddens[place], store)

        @pl.when(at_pair([place], 0))
        def _():
            for start in range(0, near.shape[1], chunk):
                store(start, firsts[place][:, start : start + chunk])

    for start in range(0, near.shape[1], chunk):
        write(start).wait()


def call(body, outs, scratch, args, kinds=None, name=None, out_kind=pltpu.VMEM, aliases=None):
    specs = [pl.BlockSpec(memory_space=kind) for kind in (kinds or [pltpu.VMEM] * len(args))]
    return pl.pallas_call(
        body,
        out_shape=outs,
        in_specs=specs,
        out_specs=[pl.BlockSpec(memory_space=out_kind)] * len(outs),
        scratch_shapes=scratch,
        input_output_aliases=aliases or {},
        compiler_params=pltpu.CompilerParams(vmem_limit_bytes=VMEM_LIMIT),
        name=name,
    )(*args)


def shards(tokens, norm_gain, w_qkv, w_rate, rate_base, init_state, w_out):
    count = lax.axis_size("seq")
    heads = rate_base.shape[1]
    rows, model = tokens.shape
    width = heads * HD
    depth = w_qkv.shape[1]
    quads = width // QUAD
    shape = jax.ShapeDtypeStruct
    in_vmem = functools.partial(pltpu.with_memory_space_constraint, memory_space=pltpu.VMEM)
    in_hbm = functools.partial(pltpu.with_memory_space_constraint, memory_space=pltpu.HBM)
    maps = shape((HD, 2 * width), BF16)
    rows_out = [shape((rows, model), BF16)] + [shape((rows, width), BF16)] * 3
    w_rate = jnp.swapaxes(w_rate, 1, 2)
    norm_gain, w_qkv, w_rate, rate_base, w_out = [in_hbm(value) for value in (norm_gain, w_qkv, w_rate, rate_base, w_out)]

    def permute(value, active, pairs):
        base = active * count
        return lax.ppermute(value, ("section", "seq"), [(base + source, base + target) for source, target in pairs])

    def swap(own, active, groups):
        return permute(own, active, [(2 * group + side, 2 * group + 1 - side) for group in groups for side in range(2)])

    def layer_reads(active, places, fetches, rows_of, weights, after):
        reads, *w_out_near = call(
            functools.partial(read_out, active, places, fetches),
            [shape((rows, 2 * width), BF16)] + [pltpu.VMEM(w_out.shape[1:], BF16)] * fetches,
            [pltpu.VMEM((depth, width // 2), BF16) if fetches else pltpu.VMEM((16, 128), BF16), pltpu.SemaphoreType.DMA((2,))],
            [*rows_of, weights, w_qkv, w_out, after],
            [pltpu.VMEM] * 5 + [pltpu.HBM, pltpu.HBM, pl.ANY],
            name=f"reads{active}_{places[0]}",
        )
        return [reads] + [in_vmem(value) for value in w_out_near]

    def hop(active, place, maps_here, state, after):
        def body(*refs):
            advance(active, place, refs[0], None if len(maps_here) == 1 else refs[1], *refs[len(maps_here) :])

        kinds = [pltpu.VMEM] * (len(maps_here) + 1) + [pl.ANY]
        (ahead,) = call(body, [shape((HD, width), BF16)], [], maps_here + [state, after], kinds, name=f"advance{active}_{place}")
        return ahead, permute(ahead, active, [(2 * place + side, 2 * place + 2 + side) for side in range(2)])

    groups = count // 2

    own, *rows_of, wq_near = call(
        first_front,
        [maps] + rows_out + [pltpu.VMEM((depth, width // 2), BF16)],
        [pltpu.VMEM(value.shape, value.dtype) for value in (tokens, norm_gain, w_rate, rate_base)]
        + [pltpu.VMEM((depth, 2 * width), BF16), pltpu.SemaphoreType.DMA((5,)), pltpu.SemaphoreType.DMA((quads, 2))],
        [in_hbm(tokens), norm_gain, w_qkv, w_rate, rate_base],
        [pltpu.HBM] * 5,
        name="first_front",
    )
    wq_near = in_vmem(wq_near)
    state_out = shape((HD, width), BF16)
    got_first = permute(own, 0, [(1, 0)])
    (stepped,) = call(first_step, [state_out], [], [own, init_state], name="first_step")
    stepped = permute(stepped, 0, [(0, 1)])
    got_rest = swap(own, 0, range(1, groups))
    read_first = layer_reads(0, [0], 1, rows_of, wq_near, init_state)
    (ahead,) = call(
        first_advance,
        [state_out],
        [],
        [own, got_first, init_state, stepped, read_first[0]],
        [pltpu.VMEM] * 4 + [pl.ANY],
        name="first_advance",
    )
    state = permute(ahead, 0, [(side, 2 + side) for side in range(2)])
    read_rest = layer_reads(0, range(1, groups), 1, rows_of, wq_near, ahead)
    (both,) = call(
        functools.partial(compose, 0), [maps], [], [own, got_rest, read_rest[0]], [pltpu.VMEM] * 2 + [pl.ANY], name="compose"
    )

    params = [norm_gain, w_qkv, w_rate, rate_base, w_out]
    gain_near, w_near, rate_near, base_near, w_out_near = call(
        load,
        [pltpu.VMEM(value.shape, value.dtype) for value in params],
        [pltpu.SemaphoreType.DMA((5,))],
        params + [both],
        [pltpu.HBM] * 5 + [pl.ANY],
        name="load",
    )
    params = [in_vmem(value) for value in (gain_near, w_near.reshape(w_qkv.shape[1:]), rate_near, base_near)]
    w_out_near = in_vmem(w_out_near.reshape(w_out.shape[1:]))

    def begin(places, first, after):
        span = range(2 * places[0], 2 * places[-1] + 2)
        hidden = lax.ppermute(first, ("section", "seq"), [(place, count + place) for place in span])
        own, *rows_of = call(
            functools.partial(later_front, places),
            [maps] + rows_out,
            [],
            [hidden, *params, after],
            [pltpu.VMEM] * 5 + [pl.ANY],
            name=f"later_front_{places[0]}",
        )
        return hidden, own, rows_of, [swap(own, 1, [place]) for place in places]

    here, passed = init_state, []
    for place in range(groups):
        got, (reads, near) = (got_rest, read_rest) if place else (stepped, read_first)
        if 0 < place < groups - 1:
            ahead, state = hop(0, place, [both], here, passed[0])
        if place + 1 == groups:
            firsts, passed = passed, []
        (first,) = call(
            functools.partial(first_finish, place),
            [shape((rows, model), BF16)],
            [],
            [here, got, reads, near, tokens, ahead, *passed],
            [pltpu.VMEM] * 5 + [pl.ANY] + [pltpu.VMEM] * len(passed),
            name=f"first_finish_{place}",
            aliases={6: 0} if passed else None,
        )
        passed, here = [first], state
    firsts += passed

    hidden, own_later, rows_later, gots = begin(range(groups - 1), firsts[0], own)
    hiddens, states, after = [hidden], [init_state], own_later
    for place in range(groups - 1):
        if place + 2 == groups:
            hidden, own_last, rows_last, got = begin([groups - 1], firsts[1], after)
            hiddens.append(hidden)
            gots += got
            reads = layer_reads(1, range(groups - 1), 0, rows_later, params[1], after)
            after = reads[0]
        after, state = hop(1, place, [own_later, gots[place]], states[-1], after)
        states.append(state)
    reads += layer_reads(1, [groups - 1], 0, rows_last, params[1], after)
    (result,) = call(
        functools.partial(last_finish, groups),
        [shape((1, rows, model), BF16)],
        [pltpu.VMEM((rows, model), BF16), pltpu.SemaphoreType.DMA((4,))],
        [w_out_near, *states, *gots, *reads, *hiddens, *firsts],
        name="last_finish",
        out_kind=pltpu.HBM,
    )
    return result


def solution(mesh):
    return jax.shard_map(
        shards,
        mesh=mesh,
        in_specs=(
            P(("traj", "seq"), None),
            P("section", None),
            P("section", None, None),
            P("section", None, None),
            P("section", None),
            P("section", None, None, None),
            P("section", None, None),
        ),
        out_specs=P("section", ("traj", "seq"), None),
        check_vma=False,
    )
```

```python
import functools

import jax
import jax.numpy as jnp
from jax import lax
from jax.experimental import pallas as pl
from jax.experimental.pallas import tpu as pltpu
from jax.sharding import PartitionSpec as P

HD = 64
PAIR = 2 * HD
QUAD = 4 * HD
F32 = jnp.float32
BF16 = jnp.bfloat16
EPS = 1e-6
VMEM_LIMIT = 16 * 1024 * 1024


def mm(a, b):
    return jnp.dot(a, b, preferred_element_type=F32)


def mm_nt(a, b):
    return lax.dot_general(a, b, (((1,), (1,)), ((), ())), preferred_element_type=F32)


def mm_tn(a, b):
    return lax.dot_general(a, b, (((0,), (0,)), ((), ())), preferred_element_type=F32)


def head_masks(rows, lanes):
    lane = lax.broadcasted_iota(jnp.int32, (rows, lanes), 1)
    return [lane // HD == index for index in range(lanes // HD)]


def spread(value):
    zero = jnp.zeros_like(value)
    masks = head_masks(*value.shape)
    return jnp.concatenate([jnp.where(mask, value, zero) for mask in masks], axis=0)


def spread_two(left, right):
    return jnp.concatenate([spread(left), spread(right)], axis=1)


def diagonal(product):
    first = lax.broadcasted_iota(jnp.int32, (HD, PAIR), 1) < HD
    return jnp.where(first, product[:HD], product[HD:])


def head_ones():
    row = lax.broadcasted_iota(jnp.int32, (QUAD, QUAD), 0) // HD
    lane = lax.broadcasted_iota(jnp.int32, (QUAD, QUAD), 1) // HD
    return jnp.where(row == lane, 1.0, 0.0).astype(BF16)


def unit_heads(value, ones):
    squares = mm((value * value).astype(BF16), ones)
    return value * lax.rsqrt(squares + EPS)


def norm_rows(hidden, gain):
    wide = hidden.astype(F32)
    mean_sq = jnp.mean(wide * wide, axis=-1, keepdims=True)
    return (wide * lax.rsqrt(mean_sq + EPS) * gain).astype(BF16)


def spread_rates(normed, w_rate, rate_base):
    rates = rate_base * jax.nn.sigmoid(mm_nt(normed, w_rate))
    high = rates.astype(BF16)
    low = (rates - high.astype(F32)).astype(BF16)
    heads = rates.shape[1]
    row = lax.broadcasted_iota(jnp.int32, (heads, heads * HD), 0)
    lane = lax.broadcasted_iota(jnp.int32, (heads, heads * HD), 1) // HD
    pick = jnp.where(row == lane, 1.0, 0.0).astype(BF16)
    return mm(high, pick) + mm(low, pick)


def start_all(copies):
    for copy in copies:
        copy.start()


def wait_all(copies):
    for copy in copies:
        copy.wait()


def on_section(active, body):
    pl.when(lax.axis_index("section") == active)(body)


def at_pair(places, active):
    pair = lax.axis_index("seq") // 2
    first, last = places[0], places[-1]
    return (lax.axis_index("section") == active) & (pair >= first) & (pair <= last)


def front(here, h_ref, gain_ref, w_ref, w_rate_ref, base_ref, maps, normed_out, keys_out, x_out, y_out, near=None):
    width = keys_out.shape[1]
    quads = width // QUAD

    def body():
        if near is None:
            groups, last = [], []
            h_in, gain, w_rate, base, weights, base_lane = h_ref, gain_ref, w_rate_ref, base_ref, w_ref, width
        else:
            wq, h_in, gain, w_rate, base, weights, small_sems, sems = near
            base_lane = 0
            pairs = [(gain_ref, gain), (w_rate_ref, w_rate), (base_ref, base), (h_ref, h_in)]
            small = [pltpu.make_async_copy(source, target, small_sems.at[index]) for index, (source, target) in enumerate(pairs)]
            half = wq.shape[1]
            last = [pltpu.make_async_copy(w_ref.at[0, :, pl.ds(0, half)], wq, small_sems.at[len(pairs)])]
            groups = [
                [
                    pltpu.make_async_copy(
                        w_ref.at[0, :, pl.ds((side + 1) * width + quad * QUAD, QUAD)],
                        weights.at[:, pl.ds(side * width + quad * QUAD, QUAD)],
                        sems.at[quad, side],
                    )
                    for side in range(2)
                ]
                for quad in range(quads)
            ]
            start_all(small)
            start_all(groups[0])
            wait_all(small)
            for group in groups[1:]:
                start_all(group)
        normed = norm_rows(h_in[...], gain[...])
        normed_out[...] = normed
        rates = spread_rates(normed, w_rate[0], base[...])
        ones = head_ones()

        def project(quad):
            if groups:
                wait_all(groups[quad])
                if quad + 1 == quads:
                    start_all(last)
            key_lane = base_lane + quad * QUAD
            return [mm(normed, weights[:, lane : lane + QUAD]) for lane in (key_lane, key_lane + width)]

        def unit(quad, keys, values):
            lanes = slice(quad * QUAD, (quad + 1) * QUAD)
            keys = unit_heads(keys, ones)
            keys_bf = keys.astype(BF16)
            keys_out[:, lanes] = keys_bf
            rate = rates[:, lanes]
            return keys_bf, rate * keys, rate * values

        def crossed(quad, keys_bf, x_all, y_all):
            return mm_nt(keys_bf[HD:], spread(keys_bf[:HD])).astype(BF16)

        def fixed(quad, cross, keys_bf, x_all, y_all):
            lanes = slice(quad * QUAD, (quad + 1) * QUAD)
            rate = rates[HD:, lanes]
            x_first, y_first = x_all[:HD].astype(BF16), y_all[:HD].astype(BF16)
            fix = mm(cross, spread_two(x_first, y_first))
            x_second = (x_all[HD:] - rate * fix[:, :QUAD]).astype(BF16)
            y_second = (y_all[HD:] - rate * fix[:, QUAD:]).astype(BF16)
            x_bf = jnp.concatenate([x_first, x_second], axis=0)
            y_bf = jnp.concatenate([y_first, y_second], axis=0)
            x_out[:, lanes] = x_bf
            y_out[:, lanes] = y_bf
            return x_bf, y_bf

        def mapped(quad, keys_bf, x_bf, y_bf):
            for half in range(2):
                own = slice(half * PAIR, (half + 1) * PAIR)
                start = quad * QUAD + half * PAIR
                both = mm_tn(keys_bf[:, own], jnp.concatenate([x_bf[:, own], y_bf[:, own]], axis=1))
                maps[:, start : start + PAIR] = diagonal(both[:, :PAIR]).astype(BF16)
                maps[:, width + start : width + start + PAIR] = diagonal(both[:, PAIR:]).astype(BF16)

        picked = range(quads)
        units = [unit(quad, *value) for quad, value in zip(picked, [project(quad) for quad in picked])]
        crosses = [crossed(quad, *value) for quad, value in zip(picked, units)]
        fixes = [fixed(quad, cross, *value) for quad, cross, value in zip(picked, crosses, units)]
        for quad, value, fix in zip(picked, units, fixes):
            mapped(quad, value[0], *fix)
        wait_all(last)

    pl.when(here)(body)


def first_front(h_hbm, gain, weights, w_rate, base, maps, normed_out, keys_out, x_out, y_out, *near):
    here = lax.axis_index("section") == 0
    front(here, h_hbm, gain, weights, w_rate, base, maps, normed_out, keys_out, x_out, y_out, near)


def later_front(places, h_ref, gain, weights, w_rate, base, after_ref, *outs):
    front(at_pair(places, 1), h_ref, gain, weights, w_rate, base, *outs)


def load(*refs):
    count = (len(refs) - 2) // 2
    sources, targets, sems = refs[:count], refs[count + 1 : -1], refs[-1]

    def body():
        copies = [pltpu.make_async_copy(source, target, sems.at[index]) for index, (source, target) in enumerate(zip(sources, targets))]
        start_all(copies)
        wait_all(copies)

    on_section(1, body)


def read_out(active, places, fetches, normed_ref, keys_ref, x_ref, y_ref, weights, w_hbm, w_out_hbm, after_ref, reads_out, *rest):
    rows, width = keys_ref.shape
    *w_out, wq, sems = rest
    half = width // 2

    def body():
        late = [pltpu.make_async_copy(w_hbm.at[0, :, pl.ds(half, half)], wq, sems.at[0])] * fetches
        fetch = [pltpu.make_async_copy(w_out_hbm.at[0], target, sems.at[1]) for target in w_out]
        start_all(late + fetch)
        normed = normed_ref[...]
        ones = head_ones()
        row = lax.broadcasted_iota(jnp.int32, (rows, 2 * rows), 0)
        lane = lax.rem(lax.broadcasted_iota(jnp.int32, (rows, 2 * rows), 1), rows)
        causal = row >= lane

        def stages(start, stop, source, base):
            quads = range(start, stop, QUAD)
            queries = [unit_heads(mm(normed, source[:, lane - base : lane - base + QUAD]), ones) for lane in quads]
            parts = [value[:, own : own + PAIR] for value in queries for own in range(0, QUAD, PAIR)]
            places = [slice(lane, lane + PAIR) for lane in range(start, stop, PAIR)]
            scores = [mm_nt(part.astype(BF16), spread(keys_ref[:, place])) for part, place in zip(parts, places)]
            scores = [jnp.where(causal, score, 0.0).astype(BF16) for score in scores]
            both = [mm(score, spread_two(x_ref[:, place], y_ref[:, place])) for score, place in zip(scores, places)]
            for part, place, value in zip(parts, places, both):
                reads_out[:, place] = (part - value[:, :PAIR]).astype(BF16)
                reads_out[:, width + place.start : width + place.stop] = value[:, PAIR:].astype(BF16)

        if fetches:
            stages(0, half, weights, 0)
            wait_all(late)
            stages(half, width, wq, half)
            wait_all(fetch)
        else:
            stages(0, width, weights, 0)

    pl.when(at_pair(places, active))(body)


def compose(active, own_ref, got_ref, after_ref, out_ref):
    width = own_ref.shape[1] // 2

    def body(first_ref, second_ref):
        for start in range(0, width, PAIR):
            s_lanes, b_lanes = slice(start, start + PAIR), slice(width + start, width + start + PAIR)
            s_second, s_first, b_first = second_ref[:, s_lanes], first_ref[:, s_lanes], first_ref[:, b_lanes]
            step = mm(s_second, spread_two(s_first, b_first))
            out_ref[:, s_lanes] = (s_second.astype(F32) + s_first.astype(F32) - step[:, :PAIR]).astype(BF16)
            out_ref[:, b_lanes] = (second_ref[:, b_lanes].astype(F32) + b_first.astype(F32) - step[:, PAIR:]).astype(BF16)

    here = lax.axis_index("section") == active
    side = lax.rem(lax.axis_index("seq"), 2)
    pl.when(here & (side == 0))(lambda: body(own_ref, got_ref))
    pl.when(here & (side == 1))(lambda: body(got_ref, own_ref))


def pair_state(init_ref, pair):
    return jnp.concatenate([init_ref[0, 2 * pair], init_ref[0, 2 * pair + 1]], axis=1)


def apply_map(state, ref, start, width):
    step = mm(ref[:, start : start + PAIR], spread(state.astype(BF16)))
    return state - step + ref[:, width + start : width + start + PAIR].astype(F32)


def moved_states(state_of, refs, width):
    starts = range(0, width, PAIR)
    states = [state_of(start) for start in starts]
    for ref in refs:
        states = [apply_map(state, ref, start, width) for state, start in zip(states, starts)]
    return states


def put_states(out_ref, states):
    for index, state in enumerate(states):
        out_ref[:, index * PAIR : (index + 1) * PAIR] = state.astype(BF16)


def advance(active, place, own_ref, got_ref, state_refs, after_ref, out_ref):
    width = out_ref.shape[1]

    def body(state_ref, refs):
        def state_of(start):
            return state_ref[:, start : start + PAIR].astype(F32) if place else pair_state(state_ref, start // PAIR)

        put_states(out_ref, moved_states(state_of, refs, width))

    here = at_pair([place], active)
    side = lax.rem(lax.axis_index("seq"), 2)
    orders = [(own_ref,)] * 2 if got_ref is None else [(own_ref, got_ref), (got_ref, own_ref)]
    if got_ref is None and len(state_refs) == 1:
        pl.when(here)(lambda: body(state_refs[0], orders[0]))
    else:
        pl.when(here & (side == 0))(lambda: body(state_refs[0], orders[0]))
        pl.when(here & (side == 1))(lambda: body(state_refs[-1], orders[1]))


def first_step(own_ref, init_ref, out_ref):
    @pl.when((lax.axis_index("section") == 0) & (lax.axis_index("seq") == 0))
    def _():
        put_states(out_ref, moved_states(lambda start: pair_state(init_ref, start // PAIR), (own_ref,), out_ref.shape[1]))


def second_step(own_ref, state_ref, after_ref, out_ref):
    @pl.when((lax.axis_index("section") == 0) & (lax.axis_index("seq") == 1))
    def _():
        put_states(
            out_ref, moved_states(lambda start: state_ref[:, start : start + PAIR].astype(F32), (own_ref,), out_ref.shape[1])
        )


def finish(here, begins, state_refs, got_ref, reads_ref, w_out_ref, h_ref, store, followed=None):
    width = w_out_ref.shape[0]
    model = h_ref.shape[1]
    chunk = model // 4

    def body():
        follows = lax.rem(lax.axis_index("seq"), 2) == 1
        starts = range(0, width, PAIR)
        if begins:
            states = [pair_state(state_refs[0], start // PAIR) for start in starts]
        else:
            states = [state_refs[0][:, start : start + PAIR].astype(F32) for start in starts]
            for ref in state_refs[1:]:
                others = [ref[:, start : start + PAIR].astype(F32) for start in starts]
                states = [jnp.where(follows, other, state) for other, state in zip(others, states)]
        if followed is None:
            moved = [apply_map(state, got_ref, start, width) for state, start in zip(states, starts)]
        else:
            moved = [followed[:, start : start + PAIR].astype(F32) for start in starts]
        states = [jnp.where(follows, after, state).astype(BF16) for after, state in zip(moved, states)]
        quads = range(0, width, QUAD)
        spreads = [spread(jnp.concatenate(states[start // PAIR : (start + QUAD) // PAIR], axis=1)) for start in quads]
        reads = [mm(reads_ref[:, start : start + QUAD], value) for start, value in zip(quads, spreads)]
        inner_bf = jnp.concatenate(
            [
                (read + reads_ref[:, width + start : width + start + QUAD].astype(F32)).astype(BF16)
                for start, read in zip(quads, reads)
            ],
            axis=1,
        )
        for start in range(0, model, chunk):
            lanes = slice(start, start + chunk)
            store(start, (h_ref[:, lanes].astype(F32) + mm(inner_bf, w_out_ref[:, lanes])).astype(BF16))

    pl.when(here)(body)


def first_finish(place, count, *refs):
    state_refs, (got_ref, reads_ref, w_out_ref, h_ref, after_ref, *rest) = refs[:count], refs[count:]
    out_ref = rest[-1]

    def store(start, value):
        out_ref[:, start : start + value.shape[1]] = value

    followed = None if place else got_ref
    finish(at_pair([place], 0), place == 0, state_refs, got_ref, reads_ref, w_out_ref, h_ref, store, followed)


def last_finish(count, w_out_ref, *refs):
    states, gots, refs = refs[:count], refs[count : 2 * count], refs[2 * count :]
    reads, hiddens, firsts = [[refs[index]] * (count - 1) + [refs[index + 1]] for index in (0, 2, 4)]
    out_hbm, near, sems = refs[6:]
    chunk = near.shape[1] // 4

    def write(start):
        lanes = pl.ds(start, chunk)
        return pltpu.make_async_copy(near.at[:, lanes], out_hbm.at[0, :, lanes], sems.at[start // chunk])

    def store(start, value):
        near[:, start : start + chunk] = value
        write(start).start()

    for place in range(count):
        finish(at_pair([place], 1), place == 0, [states[place]], gots[place], reads[place], w_out_ref, hiddens[place], store)

        @pl.when(at_pair([place], 0))
        def _():
            for start in range(0, near.shape[1], chunk):
                store(start, firsts[place][:, start : start + chunk])

    for start in range(0, near.shape[1], chunk):
        write(start).wait()


def call(body, outs, scratch, args, kinds=None, name=None, out_kind=pltpu.VMEM, aliases=None):
    specs = [pl.BlockSpec(memory_space=kind) for kind in (kinds or [pltpu.VMEM] * len(args))]
    return pl.pallas_call(
        body,
        out_shape=outs,
        in_specs=specs,
        out_specs=[pl.BlockSpec(memory_space=out_kind)] * len(outs),
        scratch_shapes=scratch,
        input_output_aliases=aliases or {},
        compiler_params=pltpu.CompilerParams(vmem_limit_bytes=VMEM_LIMIT),
        name=name,
    )(*args)


def shards(tokens, norm_gain, w_qkv, w_rate, rate_base, init_state, w_out):
    count = lax.axis_size("seq")
    heads = rate_base.shape[1]
    rows, model = tokens.shape
    width = heads * HD
    depth = w_qkv.shape[1]
    quads = width // QUAD
    shape = jax.ShapeDtypeStruct
    in_vmem = functools.partial(pltpu.with_memory_space_constraint, memory_space=pltpu.VMEM)
    in_hbm = functools.partial(pltpu.with_memory_space_constraint, memory_space=pltpu.HBM)
    maps = shape((HD, 2 * width), BF16)
    rows_out = [shape((rows, model), BF16)] + [shape((rows, width), BF16)] * 3
    w_rate = jnp.swapaxes(w_rate, 1, 2)
    norm_gain, w_qkv, w_rate, rate_base, w_out = [in_hbm(value) for value in (norm_gain, w_qkv, w_rate, rate_base, w_out)]

    def permute(value, active, pairs):
        base = active * count
        return lax.ppermute(value, ("section", "seq"), [(base + source, base + target) for source, target in pairs])

    def swap(own, active, groups):
        return permute(own, active, [(2 * group + side, 2 * group + 1 - side) for group in groups for side in range(2)])

    def layer_reads(active, places, fetches, rows_of, weights, after):
        reads, *w_out_near = call(
            functools.partial(read_out, active, places, fetches),
            [shape((rows, 2 * width), BF16)] + [pltpu.VMEM(w_out.shape[1:], BF16)] * fetches,
            [pltpu.VMEM((depth, width // 2), BF16) if fetches else pltpu.VMEM((16, 128), BF16), pltpu.SemaphoreType.DMA((2,))],
            [*rows_of, weights, w_qkv, w_out, after],
            [pltpu.VMEM] * 5 + [pltpu.HBM, pltpu.HBM, pl.ANY],
            name=f"reads{active}_{places[0]}",
        )
        return [reads] + [in_vmem(value) for value in w_out_near]

    def hop(active, place, maps_here, states, after):
        count_here = len(maps_here)

        def body(*refs):
            advance(active, place, refs[0], None if count_here == 1 else refs[1], refs[count_here:-2], *refs[-2:])

        kinds = [pltpu.VMEM] * (count_here + len(states)) + [pl.ANY]
        (ahead,) = call(body, [state_out], [], maps_here + states + [after], kinds, name=f"advance{active}_{place}")
        return ahead, [permute(ahead, active, [(2 * place + side, 2 * place + 2 + side) for side in range(2)])]

    state_out = shape((HD, width), BF16)
    groups = count // 2

    own, *rows_of, wq_near = call(
        first_front,
        [maps] + rows_out + [pltpu.VMEM((depth, width // 2), BF16)],
        [pltpu.VMEM(value.shape, value.dtype) for value in (tokens, norm_gain, w_rate, rate_base)]
        + [pltpu.VMEM((depth, 2 * width), BF16), pltpu.SemaphoreType.DMA((5,)), pltpu.SemaphoreType.DMA((quads, 2))],
        [in_hbm(tokens), norm_gain, w_qkv, w_rate, rate_base],
        [pltpu.HBM] * 5,
        name="first_front",
    )
    wq_near = in_vmem(wq_near)
    (stepped,) = call(first_step, [state_out], [], [own, init_state], name="first_step")
    stepped = permute(stepped, 0, [(0, 1)])
    got_rest = swap(own, 0, range(1, groups))
    read_first = layer_reads(0, [0], 1, rows_of, wq_near, init_state)
    (ahead,) = call(
        second_step, [state_out], [], [own, stepped, read_first[0]], [pltpu.VMEM] * 2 + [pl.ANY], name="second_step"
    )
    state = [permute(ahead, 0, [(1, 2 + side)]) for side in range(2)]
    read_rest = layer_reads(0, range(1, groups), 1, rows_of, wq_near, ahead)
    (both,) = call(
        functools.partial(compose, 0), [maps], [], [own, got_rest, read_rest[0]], [pltpu.VMEM] * 2 + [pl.ANY], name="compose"
    )

    params = [norm_gain, w_qkv, w_rate, rate_base, w_out]
    gain_near, w_near, rate_near, base_near, w_out_near = call(
        load,
        [pltpu.VMEM(value.shape, value.dtype) for value in params],
        [pltpu.SemaphoreType.DMA((5,))],
        params + [both],
        [pltpu.HBM] * 5 + [pl.ANY],
        name="load",
    )
    params = [in_vmem(value) for value in (gain_near, w_near.reshape(w_qkv.shape[1:]), rate_near, base_near)]
    w_out_near = in_vmem(w_out_near.reshape(w_out.shape[1:]))

    def begin(places, first, after):
        span = range(2 * places[0], 2 * places[-1] + 2)
        hidden = lax.ppermute(first, ("section", "seq"), [(place, count + place) for place in span])
        own, *rows_of = call(
            functools.partial(later_front, places),
            [maps] + rows_out,
            [],
            [hidden, *params, after],
            [pltpu.VMEM] * 5 + [pl.ANY],
            name=f"later_front_{places[0]}",
        )
        return hidden, own, rows_of, [swap(own, 1, [place]) for place in places]

    here, passed = [init_state], []
    for place in range(groups):
        got, (reads, near) = (got_rest, read_rest) if place else (stepped, read_first)
        if 0 < place < groups - 1:
            ahead, state = hop(0, place, [both], here, passed[0])
        if place + 1 == groups:
            firsts, passed = passed, []
        (first,) = call(
            functools.partial(first_finish, place, len(here)),
            [shape((rows, model), BF16)],
            [],
            [*here, got, reads, near, tokens, ahead, *passed],
            [pltpu.VMEM] * (len(here) + 4) + [pl.ANY] + [pltpu.VMEM] * len(passed),
            name=f"first_finish_{place}",
            aliases={len(here) + 5: 0} if passed else None,
        )
        passed, here = [first], state
    firsts += passed

    hidden, own_later, rows_later, gots = begin(range(groups - 1), firsts[0], own)
    hiddens, states, after = [hidden], [init_state], own_later
    for place in range(groups - 1):
        if place + 2 == groups:
            hidden, own_last, rows_last, got = begin([groups - 1], firsts[1], after)
            hiddens.append(hidden)
            gots += got
            reads = layer_reads(1, range(groups - 1), 0, rows_later, params[1], after)
            after = reads[0]
        after, state = hop(1, place, [own_later, gots[place]], states[-1:], after)
        states += state
    reads += layer_reads(1, [groups - 1], 0, rows_last, params[1], after)
    (result,) = call(
        functools.partial(last_finish, groups),
        [shape((1, rows, model), BF16)],
        [pltpu.VMEM((rows, model), BF16), pltpu.SemaphoreType.DMA((4,))],
        [w_out_near, *states, *gots, *reads, *hiddens, *firsts],
        name="last_finish",
        out_kind=pltpu.HBM,
    )
    return result


def solution(mesh):
    return jax.shard_map(
        shards,
        mesh=mesh,
        in_specs=(
            P(("traj", "seq"), None),
            P("section", None),
            P("section", None, None),
            P("section", None, None),
            P("section", None),
            P("section", None, None, None),
            P("section", None, None),
        ),
        out_specs=P("section", ("traj", "seq"), None),
        check_vma=False,
    )
```

```python
import functools

import jax
import jax.numpy as jnp
from jax import lax
from jax.experimental import pallas as pl
from jax.experimental.pallas import tpu as pltpu
from jax.sharding import PartitionSpec as P

HD = 64
PAIR = 2 * HD
QUAD = 4 * HD
F32 = jnp.float32
BF16 = jnp.bfloat16
EPS = 1e-6
VMEM_LIMIT = 16 * 1024 * 1024


def mm(a, b):
    return jnp.dot(a, b, preferred_element_type=F32)


def mm_nt(a, b):
    return lax.dot_general(a, b, (((1,), (1,)), ((), ())), preferred_element_type=F32)


def mm_tn(a, b):
    return lax.dot_general(a, b, (((0,), (0,)), ((), ())), preferred_element_type=F32)


def head_masks(rows, lanes):
    lane = lax.broadcasted_iota(jnp.int32, (rows, lanes), 1)
    return [lane // HD == index for index in range(lanes // HD)]


def spread(value):
    zero = jnp.zeros_like(value)
    masks = head_masks(*value.shape)
    return jnp.concatenate([jnp.where(mask, value, zero) for mask in masks], axis=0)


def spread_two(left, right):
    return jnp.concatenate([spread(left), spread(right)], axis=1)


def diagonal(product):
    first = lax.broadcasted_iota(jnp.int32, (HD, PAIR), 1) < HD
    return jnp.where(first, product[:HD], product[HD:])


def head_ones():
    row = lax.broadcasted_iota(jnp.int32, (QUAD, QUAD), 0) // HD
    lane = lax.broadcasted_iota(jnp.int32, (QUAD, QUAD), 1) // HD
    return jnp.where(row == lane, 1.0, 0.0).astype(BF16)


def unit_heads(value, ones):
    squares = mm((value * value).astype(BF16), ones)
    return value * lax.rsqrt(squares + EPS)


def norm_rows(hidden, gain):
    wide = hidden.astype(F32)
    mean_sq = jnp.mean(wide * wide, axis=-1, keepdims=True)
    return (wide * lax.rsqrt(mean_sq + EPS) * gain).astype(BF16)


def spread_rates(normed, w_rate, rate_base):
    rates = rate_base * jax.nn.sigmoid(mm_nt(normed, w_rate))
    high = rates.astype(BF16)
    low = (rates - high.astype(F32)).astype(BF16)
    heads = rates.shape[1]
    row = lax.broadcasted_iota(jnp.int32, (heads, heads * HD), 0)
    lane = lax.broadcasted_iota(jnp.int32, (heads, heads * HD), 1) // HD
    pick = jnp.where(row == lane, 1.0, 0.0).astype(BF16)
    return mm(high, pick) + mm(low, pick)


def start_all(copies):
    for copy in copies:
        copy.start()


def wait_all(copies):
    for copy in copies:
        copy.wait()


def on_section(active, body):
    pl.when(lax.axis_index("section") == active)(body)


def at_pair(places, active):
    pair = lax.axis_index("seq") // 2
    first, last = places[0], places[-1]
    return (lax.axis_index("section") == active) & (pair >= first) & (pair <= last)


def front(here, h_ref, gain_ref, w_ref, w_rate_ref, base_ref, maps, normed_out, keys_out, x_out, y_out, near=None):
    width = keys_out.shape[1]
    quads = width // QUAD

    def body():
        if near is None:
            groups, last = [], []
            h_in, gain, w_rate, base, weights, base_lane = h_ref, gain_ref, w_rate_ref, base_ref, w_ref, width
        else:
            wq, h_in, gain, w_rate, base, weights, small_sems, sems = near
            base_lane = 0
            pairs = [(gain_ref, gain), (w_rate_ref, w_rate), (base_ref, base), (h_ref, h_in)]
            small = [pltpu.make_async_copy(source, target, small_sems.at[index]) for index, (source, target) in enumerate(pairs)]
            half = wq.shape[1]
            last = [pltpu.make_async_copy(w_ref.at[0, :, pl.ds(0, half)], wq, small_sems.at[len(pairs)])]
            groups = [
                [
                    pltpu.make_async_copy(
                        w_ref.at[0, :, pl.ds((side + 1) * width + quad * QUAD, QUAD)],
                        weights.at[:, pl.ds(side * width + quad * QUAD, QUAD)],
                        sems.at[quad, side],
                    )
                    for side in range(2)
                ]
                for quad in range(quads)
            ]
            start_all(small)
            start_all(groups[0])
            wait_all(small)
            for group in groups[1:]:
                start_all(group)
        normed = norm_rows(h_in[...], gain[...])
        normed_out[...] = normed
        rates = spread_rates(normed, w_rate[0], base[...])
        ones = head_ones()

        def project(quad):
            if groups:
                wait_all(groups[quad])
                if quad + 1 == quads:
                    start_all(last)
            key_lane = base_lane + quad * QUAD
            return [mm(normed, weights[:, lane : lane + QUAD]) for lane in (key_lane, key_lane + width)]

        def unit(quad, keys, values):
            lanes = slice(quad * QUAD, (quad + 1) * QUAD)
            keys = unit_heads(keys, ones)
            keys_bf = keys.astype(BF16)
            keys_out[:, lanes] = keys_bf
            rate = rates[:, lanes]
            return keys_bf, rate * keys, rate * values

        def crossed(quad, keys_bf, x_all, y_all):
            return mm_nt(keys_bf[HD:], spread(keys_bf[:HD])).astype(BF16)

        def fixed(quad, cross, keys_bf, x_all, y_all):
            lanes = slice(quad * QUAD, (quad + 1) * QUAD)
            rate = rates[HD:, lanes]
            x_first, y_first = x_all[:HD].astype(BF16), y_all[:HD].astype(BF16)
            fix = mm(cross, spread_two(x_first, y_first))
            x_second = (x_all[HD:] - rate * fix[:, :QUAD]).astype(BF16)
            y_second = (y_all[HD:] - rate * fix[:, QUAD:]).astype(BF16)
            x_bf = jnp.concatenate([x_first, x_second], axis=0)
            y_bf = jnp.concatenate([y_first, y_second], axis=0)
            x_out[:, lanes] = x_bf
            y_out[:, lanes] = y_bf
            return x_bf, y_bf

        def mapped(quad, keys_bf, x_bf, y_bf):
            for half in range(2):
                own = slice(half * PAIR, (half + 1) * PAIR)
                start = quad * QUAD + half * PAIR
                both = mm_tn(keys_bf[:, own], jnp.concatenate([x_bf[:, own], y_bf[:, own]], axis=1))
                maps[:, start : start + PAIR] = diagonal(both[:, :PAIR]).astype(BF16)
                maps[:, width + start : width + start + PAIR] = diagonal(both[:, PAIR:]).astype(BF16)

        picked = range(quads)
        units = [unit(quad, *value) for quad, value in zip(picked, [project(quad) for quad in picked])]
        crosses = [crossed(quad, *value) for quad, value in zip(picked, units)]
        fixes = [fixed(quad, cross, *value) for quad, cross, value in zip(picked, crosses, units)]
        for quad, value, fix in zip(picked, units, fixes):
            mapped(quad, value[0], *fix)
        wait_all(last)

    pl.when(here)(body)


def first_front(h_hbm, gain, weights, w_rate, base, maps, normed_out, keys_out, x_out, y_out, *near):
    here = lax.axis_index("section") == 0
    front(here, h_hbm, gain, weights, w_rate, base, maps, normed_out, keys_out, x_out, y_out, near)


def later_front(places, h_ref, gain, weights, w_rate, base, after_ref, *outs):
    front(at_pair(places, 1), h_ref, gain, weights, w_rate, base, *outs)


def load(*refs):
    count = (len(refs) - 2) // 2
    sources, targets, sems = refs[:count], refs[count + 1 : -1], refs[-1]

    def body():
        copies = [pltpu.make_async_copy(source, target, sems.at[index]) for index, (source, target) in enumerate(zip(sources, targets))]
        start_all(copies)
        wait_all(copies)

    on_section(1, body)


def read_out(active, places, fetches, normed_ref, keys_ref, x_ref, y_ref, weights, w_hbm, w_out_hbm, after_ref, reads_out, *rest):
    rows, width = keys_ref.shape
    *w_out, wq, sems = rest
    half = width // 2

    def body():
        late = [pltpu.make_async_copy(w_hbm.at[0, :, pl.ds(half, half)], wq, sems.at[0])] * fetches
        fetch = [pltpu.make_async_copy(w_out_hbm.at[0], target, sems.at[1]) for target in w_out]
        start_all(late + fetch)
        normed = normed_ref[...]
        ones = head_ones()
        row = lax.broadcasted_iota(jnp.int32, (rows, 2 * rows), 0)
        lane = lax.rem(lax.broadcasted_iota(jnp.int32, (rows, 2 * rows), 1), rows)
        causal = row >= lane

        def stages(start, stop, source, base):
            quads = range(start, stop, QUAD)
            queries = [unit_heads(mm(normed, source[:, lane - base : lane - base + QUAD]), ones) for lane in quads]
            parts = [value[:, own : own + PAIR] for value in queries for own in range(0, QUAD, PAIR)]
            places = [slice(lane, lane + PAIR) for lane in range(start, stop, PAIR)]
            scores = [mm_nt(part.astype(BF16), spread(keys_ref[:, place])) for part, place in zip(parts, places)]
            scores = [jnp.where(causal, score, 0.0).astype(BF16) for score in scores]
            both = [mm(score, spread_two(x_ref[:, place], y_ref[:, place])) for score, place in zip(scores, places)]
            for part, place, value in zip(parts, places, both):
                reads_out[:, place] = (part - value[:, :PAIR]).astype(BF16)
                reads_out[:, width + place.start : width + place.stop] = value[:, PAIR:].astype(BF16)

        if fetches:
            stages(0, half, weights, 0)
            wait_all(late)
            stages(half, width, wq, half)
            wait_all(fetch)
        else:
            stages(0, width, weights, 0)

    pl.when(at_pair(places, active))(body)


def compose(active, own_ref, got_ref, after_ref, out_ref):
    width = own_ref.shape[1] // 2

    def body(first_ref, second_ref):
        for start in range(0, width, PAIR):
            s_lanes, b_lanes = slice(start, start + PAIR), slice(width + start, width + start + PAIR)
            s_second, s_first, b_first = second_ref[:, s_lanes], first_ref[:, s_lanes], first_ref[:, b_lanes]
            step = mm(s_second, spread_two(s_first, b_first))
            out_ref[:, s_lanes] = (s_second.astype(F32) + s_first.astype(F32) - step[:, :PAIR]).astype(BF16)
            out_ref[:, b_lanes] = (second_ref[:, b_lanes].astype(F32) + b_first.astype(F32) - step[:, PAIR:]).astype(BF16)

    here = lax.axis_index("section") == active
    side = lax.rem(lax.axis_index("seq"), 2)
    pl.when(here & (side == 0))(lambda: body(own_ref, got_ref))
    pl.when(here & (side == 1))(lambda: body(got_ref, own_ref))


def pair_state(init_ref, pair):
    return jnp.concatenate([init_ref[0, 2 * pair], init_ref[0, 2 * pair + 1]], axis=1)


def apply_map(state, ref, start, width):
    step = mm(ref[:, start : start + PAIR], spread(state.astype(BF16)))
    return state - step + ref[:, width + start : width + start + PAIR].astype(F32)


def moved_states(state_of, refs, width):
    starts = range(0, width, PAIR)
    states = [state_of(start) for start in starts]
    for ref in refs:
        states = [apply_map(state, ref, start, width) for state, start in zip(states, starts)]
    return states


def put_states(out_ref, states):
    for index, state in enumerate(states):
        out_ref[:, index * PAIR : (index + 1) * PAIR] = state.astype(BF16)


def advance(active, place, own_ref, got_ref, state_refs, after_ref, out_ref):
    width = out_ref.shape[1]

    def body(state_ref, refs):
        def state_of(start):
            return state_ref[:, start : start + PAIR].astype(F32) if place else pair_state(state_ref, start // PAIR)

        put_states(out_ref, moved_states(state_of, refs, width))

    here = at_pair([place], active)
    side = lax.rem(lax.axis_index("seq"), 2)
    orders = [(own_ref,)] * 2 if got_ref is None else [(own_ref, got_ref), (got_ref, own_ref)]
    if got_ref is None and len(state_refs) == 1:
        pl.when(here)(lambda: body(state_refs[0], orders[0]))
    else:
        pl.when(here & (side == 0))(lambda: body(state_refs[0], orders[0]))
        pl.when(here & (side == 1))(lambda: body(state_refs[-1], orders[1]))


def first_step(own_ref, init_ref, out_ref):
    @pl.when((lax.axis_index("section") == 0) & (lax.axis_index("seq") == 0))
    def _():
        put_states(out_ref, moved_states(lambda start: pair_state(init_ref, start // PAIR), (own_ref,), out_ref.shape[1]))


def second_step(own_ref, state_ref, after_ref, out_ref):
    @pl.when((lax.axis_index("section") == 0) & (lax.axis_index("seq") == 1))
    def _():
        put_states(
            out_ref, moved_states(lambda start: state_ref[:, start : start + PAIR].astype(F32), (own_ref,), out_ref.shape[1])
        )


def finish(here, begins, state_refs, got_ref, reads_ref, w_out_ref, h_ref, store, followed=None):
    width = w_out_ref.shape[0]
    model = h_ref.shape[1]
    chunk = model // 4

    def body():
        follows = lax.rem(lax.axis_index("seq"), 2) == 1
        starts = range(0, width, PAIR)
        if begins:
            states = [pair_state(state_refs[0], start // PAIR) for start in starts]
        else:
            states = [state_refs[0][:, start : start + PAIR].astype(F32) for start in starts]
            for ref in state_refs[1:]:
                others = [ref[:, start : start + PAIR].astype(F32) for start in starts]
                states = [jnp.where(follows, other, state) for other, state in zip(others, states)]
        if followed is None:
            moved = [apply_map(state, got_ref, start, width) for state, start in zip(states, starts)]
        else:
            moved = [followed[:, start : start + PAIR].astype(F32) for start in starts]
        states = [jnp.where(follows, after, state).astype(BF16) for after, state in zip(moved, states)]
        quads = range(0, width, QUAD)
        spreads = [spread(jnp.concatenate(states[start // PAIR : (start + QUAD) // PAIR], axis=1)) for start in quads]
        reads = [mm(reads_ref[:, start : start + QUAD], value) for start, value in zip(quads, spreads)]
        inner_bf = jnp.concatenate(
            [
                (read + reads_ref[:, width + start : width + start + QUAD].astype(F32)).astype(BF16)
                for start, read in zip(quads, reads)
            ],
            axis=1,
        )
        for start in range(0, model, chunk):
            lanes = slice(start, start + chunk)
            store(start, (h_ref[:, lanes].astype(F32) + mm(inner_bf, w_out_ref[:, lanes])).astype(BF16))

    pl.when(here)(body)


def first_finish(place, count, *refs):
    state_refs, (got_ref, reads_ref, w_out_ref, h_ref, after_ref, *rest) = refs[:count][::-1], refs[count:]
    out_ref = rest[-1]

    def store(start, value):
        out_ref[:, start : start + value.shape[1]] = value

    followed = None if place else got_ref
    finish(at_pair([place], 0), place == 0, state_refs, got_ref, reads_ref, w_out_ref, h_ref, store, followed)


def last_finish(count, w_out_ref, *refs):
    states, gots, refs = refs[:count], refs[count : 2 * count], refs[2 * count :]
    reads, hiddens, firsts = [[refs[index]] * (count - 1) + [refs[index + 1]] for index in (0, 2, 4)]
    out_hbm, near, sems = refs[6:]
    chunk = near.shape[1] // 4

    def write(start):
        lanes = pl.ds(start, chunk)
        return pltpu.make_async_copy(near.at[:, lanes], out_hbm.at[0, :, lanes], sems.at[start // chunk])

    def store(start, value):
        near[:, start : start + chunk] = value
        write(start).start()

    for place in range(count):
        finish(at_pair([place], 1), place == 0, [states[place]], gots[place], reads[place], w_out_ref, hiddens[place], store)

        @pl.when(at_pair([place], 0))
        def _():
            for start in range(0, near.shape[1], chunk):
                store(start, firsts[place][:, start : start + chunk])

    for start in range(0, near.shape[1], chunk):
        write(start).wait()


def call(body, outs, scratch, args, kinds=None, name=None, out_kind=pltpu.VMEM, aliases=None):
    specs = [pl.BlockSpec(memory_space=kind) for kind in (kinds or [pltpu.VMEM] * len(args))]
    return pl.pallas_call(
        body,
        out_shape=outs,
        in_specs=specs,
        out_specs=[pl.BlockSpec(memory_space=out_kind)] * len(outs),
        scratch_shapes=scratch,
        input_output_aliases=aliases or {},
        compiler_params=pltpu.CompilerParams(vmem_limit_bytes=VMEM_LIMIT),
        name=name,
    )(*args)


def shards(tokens, norm_gain, w_qkv, w_rate, rate_base, init_state, w_out):
    count = lax.axis_size("seq")
    heads = rate_base.shape[1]
    rows, model = tokens.shape
    width = heads * HD
    depth = w_qkv.shape[1]
    quads = width // QUAD
    shape = jax.ShapeDtypeStruct
    in_vmem = functools.partial(pltpu.with_memory_space_constraint, memory_space=pltpu.VMEM)
    in_hbm = functools.partial(pltpu.with_memory_space_constraint, memory_space=pltpu.HBM)
    maps = shape((HD, 2 * width), BF16)
    rows_out = [shape((rows, model), BF16)] + [shape((rows, width), BF16)] * 3
    w_rate = jnp.swapaxes(w_rate, 1, 2)
    norm_gain, w_qkv, w_rate, rate_base, w_out = [in_hbm(value) for value in (norm_gain, w_qkv, w_rate, rate_base, w_out)]

    def permute(value, active, pairs):
        base = active * count
        return lax.ppermute(value, ("section", "seq"), [(base + source, base + target) for source, target in pairs])

    def swap(own, active, groups):
        return permute(own, active, [(2 * group + side, 2 * group + 1 - side) for group in groups for side in range(2)])

    def layer_reads(active, places, fetches, rows_of, weights, after):
        reads, *w_out_near = call(
            functools.partial(read_out, active, places, fetches),
            [shape((rows, 2 * width), BF16)] + [pltpu.VMEM(w_out.shape[1:], BF16)] * fetches,
            [pltpu.VMEM((depth, width // 2), BF16) if fetches else pltpu.VMEM((16, 128), BF16), pltpu.SemaphoreType.DMA((2,))],
            [*rows_of, weights, w_qkv, w_out, after],
            [pltpu.VMEM] * 5 + [pltpu.HBM, pltpu.HBM, pl.ANY],
            name=f"reads{active}_{places[0]}",
        )
        return [reads] + [in_vmem(value) for value in w_out_near]

    def hop(active, place, maps_here, states, after):
        count_here = len(maps_here)

        def body(*refs):
            advance(active, place, refs[0], None if count_here == 1 else refs[1], refs[count_here:-2][::-1], *refs[-2:])

        kinds = [pltpu.VMEM] * (count_here + len(states)) + [pl.ANY]
        (ahead,) = call(body, [state_out], [], maps_here + states[::-1] + [after], kinds, name=f"advance{active}_{place}")
        return ahead, [permute(ahead, active, [(2 * place + side, 2 * place + 2 + side) for side in range(2)])]

    state_out = shape((HD, width), BF16)
    groups = count // 2

    own, *rows_of, wq_near = call(
        first_front,
        [maps] + rows_out + [pltpu.VMEM((depth, width // 2), BF16)],
        [pltpu.VMEM(value.shape, value.dtype) for value in (tokens, norm_gain, w_rate, rate_base)]
        + [pltpu.VMEM((depth, 2 * width), BF16), pltpu.SemaphoreType.DMA((5,)), pltpu.SemaphoreType.DMA((quads, 2))],
        [in_hbm(tokens), norm_gain, w_qkv, w_rate, rate_base],
        [pltpu.HBM] * 5,
        name="first_front",
    )
    wq_near = in_vmem(wq_near)
    (stepped,) = call(first_step, [state_out], [], [own, init_state], name="first_step")
    stepped = permute(stepped, 0, [(0, 1)])
    got_rest = swap(own, 0, range(1, groups))
    read_first = layer_reads(0, [0], 1, rows_of, wq_near, init_state)
    (ahead,) = call(
        second_step, [state_out], [], [own, stepped, read_first[0]], [pltpu.VMEM] * 2 + [pl.ANY], name="second_step"
    )
    state = [permute(ahead, 0, [(1, 2 + side)]) for side in range(2)]
    read_rest = layer_reads(0, range(1, groups), 1, rows_of, wq_near, ahead)
    (both,) = call(
        functools.partial(compose, 0), [maps], [], [own, got_rest, read_rest[0]], [pltpu.VMEM] * 2 + [pl.ANY], name="compose"
    )

    params = [norm_gain, w_qkv, w_rate, rate_base, w_out]
    gain_near, w_near, rate_near, base_near, w_out_near = call(
        load,
        [pltpu.VMEM(value.shape, value.dtype) for value in params],
        [pltpu.SemaphoreType.DMA((5,))],
        params + [both],
        [pltpu.HBM] * 5 + [pl.ANY],
        name="load",
    )
    params = [in_vmem(value) for value in (gain_near, w_near.reshape(w_qkv.shape[1:]), rate_near, base_near)]
    w_out_near = in_vmem(w_out_near.reshape(w_out.shape[1:]))

    def begin(places, first, after):
        span = range(2 * places[0], 2 * places[-1] + 2)
        hidden = lax.ppermute(first, ("section", "seq"), [(place, count + place) for place in span])
        own, *rows_of = call(
            functools.partial(later_front, places),
            [maps] + rows_out,
            [],
            [hidden, *params, after],
            [pltpu.VMEM] * 5 + [pl.ANY],
            name=f"later_front_{places[0]}",
        )
        return hidden, own, rows_of, [swap(own, 1, [place]) for place in places]

    here, passed = [init_state], []
    for place in range(groups):
        got, (reads, near) = (got_rest, read_rest) if place else (stepped, read_first)
        if 0 < place < groups - 1:
            ahead, state = hop(0, place, [both], here, passed[0])
        if place + 1 == groups:
            firsts, passed = passed, []
        (first,) = call(
            functools.partial(first_finish, place, len(here)),
            [shape((rows, model), BF16)],
            [],
            [*here[::-1], got, reads, near, tokens, ahead, *passed],
            [pltpu.VMEM] * (len(here) + 4) + [pl.ANY] + [pltpu.VMEM] * len(passed),
            name=f"first_finish_{place}",
            aliases={len(here) + 5: 0} if passed else None,
        )
        passed, here = [first], state
    firsts += passed

    hidden, own_later, rows_later, gots = begin(range(groups - 1), firsts[0], own)
    hiddens, states, after = [hidden], [init_state], own_later
    for place in range(groups - 1):
        if place + 2 == groups:
            hidden, own_last, rows_last, got = begin([groups - 1], firsts[1], after)
            hiddens.append(hidden)
            gots += got
            reads = layer_reads(1, range(groups - 1), 0, rows_later, params[1], after)
            after = reads[0]
        after, state = hop(1, place, [own_later, gots[place]], states[-1:], after)
        states += state
    reads += layer_reads(1, [groups - 1], 0, rows_last, params[1], after)
    (result,) = call(
        functools.partial(last_finish, groups),
        [shape((1, rows, model), BF16)],
        [pltpu.VMEM((rows, model), BF16), pltpu.SemaphoreType.DMA((4,))],
        [w_out_near, *states, *gots, *reads, *hiddens, *firsts],
        name="last_finish",
        out_kind=pltpu.HBM,
    )
    return result


def solution(mesh):
    return jax.shard_map(
        shards,
        mesh=mesh,
        in_specs=(
            P(("traj", "seq"), None),
            P("section", None),
            P("section", None, None),
            P("section", None, None),
            P("section", None),
            P("section", None, None, None),
            P("section", None, None),
        ),
        out_specs=P("section", ("traj", "seq"), None),
        check_vma=False,
    )
```

```python
import functools

import jax
import jax.numpy as jnp
from jax import lax
from jax.experimental import pallas as pl
from jax.experimental.pallas import tpu as pltpu
from jax.sharding import PartitionSpec as P

HD = 64
PAIR = 2 * HD
QUAD = 4 * HD
F32 = jnp.float32
BF16 = jnp.bfloat16
EPS = 1e-6
VMEM_LIMIT = 16 * 1024 * 1024


def mm(a, b):
    return jnp.dot(a, b, preferred_element_type=F32)


def mm_nt(a, b):
    return lax.dot_general(a, b, (((1,), (1,)), ((), ())), preferred_element_type=F32)


def mm_tn(a, b):
    return lax.dot_general(a, b, (((0,), (0,)), ((), ())), preferred_element_type=F32)


def head_masks(rows, lanes):
    lane = lax.broadcasted_iota(jnp.int32, (rows, lanes), 1)
    return [lane // HD == index for index in range(lanes // HD)]


def spread(value):
    zero = jnp.zeros_like(value)
    masks = head_masks(*value.shape)
    return jnp.concatenate([jnp.where(mask, value, zero) for mask in masks], axis=0)


def spread_two(left, right):
    return jnp.concatenate([spread(left), spread(right)], axis=1)


def diagonal(product):
    first = lax.broadcasted_iota(jnp.int32, (HD, PAIR), 1) < HD
    return jnp.where(first, product[:HD], product[HD:])


def head_ones():
    row = lax.broadcasted_iota(jnp.int32, (QUAD, QUAD), 0) // HD
    lane = lax.broadcasted_iota(jnp.int32, (QUAD, QUAD), 1) // HD
    return jnp.where(row == lane, 1.0, 0.0).astype(BF16)


def unit_heads(value, ones):
    squares = mm((value * value).astype(BF16), ones)
    return value * lax.rsqrt(squares + EPS)


def norm_rows(hidden, gain):
    wide = hidden.astype(F32)
    mean_sq = jnp.mean(wide * wide, axis=-1, keepdims=True)
    return (wide * lax.rsqrt(mean_sq + EPS) * gain).astype(BF16)


def spread_rates(normed, w_rate, rate_base):
    rates = rate_base * jax.nn.sigmoid(mm_nt(normed, w_rate))
    high = rates.astype(BF16)
    low = (rates - high.astype(F32)).astype(BF16)
    heads = rates.shape[1]
    row = lax.broadcasted_iota(jnp.int32, (heads, heads * HD), 0)
    lane = lax.broadcasted_iota(jnp.int32, (heads, heads * HD), 1) // HD
    pick = jnp.where(row == lane, 1.0, 0.0).astype(BF16)
    return mm(high, pick) + mm(low, pick)


def start_all(copies):
    for copy in copies:
        copy.start()


def wait_all(copies):
    for copy in copies:
        copy.wait()


def on_section(active, body):
    pl.when(lax.axis_index("section") == active)(body)


def at_pair(places, active):
    pair = lax.axis_index("seq") // 2
    first, last = places[0], places[-1]
    return (lax.axis_index("section") == active) & (pair >= first) & (pair <= last)


def front(here, h_ref, gain_ref, w_ref, w_rate_ref, base_ref, maps, normed_out, keys_out, x_out, y_out, near=None):
    width = keys_out.shape[1]
    quads = width // QUAD

    def body():
        if near is None:
            copies = None
            h_in, gain, w_rate, base, weights, base_lane = h_ref, gain_ref, w_rate_ref, base_ref, w_ref, width
        else:
            h_in, gain, w_rate, base, weights, small_sems, sems = near
            base_lane = 0
            pairs = [(gain_ref, gain), (w_rate_ref, w_rate), (base_ref, base), (h_ref, h_in)]
            small = [pltpu.make_async_copy(source, target, small_sems.at[index]) for index, (source, target) in enumerate(pairs)]
            copies = [
                [
                    pltpu.make_async_copy(
                        w_ref.at[0, :, pl.ds((side + 1) * width + quad * QUAD, QUAD)],
                        weights.at[:, pl.ds(side * width + quad * QUAD, QUAD)],
                        sems.at[quad, side],
                    )
                    for quad in range(quads)
                ]
                for side in range(2)
            ]
            start_all(small)
            start_all(copies[0][:1])
            wait_all(small)
            start_all(copies[0][1:])
        normed = norm_rows(h_in[...], gain[...])
        normed_out[...] = normed
        rates = spread_rates(normed, w_rate[0], base[...])
        ones = head_ones()

        def project(side, quad):
            if copies is not None:
                wait_all([copies[side][quad]])
                if side == 0:
                    start_all([copies[1][quad]])
            lane = base_lane + side * width + quad * QUAD
            return mm(normed, weights[:, lane : lane + QUAD])

        def unit(quad, keys):
            lanes = slice(quad * QUAD, (quad + 1) * QUAD)
            keys = unit_heads(keys, ones)
            keys_bf = keys.astype(BF16)
            keys_out[:, lanes] = keys_bf
            return keys_bf, rates[:, lanes] * keys

        def crossed(quad, keys_bf, x_all):
            return mm_nt(keys_bf[HD:], spread(keys_bf[:HD])).astype(BF16)

        def fixed(quad, cross, values, keys_bf, x_all):
            lanes = slice(quad * QUAD, (quad + 1) * QUAD)
            y_all = rates[:, lanes] * values
            rate = rates[HD:, lanes]
            x_first, y_first = x_all[:HD].astype(BF16), y_all[:HD].astype(BF16)
            fix = mm(cross, spread_two(x_first, y_first))
            x_second = (x_all[HD:] - rate * fix[:, :QUAD]).astype(BF16)
            y_second = (y_all[HD:] - rate * fix[:, QUAD:]).astype(BF16)
            x_bf = jnp.concatenate([x_first, x_second], axis=0)
            y_bf = jnp.concatenate([y_first, y_second], axis=0)
            x_out[:, lanes] = x_bf
            y_out[:, lanes] = y_bf
            return x_bf, y_bf

        def mapped(quad, keys_bf, x_bf, y_bf):
            for half in range(2):
                own = slice(half * PAIR, (half + 1) * PAIR)
                start = quad * QUAD + half * PAIR
                both = mm_tn(keys_bf[:, own], jnp.concatenate([x_bf[:, own], y_bf[:, own]], axis=1))
                maps[:, start : start + PAIR] = diagonal(both[:, :PAIR]).astype(BF16)
                maps[:, width + start : width + start + PAIR] = diagonal(both[:, PAIR:]).astype(BF16)

        picked = range(quads)
        units = [unit(quad, keys) for quad, keys in zip(picked, [project(0, quad) for quad in picked])]
        crosses = [crossed(quad, *value) for quad, value in zip(picked, units)]
        values = [project(1, quad) for quad in picked]
        fixes = [fixed(quad, cross, value, *pair) for quad, cross, value, pair in zip(picked, crosses, values, units)]
        for quad, value, fix in zip(picked, units, fixes):
            mapped(quad, value[0], *fix)

    pl.when(here)(body)


def first_front(h_hbm, gain, weights, w_rate, base, maps, normed_out, keys_out, x_out, y_out, *near):
    here = lax.axis_index("section") == 0
    front(here, h_hbm, gain, weights, w_rate, base, maps, normed_out, keys_out, x_out, y_out, near)


def later_front(places, h_ref, gain, weights, w_rate, base, after_ref, *outs):
    front(at_pair(places, 1), h_ref, gain, weights, w_rate, base, *outs)


def load(*refs):
    count = (len(refs) - 2) // 2
    sources, targets, sems = refs[:count], refs[count + 1 : -1], refs[-1]

    def body():
        copies = [pltpu.make_async_copy(source, target, sems.at[index]) for index, (source, target) in enumerate(zip(sources, targets))]
        start_all(copies)
        wait_all(copies)

    on_section(1, body)


def read_out(active, places, fetches, normed_ref, keys_ref, x_ref, y_ref, weights, w_out_hbm, after_ref, reads_out, *rest):
    rows, width = keys_ref.shape
    *w_out, wq, sems = rest
    half = width // 2

    def body():
        fetch = [pltpu.make_async_copy(w_out_hbm.at[0], target, sems.at[2]) for target in w_out]
        halves = [pl.ds(index * half, half) for index in range(2)] if fetches else []
        late = [pltpu.make_async_copy(weights.at[0, :, lanes], wq.at[:, lanes], sems.at[index]) for index, lanes in enumerate(halves)]
        start_all(late)
        normed = normed_ref[...]
        ones = head_ones()
        row = lax.broadcasted_iota(jnp.int32, (rows, 2 * rows), 0)
        lane = lax.rem(lax.broadcasted_iota(jnp.int32, (rows, 2 * rows), 1), rows)
        causal = row >= lane

        def stages(start, stop, source):
            quads = range(start, stop, QUAD)
            queries = [unit_heads(mm(normed, source[:, lane : lane + QUAD]), ones) for lane in quads]
            parts = [value[:, own : own + PAIR] for value in queries for own in range(0, QUAD, PAIR)]
            places = [slice(lane, lane + PAIR) for lane in range(start, stop, PAIR)]
            scores = [mm_nt(part.astype(BF16), spread(keys_ref[:, place])) for part, place in zip(parts, places)]
            scores = [jnp.where(causal, score, 0.0).astype(BF16) for score in scores]
            both = [mm(score, spread_two(x_ref[:, place], y_ref[:, place])) for score, place in zip(scores, places)]
            for part, place, value in zip(parts, places, both):
                reads_out[:, place] = (part - value[:, :PAIR]).astype(BF16)
                reads_out[:, width + place.start : width + place.stop] = value[:, PAIR:].astype(BF16)

        if fetches:
            wait_all(late[:1])
            start_all(fetch)
            stages(0, half, wq)
            wait_all(late[1:])
            stages(half, width, wq)
            wait_all(fetch)
        else:
            stages(0, width, weights)

    pl.when(at_pair(places, active))(body)


def compose(active, own_ref, got_ref, after_ref, out_ref):
    width = own_ref.shape[1] // 2

    def body(first_ref, second_ref):
        for start in range(0, width, PAIR):
            s_lanes, b_lanes = slice(start, start + PAIR), slice(width + start, width + start + PAIR)
            s_second, s_first, b_first = second_ref[:, s_lanes], first_ref[:, s_lanes], first_ref[:, b_lanes]
            step = mm(s_second, spread_two(s_first, b_first))
            out_ref[:, s_lanes] = (s_second.astype(F32) + s_first.astype(F32) - step[:, :PAIR]).astype(BF16)
            out_ref[:, b_lanes] = (second_ref[:, b_lanes].astype(F32) + b_first.astype(F32) - step[:, PAIR:]).astype(BF16)

    here = lax.axis_index("section") == active
    side = lax.rem(lax.axis_index("seq"), 2)
    pl.when(here & (side == 0))(lambda: body(own_ref, got_ref))
    pl.when(here & (side == 1))(lambda: body(got_ref, own_ref))


def pair_state(init_ref, pair):
    return jnp.concatenate([init_ref[0, 2 * pair], init_ref[0, 2 * pair + 1]], axis=1)


def apply_map(state, ref, start, width):
    step = mm(ref[:, start : start + PAIR], spread(state.astype(BF16)))
    return state - step + ref[:, width + start : width + start + PAIR].astype(F32)


def moved_states(state_of, refs, width):
    starts = range(0, width, PAIR)
    states = [state_of(start) for start in starts]
    for ref in refs:
        states = [apply_map(state, ref, start, width) for state, start in zip(states, starts)]
    return states


def put_states(out_ref, states):
    for index, state in enumerate(states):
        out_ref[:, index * PAIR : (index + 1) * PAIR] = state.astype(BF16)


def advance(active, place, own_ref, got_ref, state_refs, after_ref, out_ref):
    width = out_ref.shape[1]

    def body(state_ref, refs):
        def state_of(start):
            return state_ref[:, start : start + PAIR].astype(F32) if place else pair_state(state_ref, start // PAIR)

        put_states(out_ref, moved_states(state_of, refs, width))

    here = at_pair([place], active)
    side = lax.rem(lax.axis_index("seq"), 2)
    orders = [(own_ref,)] * 2 if got_ref is None else [(own_ref, got_ref), (got_ref, own_ref)]
    if got_ref is None and len(state_refs) == 1:
        pl.when(here)(lambda: body(state_refs[0], orders[0]))
    else:
        pl.when(here & (side == 0))(lambda: body(state_refs[0], orders[0]))
        pl.when(here & (side == 1))(lambda: body(state_refs[-1], orders[1]))


def first_step(own_ref, init_ref, out_ref):
    @pl.when((lax.axis_index("section") == 0) & (lax.axis_index("seq") == 0))
    def _():
        put_states(out_ref, moved_states(lambda start: pair_state(init_ref, start // PAIR), (own_ref,), out_ref.shape[1]))


def second_step(own_ref, state_ref, after_ref, out_ref):
    @pl.when((lax.axis_index("section") == 0) & (lax.axis_index("seq") == 1))
    def _():
        put_states(
            out_ref, moved_states(lambda start: state_ref[:, start : start + PAIR].astype(F32), (own_ref,), out_ref.shape[1])
        )


def finish(here, begins, state_refs, got_ref, reads_ref, w_out_ref, h_ref, store, followed=None):
    width = w_out_ref.shape[0]
    model = h_ref.shape[1]
    chunk = model // 4

    def body():
        follows = lax.rem(lax.axis_index("seq"), 2) == 1
        starts = range(0, width, PAIR)
        if begins:
            states = [pair_state(state_refs[0], start // PAIR) for start in starts]
        else:
            states = [state_refs[0][:, start : start + PAIR].astype(F32) for start in starts]
            for ref in state_refs[1:]:
                others = [ref[:, start : start + PAIR].astype(F32) for start in starts]
                states = [jnp.where(follows, other, state) for other, state in zip(others, states)]
        if followed is None:
            moved = [apply_map(state, got_ref, start, width) for state, start in zip(states, starts)]
        else:
            moved = [followed[:, start : start + PAIR].astype(F32) for start in starts]
        states = [jnp.where(follows, after, state).astype(BF16) for after, state in zip(moved, states)]
        quads = range(0, width, QUAD)
        spreads = [spread(jnp.concatenate(states[start // PAIR : (start + QUAD) // PAIR], axis=1)) for start in quads]
        reads = [mm(reads_ref[:, start : start + QUAD], value) for start, value in zip(quads, spreads)]
        inner_bf = jnp.concatenate(
            [
                (read + reads_ref[:, width + start : width + start + QUAD].astype(F32)).astype(BF16)
                for start, read in zip(quads, reads)
            ],
            axis=1,
        )
        for start in range(0, model, chunk):
            lanes = slice(start, start + chunk)
            store(start, (h_ref[:, lanes].astype(F32) + mm(inner_bf, w_out_ref[:, lanes])).astype(BF16))

    pl.when(here)(body)


def first_finish(place, count, *refs):
    state_refs, (got_ref, reads_ref, w_out_ref, h_ref, after_ref, *rest) = refs[:count][::-1], refs[count:]
    out_ref = rest[-1]

    def store(start, value):
        out_ref[:, start : start + value.shape[1]] = value

    followed = None if place else got_ref
    finish(at_pair([place], 0), place == 0, state_refs, got_ref, reads_ref, w_out_ref, h_ref, store, followed)


def last_finish(count, w_out_ref, *refs):
    states, gots, refs = refs[:count], refs[count : 2 * count], refs[2 * count :]
    reads, hiddens, firsts = [[refs[index]] * (count - 1) + [refs[index + 1]] for index in (0, 2, 4)]
    out_hbm, near, sems = refs[6:]
    chunk = near.shape[1] // 4

    def write(start):
        lanes = pl.ds(start, chunk)
        return pltpu.make_async_copy(near.at[:, lanes], out_hbm.at[0, :, lanes], sems.at[start // chunk])

    def store(start, value):
        near[:, start : start + chunk] = value
        write(start).start()

    for place in range(count):
        finish(at_pair([place], 1), place == 0, [states[place]], gots[place], reads[place], w_out_ref, hiddens[place], store)

        @pl.when(at_pair([place], 0))
        def _():
            for start in range(0, near.shape[1], chunk):
                store(start, firsts[place][:, start : start + chunk])

    for start in range(0, near.shape[1], chunk):
        write(start).wait()


def call(body, outs, scratch, args, kinds=None, name=None, out_kind=pltpu.VMEM, aliases=None):
    specs = [pl.BlockSpec(memory_space=kind) for kind in (kinds or [pltpu.VMEM] * len(args))]
    return pl.pallas_call(
        body,
        out_shape=outs,
        in_specs=specs,
        out_specs=[pl.BlockSpec(memory_space=out_kind)] * len(outs),
        scratch_shapes=scratch,
        input_output_aliases=aliases or {},
        compiler_params=pltpu.CompilerParams(vmem_limit_bytes=VMEM_LIMIT),
        name=name,
    )(*args)


def shards(tokens, norm_gain, w_qkv, w_rate, rate_base, init_state, w_out):
    count = lax.axis_size("seq")
    heads = rate_base.shape[1]
    rows, model = tokens.shape
    width = heads * HD
    depth = w_qkv.shape[1]
    quads = width // QUAD
    shape = jax.ShapeDtypeStruct
    in_vmem = functools.partial(pltpu.with_memory_space_constraint, memory_space=pltpu.VMEM)
    in_hbm = functools.partial(pltpu.with_memory_space_constraint, memory_space=pltpu.HBM)
    maps = shape((HD, 2 * width), BF16)
    rows_out = [shape((rows, model), BF16)] + [shape((rows, width), BF16)] * 3
    w_rate = jnp.swapaxes(w_rate, 1, 2)
    norm_gain, w_qkv, w_rate, rate_base, w_out = [in_hbm(value) for value in (norm_gain, w_qkv, w_rate, rate_base, w_out)]

    def permute(value, active, pairs):
        base = active * count
        return lax.ppermute(value, ("section", "seq"), [(base + source, base + target) for source, target in pairs])

    def swap(own, active, groups):
        return permute(own, active, [(2 * group + side, 2 * group + 1 - side) for group in groups for side in range(2)])

    def layer_reads(active, places, fetches, rows_of, weights, after):
        reads, *w_out_near = call(
            functools.partial(read_out, active, places, fetches),
            [shape((rows, 2 * width), BF16)] + [pltpu.VMEM(w_out.shape[1:], BF16)] * fetches,
            [pltpu.VMEM((depth, width) if fetches else (16, 128), BF16), pltpu.SemaphoreType.DMA((3,))],
            [*rows_of, weights, w_out, after],
            [pltpu.VMEM] * 4 + [pltpu.HBM if fetches else pltpu.VMEM, pltpu.HBM, pl.ANY],
            name=f"reads{active}_{places[0]}",
        )
        return [reads] + [in_vmem(value) for value in w_out_near]

    def hop(active, place, maps_here, states, after):
        count_here = len(maps_here)

        def body(*refs):
            advance(active, place, refs[0], None if count_here == 1 else refs[1], refs[count_here:-2][::-1], *refs[-2:])

        kinds = [pltpu.VMEM] * (count_here + len(states)) + [pl.ANY]
        (ahead,) = call(body, [state_out], [], maps_here + states[::-1] + [after], kinds, name=f"advance{active}_{place}")
        return ahead, [permute(ahead, active, [(2 * place + side, 2 * place + 2 + side) for side in range(2)])]

    state_out = shape((HD, width), BF16)
    groups = count // 2

    own, *rows_of = call(
        first_front,
        [maps] + rows_out,
        [pltpu.VMEM(value.shape, value.dtype) for value in (tokens, norm_gain, w_rate, rate_base)]
        + [pltpu.VMEM((depth, 2 * width), BF16), pltpu.SemaphoreType.DMA((4,)), pltpu.SemaphoreType.DMA((quads, 2))],
        [in_hbm(tokens), norm_gain, w_qkv, w_rate, rate_base],
        [pltpu.HBM] * 5,
        name="first_front",
    )
    (stepped,) = call(first_step, [state_out], [], [own, init_state], name="first_step")
    stepped = permute(stepped, 0, [(0, 1)])
    got_rest = swap(own, 0, range(1, groups))
    read_first = layer_reads(0, [0], 1, rows_of, w_qkv, init_state)
    (ahead,) = call(
        second_step, [state_out], [], [own, stepped, read_first[0]], [pltpu.VMEM] * 2 + [pl.ANY], name="second_step"
    )
    state = [permute(ahead, 0, [(1, 2 + side)]) for side in range(2)]
    read_rest = layer_reads(0, range(1, groups), 1, rows_of, w_qkv, ahead)
    (both,) = call(
        functools.partial(compose, 0), [maps], [], [own, got_rest, read_rest[0]], [pltpu.VMEM] * 2 + [pl.ANY], name="compose"
    )

    params = [norm_gain, w_qkv, w_rate, rate_base, w_out]
    gain_near, w_near, rate_near, base_near, w_out_near = call(
        load,
        [pltpu.VMEM(value.shape, value.dtype) for value in params],
        [pltpu.SemaphoreType.DMA((5,))],
        params + [both],
        [pltpu.HBM] * 5 + [pl.ANY],
        name="load",
    )
    params = [in_vmem(value) for value in (gain_near, w_near.reshape(w_qkv.shape[1:]), rate_near, base_near)]
    w_out_near = in_vmem(w_out_near.reshape(w_out.shape[1:]))

    def begin(places, first, after):
        span = range(2 * places[0], 2 * places[-1] + 2)
        hidden = lax.ppermute(first, ("section", "seq"), [(place, count + place) for place in span])
        own, *rows_of = call(
            functools.partial(later_front, places),
            [maps] + rows_out,
            [],
            [hidden, *params, after],
            [pltpu.VMEM] * 5 + [pl.ANY],
            name=f"later_front_{places[0]}",
        )
        return hidden, own, rows_of, [swap(own, 1, [place]) for place in places]

    here, passed = [init_state], []
    for place in range(groups):
        got, (reads, near) = (got_rest, read_rest) if place else (stepped, read_first)
        if 0 < place < groups - 1:
            ahead, state = hop(0, place, [both], here, passed[0])
        if place + 1 == groups:
            firsts, passed = passed, []
        (first,) = call(
            functools.partial(first_finish, place, len(here)),
            [shape((rows, model), BF16)],
            [],
            [*here[::-1], got, reads, near, tokens, ahead, *passed],
            [pltpu.VMEM] * (len(here) + 4) + [pl.ANY] + [pltpu.VMEM] * len(passed),
            name=f"first_finish_{place}",
            aliases={len(here) + 5: 0} if passed else None,
        )
        passed, here = [first], state
    firsts += passed

    hidden, own_later, rows_later, gots = begin(range(groups - 1), firsts[0], own)
    hiddens, states, after = [hidden], [init_state], own_later
    for place in range(groups - 1):
        if place + 2 == groups:
            hidden, own_last, rows_last, got = begin([groups - 1], firsts[1], after)
            hiddens.append(hidden)
            gots += got
            reads = layer_reads(1, range(groups - 1), 0, rows_later, params[1], after)
            after = reads[0]
        after, state = hop(1, place, [own_later, gots[place]], states[-1:], after)
        states += state
    reads += layer_reads(1, [groups - 1], 0, rows_last, params[1], after)
    (result,) = call(
        functools.partial(last_finish, groups),
        [shape((1, rows, model), BF16)],
        [pltpu.VMEM((rows, model), BF16), pltpu.SemaphoreType.DMA((4,))],
        [w_out_near, *states, *gots, *reads, *hiddens, *firsts],
        name="last_finish",
        out_kind=pltpu.HBM,
    )
    return result


def solution(mesh):
    return jax.shard_map(
        shards,
        mesh=mesh,
        in_specs=(
            P(("traj", "seq"), None),
            P("section", None),
            P("section", None, None),
            P("section", None, None),
            P("section", None),
            P("section", None, None, None),
            P("section", None, None),
        ),
        out_specs=P("section", ("traj", "seq"), None),
        check_vma=False,
    )
```

```python
import functools

import jax
import jax.numpy as jnp
from jax import lax
from jax.experimental import pallas as pl
from jax.experimental.pallas import tpu as pltpu
from jax.sharding import PartitionSpec as P

HD = 64
PAIR = 2 * HD
QUAD = 4 * HD
F32 = jnp.float32
BF16 = jnp.bfloat16
EPS = 1e-6
VMEM_LIMIT = 16 * 1024 * 1024


def mm(a, b):
    return jnp.dot(a, b, preferred_element_type=F32)


def mm_nt(a, b):
    return lax.dot_general(a, b, (((1,), (1,)), ((), ())), preferred_element_type=F32)


def mm_tn(a, b):
    return lax.dot_general(a, b, (((0,), (0,)), ((), ())), preferred_element_type=F32)


def head_masks(rows, lanes):
    lane = lax.broadcasted_iota(jnp.int32, (rows, lanes), 1)
    return [lane // HD == index for index in range(lanes // HD)]


def spread(value):
    zero = jnp.zeros_like(value)
    masks = head_masks(*value.shape)
    return jnp.concatenate([jnp.where(mask, value, zero) for mask in masks], axis=0)


def spread_two(left, right):
    return jnp.concatenate([spread(left), spread(right)], axis=1)


def diagonal(product):
    first = lax.broadcasted_iota(jnp.int32, (HD, PAIR), 1) < HD
    return jnp.where(first, product[:HD], product[HD:])


def head_ones():
    row = lax.broadcasted_iota(jnp.int32, (QUAD, QUAD), 0) // HD
    lane = lax.broadcasted_iota(jnp.int32, (QUAD, QUAD), 1) // HD
    return jnp.where(row == lane, 1.0, 0.0).astype(BF16)


def unit_heads(value, ones):
    squares = mm((value * value).astype(BF16), ones)
    return value * lax.rsqrt(squares + EPS)


def norm_rows(hidden, gain):
    wide = hidden.astype(F32)
    mean_sq = jnp.mean(wide * wide, axis=-1, keepdims=True)
    return (wide * lax.rsqrt(mean_sq + EPS) * gain).astype(BF16)


def spread_rates(normed, w_rate, rate_base):
    rates = rate_base * jax.nn.sigmoid(mm_nt(normed, w_rate))
    high = rates.astype(BF16)
    low = (rates - high.astype(F32)).astype(BF16)
    heads = rates.shape[1]
    row = lax.broadcasted_iota(jnp.int32, (heads, heads * HD), 0)
    lane = lax.broadcasted_iota(jnp.int32, (heads, heads * HD), 1) // HD
    pick = jnp.where(row == lane, 1.0, 0.0).astype(BF16)
    return mm(high, pick) + mm(low, pick)


def start_all(copies):
    for copy in copies:
        copy.start()


def wait_all(copies):
    for copy in copies:
        copy.wait()


def on_section(active, body):
    pl.when(lax.axis_index("section") == active)(body)


def at_pair(places, active):
    pair = lax.axis_index("seq") // 2
    first, last = places[0], places[-1]
    return (lax.axis_index("section") == active) & (pair >= first) & (pair <= last)


def front(here, h_ref, gain_ref, w_ref, w_rate_ref, base_ref, maps, normed_out, keys_out, x_out, y_out, near=None):
    width = keys_out.shape[1]
    quads = width // QUAD

    def body():
        if near is None:
            copies = None
            h_in, gain, w_rate, base, weights, base_lane = h_ref, gain_ref, w_rate_ref, base_ref, w_ref, width
        else:
            h_in, gain, w_rate, base, weights, small_sems, sems = near
            base_lane = 0
            pairs = [(gain_ref, gain), (w_rate_ref, w_rate), (base_ref, base), (h_ref, h_in)]
            small = [pltpu.make_async_copy(source, target, small_sems.at[index]) for index, (source, target) in enumerate(pairs)]
            copies = [
                [
                    pltpu.make_async_copy(
                        w_ref.at[0, :, pl.ds((side + 1) * width + quad * QUAD, QUAD)],
                        weights.at[:, pl.ds(side * width + quad * QUAD, QUAD)],
                        sems.at[quad, side],
                    )
                    for quad in range(quads)
                ]
                for side in range(2)
            ]
            start_all(small)
            start_all(copies[0][:2])
            wait_all(small)
            start_all(copies[0][2:])
        normed = norm_rows(h_in[...], gain[...])
        normed_out[...] = normed
        if copies is not None:
            start_all(copies[1][:2])
        rates = spread_rates(normed, w_rate[0], base[...])
        ones = head_ones()

        def project(side, quad):
            if copies is not None:
                wait_all([copies[side][quad]])
                if (side, quad) == (0, 1):
                    start_all(copies[1][2:])
            lane = base_lane + side * width + quad * QUAD
            return mm(normed, weights[:, lane : lane + QUAD])

        def unit(quad, keys):
            lanes = slice(quad * QUAD, (quad + 1) * QUAD)
            keys = unit_heads(keys, ones)
            keys_bf = keys.astype(BF16)
            keys_out[:, lanes] = keys_bf
            return keys_bf, rates[:, lanes] * keys

        def crossed(quad, keys_bf, x_all):
            return mm_nt(keys_bf[HD:], spread(keys_bf[:HD])).astype(BF16)

        def fixed(quad, cross, values, keys_bf, x_all):
            lanes = slice(quad * QUAD, (quad + 1) * QUAD)
            y_all = rates[:, lanes] * values
            rate = rates[HD:, lanes]
            x_first, y_first = x_all[:HD].astype(BF16), y_all[:HD].astype(BF16)
            fix = mm(cross, spread_two(x_first, y_first))
            x_second = (x_all[HD:] - rate * fix[:, :QUAD]).astype(BF16)
            y_second = (y_all[HD:] - rate * fix[:, QUAD:]).astype(BF16)
            x_bf = jnp.concatenate([x_first, x_second], axis=0)
            y_bf = jnp.concatenate([y_first, y_second], axis=0)
            x_out[:, lanes] = x_bf
            y_out[:, lanes] = y_bf
            return x_bf, y_bf

        def mapped(quad, keys_bf, x_bf, y_bf):
            for half in range(2):
                own = slice(half * PAIR, (half + 1) * PAIR)
                start = quad * QUAD + half * PAIR
                both = mm_tn(keys_bf[:, own], jnp.concatenate([x_bf[:, own], y_bf[:, own]], axis=1))
                maps[:, start : start + PAIR] = diagonal(both[:, :PAIR]).astype(BF16)
                maps[:, width + start : width + start + PAIR] = diagonal(both[:, PAIR:]).astype(BF16)

        picked = range(quads)
        units = [unit(quad, keys) for quad, keys in zip(picked, [project(0, quad) for quad in picked])]
        crosses = [crossed(quad, *value) for quad, value in zip(picked, units)]
        values = [project(1, quad) for quad in picked]
        fixes = [fixed(quad, cross, value, *pair) for quad, cross, value, pair in zip(picked, crosses, values, units)]
        for quad, value, fix in zip(picked, units, fixes):
            mapped(quad, value[0], *fix)

    pl.when(here)(body)


def first_front(h_hbm, gain, weights, w_rate, base, maps, normed_out, keys_out, x_out, y_out, *near):
    here = lax.axis_index("section") == 0
    front(here, h_hbm, gain, weights, w_rate, base, maps, normed_out, keys_out, x_out, y_out, near)


def later_front(places, h_ref, gain, weights, w_rate, base, after_ref, *outs):
    front(at_pair(places, 1), h_ref, gain, weights, w_rate, base, *outs)


def load(*refs):
    count = (len(refs) - 2) // 2
    sources, targets, sems = refs[:count], refs[count + 1 : -1], refs[-1]

    def body():
        copies = [pltpu.make_async_copy(source, target, sems.at[index]) for index, (source, target) in enumerate(zip(sources, targets))]
        start_all(copies)
        wait_all(copies)

    on_section(1, body)


def read_out(active, places, fetches, normed_ref, keys_ref, x_ref, y_ref, weights, w_out_hbm, after_ref, reads_out, *rest):
    rows, width = keys_ref.shape
    *w_out, wq, sems = rest
    half = width // 2

    def body():
        fetch = [pltpu.make_async_copy(w_out_hbm.at[0], target, sems.at[2]) for target in w_out]
        halves = [pl.ds(index * half, half) for index in range(2)] if fetches else []
        late = [pltpu.make_async_copy(weights.at[0, :, lanes], wq.at[:, lanes], sems.at[index]) for index, lanes in enumerate(halves)]
        start_all(late)
        normed = normed_ref[...]
        ones = head_ones()
        row = lax.broadcasted_iota(jnp.int32, (rows, 2 * rows), 0)
        lane = lax.rem(lax.broadcasted_iota(jnp.int32, (rows, 2 * rows), 1), rows)
        causal = row >= lane

        def stages(start, stop, source):
            quads = range(start, stop, QUAD)
            queries = [unit_heads(mm(normed, source[:, lane : lane + QUAD]), ones) for lane in quads]
            parts = [value[:, own : own + PAIR] for value in queries for own in range(0, QUAD, PAIR)]
            places = [slice(lane, lane + PAIR) for lane in range(start, stop, PAIR)]
            scores = [mm_nt(part.astype(BF16), spread(keys_ref[:, place])) for part, place in zip(parts, places)]
            scores = [jnp.where(causal, score, 0.0).astype(BF16) for score in scores]
            both = [mm(score, spread_two(x_ref[:, place], y_ref[:, place])) for score, place in zip(scores, places)]
            for part, place, value in zip(parts, places, both):
                reads_out[:, place] = (part - value[:, :PAIR]).astype(BF16)
                reads_out[:, width + place.start : width + place.stop] = value[:, PAIR:].astype(BF16)

        if fetches:
            wait_all(late[:1])
            start_all(fetch)
            stages(0, half, wq)
            wait_all(late[1:])
            stages(half, width, wq)
            wait_all(fetch)
        else:
            stages(0, width, weights)

    pl.when(at_pair(places, active))(body)


def compose(active, own_ref, got_ref, after_ref, out_ref):
    width = own_ref.shape[1] // 2

    def body(first_ref, second_ref):
        for start in range(0, width, PAIR):
            s_lanes, b_lanes = slice(start, start + PAIR), slice(width + start, width + start + PAIR)
            s_second, s_first, b_first = second_ref[:, s_lanes], first_ref[:, s_lanes], first_ref[:, b_lanes]
            step = mm(s_second, spread_two(s_first, b_first))
            out_ref[:, s_lanes] = (s_second.astype(F32) + s_first.astype(F32) - step[:, :PAIR]).astype(BF16)
            out_ref[:, b_lanes] = (second_ref[:, b_lanes].astype(F32) + b_first.astype(F32) - step[:, PAIR:]).astype(BF16)

    here = lax.axis_index("section") == active
    side = lax.rem(lax.axis_index("seq"), 2)
    pl.when(here & (side == 0))(lambda: body(own_ref, got_ref))
    pl.when(here & (side == 1))(lambda: body(got_ref, own_ref))


def pair_state(init_ref, pair):
    return jnp.concatenate([init_ref[0, 2 * pair], init_ref[0, 2 * pair + 1]], axis=1)


def apply_map(state, ref, start, width):
    step = mm(ref[:, start : start + PAIR], spread(state.astype(BF16)))
    return state - step + ref[:, width + start : width + start + PAIR].astype(F32)


def moved_states(state_of, refs, width):
    starts = range(0, width, PAIR)
    states = [state_of(start) for start in starts]
    for ref in refs:
        states = [apply_map(state, ref, start, width) for state, start in zip(states, starts)]
    return states


def put_states(out_ref, states):
    for index, state in enumerate(states):
        out_ref[:, index * PAIR : (index + 1) * PAIR] = state.astype(BF16)


def advance(active, place, own_ref, got_ref, state_refs, after_ref, out_ref):
    width = out_ref.shape[1]

    def body(state_ref, refs):
        def state_of(start):
            return state_ref[:, start : start + PAIR].astype(F32) if place else pair_state(state_ref, start // PAIR)

        put_states(out_ref, moved_states(state_of, refs, width))

    here = at_pair([place], active)
    side = lax.rem(lax.axis_index("seq"), 2)
    orders = [(own_ref,)] * 2 if got_ref is None else [(own_ref, got_ref), (got_ref, own_ref)]
    if got_ref is None and len(state_refs) == 1:
        pl.when(here)(lambda: body(state_refs[0], orders[0]))
    else:
        pl.when(here & (side == 0))(lambda: body(state_refs[0], orders[0]))
        pl.when(here & (side == 1))(lambda: body(state_refs[-1], orders[1]))


def first_step(own_ref, init_ref, out_ref):
    @pl.when((lax.axis_index("section") == 0) & (lax.axis_index("seq") == 0))
    def _():
        put_states(out_ref, moved_states(lambda start: pair_state(init_ref, start // PAIR), (own_ref,), out_ref.shape[1]))


def second_step(own_ref, state_ref, after_ref, out_ref):
    @pl.when((lax.axis_index("section") == 0) & (lax.axis_index("seq") == 1))
    def _():
        put_states(
            out_ref, moved_states(lambda start: state_ref[:, start : start + PAIR].astype(F32), (own_ref,), out_ref.shape[1])
        )


def finish(here, begins, state_refs, got_ref, reads_ref, w_out_ref, h_ref, store, followed=None):
    width = w_out_ref.shape[0]
    model = h_ref.shape[1]
    chunk = model // 4

    def body():
        follows = lax.rem(lax.axis_index("seq"), 2) == 1
        starts = range(0, width, PAIR)
        if begins:
            states = [pair_state(state_refs[0], start // PAIR) for start in starts]
        else:
            states = [state_refs[0][:, start : start + PAIR].astype(F32) for start in starts]
            for ref in state_refs[1:]:
                others = [ref[:, start : start + PAIR].astype(F32) for start in starts]
                states = [jnp.where(follows, other, state) for other, state in zip(others, states)]
        if followed is None:
            moved = [apply_map(state, got_ref, start, width) for state, start in zip(states, starts)]
        else:
            moved = [followed[:, start : start + PAIR].astype(F32) for start in starts]
        states = [jnp.where(follows, after, state).astype(BF16) for after, state in zip(moved, states)]
        quads = range(0, width, QUAD)
        spreads = [spread(jnp.concatenate(states[start // PAIR : (start + QUAD) // PAIR], axis=1)) for start in quads]
        reads = [mm(reads_ref[:, start : start + QUAD], value) for start, value in zip(quads, spreads)]
        inner_bf = jnp.concatenate(
            [
                (read + reads_ref[:, width + start : width + start + QUAD].astype(F32)).astype(BF16)
                for start, read in zip(quads, reads)
            ],
            axis=1,
        )
        for start in range(0, model, chunk):
            lanes = slice(start, start + chunk)
            store(start, (h_ref[:, lanes].astype(F32) + mm(inner_bf, w_out_ref[:, lanes])).astype(BF16))

    pl.when(here)(body)


def first_finish(place, count, *refs):
    state_refs, (got_ref, reads_ref, w_out_ref, h_ref, after_ref, *rest) = refs[:count][::-1], refs[count:]
    out_ref = rest[-1]

    def store(start, value):
        out_ref[:, start : start + value.shape[1]] = value

    followed = None if place else got_ref
    finish(at_pair([place], 0), place == 0, state_refs, got_ref, reads_ref, w_out_ref, h_ref, store, followed)


def last_finish(count, w_out_ref, *refs):
    states, gots, refs = refs[:count], refs[count : 2 * count], refs[2 * count :]
    reads, hiddens, firsts = [[refs[index]] * (count - 1) + [refs[index + 1]] for index in (0, 2, 4)]
    out_hbm, near, sems = refs[6:]
    chunk = near.shape[1] // 4

    def write(start):
        lanes = pl.ds(start, chunk)
        return pltpu.make_async_copy(near.at[:, lanes], out_hbm.at[0, :, lanes], sems.at[start // chunk])

    def store(start, value):
        near[:, start : start + chunk] = value
        write(start).start()

    for place in range(count):
        finish(at_pair([place], 1), place == 0, [states[place]], gots[place], reads[place], w_out_ref, hiddens[place], store)

        @pl.when(at_pair([place], 0))
        def _():
            for start in range(0, near.shape[1], chunk):
                store(start, firsts[place][:, start : start + chunk])

    for start in range(0, near.shape[1], chunk):
        write(start).wait()


def call(body, outs, scratch, args, kinds=None, name=None, out_kind=pltpu.VMEM, aliases=None):
    specs = [pl.BlockSpec(memory_space=kind) for kind in (kinds or [pltpu.VMEM] * len(args))]
    return pl.pallas_call(
        body,
        out_shape=outs,
        in_specs=specs,
        out_specs=[pl.BlockSpec(memory_space=out_kind)] * len(outs),
        scratch_shapes=scratch,
        input_output_aliases=aliases or {},
        compiler_params=pltpu.CompilerParams(vmem_limit_bytes=VMEM_LIMIT),
        name=name,
    )(*args)


def shards(tokens, norm_gain, w_qkv, w_rate, rate_base, init_state, w_out):
    count = lax.axis_size("seq")
    heads = rate_base.shape[1]
    rows, model = tokens.shape
    width = heads * HD
    depth = w_qkv.shape[1]
    quads = width // QUAD
    shape = jax.ShapeDtypeStruct
    in_vmem = functools.partial(pltpu.with_memory_space_constraint, memory_space=pltpu.VMEM)
    in_hbm = functools.partial(pltpu.with_memory_space_constraint, memory_space=pltpu.HBM)
    maps = shape((HD, 2 * width), BF16)
    rows_out = [shape((rows, model), BF16)] + [shape((rows, width), BF16)] * 3
    w_rate = jnp.swapaxes(w_rate, 1, 2)
    norm_gain, w_qkv, w_rate, rate_base, w_out = [in_hbm(value) for value in (norm_gain, w_qkv, w_rate, rate_base, w_out)]

    def permute(value, active, pairs):
        base = active * count
        return lax.ppermute(value, ("section", "seq"), [(base + source, base + target) for source, target in pairs])

    def swap(own, active, groups):
        return permute(own, active, [(2 * group + side, 2 * group + 1 - side) for group in groups for side in range(2)])

    def layer_reads(active, places, fetches, rows_of, weights, after):
        reads, *w_out_near = call(
            functools.partial(read_out, active, places, fetches),
            [shape((rows, 2 * width), BF16)] + [pltpu.VMEM(w_out.shape[1:], BF16)] * fetches,
            [pltpu.VMEM((depth, width) if fetches else (16, 128), BF16), pltpu.SemaphoreType.DMA((3,))],
            [*rows_of, weights, w_out, after],
            [pltpu.VMEM] * 4 + [pltpu.HBM if fetches else pltpu.VMEM, pltpu.HBM, pl.ANY],
            name=f"reads{active}_{places[0]}",
        )
        return [reads] + [in_vmem(value) for value in w_out_near]

    def hop(active, place, maps_here, states, after):
        count_here = len(maps_here)

        def body(*refs):
            advance(active, place, refs[0], None if count_here == 1 else refs[1], refs[count_here:-2][::-1], *refs[-2:])

        kinds = [pltpu.VMEM] * (count_here + len(states)) + [pl.ANY]
        (ahead,) = call(body, [state_out], [], maps_here + states[::-1] + [after], kinds, name=f"advance{active}_{place}")
        return ahead, [permute(ahead, active, [(2 * place + side, 2 * place + 2 + side) for side in range(2)])]

    state_out = shape((HD, width), BF16)
    groups = count // 2

    own, *rows_of = call(
        first_front,
        [maps] + rows_out,
        [pltpu.VMEM(value.shape, value.dtype) for value in (tokens, norm_gain, w_rate, rate_base)]
        + [pltpu.VMEM((depth, 2 * width), BF16), pltpu.SemaphoreType.DMA((4,)), pltpu.SemaphoreType.DMA((quads, 2))],
        [in_hbm(tokens), norm_gain, w_qkv, w_rate, rate_base],
        [pltpu.HBM] * 5,
        name="first_front",
    )
    (stepped,) = call(first_step, [state_out], [], [own, init_state], name="first_step")
    stepped = permute(stepped, 0, [(0, 1)])
    got_rest = swap(own, 0, range(1, groups))
    read_first = layer_reads(0, [0], 1, rows_of, w_qkv, init_state)
    (ahead,) = call(
        second_step, [state_out], [], [own, stepped, read_first[0]], [pltpu.VMEM] * 2 + [pl.ANY], name="second_step"
    )
    state = [permute(ahead, 0, [(1, 2 + side)]) for side in range(2)]
    read_rest = layer_reads(0, range(1, groups), 1, rows_of, w_qkv, ahead)
    (both,) = call(
        functools.partial(compose, 0), [maps], [], [own, got_rest, read_rest[0]], [pltpu.VMEM] * 2 + [pl.ANY], name="compose"
    )

    params = [norm_gain, w_qkv, w_rate, rate_base, w_out]
    gain_near, w_near, rate_near, base_near, w_out_near = call(
        load,
        [pltpu.VMEM(value.shape, value.dtype) for value in params],
        [pltpu.SemaphoreType.DMA((5,))],
        params + [both],
        [pltpu.HBM] * 5 + [pl.ANY],
        name="load",
    )
    params = [in_vmem(value) for value in (gain_near, w_near.reshape(w_qkv.shape[1:]), rate_near, base_near)]
    w_out_near = in_vmem(w_out_near.reshape(w_out.shape[1:]))

    def begin(places, first, after):
        span = range(2 * places[0], 2 * places[-1] + 2)
        hidden = lax.ppermute(first, ("section", "seq"), [(place, count + place) for place in span])
        own, *rows_of = call(
            functools.partial(later_front, places),
            [maps] + rows_out,
            [],
            [hidden, *params, after],
            [pltpu.VMEM] * 5 + [pl.ANY],
            name=f"later_front_{places[0]}",
        )
        return hidden, own, rows_of, [swap(own, 1, [place]) for place in places]

    here, passed = [init_state], []
    for place in range(groups):
        got, (reads, near) = (got_rest, read_rest) if place else (stepped, read_first)
        if 0 < place < groups - 1:
            ahead, state = hop(0, place, [both], here, passed[0])
        if place + 1 == groups:
            firsts, passed = passed, []
        (first,) = call(
            functools.partial(first_finish, place, len(here)),
            [shape((rows, model), BF16)],
            [],
            [*here[::-1], got, reads, near, tokens, ahead, *passed],
            [pltpu.VMEM] * (len(here) + 4) + [pl.ANY] + [pltpu.VMEM] * len(passed),
            name=f"first_finish_{place}",
            aliases={len(here) + 5: 0} if passed else None,
        )
        passed, here = [first], state
    firsts += passed

    hidden, own_later, rows_later, gots = begin(range(groups - 1), firsts[0], own)
    hiddens, states, after = [hidden], [init_state], own_later
    for place in range(groups - 1):
        if place + 2 == groups:
            hidden, own_last, rows_last, got = begin([groups - 1], firsts[1], after)
            hiddens.append(hidden)
            gots += got
            reads = layer_reads(1, range(groups - 1), 0, rows_later, params[1], after)
            after = reads[0]
        after, state = hop(1, place, [own_later, gots[place]], states[-1:], after)
        states += state
    reads += layer_reads(1, [groups - 1], 0, rows_last, params[1], after)
    (result,) = call(
        functools.partial(last_finish, groups),
        [shape((1, rows, model), BF16)],
        [pltpu.VMEM((rows, model), BF16), pltpu.SemaphoreType.DMA((4,))],
        [w_out_near, *states, *gots, *reads, *hiddens, *firsts],
        name="last_finish",
        out_kind=pltpu.HBM,
    )
    return result


def solution(mesh):
    return jax.shard_map(
        shards,
        mesh=mesh,
        in_specs=(
            P(("traj", "seq"), None),
            P("section", None),
            P("section", None, None),
            P("section", None, None),
            P("section", None),
            P("section", None, None, None),
            P("section", None, None),
        ),
        out_specs=P("section", ("traj", "seq"), None),
        check_vma=False,
    )
```

```python
import functools

import jax
import jax.numpy as jnp
from jax import lax
from jax.experimental import pallas as pl
from jax.experimental.pallas import tpu as pltpu
from jax.sharding import PartitionSpec as P

HD = 64
PAIR = 2 * HD
QUAD = 4 * HD
F32 = jnp.float32
BF16 = jnp.bfloat16
EPS = 1e-6
VMEM_LIMIT = 16 * 1024 * 1024


def mm(a, b):
    return jnp.dot(a, b, preferred_element_type=F32)


def mm_nt(a, b):
    return lax.dot_general(a, b, (((1,), (1,)), ((), ())), preferred_element_type=F32)


def mm_tn(a, b):
    return lax.dot_general(a, b, (((0,), (0,)), ((), ())), preferred_element_type=F32)


def head_masks(rows, lanes):
    lane = lax.broadcasted_iota(jnp.int32, (rows, lanes), 1)
    return [lane // HD == index for index in range(lanes // HD)]


def spread(value):
    zero = jnp.zeros_like(value)
    masks = head_masks(*value.shape)
    return jnp.concatenate([jnp.where(mask, value, zero) for mask in masks], axis=0)


def spread_two(left, right):
    return jnp.concatenate([spread(left), spread(right)], axis=1)


def diagonal(product):
    first = lax.broadcasted_iota(jnp.int32, (HD, PAIR), 1) < HD
    return jnp.where(first, product[:HD], product[HD:])


def head_ones():
    row = lax.broadcasted_iota(jnp.int32, (QUAD, QUAD), 0) // HD
    lane = lax.broadcasted_iota(jnp.int32, (QUAD, QUAD), 1) // HD
    return jnp.where(row == lane, 1.0, 0.0).astype(BF16)


def unit_heads(value, ones):
    squares = mm((value * value).astype(BF16), ones)
    return value * lax.rsqrt(squares + EPS)


def norm_rows(hidden, gain):
    wide = hidden.astype(F32)
    mean_sq = jnp.mean(wide * wide, axis=-1, keepdims=True)
    return (wide * lax.rsqrt(mean_sq + EPS) * gain).astype(BF16)


def spread_rates(normed, w_rate, rate_base):
    rates = rate_base * jax.nn.sigmoid(mm_nt(normed, w_rate))
    high = rates.astype(BF16)
    low = (rates - high.astype(F32)).astype(BF16)
    heads = rates.shape[1]
    row = lax.broadcasted_iota(jnp.int32, (heads, heads * HD), 0)
    lane = lax.broadcasted_iota(jnp.int32, (heads, heads * HD), 1) // HD
    pick = jnp.where(row == lane, 1.0, 0.0).astype(BF16)
    return mm(high, pick) + mm(low, pick)


def start_all(copies):
    for copy in copies:
        copy.start()


def wait_all(copies):
    for copy in copies:
        copy.wait()


def on_section(active, body):
    pl.when(lax.axis_index("section") == active)(body)


def at_pair(places, active):
    pair = lax.axis_index("seq") // 2
    first, last = places[0], places[-1]
    return (lax.axis_index("section") == active) & (pair >= first) & (pair <= last)


def front(here, h_ref, gain_ref, w_ref, w_rate_ref, base_ref, maps, normed_out, keys_out, x_out, y_out, near=None):
    width = keys_out.shape[1]
    quads = width // QUAD

    def body():
        if near is None:
            copies = None
            h_in, gain, w_rate, base, weights, base_lane = h_ref, gain_ref, w_rate_ref, base_ref, w_ref, width
        else:
            h_in, gain, w_rate, base, weights, small_sems, sems = near
            base_lane = 0
            pairs = [(gain_ref, gain), (w_rate_ref, w_rate), (base_ref, base), (h_ref, h_in)]
            small = [pltpu.make_async_copy(source, target, small_sems.at[index]) for index, (source, target) in enumerate(pairs)]
            copies = [
                pltpu.make_async_copy(
                    w_ref.at[0, :, pl.ds((side + 1) * width, width)], weights.at[:, pl.ds(side * width, width)], sems.at[side]
                )
                for side in range(2)
            ]
            start_all(small)
            start_all(copies[:1])
            wait_all(small)
            start_all(copies[1:])
        normed = norm_rows(h_in[...], gain[...])
        normed_out[...] = normed
        rates = spread_rates(normed, w_rate[0], base[...])
        ones = head_ones()

        def project(side, quad):
            if copies is not None and quad == 0:
                wait_all([copies[side]])
            lane = base_lane + side * width + quad * QUAD
            return mm(normed, weights[:, lane : lane + QUAD])

        def unit(quad, keys):
            lanes = slice(quad * QUAD, (quad + 1) * QUAD)
            keys = unit_heads(keys, ones)
            keys_bf = keys.astype(BF16)
            keys_out[:, lanes] = keys_bf
            return keys_bf, rates[:, lanes] * keys

        def crossed(quad, keys_bf, x_all):
            return mm_nt(keys_bf[HD:], spread(keys_bf[:HD])).astype(BF16)

        def fixed(quad, cross, values, keys_bf, x_all):
            lanes = slice(quad * QUAD, (quad + 1) * QUAD)
            y_all = rates[:, lanes] * values
            rate = rates[HD:, lanes]
            x_first, y_first = x_all[:HD].astype(BF16), y_all[:HD].astype(BF16)
            fix = mm(cross, spread_two(x_first, y_first))
            x_second = (x_all[HD:] - rate * fix[:, :QUAD]).astype(BF16)
            y_second = (y_all[HD:] - rate * fix[:, QUAD:]).astype(BF16)
            x_bf = jnp.concatenate([x_first, x_second], axis=0)
            y_bf = jnp.concatenate([y_first, y_second], axis=0)
            x_out[:, lanes] = x_bf
            y_out[:, lanes] = y_bf
            return x_bf, y_bf

        def mapped(quad, keys_bf, x_bf, y_bf):
            for half in range(2):
                own = slice(half * PAIR, (half + 1) * PAIR)
                start = quad * QUAD + half * PAIR
                both = mm_tn(keys_bf[:, own], jnp.concatenate([x_bf[:, own], y_bf[:, own]], axis=1))
                maps[:, start : start + PAIR] = diagonal(both[:, :PAIR]).astype(BF16)
                maps[:, width + start : width + start + PAIR] = diagonal(both[:, PAIR:]).astype(BF16)

        picked = range(quads)
        units = [unit(quad, keys) for quad, keys in zip(picked, [project(0, quad) for quad in picked])]
        crosses = [crossed(quad, *value) for quad, value in zip(picked, units)]
        values = [project(1, quad) for quad in picked]
        fixes = [fixed(quad, cross, value, *pair) for quad, cross, value, pair in zip(picked, crosses, values, units)]
        for quad, value, fix in zip(picked, units, fixes):
            mapped(quad, value[0], *fix)

    pl.when(here)(body)


def first_front(h_hbm, gain, weights, w_rate, base, maps, normed_out, keys_out, x_out, y_out, *near):
    here = lax.axis_index("section") == 0
    front(here, h_hbm, gain, weights, w_rate, base, maps, normed_out, keys_out, x_out, y_out, near)


def later_front(places, h_ref, gain, weights, w_rate, base, after_ref, *outs):
    front(at_pair(places, 1), h_ref, gain, weights, w_rate, base, *outs)


def load(*refs):
    count = (len(refs) - 2) // 2
    sources, targets, sems = refs[:count], refs[count + 1 : -1], refs[-1]

    def body():
        copies = [pltpu.make_async_copy(source, target, sems.at[index]) for index, (source, target) in enumerate(zip(sources, targets))]
        start_all(copies)
        wait_all(copies)

    on_section(1, body)


def read_out(active, places, fetches, normed_ref, keys_ref, x_ref, y_ref, weights, w_out_hbm, after_ref, reads_out, *rest):
    rows, width = keys_ref.shape
    *w_out, wq, sems = rest

    def body():
        fetch = [pltpu.make_async_copy(w_out_hbm.at[0], target, sems.at[1]) for target in w_out]
        late = [pltpu.make_async_copy(weights.at[0, :, pl.ds(0, width)], wq, sems.at[0])] if fetches else []
        start_all(late)
        normed = normed_ref[...]
        ones = head_ones()
        row = lax.broadcasted_iota(jnp.int32, (rows, 2 * rows), 0)
        lane = lax.rem(lax.broadcasted_iota(jnp.int32, (rows, 2 * rows), 1), rows)
        causal = row >= lane

        def stages(start, stop, source):
            quads = range(start, stop, QUAD)
            queries = [unit_heads(mm(normed, source[:, lane : lane + QUAD]), ones) for lane in quads]
            parts = [value[:, own : own + PAIR] for value in queries for own in range(0, QUAD, PAIR)]
            places = [slice(lane, lane + PAIR) for lane in range(start, stop, PAIR)]
            scores = [mm_nt(part.astype(BF16), spread(keys_ref[:, place])) for part, place in zip(parts, places)]
            scores = [jnp.where(causal, score, 0.0).astype(BF16) for score in scores]
            both = [mm(score, spread_two(x_ref[:, place], y_ref[:, place])) for score, place in zip(scores, places)]
            for part, place, value in zip(parts, places, both):
                reads_out[:, place] = (part - value[:, :PAIR]).astype(BF16)
                reads_out[:, width + place.start : width + place.stop] = value[:, PAIR:].astype(BF16)

        if fetches:
            start_all(fetch)
            wait_all(late)
            stages(0, width, wq)
            wait_all(fetch)
        else:
            stages(0, width, weights)

    pl.when(at_pair(places, active))(body)


def compose(active, own_ref, got_ref, after_ref, out_ref):
    width = own_ref.shape[1] // 2

    def body(first_ref, second_ref):
        for start in range(0, width, PAIR):
            s_lanes, b_lanes = slice(start, start + PAIR), slice(width + start, width + start + PAIR)
            s_second, s_first, b_first = second_ref[:, s_lanes], first_ref[:, s_lanes], first_ref[:, b_lanes]
            step = mm(s_second, spread_two(s_first, b_first))
            out_ref[:, s_lanes] = (s_second.astype(F32) + s_first.astype(F32) - step[:, :PAIR]).astype(BF16)
            out_ref[:, b_lanes] = (second_ref[:, b_lanes].astype(F32) + b_first.astype(F32) - step[:, PAIR:]).astype(BF16)

    here = lax.axis_index("section") == active
    side = lax.rem(lax.axis_index("seq"), 2)
    pl.when(here & (side == 0))(lambda: body(own_ref, got_ref))
    pl.when(here & (side == 1))(lambda: body(got_ref, own_ref))


def pair_state(init_ref, pair):
    return jnp.concatenate([init_ref[0, 2 * pair], init_ref[0, 2 * pair + 1]], axis=1)


def apply_map(state, ref, start, width):
    step = mm(ref[:, start : start + PAIR], spread(state.astype(BF16)))
    return state - step + ref[:, width + start : width + start + PAIR].astype(F32)


def moved_states(state_of, refs, width):
    starts = range(0, width, PAIR)
    states = [state_of(start) for start in starts]
    for ref in refs:
        states = [apply_map(state, ref, start, width) for state, start in zip(states, starts)]
    return states


def put_states(out_ref, states):
    for index, state in enumerate(states):
        out_ref[:, index * PAIR : (index + 1) * PAIR] = state.astype(BF16)


def advance(active, place, own_ref, got_ref, state_refs, after_ref, out_ref):
    width = out_ref.shape[1]

    def body(state_ref, refs):
        def state_of(start):
            return state_ref[:, start : start + PAIR].astype(F32) if place else pair_state(state_ref, start // PAIR)

        put_states(out_ref, moved_states(state_of, refs, width))

    here = at_pair([place], active)
    side = lax.rem(lax.axis_index("seq"), 2)
    orders = [(own_ref,)] * 2 if got_ref is None else [(own_ref, got_ref), (got_ref, own_ref)]
    if got_ref is None and len(state_refs) == 1:
        pl.when(here)(lambda: body(state_refs[0], orders[0]))
    else:
        pl.when(here & (side == 0))(lambda: body(state_refs[0], orders[0]))
        pl.when(here & (side == 1))(lambda: body(state_refs[-1], orders[1]))


def first_step(own_ref, init_ref, out_ref):
    @pl.when((lax.axis_index("section") == 0) & (lax.axis_index("seq") == 0))
    def _():
        put_states(out_ref, moved_states(lambda start: pair_state(init_ref, start // PAIR), (own_ref,), out_ref.shape[1]))


def second_step(own_ref, state_ref, after_ref, out_ref):
    @pl.when((lax.axis_index("section") == 0) & (lax.axis_index("seq") == 1))
    def _():
        put_states(
            out_ref, moved_states(lambda start: state_ref[:, start : start + PAIR].astype(F32), (own_ref,), out_ref.shape[1])
        )


def finish(here, begins, state_refs, got_ref, reads_ref, w_out_ref, h_ref, store, followed=None):
    width = w_out_ref.shape[0]
    model = h_ref.shape[1]
    chunk = model // 4

    def body():
        follows = lax.rem(lax.axis_index("seq"), 2) == 1
        starts = range(0, width, PAIR)
        if begins:
            states = [pair_state(state_refs[0], start // PAIR) for start in starts]
        else:
            states = [state_refs[0][:, start : start + PAIR].astype(F32) for start in starts]
            for ref in state_refs[1:]:
                others = [ref[:, start : start + PAIR].astype(F32) for start in starts]
                states = [jnp.where(follows, other, state) for other, state in zip(others, states)]
        if followed is None:
            moved = [apply_map(state, got_ref, start, width) for state, start in zip(states, starts)]
        else:
            moved = [followed[:, start : start + PAIR].astype(F32) for start in starts]
        states = [jnp.where(follows, after, state).astype(BF16) for after, state in zip(moved, states)]
        quads = range(0, width, QUAD)
        spreads = [spread(jnp.concatenate(states[start // PAIR : (start + QUAD) // PAIR], axis=1)) for start in quads]
        reads = [mm(reads_ref[:, start : start + QUAD], value) for start, value in zip(quads, spreads)]
        inner_bf = jnp.concatenate(
            [
                (read + reads_ref[:, width + start : width + start + QUAD].astype(F32)).astype(BF16)
                for start, read in zip(quads, reads)
            ],
            axis=1,
        )
        for start in range(0, model, chunk):
            lanes = slice(start, start + chunk)
            store(start, (h_ref[:, lanes].astype(F32) + mm(inner_bf, w_out_ref[:, lanes])).astype(BF16))

    pl.when(here)(body)


def first_finish(place, count, *refs):
    state_refs, (got_ref, reads_ref, w_out_ref, h_ref, after_ref, *rest) = refs[:count][::-1], refs[count:]
    out_ref = rest[-1]

    def store(start, value):
        out_ref[:, start : start + value.shape[1]] = value

    followed = None if place else got_ref
    finish(at_pair([place], 0), place == 0, state_refs, got_ref, reads_ref, w_out_ref, h_ref, store, followed)


def last_finish(count, w_out_ref, *refs):
    states, gots, refs = refs[:count], refs[count : 2 * count], refs[2 * count :]
    reads, hiddens, firsts = [[refs[index]] * (count - 1) + [refs[index + 1]] for index in (0, 2, 4)]
    out_hbm, near, sems = refs[6:]
    chunk = near.shape[1] // 4

    def write(start):
        lanes = pl.ds(start, chunk)
        return pltpu.make_async_copy(near.at[:, lanes], out_hbm.at[0, :, lanes], sems.at[start // chunk])

    def store(start, value):
        near[:, start : start + chunk] = value
        write(start).start()

    for place in range(count):
        finish(at_pair([place], 1), place == 0, [states[place]], gots[place], reads[place], w_out_ref, hiddens[place], store)

        @pl.when(at_pair([place], 0))
        def _():
            for start in range(0, near.shape[1], chunk):
                store(start, firsts[place][:, start : start + chunk])

    for start in range(0, near.shape[1], chunk):
        write(start).wait()


def call(body, outs, scratch, args, kinds=None, name=None, out_kind=pltpu.VMEM, aliases=None):
    specs = [pl.BlockSpec(memory_space=kind) for kind in (kinds or [pltpu.VMEM] * len(args))]
    return pl.pallas_call(
        body,
        out_shape=outs,
        in_specs=specs,
        out_specs=[pl.BlockSpec(memory_space=out_kind)] * len(outs),
        scratch_shapes=scratch,
        input_output_aliases=aliases or {},
        compiler_params=pltpu.CompilerParams(vmem_limit_bytes=VMEM_LIMIT),
        name=name,
    )(*args)


def shards(tokens, norm_gain, w_qkv, w_rate, rate_base, init_state, w_out):
    count = lax.axis_size("seq")
    heads = rate_base.shape[1]
    rows, model = tokens.shape
    width = heads * HD
    depth = w_qkv.shape[1]
    quads = width // QUAD
    shape = jax.ShapeDtypeStruct
    in_vmem = functools.partial(pltpu.with_memory_space_constraint, memory_space=pltpu.VMEM)
    in_hbm = functools.partial(pltpu.with_memory_space_constraint, memory_space=pltpu.HBM)
    maps = shape((HD, 2 * width), BF16)
    rows_out = [shape((rows, model), BF16)] + [shape((rows, width), BF16)] * 3
    w_rate = jnp.swapaxes(w_rate, 1, 2)
    norm_gain, w_qkv, w_rate, rate_base, w_out = [in_hbm(value) for value in (norm_gain, w_qkv, w_rate, rate_base, w_out)]

    def permute(value, active, pairs):
        base = active * count
        return lax.ppermute(value, ("section", "seq"), [(base + source, base + target) for source, target in pairs])

    def swap(own, active, groups):
        return permute(own, active, [(2 * group + side, 2 * group + 1 - side) for group in groups for side in range(2)])

    def layer_reads(active, places, fetches, rows_of, weights, after):
        reads, *w_out_near = call(
            functools.partial(read_out, active, places, fetches),
            [shape((rows, 2 * width), BF16)] + [pltpu.VMEM(w_out.shape[1:], BF16)] * fetches,
            [pltpu.VMEM((depth, width) if fetches else (16, 128), BF16), pltpu.SemaphoreType.DMA((2,))],
            [*rows_of, weights, w_out, after],
            [pltpu.VMEM] * 4 + [pltpu.HBM if fetches else pltpu.VMEM, pltpu.HBM, pl.ANY],
            name=f"reads{active}_{places[0]}",
        )
        return [reads] + [in_vmem(value) for value in w_out_near]

    def hop(active, place, maps_here, states, after):
        count_here = len(maps_here)

        def body(*refs):
            advance(active, place, refs[0], None if count_here == 1 else refs[1], refs[count_here:-2][::-1], *refs[-2:])

        kinds = [pltpu.VMEM] * (count_here + len(states)) + [pl.ANY]
        (ahead,) = call(body, [state_out], [], maps_here + states[::-1] + [after], kinds, name=f"advance{active}_{place}")
        return ahead, [permute(ahead, active, [(2 * place + side, 2 * place + 2 + side) for side in range(2)])]

    state_out = shape((HD, width), BF16)
    groups = count // 2

    own, *rows_of = call(
        first_front,
        [maps] + rows_out,
        [pltpu.VMEM(value.shape, value.dtype) for value in (tokens, norm_gain, w_rate, rate_base)]
        + [pltpu.VMEM((depth, 2 * width), BF16), pltpu.SemaphoreType.DMA((4,)), pltpu.SemaphoreType.DMA((2,))],
        [in_hbm(tokens), norm_gain, w_qkv, w_rate, rate_base],
        [pltpu.HBM] * 5,
        name="first_front",
    )
    (stepped,) = call(first_step, [state_out], [], [own, init_state], name="first_step")
    stepped = permute(stepped, 0, [(0, 1)])
    got_rest = swap(own, 0, range(1, groups))
    read_first = layer_reads(0, [0], 1, rows_of, w_qkv, init_state)
    (ahead,) = call(
        second_step, [state_out], [], [own, stepped, read_first[0]], [pltpu.VMEM] * 2 + [pl.ANY], name="second_step"
    )
    state = [permute(ahead, 0, [(1, 2 + side)]) for side in range(2)]
    read_rest = layer_reads(0, range(1, groups), 1, rows_of, w_qkv, ahead)
    (both,) = call(
        functools.partial(compose, 0), [maps], [], [own, got_rest, read_rest[0]], [pltpu.VMEM] * 2 + [pl.ANY], name="compose"
    )

    params = [norm_gain, w_qkv, w_rate, rate_base, w_out]
    gain_near, w_near, rate_near, base_near, w_out_near = call(
        load,
        [pltpu.VMEM(value.shape, value.dtype) for value in params],
        [pltpu.SemaphoreType.DMA((5,))],
        params + [both],
        [pltpu.HBM] * 5 + [pl.ANY],
        name="load",
    )
    params = [in_vmem(value) for value in (gain_near, w_near.reshape(w_qkv.shape[1:]), rate_near, base_near)]
    w_out_near = in_vmem(w_out_near.reshape(w_out.shape[1:]))

    def begin(places, first, after):
        span = range(2 * places[0], 2 * places[-1] + 2)
        hidden = lax.ppermute(first, ("section", "seq"), [(place, count + place) for place in span])
        own, *rows_of = call(
            functools.partial(later_front, places),
            [maps] + rows_out,
            [],
            [hidden, *params, after],
            [pltpu.VMEM] * 5 + [pl.ANY],
            name=f"later_front_{places[0]}",
        )
        return hidden, own, rows_of, [swap(own, 1, [place]) for place in places]

    here, passed = [init_state], []
    for place in range(groups):
        got, (reads, near) = (got_rest, read_rest) if place else (stepped, read_first)
        if 0 < place < groups - 1:
            ahead, state = hop(0, place, [both], here, passed[0])
        if place + 1 == groups:
            firsts, passed = passed, []
        (first,) = call(
            functools.partial(first_finish, place, len(here)),
            [shape((rows, model), BF16)],
            [],
            [*here[::-1], got, reads, near, tokens, ahead, *passed],
            [pltpu.VMEM] * (len(here) + 4) + [pl.ANY] + [pltpu.VMEM] * len(passed),
            name=f"first_finish_{place}",
            aliases={len(here) + 5: 0} if passed else None,
        )
        passed, here = [first], state
    firsts += passed

    hidden, own_later, rows_later, gots = begin(range(groups - 1), firsts[0], own)
    hiddens, states, after = [hidden], [init_state], own_later
    for place in range(groups - 1):
        if place + 2 == groups:
            hidden, own_last, rows_last, got = begin([groups - 1], firsts[1], after)
            hiddens.append(hidden)
            gots += got
            reads = layer_reads(1, range(groups - 1), 0, rows_later, params[1], after)
            after = reads[0]
        after, state = hop(1, place, [own_later, gots[place]], states[-1:], after)
        states += state
    reads += layer_reads(1, [groups - 1], 0, rows_last, params[1], after)
    (result,) = call(
        functools.partial(last_finish, groups),
        [shape((1, rows, model), BF16)],
        [pltpu.VMEM((rows, model), BF16), pltpu.SemaphoreType.DMA((4,))],
        [w_out_near, *states, *gots, *reads, *hiddens, *firsts],
        name="last_finish",
        out_kind=pltpu.HBM,
    )
    return result


def solution(mesh):
    return jax.shard_map(
        shards,
        mesh=mesh,
        in_specs=(
            P(("traj", "seq"), None),
            P("section", None),
            P("section", None, None),
            P("section", None, None),
            P("section", None),
            P("section", None, None, None),
            P("section", None, None),
        ),
        out_specs=P("section", ("traj", "seq"), None),
        check_vma=False,
    )
```

```python
import functools

import jax
import jax.numpy as jnp
from jax import lax
from jax.experimental import pallas as pl
from jax.experimental.pallas import tpu as pltpu
from jax.sharding import PartitionSpec as P

HD = 64
PAIR = 2 * HD
QUAD = 4 * HD
F32 = jnp.float32
BF16 = jnp.bfloat16
EPS = 1e-6
VMEM_LIMIT = 16 * 1024 * 1024


def mm(a, b):
    return jnp.dot(a, b, preferred_element_type=F32)


def mm_nt(a, b):
    return lax.dot_general(a, b, (((1,), (1,)), ((), ())), preferred_element_type=F32)


def mm_tn(a, b):
    return lax.dot_general(a, b, (((0,), (0,)), ((), ())), preferred_element_type=F32)


def head_masks(rows, lanes):
    lane = lax.broadcasted_iota(jnp.int32, (rows, lanes), 1)
    return [lane // HD == index for index in range(lanes // HD)]


def spread(value):
    zero = jnp.zeros_like(value)
    masks = head_masks(*value.shape)
    return jnp.concatenate([jnp.where(mask, value, zero) for mask in masks], axis=0)


def spread_two(left, right):
    return jnp.concatenate([spread(left), spread(right)], axis=1)


def diagonal(product):
    first = lax.broadcasted_iota(jnp.int32, (HD, PAIR), 1) < HD
    return jnp.where(first, product[:HD], product[HD:])


def head_ones():
    row = lax.broadcasted_iota(jnp.int32, (QUAD, QUAD), 0) // HD
    lane = lax.broadcasted_iota(jnp.int32, (QUAD, QUAD), 1) // HD
    return jnp.where(row == lane, 1.0, 0.0).astype(BF16)


def unit_heads(value, ones):
    squares = mm((value * value).astype(BF16), ones)
    return value * lax.rsqrt(squares + EPS)


def norm_rows(hidden, gain):
    wide = hidden.astype(F32)
    mean_sq = jnp.mean(wide * wide, axis=-1, keepdims=True)
    return (wide * lax.rsqrt(mean_sq + EPS) * gain).astype(BF16)


def spread_rates(normed, w_rate, rate_base):
    rates = rate_base * jax.nn.sigmoid(mm_nt(normed, w_rate))
    high = rates.astype(BF16)
    low = (rates - high.astype(F32)).astype(BF16)
    heads = rates.shape[1]
    row = lax.broadcasted_iota(jnp.int32, (heads, heads * HD), 0)
    lane = lax.broadcasted_iota(jnp.int32, (heads, heads * HD), 1) // HD
    pick = jnp.where(row == lane, 1.0, 0.0).astype(BF16)
    return mm(high, pick) + mm(low, pick)


def start_all(copies):
    for copy in copies:
        copy.start()


def wait_all(copies):
    for copy in copies:
        copy.wait()


def on_section(active, body):
    pl.when(lax.axis_index("section") == active)(body)


def at_pair(places, active):
    pair = lax.axis_index("seq") // 2
    first, last = places[0], places[-1]
    return (lax.axis_index("section") == active) & (pair >= first) & (pair <= last)


def front(here, h_ref, gain_ref, w_ref, w_rate_ref, base_ref, maps, normed_out, keys_out, x_out, y_out, near=None):
    width = keys_out.shape[1]
    quads = width // QUAD

    def body():
        if near is None:
            copies = None
            h_in, gain, w_rate, base, weights, base_lane = h_ref, gain_ref, w_rate_ref, base_ref, w_ref, width
        else:
            h_in, gain, w_rate, base, weights, small_sems, sems = near
            base_lane = 0
            pairs = [(gain_ref, gain), (w_rate_ref, w_rate), (base_ref, base), (h_ref, h_in)]
            small = [pltpu.make_async_copy(source, target, small_sems.at[index]) for index, (source, target) in enumerate(pairs)]
            copies = [
                pltpu.make_async_copy(
                    w_ref.at[0, :, pl.ds((side + 1) * width, width)], weights.at[:, pl.ds(side * width, width)], sems.at[side]
                )
                for side in range(2)
            ]
            start_all(small)
            start_all(copies[:1])
            wait_all(small)
            start_all(copies[1:])
        normed = norm_rows(h_in[...], gain[...])
        normed_out[...] = normed
        rates = spread_rates(normed, w_rate[0], base[...])
        ones = head_ones()

        def project(side, quad):
            if copies is not None and quad == 0:
                wait_all([copies[side]])
            lane = base_lane + side * width + quad * QUAD
            return mm(normed, weights[:, lane : lane + QUAD])

        def unit(quad, keys):
            lanes = slice(quad * QUAD, (quad + 1) * QUAD)
            keys = unit_heads(keys, ones)
            keys_bf = keys.astype(BF16)
            keys_out[:, lanes] = keys_bf
            return keys_bf, rates[:, lanes] * keys

        def crossed(quad, keys_bf, x_all):
            return mm_nt(keys_bf[HD:], spread(keys_bf[:HD])).astype(BF16)

        def fixed(quad, cross, values, keys_bf, x_all):
            lanes = slice(quad * QUAD, (quad + 1) * QUAD)
            y_all = rates[:, lanes] * values
            rate = rates[HD:, lanes]
            x_first, y_first = x_all[:HD].astype(BF16), y_all[:HD].astype(BF16)
            fix = mm(cross, spread_two(x_first, y_first))
            x_second = (x_all[HD:] - rate * fix[:, :QUAD]).astype(BF16)
            y_second = (y_all[HD:] - rate * fix[:, QUAD:]).astype(BF16)
            x_bf = jnp.concatenate([x_first, x_second], axis=0)
            y_bf = jnp.concatenate([y_first, y_second], axis=0)
            x_out[:, lanes] = x_bf
            y_out[:, lanes] = y_bf
            return x_bf, y_bf

        def mapped(quad, keys_bf, x_bf, y_bf):
            for half in range(2):
                own = slice(half * PAIR, (half + 1) * PAIR)
                start = quad * QUAD + half * PAIR
                both = mm_tn(keys_bf[:, own], jnp.concatenate([x_bf[:, own], y_bf[:, own]], axis=1))
                maps[:, start : start + PAIR] = diagonal(both[:, :PAIR]).astype(BF16)
                maps[:, width + start : width + start + PAIR] = diagonal(both[:, PAIR:]).astype(BF16)

        picked = range(quads)
        units = [unit(quad, keys) for quad, keys in zip(picked, [project(0, quad) for quad in picked])]
        crosses = [crossed(quad, *value) for quad, value in zip(picked, units)]
        values = [project(1, quad) for quad in picked]
        fixes = [fixed(quad, cross, value, *pair) for quad, cross, value, pair in zip(picked, crosses, values, units)]
        for quad, value, fix in zip(picked, units, fixes):
            mapped(quad, value[0], *fix)

    pl.when(here)(body)


def first_front(h_hbm, gain, weights, w_rate, base, maps, normed_out, keys_out, x_out, y_out, *near):
    here = lax.axis_index("section") == 0
    front(here, h_hbm, gain, weights, w_rate, base, maps, normed_out, keys_out, x_out, y_out, near)


def later_front(places, h_ref, gain, weights, w_rate, base, after_ref, *outs):
    front(at_pair(places, 1), h_ref, gain, weights, w_rate, base, *outs)


def load(*refs):
    count = (len(refs) - 2) // 2
    sources, targets, sems = refs[:count], refs[count + 1 : -1], refs[-1]

    def body():
        copies = [pltpu.make_async_copy(source, target, sems.at[index]) for index, (source, target) in enumerate(zip(sources, targets))]
        start_all(copies)
        wait_all(copies)

    on_section(1, body)


def read_out(active, places, fetches, normed_ref, keys_ref, x_ref, y_ref, weights, w_out_hbm, after_ref, reads_out, *rest):
    rows, width = keys_ref.shape
    *w_out, wq, sems = rest

    def body():
        fetch = [pltpu.make_async_copy(w_out_hbm.at[0], target, sems.at[1]) for target in w_out]
        late = [pltpu.make_async_copy(weights.at[0, :, pl.ds(0, width)], wq, sems.at[0])] if fetches else []
        start_all(late)
        normed = normed_ref[...]
        ones = head_ones()
        row = lax.broadcasted_iota(jnp.int32, (rows, 2 * rows), 0)
        lane = lax.rem(lax.broadcasted_iota(jnp.int32, (rows, 2 * rows), 1), rows)
        causal = row >= lane

        def stages(start, stop, source):
            quads = range(start, stop, QUAD)
            queries = [unit_heads(mm(normed, source[:, lane : lane + QUAD]), ones) for lane in quads]
            parts = [value[:, own : own + PAIR] for value in queries for own in range(0, QUAD, PAIR)]
            places = [slice(lane, lane + PAIR) for lane in range(start, stop, PAIR)]
            scores = [mm_nt(part.astype(BF16), spread(keys_ref[:, place])) for part, place in zip(parts, places)]
            scores = [jnp.where(causal, score, 0.0).astype(BF16) for score in scores]
            both = [mm(score, spread_two(x_ref[:, place], y_ref[:, place])) for score, place in zip(scores, places)]
            for part, place, value in zip(parts, places, both):
                reads_out[:, place] = (part - value[:, :PAIR]).astype(BF16)
                reads_out[:, width + place.start : width + place.stop] = value[:, PAIR:].astype(BF16)

        if fetches:
            start_all(fetch)
            wait_all(late)
            stages(0, width, wq)
            wait_all(fetch)
        else:
            stages(0, width, weights)

    pl.when(at_pair(places, active))(body)


def compose(active, places, own_ref, got_ref, after_ref, out_ref):
    width = own_ref.shape[1] // 2

    def body(first_ref, second_ref):
        for start in range(0, width, PAIR):
            s_lanes, b_lanes = slice(start, start + PAIR), slice(width + start, width + start + PAIR)
            s_second, s_first, b_first = second_ref[:, s_lanes], first_ref[:, s_lanes], first_ref[:, b_lanes]
            step = mm(s_second, spread_two(s_first, b_first))
            out_ref[:, s_lanes] = (s_second.astype(F32) + s_first.astype(F32) - step[:, :PAIR]).astype(BF16)
            out_ref[:, b_lanes] = (second_ref[:, b_lanes].astype(F32) + b_first.astype(F32) - step[:, PAIR:]).astype(BF16)

    here = at_pair(places, active)
    side = lax.rem(lax.axis_index("seq"), 2)
    pl.when(here & (side == 0))(lambda: body(own_ref, got_ref))
    pl.when(here & (side == 1))(lambda: body(got_ref, own_ref))


def pair_state(init_ref, pair):
    return jnp.concatenate([init_ref[0, 2 * pair], init_ref[0, 2 * pair + 1]], axis=1)


def apply_map(state, ref, start, width):
    step = mm(ref[:, start : start + PAIR], spread(state.astype(BF16)))
    return state - step + ref[:, width + start : width + start + PAIR].astype(F32)


def moved_states(state_of, refs, width):
    starts = range(0, width, PAIR)
    states = [state_of(start) for start in starts]
    for ref in refs:
        states = [apply_map(state, ref, start, width) for state, start in zip(states, starts)]
    return states


def put_states(out_ref, states):
    for index, state in enumerate(states):
        out_ref[:, index * PAIR : (index + 1) * PAIR] = state.astype(BF16)


def advance(active, place, own_ref, got_ref, state_refs, after_ref, out_ref):
    width = out_ref.shape[1]

    def body(state_ref, refs):
        def state_of(start):
            return state_ref[:, start : start + PAIR].astype(F32) if place else pair_state(state_ref, start // PAIR)

        put_states(out_ref, moved_states(state_of, refs, width))

    here = at_pair([place], active)
    side = lax.rem(lax.axis_index("seq"), 2)
    orders = [(own_ref,)] * 2 if got_ref is None else [(own_ref, got_ref), (got_ref, own_ref)]
    if got_ref is None and len(state_refs) == 1:
        pl.when(here)(lambda: body(state_refs[0], orders[0]))
    else:
        pl.when(here & (side == 0))(lambda: body(state_refs[0], orders[0]))
        pl.when(here & (side == 1))(lambda: body(state_refs[-1], orders[1]))


def first_step(own_ref, init_ref, out_ref):
    @pl.when((lax.axis_index("section") == 0) & (lax.axis_index("seq") == 0))
    def _():
        put_states(out_ref, moved_states(lambda start: pair_state(init_ref, start // PAIR), (own_ref,), out_ref.shape[1]))


def second_step(own_ref, state_ref, after_ref, out_ref):
    @pl.when((lax.axis_index("section") == 0) & (lax.axis_index("seq") == 1))
    def _():
        put_states(
            out_ref, moved_states(lambda start: state_ref[:, start : start + PAIR].astype(F32), (own_ref,), out_ref.shape[1])
        )


def finish(here, begins, state_refs, got_ref, reads_ref, w_out_ref, h_ref, store, followed=None):
    width = w_out_ref.shape[0]
    model = h_ref.shape[1]
    chunk = model // 4

    def body(follows):
        state_ref = state_refs[-1] if follows else state_refs[0]
        starts = range(0, width, PAIR)
        if follows and followed is not None:
            states = [followed[:, start : start + PAIR].astype(F32) for start in starts]
        elif begins:
            states = [pair_state(state_ref, start // PAIR) for start in starts]
        else:
            states = [state_ref[:, start : start + PAIR].astype(F32) for start in starts]
        if follows and followed is None:
            states = [apply_map(state, got_ref, start, width) for state, start in zip(states, starts)]
        states = [state.astype(BF16) for state in states]
        quads = range(0, width, QUAD)
        spreads = [spread(jnp.concatenate(states[start // PAIR : (start + QUAD) // PAIR], axis=1)) for start in quads]
        reads = [mm(reads_ref[:, start : start + QUAD], value) for start, value in zip(quads, spreads)]
        inner_bf = jnp.concatenate(
            [
                (read + reads_ref[:, width + start : width + start + QUAD].astype(F32)).astype(BF16)
                for start, read in zip(quads, reads)
            ],
            axis=1,
        )
        for start in range(0, model, chunk):
            lanes = slice(start, start + chunk)
            store(start, (h_ref[:, lanes].astype(F32) + mm(inner_bf, w_out_ref[:, lanes])).astype(BF16))

    side = lax.rem(lax.axis_index("seq"), 2)
    pl.when(here & (side == 0))(lambda: body(False))
    pl.when(here & (side == 1))(lambda: body(True))


def first_finish(place, count, *refs):
    state_refs, (got_ref, reads_ref, w_out_ref, h_ref, after_ref, *rest) = refs[:count][::-1], refs[count:]
    out_ref = rest[-1]

    def store(start, value):
        out_ref[:, start : start + value.shape[1]] = value

    followed = None if place else got_ref
    finish(at_pair([place], 0), place == 0, state_refs, got_ref, reads_ref, w_out_ref, h_ref, store, followed)


def last_finish(count, w_out_ref, *refs):
    states, gots, refs = refs[:count], refs[count : 2 * count], refs[2 * count :]
    reads, hiddens, firsts = [[refs[index]] * (count - 1) + [refs[index + 1]] for index in (0, 2, 4)]
    out_hbm, near, sems = refs[6:]
    chunk = near.shape[1] // 4

    def write(start):
        lanes = pl.ds(start, chunk)
        return pltpu.make_async_copy(near.at[:, lanes], out_hbm.at[0, :, lanes], sems.at[start // chunk])

    def store(start, value):
        near[:, start : start + chunk] = value
        write(start).start()

    for place in range(count):
        finish(at_pair([place], 1), place == 0, [states[place]], gots[place], reads[place], w_out_ref, hiddens[place], store)

        @pl.when(at_pair([place], 0))
        def _():
            for start in range(0, near.shape[1], chunk):
                store(start, firsts[place][:, start : start + chunk])

    for start in range(0, near.shape[1], chunk):
        write(start).wait()


def call(body, outs, scratch, args, kinds=None, name=None, out_kind=pltpu.VMEM, aliases=None):
    specs = [pl.BlockSpec(memory_space=kind) for kind in (kinds or [pltpu.VMEM] * len(args))]
    return pl.pallas_call(
        body,
        out_shape=outs,
        in_specs=specs,
        out_specs=[pl.BlockSpec(memory_space=out_kind)] * len(outs),
        scratch_shapes=scratch,
        input_output_aliases=aliases or {},
        compiler_params=pltpu.CompilerParams(vmem_limit_bytes=VMEM_LIMIT),
        name=name,
    )(*args)


def shards(tokens, norm_gain, w_qkv, w_rate, rate_base, init_state, w_out):
    count = lax.axis_size("seq")
    heads = rate_base.shape[1]
    rows, model = tokens.shape
    width = heads * HD
    depth = w_qkv.shape[1]
    quads = width // QUAD
    shape = jax.ShapeDtypeStruct
    in_vmem = functools.partial(pltpu.with_memory_space_constraint, memory_space=pltpu.VMEM)
    in_hbm = functools.partial(pltpu.with_memory_space_constraint, memory_space=pltpu.HBM)
    maps = shape((HD, 2 * width), BF16)
    rows_out = [shape((rows, model), BF16)] + [shape((rows, width), BF16)] * 3
    w_rate = jnp.swapaxes(w_rate, 1, 2)
    norm_gain, w_qkv, w_rate, rate_base, w_out = [in_hbm(value) for value in (norm_gain, w_qkv, w_rate, rate_base, w_out)]

    def permute(value, active, pairs):
        base = active * count
        return lax.ppermute(value, ("section", "seq"), [(base + source, base + target) for source, target in pairs])

    def swap(own, active, groups):
        return permute(own, active, [(2 * group + side, 2 * group + 1 - side) for group in groups for side in range(2)])

    def layer_reads(active, places, fetches, rows_of, weights, after):
        reads, *w_out_near = call(
            functools.partial(read_out, active, places, fetches),
            [shape((rows, 2 * width), BF16)] + [pltpu.VMEM(w_out.shape[1:], BF16)] * fetches,
            [pltpu.VMEM((depth, width) if fetches else (16, 128), BF16), pltpu.SemaphoreType.DMA((2,))],
            [*rows_of, weights, w_out, after],
            [pltpu.VMEM] * 4 + [pltpu.HBM if fetches else pltpu.VMEM, pltpu.HBM, pl.ANY],
            name=f"reads{active}_{places[0]}",
        )
        return [reads] + [in_vmem(value) for value in w_out_near]

    def hop(active, place, maps_here, states, after):
        count_here = len(maps_here)

        def body(*refs):
            advance(active, place, refs[0], None if count_here == 1 else refs[1], refs[count_here:-2][::-1], *refs[-2:])

        kinds = [pltpu.VMEM] * (count_here + len(states)) + [pl.ANY]
        (ahead,) = call(body, [state_out], [], maps_here + states[::-1] + [after], kinds, name=f"advance{active}_{place}")
        return ahead, [permute(ahead, active, [(2 * place + side, 2 * place + 2 + side) for side in range(2)])]

    state_out = shape((HD, width), BF16)
    groups = count // 2

    own, *rows_of = call(
        first_front,
        [maps] + rows_out,
        [pltpu.VMEM(value.shape, value.dtype) for value in (tokens, norm_gain, w_rate, rate_base)]
        + [pltpu.VMEM((depth, 2 * width), BF16), pltpu.SemaphoreType.DMA((4,)), pltpu.SemaphoreType.DMA((2,))],
        [in_hbm(tokens), norm_gain, w_qkv, w_rate, rate_base],
        [pltpu.HBM] * 5,
        name="first_front",
    )
    (stepped,) = call(first_step, [state_out], [], [own, init_state], name="first_step")
    stepped = permute(stepped, 0, [(0, 1)])
    got_rest = swap(own, 0, range(1, groups))
    read_first = layer_reads(0, [0], 1, rows_of, w_qkv, init_state)
    (ahead,) = call(
        second_step, [state_out], [], [own, stepped, read_first[0]], [pltpu.VMEM] * 2 + [pl.ANY], name="second_step"
    )
    state = [permute(ahead, 0, [(1, 2 + side)]) for side in range(2)]
    read_rest = layer_reads(0, range(1, groups), 1, rows_of, w_qkv, ahead)
    def composed(active, places, own, got, after):
        (both,) = call(
            functools.partial(compose, active, places),
            [maps],
            [],
            [own, got, after],
            [pltpu.VMEM] * 2 + [pl.ANY],
            name=f"compose{active}_{places[0]}",
        )
        return both

    both = composed(0, range(1, groups), own, got_rest, read_rest[0])

    params = [norm_gain, w_qkv, w_rate, rate_base, w_out]
    gain_near, w_near, rate_near, base_near, w_out_near = call(
        load,
        [pltpu.VMEM(value.shape, value.dtype) for value in params],
        [pltpu.SemaphoreType.DMA((5,))],
        params + [both],
        [pltpu.HBM] * 5 + [pl.ANY],
        name="load",
    )
    params = [in_vmem(value) for value in (gain_near, w_near.reshape(w_qkv.shape[1:]), rate_near, base_near)]
    w_out_near = in_vmem(w_out_near.reshape(w_out.shape[1:]))

    def begin(places, first, after):
        span = range(2 * places[0], 2 * places[-1] + 2)
        hidden = lax.ppermute(first, ("section", "seq"), [(place, count + place) for place in span])
        own, *rows_of = call(
            functools.partial(later_front, places),
            [maps] + rows_out,
            [],
            [hidden, *params, after],
            [pltpu.VMEM] * 5 + [pl.ANY],
            name=f"later_front_{places[0]}",
        )
        return hidden, own, rows_of, [swap(own, 1, [place]) for place in places]

    here, passed = [init_state], []
    for place in range(groups):
        got, (reads, near) = (got_rest, read_rest) if place else (stepped, read_first)
        if 0 < place < groups - 1:
            ahead, state = hop(0, place, [both], here, passed[0])
        if place + 1 == groups:
            firsts, passed = passed, []
        (first,) = call(
            functools.partial(first_finish, place, len(here)),
            [shape((rows, model), BF16)],
            [],
            [*here[::-1], got, reads, near, tokens, ahead, *passed],
            [pltpu.VMEM] * (len(here) + 4) + [pl.ANY] + [pltpu.VMEM] * len(passed),
            name=f"first_finish_{place}",
            aliases={len(here) + 5: 0} if passed else None,
        )
        passed, here = [first], state
    firsts += passed

    hidden, own_later, rows_later, gots = begin(range(groups - 1), firsts[0], own)
    hiddens, states, after = [hidden], [init_state], own_later
    for place in range(groups - 1):
        if place + 2 == groups:
            hidden, own_last, rows_last, got = begin([groups - 1], firsts[1], after)
            hiddens.append(hidden)
            gots += got
            reads = layer_reads(1, range(groups - 1), 0, rows_later, params[1], after)
            after = reads[0]
        own_maps = [composed(1, [place], own_later, gots[place], after)] if place else [own_later, gots[place]]
        after, state = hop(1, place, own_maps, states[-1:], after)
        states += state
    reads += layer_reads(1, [groups - 1], 0, rows_last, params[1], after)
    (result,) = call(
        functools.partial(last_finish, groups),
        [shape((1, rows, model), BF16)],
        [pltpu.VMEM((rows, model), BF16), pltpu.SemaphoreType.DMA((4,))],
        [w_out_near, *states, *gots, *reads, *hiddens, *firsts],
        name="last_finish",
        out_kind=pltpu.HBM,
    )
    return result


def solution(mesh):
    return jax.shard_map(
        shards,
        mesh=mesh,
        in_specs=(
            P(("traj", "seq"), None),
            P("section", None),
            P("section", None, None),
            P("section", None, None),
            P("section", None),
            P("section", None, None, None),
            P("section", None, None),
        ),
        out_specs=P("section", ("traj", "seq"), None),
        check_vma=False,
    )
```

```python
import functools

import jax
import jax.numpy as jnp
from jax import lax
from jax.experimental import pallas as pl
from jax.experimental.pallas import tpu as pltpu
from jax.sharding import PartitionSpec as P

HD = 64
PAIR = 2 * HD
QUAD = 4 * HD
F32 = jnp.float32
BF16 = jnp.bfloat16
EPS = 1e-6
VMEM_LIMIT = 16 * 1024 * 1024


def mm(a, b):
    return jnp.dot(a, b, preferred_element_type=F32)


def mm_nt(a, b):
    return lax.dot_general(a, b, (((1,), (1,)), ((), ())), preferred_element_type=F32)


def mm_tn(a, b):
    return lax.dot_general(a, b, (((0,), (0,)), ((), ())), preferred_element_type=F32)


def head_masks(rows, lanes):
    lane = lax.broadcasted_iota(jnp.int32, (rows, lanes), 1)
    return [lane // HD == index for index in range(lanes // HD)]


def spread(value):
    zero = jnp.zeros_like(value)
    masks = head_masks(*value.shape)
    return jnp.concatenate([jnp.where(mask, value, zero) for mask in masks], axis=0)


def spread_two(left, right):
    return jnp.concatenate([spread(left), spread(right)], axis=1)


def diagonal(product):
    first = lax.broadcasted_iota(jnp.int32, (HD, PAIR), 1) < HD
    return jnp.where(first, product[:HD], product[HD:])


def head_ones():
    row = lax.broadcasted_iota(jnp.int32, (QUAD, QUAD), 0) // HD
    lane = lax.broadcasted_iota(jnp.int32, (QUAD, QUAD), 1) // HD
    return jnp.where(row == lane, 1.0, 0.0).astype(BF16)


def unit_heads(value, ones):
    squares = mm((value * value).astype(BF16), ones)
    return value * lax.rsqrt(squares + EPS)


def norm_rows(hidden, gain):
    wide = hidden.astype(F32)
    mean_sq = jnp.mean(wide * wide, axis=-1, keepdims=True)
    return (wide * lax.rsqrt(mean_sq + EPS) * gain).astype(BF16)


def spread_rates(normed, w_rate, rate_base):
    rates = rate_base * jax.nn.sigmoid(mm_nt(normed, w_rate))
    high = rates.astype(BF16)
    low = (rates - high.astype(F32)).astype(BF16)
    heads = rates.shape[1]
    row = lax.broadcasted_iota(jnp.int32, (heads, heads * HD), 0)
    lane = lax.broadcasted_iota(jnp.int32, (heads, heads * HD), 1) // HD
    pick = jnp.where(row == lane, 1.0, 0.0).astype(BF16)
    return mm(high, pick) + mm(low, pick)


def start_all(copies):
    for copy in copies:
        copy.start()


def wait_all(copies):
    for copy in copies:
        copy.wait()


def on_section(active, body):
    pl.when(lax.axis_index("section") == active)(body)


def at_pair(places, active):
    pair = lax.axis_index("seq") // 2
    first, last = places[0], places[-1]
    return (lax.axis_index("section") == active) & (pair >= first) & (pair <= last)


def front(here, h_ref, gain_ref, w_ref, w_rate_ref, base_ref, maps, normed_out, keys_out, x_out, y_out, near=None):
    width = keys_out.shape[1]
    quads = width // QUAD

    def body():
        if near is None:
            copies = None
            h_in, gain, w_rate, base, weights, base_lane = h_ref, gain_ref, w_rate_ref, base_ref, w_ref, width
        else:
            h_in, gain, w_rate, base, weights, small_sems, sems = near
            base_lane = 0
            pairs = [(gain_ref, gain), (w_rate_ref, w_rate), (base_ref, base), (h_ref, h_in)]
            small = [pltpu.make_async_copy(source, target, small_sems.at[index]) for index, (source, target) in enumerate(pairs)]
            half = width // 2
            cuts = [(0, width), (width, half), (width + half, half)]
            copies = [
                pltpu.make_async_copy(
                    w_ref.at[0, :, pl.ds(width + start, size)], weights.at[:, pl.ds(start, size)], sems.at[index]
                )
                for index, (start, size) in enumerate(cuts)
            ]
            start_all(small)
            start_all(copies[:1])
            wait_all(small)
            start_all(copies[1:2])
        normed = norm_rows(h_in[...], gain[...])
        normed_out[...] = normed
        if copies is not None:
            start_all(copies[2:])
        rates = spread_rates(normed, w_rate[0], base[...])
        ones = head_ones()

        def project(side, quad):
            if copies is not None and quad % (quads // 2) == 0 and (side or quad == 0):
                wait_all([copies[side + (2 * quad) // quads]])
            lane = base_lane + side * width + quad * QUAD
            return mm(normed, weights[:, lane : lane + QUAD])

        def unit(quad, keys):
            lanes = slice(quad * QUAD, (quad + 1) * QUAD)
            keys = unit_heads(keys, ones)
            keys_bf = keys.astype(BF16)
            keys_out[:, lanes] = keys_bf
            return keys_bf, rates[:, lanes] * keys

        def crossed(quad, keys_bf, x_all):
            return mm_nt(keys_bf[HD:], spread(keys_bf[:HD])).astype(BF16)

        def fixed(quad, cross, values, keys_bf, x_all):
            lanes = slice(quad * QUAD, (quad + 1) * QUAD)
            y_all = rates[:, lanes] * values
            rate = rates[HD:, lanes]
            x_first, y_first = x_all[:HD].astype(BF16), y_all[:HD].astype(BF16)
            fix = mm(cross, spread_two(x_first, y_first))
            x_second = (x_all[HD:] - rate * fix[:, :QUAD]).astype(BF16)
            y_second = (y_all[HD:] - rate * fix[:, QUAD:]).astype(BF16)
            x_bf = jnp.concatenate([x_first, x_second], axis=0)
            y_bf = jnp.concatenate([y_first, y_second], axis=0)
            x_out[:, lanes] = x_bf
            y_out[:, lanes] = y_bf
            return x_bf, y_bf

        def mapped(quad, keys_bf, x_bf, y_bf):
            for half in range(2):
                own = slice(half * PAIR, (half + 1) * PAIR)
                start = quad * QUAD + half * PAIR
                both = mm_tn(keys_bf[:, own], jnp.concatenate([x_bf[:, own], y_bf[:, own]], axis=1))
                maps[:, start : start + PAIR] = diagonal(both[:, :PAIR]).astype(BF16)
                maps[:, width + start : width + start + PAIR] = diagonal(both[:, PAIR:]).astype(BF16)

        picked = range(quads)
        units = [unit(quad, keys) for quad, keys in zip(picked, [project(0, quad) for quad in picked])]
        crosses = [crossed(quad, *value) for quad, value in zip(picked, units)]
        values = [project(1, quad) for quad in picked]
        fixes = [fixed(quad, cross, value, *pair) for quad, cross, value, pair in zip(picked, crosses, values, units)]
        for quad, value, fix in zip(picked, units, fixes):
            mapped(quad, value[0], *fix)

    pl.when(here)(body)


def first_front(h_hbm, gain, weights, w_rate, base, maps, normed_out, keys_out, x_out, y_out, *near):
    here = lax.axis_index("section") == 0
    front(here, h_hbm, gain, weights, w_rate, base, maps, normed_out, keys_out, x_out, y_out, near)


def later_front(places, h_ref, gain, weights, w_rate, base, after_ref, *outs):
    front(at_pair(places, 1), h_ref, gain, weights, w_rate, base, *outs)


def load(*refs):
    count = (len(refs) - 2) // 2
    sources, targets, sems = refs[:count], refs[count + 1 : -1], refs[-1]

    def body():
        copies = [pltpu.make_async_copy(source, target, sems.at[index]) for index, (source, target) in enumerate(zip(sources, targets))]
        start_all(copies)
        wait_all(copies)

    on_section(1, body)


def read_out(active, places, fetches, normed_ref, keys_ref, x_ref, y_ref, weights, w_out_hbm, after_ref, reads_out, *rest):
    rows, width = keys_ref.shape
    *w_out, wq, sems = rest

    def body():
        fetch = [pltpu.make_async_copy(w_out_hbm.at[0], target, sems.at[1]) for target in w_out]
        late = [pltpu.make_async_copy(weights.at[0, :, pl.ds(0, width)], wq, sems.at[0])] if fetches else []
        start_all(late)
        normed = normed_ref[...]
        ones = head_ones()
        row = lax.broadcasted_iota(jnp.int32, (rows, 2 * rows), 0)
        lane = lax.rem(lax.broadcasted_iota(jnp.int32, (rows, 2 * rows), 1), rows)
        causal = row >= lane

        def stages(start, stop, source):
            quads = range(start, stop, QUAD)
            queries = [unit_heads(mm(normed, source[:, lane : lane + QUAD]), ones) for lane in quads]
            parts = [value[:, own : own + PAIR] for value in queries for own in range(0, QUAD, PAIR)]
            places = [slice(lane, lane + PAIR) for lane in range(start, stop, PAIR)]
            scores = [mm_nt(part.astype(BF16), spread(keys_ref[:, place])) for part, place in zip(parts, places)]
            scores = [jnp.where(causal, score, 0.0).astype(BF16) for score in scores]
            both = [mm(score, spread_two(x_ref[:, place], y_ref[:, place])) for score, place in zip(scores, places)]
            for part, place, value in zip(parts, places, both):
                reads_out[:, place] = (part - value[:, :PAIR]).astype(BF16)
                reads_out[:, width + place.start : width + place.stop] = value[:, PAIR:].astype(BF16)

        if fetches:
            start_all(fetch)
            wait_all(late)
            stages(0, width, wq)
            wait_all(fetch)
        else:
            stages(0, width, weights)

    pl.when(at_pair(places, active))(body)


def compose(active, places, own_ref, got_ref, after_ref, out_ref):
    width = own_ref.shape[1] // 2

    def body(first_ref, second_ref):
        for start in range(0, width, PAIR):
            s_lanes, b_lanes = slice(start, start + PAIR), slice(width + start, width + start + PAIR)
            s_second, s_first, b_first = second_ref[:, s_lanes], first_ref[:, s_lanes], first_ref[:, b_lanes]
            step = mm(s_second, spread_two(s_first, b_first))
            out_ref[:, s_lanes] = (s_second.astype(F32) + s_first.astype(F32) - step[:, :PAIR]).astype(BF16)
            out_ref[:, b_lanes] = (second_ref[:, b_lanes].astype(F32) + b_first.astype(F32) - step[:, PAIR:]).astype(BF16)

    here = at_pair(places, active)
    side = lax.rem(lax.axis_index("seq"), 2)
    pl.when(here & (side == 0))(lambda: body(own_ref, got_ref))
    pl.when(here & (side == 1))(lambda: body(got_ref, own_ref))


def pair_state(init_ref, pair):
    return jnp.concatenate([init_ref[0, 2 * pair], init_ref[0, 2 * pair + 1]], axis=1)


def apply_map(state, ref, start, width):
    step = mm(ref[:, start : start + PAIR], spread(state.astype(BF16)))
    return state - step + ref[:, width + start : width + start + PAIR].astype(F32)


def moved_states(state_of, refs, width):
    starts = range(0, width, PAIR)
    states = [state_of(start) for start in starts]
    for ref in refs:
        states = [apply_map(state, ref, start, width) for state, start in zip(states, starts)]
    return states


def put_states(out_ref, states):
    for index, state in enumerate(states):
        out_ref[:, index * PAIR : (index + 1) * PAIR] = state.astype(BF16)


def advance(active, place, own_ref, got_ref, state_refs, after_ref, out_ref):
    width = out_ref.shape[1]

    def body(state_ref, refs):
        def state_of(start):
            return state_ref[:, start : start + PAIR].astype(F32) if place else pair_state(state_ref, start // PAIR)

        put_states(out_ref, moved_states(state_of, refs, width))

    here = at_pair([place], active)
    side = lax.rem(lax.axis_index("seq"), 2)
    orders = [(own_ref,)] * 2 if got_ref is None else [(own_ref, got_ref), (got_ref, own_ref)]
    if got_ref is None and len(state_refs) == 1:
        pl.when(here)(lambda: body(state_refs[0], orders[0]))
    else:
        pl.when(here & (side == 0))(lambda: body(state_refs[0], orders[0]))
        pl.when(here & (side == 1))(lambda: body(state_refs[-1], orders[1]))


def first_step(own_ref, init_ref, out_ref):
    @pl.when((lax.axis_index("section") == 0) & (lax.axis_index("seq") == 0))
    def _():
        put_states(out_ref, moved_states(lambda start: pair_state(init_ref, start // PAIR), (own_ref,), out_ref.shape[1]))


def second_step(own_ref, state_ref, after_ref, out_ref):
    @pl.when((lax.axis_index("section") == 0) & (lax.axis_index("seq") == 1))
    def _():
        put_states(
            out_ref, moved_states(lambda start: state_ref[:, start : start + PAIR].astype(F32), (own_ref,), out_ref.shape[1])
        )


def finish(here, begins, state_refs, got_ref, reads_ref, w_out_ref, h_ref, store, followed=None):
    width = w_out_ref.shape[0]
    model = h_ref.shape[1]
    chunk = model // 4

    def body(follows):
        state_ref = state_refs[-1] if follows else state_refs[0]
        starts = range(0, width, PAIR)
        if follows and followed is not None:
            states = [followed[:, start : start + PAIR].astype(F32) for start in starts]
        elif begins:
            states = [pair_state(state_ref, start // PAIR) for start in starts]
        else:
            states = [state_ref[:, start : start + PAIR].astype(F32) for start in starts]
        if follows and followed is None:
            states = [apply_map(state, got_ref, start, width) for state, start in zip(states, starts)]
        states = [state.astype(BF16) for state in states]
        quads = range(0, width, QUAD)
        spreads = [spread(jnp.concatenate(states[start // PAIR : (start + QUAD) // PAIR], axis=1)) for start in quads]
        reads = [mm(reads_ref[:, start : start + QUAD], value) for start, value in zip(quads, spreads)]
        inner_bf = jnp.concatenate(
            [
                (read + reads_ref[:, width + start : width + start + QUAD].astype(F32)).astype(BF16)
                for start, read in zip(quads, reads)
            ],
            axis=1,
        )
        for start in range(0, model, chunk):
            lanes = slice(start, start + chunk)
            store(start, (h_ref[:, lanes].astype(F32) + mm(inner_bf, w_out_ref[:, lanes])).astype(BF16))

    side = lax.rem(lax.axis_index("seq"), 2)
    pl.when(here & (side == 0))(lambda: body(False))
    pl.when(here & (side == 1))(lambda: body(True))


def first_finish(place, count, *refs):
    state_refs, (got_ref, reads_ref, w_out_ref, h_ref, after_ref, *rest) = refs[:count][::-1], refs[count:]
    out_ref = rest[-1]

    def store(start, value):
        out_ref[:, start : start + value.shape[1]] = value

    followed = None if place else got_ref
    finish(at_pair([place], 0), place == 0, state_refs, got_ref, reads_ref, w_out_ref, h_ref, store, followed)


def last_finish(count, w_out_ref, *refs):
    states, gots, refs = refs[:count], refs[count : 2 * count], refs[2 * count :]
    reads, hiddens, firsts = [[refs[index]] * (count - 1) + [refs[index + 1]] for index in (0, 2, 4)]
    out_hbm, near, sems = refs[6:]
    chunk = near.shape[1] // 4

    def write(start):
        lanes = pl.ds(start, chunk)
        return pltpu.make_async_copy(near.at[:, lanes], out_hbm.at[0, :, lanes], sems.at[start // chunk])

    def store(start, value):
        near[:, start : start + chunk] = value
        write(start).start()

    for place in range(count):
        finish(at_pair([place], 1), place == 0, [states[place]], gots[place], reads[place], w_out_ref, hiddens[place], store)

        @pl.when(at_pair([place], 0))
        def _():
            for start in range(0, near.shape[1], chunk):
                store(start, firsts[place][:, start : start + chunk])

    for start in range(0, near.shape[1], chunk):
        write(start).wait()


def call(body, outs, scratch, args, kinds=None, name=None, out_kind=pltpu.VMEM, aliases=None):
    specs = [pl.BlockSpec(memory_space=kind) for kind in (kinds or [pltpu.VMEM] * len(args))]
    return pl.pallas_call(
        body,
        out_shape=outs,
        in_specs=specs,
        out_specs=[pl.BlockSpec(memory_space=out_kind)] * len(outs),
        scratch_shapes=scratch,
        input_output_aliases=aliases or {},
        compiler_params=pltpu.CompilerParams(vmem_limit_bytes=VMEM_LIMIT),
        name=name,
    )(*args)


def shards(tokens, norm_gain, w_qkv, w_rate, rate_base, init_state, w_out):
    count = lax.axis_size("seq")
    heads = rate_base.shape[1]
    rows, model = tokens.shape
    width = heads * HD
    depth = w_qkv.shape[1]
    quads = width // QUAD
    shape = jax.ShapeDtypeStruct
    in_vmem = functools.partial(pltpu.with_memory_space_constraint, memory_space=pltpu.VMEM)
    in_hbm = functools.partial(pltpu.with_memory_space_constraint, memory_space=pltpu.HBM)
    maps = shape((HD, 2 * width), BF16)
    rows_out = [shape((rows, model), BF16)] + [shape((rows, width), BF16)] * 3
    w_rate = jnp.swapaxes(w_rate, 1, 2)
    norm_gain, w_qkv, w_rate, rate_base, w_out = [in_hbm(value) for value in (norm_gain, w_qkv, w_rate, rate_base, w_out)]

    def permute(value, active, pairs):
        base = active * count
        return lax.ppermute(value, ("section", "seq"), [(base + source, base + target) for source, target in pairs])

    def swap(own, active, groups):
        return permute(own, active, [(2 * group + side, 2 * group + 1 - side) for group in groups for side in range(2)])

    def layer_reads(active, places, fetches, rows_of, weights, after):
        reads, *w_out_near = call(
            functools.partial(read_out, active, places, fetches),
            [shape((rows, 2 * width), BF16)] + [pltpu.VMEM(w_out.shape[1:], BF16)] * fetches,
            [pltpu.VMEM((depth, width) if fetches else (16, 128), BF16), pltpu.SemaphoreType.DMA((2,))],
            [*rows_of, weights, w_out, after],
            [pltpu.VMEM] * 4 + [pltpu.HBM if fetches else pltpu.VMEM, pltpu.HBM, pl.ANY],
            name=f"reads{active}_{places[0]}",
        )
        return [reads] + [in_vmem(value) for value in w_out_near]

    def hop(active, place, maps_here, states, after):
        count_here = len(maps_here)

        def body(*refs):
            advance(active, place, refs[0], None if count_here == 1 else refs[1], refs[count_here:-2][::-1], *refs[-2:])

        kinds = [pltpu.VMEM] * (count_here + len(states)) + [pl.ANY]
        (ahead,) = call(body, [state_out], [], maps_here + states[::-1] + [after], kinds, name=f"advance{active}_{place}")
        return ahead, [permute(ahead, active, [(2 * place + side, 2 * place + 2 + side) for side in range(2)])]

    state_out = shape((HD, width), BF16)
    groups = count // 2

    own, *rows_of = call(
        first_front,
        [maps] + rows_out,
        [pltpu.VMEM(value.shape, value.dtype) for value in (tokens, norm_gain, w_rate, rate_base)]
        + [pltpu.VMEM((depth, 2 * width), BF16), pltpu.SemaphoreType.DMA((4,)), pltpu.SemaphoreType.DMA((3,))],
        [in_hbm(tokens), norm_gain, w_qkv, w_rate, rate_base],
        [pltpu.HBM] * 5,
        name="first_front",
    )
    (stepped,) = call(first_step, [state_out], [], [own, init_state], name="first_step")
    stepped = permute(stepped, 0, [(0, 1)])
    got_rest = swap(own, 0, range(1, groups))
    read_first = layer_reads(0, [0], 1, rows_of, w_qkv, init_state)
    (ahead,) = call(
        second_step, [state_out], [], [own, stepped, read_first[0]], [pltpu.VMEM] * 2 + [pl.ANY], name="second_step"
    )
    state = [permute(ahead, 0, [(1, 2 + side)]) for side in range(2)]
    read_rest = layer_reads(0, range(1, groups), 1, rows_of, w_qkv, ahead)
    def composed(active, places, own, got, after):
        (both,) = call(
            functools.partial(compose, active, places),
            [maps],
            [],
            [own, got, after],
            [pltpu.VMEM] * 2 + [pl.ANY],
            name=f"compose{active}_{places[0]}",
        )
        return both

    both = composed(0, range(1, groups), own, got_rest, read_rest[0])

    params = [norm_gain, w_qkv, w_rate, rate_base, w_out]
    gain_near, w_near, rate_near, base_near, w_out_near = call(
        load,
        [pltpu.VMEM(value.shape, value.dtype) for value in params],
        [pltpu.SemaphoreType.DMA((5,))],
        params + [both],
        [pltpu.HBM] * 5 + [pl.ANY],
        name="load",
    )
    params = [in_vmem(value) for value in (gain_near, w_near.reshape(w_qkv.shape[1:]), rate_near, base_near)]
    w_out_near = in_vmem(w_out_near.reshape(w_out.shape[1:]))

    def begin(places, first, after):
        span = range(2 * places[0], 2 * places[-1] + 2)
        hidden = lax.ppermute(first, ("section", "seq"), [(place, count + place) for place in span])
        own, *rows_of = call(
            functools.partial(later_front, places),
            [maps] + rows_out,
            [],
            [hidden, *params, after],
            [pltpu.VMEM] * 5 + [pl.ANY],
            name=f"later_front_{places[0]}",
        )
        return hidden, own, rows_of, [swap(own, 1, [place]) for place in places]

    here, passed = [init_state], []
    for place in range(groups):
        got, (reads, near) = (got_rest, read_rest) if place else (stepped, read_first)
        if 0 < place < groups - 1:
            ahead, state = hop(0, place, [both], here, passed[0])
        if place + 1 == groups:
            firsts, passed = passed, []
        (first,) = call(
            functools.partial(first_finish, place, len(here)),
            [shape((rows, model), BF16)],
            [],
            [*here[::-1], got, reads, near, tokens, ahead, *passed],
            [pltpu.VMEM] * (len(here) + 4) + [pl.ANY] + [pltpu.VMEM] * len(passed),
            name=f"first_finish_{place}",
            aliases={len(here) + 5: 0} if passed else None,
        )
        passed, here = [first], state
    firsts += passed

    hidden, own_later, rows_later, gots = begin(range(groups - 1), firsts[0], own)
    hiddens, states, after = [hidden], [init_state], own_later
    for place in range(groups - 1):
        if place + 2 == groups:
            hidden, own_last, rows_last, got = begin([groups - 1], firsts[1], after)
            hiddens.append(hidden)
            gots += got
            reads = layer_reads(1, range(groups - 1), 0, rows_later, params[1], after)
            after = reads[0]
        own_maps = [composed(1, [place], own_later, gots[place], after)] if place else [own_later, gots[place]]
        after, state = hop(1, place, own_maps, states[-1:], after)
        states += state
    reads += layer_reads(1, [groups - 1], 0, rows_last, params[1], after)
    (result,) = call(
        functools.partial(last_finish, groups),
        [shape((1, rows, model), BF16)],
        [pltpu.VMEM((rows, model), BF16), pltpu.SemaphoreType.DMA((4,))],
        [w_out_near, *states, *gots, *reads, *hiddens, *firsts],
        name="last_finish",
        out_kind=pltpu.HBM,
    )
    return result


def solution(mesh):
    return jax.shard_map(
        shards,
        mesh=mesh,
        in_specs=(
            P(("traj", "seq"), None),
            P("section", None),
            P("section", None, None),
            P("section", None, None),
            P("section", None),
            P("section", None, None, None),
            P("section", None, None),
        ),
        out_specs=P("section", ("traj", "seq"), None),
        check_vma=False,
    )
```

```python
import functools

import jax
import jax.numpy as jnp
from jax import lax
from jax.experimental import pallas as pl
from jax.experimental.pallas import tpu as pltpu
from jax.sharding import PartitionSpec as P

HD = 64
PAIR = 2 * HD
QUAD = 4 * HD
F32 = jnp.float32
BF16 = jnp.bfloat16
EPS = 1e-6
VMEM_LIMIT = 16 * 1024 * 1024


def mm(a, b):
    return jnp.dot(a, b, preferred_element_type=F32)


def mm_nt(a, b):
    return lax.dot_general(a, b, (((1,), (1,)), ((), ())), preferred_element_type=F32)


def mm_tn(a, b):
    return lax.dot_general(a, b, (((0,), (0,)), ((), ())), preferred_element_type=F32)


def head_masks(rows, lanes):
    lane = lax.broadcasted_iota(jnp.int32, (rows, lanes), 1)
    return [lane // HD == index for index in range(lanes // HD)]


def spread(value):
    zero = jnp.zeros_like(value)
    masks = head_masks(*value.shape)
    return jnp.concatenate([jnp.where(mask, value, zero) for mask in masks], axis=0)


def spread_two(left, right):
    return jnp.concatenate([spread(left), spread(right)], axis=1)


def diagonal(product):
    first = lax.broadcasted_iota(jnp.int32, (HD, PAIR), 1) < HD
    return jnp.where(first, product[:HD], product[HD:])


def head_ones():
    row = lax.broadcasted_iota(jnp.int32, (QUAD, QUAD), 0) // HD
    lane = lax.broadcasted_iota(jnp.int32, (QUAD, QUAD), 1) // HD
    return jnp.where(row == lane, 1.0, 0.0).astype(BF16)


def unit_heads(value, ones):
    squares = mm((value * value).astype(BF16), ones)
    return value * lax.rsqrt(squares + EPS)


def norm_rows(hidden, gain):
    wide = hidden.astype(F32)
    mean_sq = jnp.mean(wide * wide, axis=-1, keepdims=True)
    return (wide * lax.rsqrt(mean_sq + EPS) * gain).astype(BF16)


def spread_rates(normed, w_rate, rate_base):
    rates = rate_base * jax.nn.sigmoid(mm_nt(normed, w_rate))
    high = rates.astype(BF16)
    low = (rates - high.astype(F32)).astype(BF16)
    heads = rates.shape[1]
    row = lax.broadcasted_iota(jnp.int32, (heads, heads * HD), 0)
    lane = lax.broadcasted_iota(jnp.int32, (heads, heads * HD), 1) // HD
    pick = jnp.where(row == lane, 1.0, 0.0).astype(BF16)
    return mm(high, pick) + mm(low, pick)


def start_all(copies):
    for copy in copies:
        copy.start()


def wait_all(copies):
    for copy in copies:
        copy.wait()


def on_section(active, body):
    pl.when(lax.axis_index("section") == active)(body)


def at_pair(places, active):
    pair = lax.axis_index("seq") // 2
    first, last = places[0], places[-1]
    return (lax.axis_index("section") == active) & (pair >= first) & (pair <= last)


def front(here, h_ref, gain_ref, w_ref, w_rate_ref, base_ref, maps, normed_out, keys_out, x_out, y_out, near=None):
    width = keys_out.shape[1]
    quads = width // QUAD

    def body():
        if near is None:
            copies = None
            h_in, gain, w_rate, base, weights, base_lane = h_ref, gain_ref, w_rate_ref, base_ref, w_ref, width
        else:
            h_in, gain, w_rate, base, weights, small_sems, sems = near
            base_lane = 0
            pairs = [(gain_ref, gain), (w_rate_ref, w_rate), (base_ref, base), (h_ref, h_in)]
            small = [pltpu.make_async_copy(source, target, small_sems.at[index]) for index, (source, target) in enumerate(pairs)]
            half = width // 2
            cuts = [(index * half, half) for index in range(4)]
            copies = [
                pltpu.make_async_copy(
                    w_ref.at[0, :, pl.ds(width + start, size)], weights.at[:, pl.ds(start, size)], sems.at[index]
                )
                for index, (start, size) in enumerate(cuts)
            ]
            start_all(small)
            start_all(copies[:1])
            wait_all(small)
            start_all(copies[1:3])
        normed = norm_rows(h_in[...], gain[...])
        normed_out[...] = normed
        if copies is not None:
            start_all(copies[3:])
        rates = spread_rates(normed, w_rate[0], base[...])
        ones = head_ones()

        def project(side, quad):
            if copies is not None and quad % (quads // 2) == 0:
                wait_all([copies[2 * side + (2 * quad) // quads]])
            lane = base_lane + side * width + quad * QUAD
            return mm(normed, weights[:, lane : lane + QUAD])

        def unit(quad, keys):
            lanes = slice(quad * QUAD, (quad + 1) * QUAD)
            keys = unit_heads(keys, ones)
            keys_bf = keys.astype(BF16)
            keys_out[:, lanes] = keys_bf
            return keys_bf, rates[:, lanes] * keys

        def crossed(quad, keys_bf, x_all):
            return mm_nt(keys_bf[HD:], spread(keys_bf[:HD])).astype(BF16)

        def fixed(quad, cross, values, keys_bf, x_all):
            lanes = slice(quad * QUAD, (quad + 1) * QUAD)
            y_all = rates[:, lanes] * values
            rate = rates[HD:, lanes]
            x_first, y_first = x_all[:HD].astype(BF16), y_all[:HD].astype(BF16)
            fix = mm(cross, spread_two(x_first, y_first))
            x_second = (x_all[HD:] - rate * fix[:, :QUAD]).astype(BF16)
            y_second = (y_all[HD:] - rate * fix[:, QUAD:]).astype(BF16)
            x_bf = jnp.concatenate([x_first, x_second], axis=0)
            y_bf = jnp.concatenate([y_first, y_second], axis=0)
            x_out[:, lanes] = x_bf
            y_out[:, lanes] = y_bf
            return x_bf, y_bf

        def mapped(quad, keys_bf, x_bf, y_bf):
            for half in range(2):
                own = slice(half * PAIR, (half + 1) * PAIR)
                start = quad * QUAD + half * PAIR
                both = mm_tn(keys_bf[:, own], jnp.concatenate([x_bf[:, own], y_bf[:, own]], axis=1))
                maps[:, start : start + PAIR] = diagonal(both[:, :PAIR]).astype(BF16)
                maps[:, width + start : width + start + PAIR] = diagonal(both[:, PAIR:]).astype(BF16)

        picked = range(quads)
        units = [unit(quad, keys) for quad, keys in zip(picked, [project(0, quad) for quad in picked])]
        crosses = [crossed(quad, *value) for quad, value in zip(picked, units)]
        values = [project(1, quad) for quad in picked]
        fixes = [fixed(quad, cross, value, *pair) for quad, cross, value, pair in zip(picked, crosses, values, units)]
        for quad, value, fix in zip(picked, units, fixes):
            mapped(quad, value[0], *fix)

    pl.when(here)(body)


def first_front(h_hbm, gain, weights, w_rate, base, maps, normed_out, keys_out, x_out, y_out, *near):
    here = lax.axis_index("section") == 0
    front(here, h_hbm, gain, weights, w_rate, base, maps, normed_out, keys_out, x_out, y_out, near)


def later_front(places, h_ref, gain, weights, w_rate, base, after_ref, *outs):
    front(at_pair(places, 1), h_ref, gain, weights, w_rate, base, *outs)


def load(*refs):
    count = (len(refs) - 2) // 2
    sources, targets, sems = refs[:count], refs[count + 1 : -1], refs[-1]

    def body():
        copies = [pltpu.make_async_copy(source, target, sems.at[index]) for index, (source, target) in enumerate(zip(sources, targets))]
        start_all(copies)
        wait_all(copies)

    on_section(1, body)


def read_out(active, places, fetches, normed_ref, keys_ref, x_ref, y_ref, weights, w_out_hbm, after_ref, reads_out, *rest):
    rows, width = keys_ref.shape
    *w_out, wq, sems = rest

    def body():
        fetch = [pltpu.make_async_copy(w_out_hbm.at[0], target, sems.at[1]) for target in w_out]
        late = [pltpu.make_async_copy(weights.at[0, :, pl.ds(0, width)], wq, sems.at[0])] if fetches else []
        start_all(late)
        normed = normed_ref[...]
        ones = head_ones()
        row = lax.broadcasted_iota(jnp.int32, (rows, 2 * rows), 0)
        lane = lax.rem(lax.broadcasted_iota(jnp.int32, (rows, 2 * rows), 1), rows)
        causal = row >= lane

        def stages(start, stop, source):
            quads = range(start, stop, QUAD)
            queries = [unit_heads(mm(normed, source[:, lane : lane + QUAD]), ones) for lane in quads]
            parts = [value[:, own : own + PAIR] for value in queries for own in range(0, QUAD, PAIR)]
            places = [slice(lane, lane + PAIR) for lane in range(start, stop, PAIR)]
            scores = [mm_nt(part.astype(BF16), spread(keys_ref[:, place])) for part, place in zip(parts, places)]
            scores = [jnp.where(causal, score, 0.0).astype(BF16) for score in scores]
            both = [mm(score, spread_two(x_ref[:, place], y_ref[:, place])) for score, place in zip(scores, places)]
            for part, place, value in zip(parts, places, both):
                reads_out[:, place] = (part - value[:, :PAIR]).astype(BF16)
                reads_out[:, width + place.start : width + place.stop] = value[:, PAIR:].astype(BF16)

        if fetches:
            start_all(fetch)
            wait_all(late)
            stages(0, width, wq)
            wait_all(fetch)
        else:
            stages(0, width, weights)

    pl.when(at_pair(places, active))(body)


def compose(active, places, own_ref, got_ref, after_ref, out_ref):
    width = own_ref.shape[1] // 2

    def body(first_ref, second_ref):
        for start in range(0, width, PAIR):
            s_lanes, b_lanes = slice(start, start + PAIR), slice(width + start, width + start + PAIR)
            s_second, s_first, b_first = second_ref[:, s_lanes], first_ref[:, s_lanes], first_ref[:, b_lanes]
            step = mm(s_second, spread_two(s_first, b_first))
            out_ref[:, s_lanes] = (s_second.astype(F32) + s_first.astype(F32) - step[:, :PAIR]).astype(BF16)
            out_ref[:, b_lanes] = (second_ref[:, b_lanes].astype(F32) + b_first.astype(F32) - step[:, PAIR:]).astype(BF16)

    here = at_pair(places, active)
    side = lax.rem(lax.axis_index("seq"), 2)
    pl.when(here & (side == 0))(lambda: body(own_ref, got_ref))
    pl.when(here & (side == 1))(lambda: body(got_ref, own_ref))


def pair_state(init_ref, pair):
    return jnp.concatenate([init_ref[0, 2 * pair], init_ref[0, 2 * pair + 1]], axis=1)


def apply_map(state, ref, start, width):
    step = mm(ref[:, start : start + PAIR], spread(state.astype(BF16)))
    return state - step + ref[:, width + start : width + start + PAIR].astype(F32)


def moved_states(state_of, refs, width):
    starts = range(0, width, PAIR)
    states = [state_of(start) for start in starts]
    for ref in refs:
        states = [apply_map(state, ref, start, width) for state, start in zip(states, starts)]
    return states


def put_states(out_ref, states):
    for index, state in enumerate(states):
        out_ref[:, index * PAIR : (index + 1) * PAIR] = state.astype(BF16)


def advance(active, place, own_ref, got_ref, state_refs, after_ref, out_ref):
    width = out_ref.shape[1]

    def body(state_ref, refs):
        def state_of(start):
            return state_ref[:, start : start + PAIR].astype(F32) if place else pair_state(state_ref, start // PAIR)

        put_states(out_ref, moved_states(state_of, refs, width))

    here = at_pair([place], active)
    side = lax.rem(lax.axis_index("seq"), 2)
    orders = [(own_ref,)] * 2 if got_ref is None else [(own_ref, got_ref), (got_ref, own_ref)]
    if got_ref is None and len(state_refs) == 1:
        pl.when(here)(lambda: body(state_refs[0], orders[0]))
    else:
        pl.when(here & (side == 0))(lambda: body(state_refs[0], orders[0]))
        pl.when(here & (side == 1))(lambda: body(state_refs[-1], orders[1]))


def first_step(own_ref, init_ref, out_ref):
    @pl.when((lax.axis_index("section") == 0) & (lax.axis_index("seq") == 0))
    def _():
        put_states(out_ref, moved_states(lambda start: pair_state(init_ref, start // PAIR), (own_ref,), out_ref.shape[1]))


def second_step(own_ref, state_ref, after_ref, out_ref):
    @pl.when((lax.axis_index("section") == 0) & (lax.axis_index("seq") == 1))
    def _():
        put_states(
            out_ref, moved_states(lambda start: state_ref[:, start : start + PAIR].astype(F32), (own_ref,), out_ref.shape[1])
        )


def finish(here, begins, state_refs, got_ref, reads_ref, w_out_ref, h_ref, store, followed=None):
    width = w_out_ref.shape[0]
    model = h_ref.shape[1]
    chunk = model // 4

    def body(follows):
        state_ref = state_refs[-1] if follows else state_refs[0]
        starts = range(0, width, PAIR)
        if follows and followed is not None:
            states = [followed[:, start : start + PAIR].astype(F32) for start in starts]
        elif begins:
            states = [pair_state(state_ref, start // PAIR) for start in starts]
        else:
            states = [state_ref[:, start : start + PAIR].astype(F32) for start in starts]
        if follows and followed is None:
            states = [apply_map(state, got_ref, start, width) for state, start in zip(states, starts)]
        states = [state.astype(BF16) for state in states]
        quads = range(0, width, QUAD)
        spreads = [spread(jnp.concatenate(states[start // PAIR : (start + QUAD) // PAIR], axis=1)) for start in quads]
        reads = [mm(reads_ref[:, start : start + QUAD], value) for start, value in zip(quads, spreads)]
        inner_bf = jnp.concatenate(
            [
                (read + reads_ref[:, width + start : width + start + QUAD].astype(F32)).astype(BF16)
                for start, read in zip(quads, reads)
            ],
            axis=1,
        )
        for start in range(0, model, chunk):
            lanes = slice(start, start + chunk)
            store(start, (h_ref[:, lanes].astype(F32) + mm(inner_bf, w_out_ref[:, lanes])).astype(BF16))

    side = lax.rem(lax.axis_index("seq"), 2)
    pl.when(here & (side == 0))(lambda: body(False))
    pl.when(here & (side == 1))(lambda: body(True))


def first_finish(place, count, *refs):
    state_refs, (got_ref, reads_ref, w_out_ref, h_ref, after_ref, *rest) = refs[:count][::-1], refs[count:]
    out_ref = rest[-1]

    def store(start, value):
        out_ref[:, start : start + value.shape[1]] = value

    followed = None if place else got_ref
    finish(at_pair([place], 0), place == 0, state_refs, got_ref, reads_ref, w_out_ref, h_ref, store, followed)


def last_finish(count, w_out_ref, *refs):
    states, gots, refs = refs[:count], refs[count : 2 * count], refs[2 * count :]
    reads, hiddens, firsts = [[refs[index]] * (count - 1) + [refs[index + 1]] for index in (0, 2, 4)]
    out_hbm, near, sems = refs[6:]
    chunk = near.shape[1] // 4

    def write(start):
        lanes = pl.ds(start, chunk)
        return pltpu.make_async_copy(near.at[:, lanes], out_hbm.at[0, :, lanes], sems.at[start // chunk])

    def store(start, value):
        near[:, start : start + chunk] = value
        write(start).start()

    for place in range(count):
        finish(at_pair([place], 1), place == 0, [states[place]], gots[place], reads[place], w_out_ref, hiddens[place], store)

        @pl.when(at_pair([place], 0))
        def _():
            for start in range(0, near.shape[1], chunk):
                store(start, firsts[place][:, start : start + chunk])

    for start in range(0, near.shape[1], chunk):
        write(start).wait()


def call(body, outs, scratch, args, kinds=None, name=None, out_kind=pltpu.VMEM, aliases=None):
    specs = [pl.BlockSpec(memory_space=kind) for kind in (kinds or [pltpu.VMEM] * len(args))]
    return pl.pallas_call(
        body,
        out_shape=outs,
        in_specs=specs,
        out_specs=[pl.BlockSpec(memory_space=out_kind)] * len(outs),
        scratch_shapes=scratch,
        input_output_aliases=aliases or {},
        compiler_params=pltpu.CompilerParams(vmem_limit_bytes=VMEM_LIMIT),
        name=name,
    )(*args)


def shards(tokens, norm_gain, w_qkv, w_rate, rate_base, init_state, w_out):
    count = lax.axis_size("seq")
    heads = rate_base.shape[1]
    rows, model = tokens.shape
    width = heads * HD
    depth = w_qkv.shape[1]
    quads = width // QUAD
    shape = jax.ShapeDtypeStruct
    in_vmem = functools.partial(pltpu.with_memory_space_constraint, memory_space=pltpu.VMEM)
    in_hbm = functools.partial(pltpu.with_memory_space_constraint, memory_space=pltpu.HBM)
    maps = shape((HD, 2 * width), BF16)
    rows_out = [shape((rows, model), BF16)] + [shape((rows, width), BF16)] * 3
    w_rate = jnp.swapaxes(w_rate, 1, 2)
    norm_gain, w_qkv, w_rate, rate_base, w_out = [in_hbm(value) for value in (norm_gain, w_qkv, w_rate, rate_base, w_out)]

    def permute(value, active, pairs):
        base = active * count
        return lax.ppermute(value, ("section", "seq"), [(base + source, base + target) for source, target in pairs])

    def swap(own, active, groups):
        return permute(own, active, [(2 * group + side, 2 * group + 1 - side) for group in groups for side in range(2)])

    def layer_reads(active, places, fetches, rows_of, weights, after):
        reads, *w_out_near = call(
            functools.partial(read_out, active, places, fetches),
            [shape((rows, 2 * width), BF16)] + [pltpu.VMEM(w_out.shape[1:], BF16)] * fetches,
            [pltpu.VMEM((depth, width) if fetches else (16, 128), BF16), pltpu.SemaphoreType.DMA((2,))],
            [*rows_of, weights, w_out, after],
            [pltpu.VMEM] * 4 + [pltpu.HBM if fetches else pltpu.VMEM, pltpu.HBM, pl.ANY],
            name=f"reads{active}_{places[0]}",
        )
        return [reads] + [in_vmem(value) for value in w_out_near]

    def hop(active, place, maps_here, states, after):
        count_here = len(maps_here)

        def body(*refs):
            advance(active, place, refs[0], None if count_here == 1 else refs[1], refs[count_here:-2][::-1], *refs[-2:])

        kinds = [pltpu.VMEM] * (count_here + len(states)) + [pl.ANY]
        (ahead,) = call(body, [state_out], [], maps_here + states[::-1] + [after], kinds, name=f"advance{active}_{place}")
        return ahead, [permute(ahead, active, [(2 * place + side, 2 * place + 2 + side) for side in range(2)])]

    state_out = shape((HD, width), BF16)
    groups = count // 2

    own, *rows_of = call(
        first_front,
        [maps] + rows_out,
        [pltpu.VMEM(value.shape, value.dtype) for value in (tokens, norm_gain, w_rate, rate_base)]
        + [pltpu.VMEM((depth, 2 * width), BF16), pltpu.SemaphoreType.DMA((4,)), pltpu.SemaphoreType.DMA((4,))],
        [in_hbm(tokens), norm_gain, w_qkv, w_rate, rate_base],
        [pltpu.HBM] * 5,
        name="first_front",
    )
    (stepped,) = call(first_step, [state_out], [], [own, init_state], name="first_step")
    stepped = permute(stepped, 0, [(0, 1)])
    got_rest = swap(own, 0, range(1, groups))
    read_first = layer_reads(0, [0], 1, rows_of, w_qkv, init_state)
    (ahead,) = call(
        second_step, [state_out], [], [own, stepped, read_first[0]], [pltpu.VMEM] * 2 + [pl.ANY], name="second_step"
    )
    state = [permute(ahead, 0, [(1, 2 + side)]) for side in range(2)]
    read_rest = layer_reads(0, range(1, groups), 1, rows_of, w_qkv, ahead)
    def composed(active, places, own, got, after):
        (both,) = call(
            functools.partial(compose, active, places),
            [maps],
            [],
            [own, got, after],
            [pltpu.VMEM] * 2 + [pl.ANY],
            name=f"compose{active}_{places[0]}",
        )
        return both

    both = composed(0, range(1, groups), own, got_rest, read_rest[0])

    params = [norm_gain, w_qkv, w_rate, rate_base, w_out]
    gain_near, w_near, rate_near, base_near, w_out_near = call(
        load,
        [pltpu.VMEM(value.shape, value.dtype) for value in params],
        [pltpu.SemaphoreType.DMA((5,))],
        params + [both],
        [pltpu.HBM] * 5 + [pl.ANY],
        name="load",
    )
    params = [in_vmem(value) for value in (gain_near, w_near.reshape(w_qkv.shape[1:]), rate_near, base_near)]
    w_out_near = in_vmem(w_out_near.reshape(w_out.shape[1:]))

    def begin(places, first, after):
        span = range(2 * places[0], 2 * places[-1] + 2)
        hidden = lax.ppermute(first, ("section", "seq"), [(place, count + place) for place in span])
        own, *rows_of = call(
            functools.partial(later_front, places),
            [maps] + rows_out,
            [],
            [hidden, *params, after],
            [pltpu.VMEM] * 5 + [pl.ANY],
            name=f"later_front_{places[0]}",
        )
        return hidden, own, rows_of, [swap(own, 1, [place]) for place in places]

    here, passed = [init_state], []
    for place in range(groups):
        got, (reads, near) = (got_rest, read_rest) if place else (stepped, read_first)
        if 0 < place < groups - 1:
            ahead, state = hop(0, place, [both], here, passed[0])
        if place + 1 == groups:
            firsts, passed = passed, []
        (first,) = call(
            functools.partial(first_finish, place, len(here)),
            [shape((rows, model), BF16)],
            [],
            [*here[::-1], got, reads, near, tokens, ahead, *passed],
            [pltpu.VMEM] * (len(here) + 4) + [pl.ANY] + [pltpu.VMEM] * len(passed),
            name=f"first_finish_{place}",
            aliases={len(here) + 5: 0} if passed else None,
        )
        passed, here = [first], state
    firsts += passed

    hidden, own_later, rows_later, gots = begin(range(groups - 1), firsts[0], own)
    hiddens, states, after = [hidden], [init_state], own_later
    for place in range(groups - 1):
        if place + 2 == groups:
            hidden, own_last, rows_last, got = begin([groups - 1], firsts[1], after)
            hiddens.append(hidden)
            gots += got
            reads = layer_reads(1, range(groups - 1), 0, rows_later, params[1], after)
            after = reads[0]
        own_maps = [composed(1, [place], own_later, gots[place], after)] if place else [own_later, gots[place]]
        after, state = hop(1, place, own_maps, states[-1:], after)
        states += state
    reads += layer_reads(1, [groups - 1], 0, rows_last, params[1], after)
    (result,) = call(
        functools.partial(last_finish, groups),
        [shape((1, rows, model), BF16)],
        [pltpu.VMEM((rows, model), BF16), pltpu.SemaphoreType.DMA((4,))],
        [w_out_near, *states, *gots, *reads, *hiddens, *firsts],
        name="last_finish",
        out_kind=pltpu.HBM,
    )
    return result


def solution(mesh):
    return jax.shard_map(
        shards,
        mesh=mesh,
        in_specs=(
            P(("traj", "seq"), None),
            P("section", None),
            P("section", None, None),
            P("section", None, None),
            P("section", None),
            P("section", None, None, None),
            P("section", None, None),
        ),
        out_specs=P("section", ("traj", "seq"), None),
        check_vma=False,
    )
```
